512 devices in a mesh: gx: 64 (over x_hi, z, core), gy: 8 (over y, x_lo).
Axes of the slice: x: 4 (x_hi: 2, x_lo: 2; x = x_hi * 2 + x_lo), y: 4, z: 16, core: 2. Of those that a mesh axis runs over, the one named last changes fastest.
Arguments:
- flow_populations: float32 [19, 128, 16, 1024], P(None, 'gx', None, 'gy'), as said below
- heat_populations: float32 [7, 128, 16, 1024], P(None, 'gx', None, 'gy'), as said below
- flow_weight: float32 [3, 128, 16, 1024], P(None, 'gx', None, 'gy'), may hold values from -48 to 48
- heat_weight: float32 [128, 16, 1024], P('gx', None, 'gy'), may hold values from -192 to 192
- resistance: float32 [128, 16, 1024], P('gx', None, 'gy'), may hold values from 0.05 to 2
- conductivity: float32 [128, 16, 1024], P('gx', None, 'gy'), may hold values from 0.5 to 2
- solid_mask: int32 [128, 16, 1024], P('gx', None, 'gy'), may hold values 0 or 1
Outputs:
- resistance_sensitivity: float32 [128, 16, 1024], P('gx', None, 'gy')
- conductivity_sensitivity: float32 [128, 16, 1024], P('gx', None, 'gy')
The draws below stay inside these ranges and needn't reach their ends.
Inputs may be any that keep to these rules, and one draw needn't show every extreme that they name: `solid_mask`: 1 marks a solid voxel, 0 a fluid one. `flow_populations`: positive. `heat_populations`: positive.
All inputs are finite; a program needn't handle non-finite values. No bound on the sum of `solid_mask` on one device may be relied on, other than what follows from the above.
Results may differ from the reference program's by a relative error of at most 0.0003.
Values sent between devices are 32-bit elements; how exact they have to be, the bound alone decides.
No kernel may reach another device: no remote copies, remote signals or barrier semaphores. Data moves between devices by JAX's collectives and lax.ppermute only.
A program may use at most 64 MiB of HBM per device.

```python
import math
import jax
import jax.numpy as jnp
import numpy as np
from jax import lax

STEPS = 3
CELLS_WIDTHWISE = 128
CELLS_DEPTHWISE = 1024
CELLS_HEIGHTWISE = 16


def velocity_columns():
    velocity = np.array([[0, 0, 0], [1, 0, 0], [-1, 0, 0], [0, 1, 0], [0, -1, 0], [0, 0, 1], [0, 0, -1], [1, 1, 0], [-1, -1, 0], [1, -1, 0], [-1, 1, 0], [1, 0, 1], [-1, 0, -1], [1, 0, -1], [-1, 0, 1], [0, 1, 1], [0, -1, -1], [0, 1, -1], [0, -1, 1]], np.float32)
    weights = np.array([1.0 / 3.0] + [1.0 / 18.0] * 6 + [1.0 / 36.0] * 12, np.float32)
    return (velocity, weights)


def disturbance_grid(key, shape, spread):
    return spread * jax.random.truncated_normal(key, -3.0, 3.0, shape, jnp.float32)


def draw_flow_populations(key, part):
    key = jax.random.fold_in(key, 11)
    key_density, key_drift, key_noise = jax.random.split(key, 3)
    velocity, weights = velocity_columns()
    density = 1.0 + disturbance_grid(key_density, (CELLS_WIDTHWISE, CELLS_HEIGHTWISE, CELLS_DEPTHWISE), 0.05)
    drift = jnp.array([0.08, 0.03, 0.0], jnp.float32)[:, None, None, None] + disturbance_grid(key_drift, (3, CELLS_WIDTHWISE, CELLS_HEIGHTWISE, CELLS_DEPTHWISE), 0.03)
    chosen_heading = velocity[:, 0, None, None, None] * drift[0] + velocity[:, 1, None, None, None] * drift[1] + velocity[:, 2, None, None, None] * drift[2]
    kinetic = drift[0] * drift[0] + drift[1] * drift[1] + drift[2] * drift[2]
    balance = weights[:, None, None, None] * (density + 3.0 * chosen_heading + 4.5 * chosen_heading * chosen_heading - 1.5 * kinetic)
    stochastic_nudge = disturbance_grid(key_noise, (19, CELLS_WIDTHWISE, CELLS_HEIGHTWISE, CELLS_DEPTHWISE), 1.0)
    return balance * (1.0 + 0.1 * stochastic_nudge)


def draw_heat_populations(key, part):
    key = jax.random.fold_in(key, 23)
    tier_seed_handle, key_noise = jax.random.split(key, 2)
    energy_stencil_factors = np.array([0.25] + [0.125] * 6, np.float32)
    warmth_grid = 1.0 + disturbance_grid(tier_seed_handle, (CELLS_WIDTHWISE, CELLS_HEIGHTWISE, CELLS_DEPTHWISE), 0.1)
    stochastic_nudge = disturbance_grid(key_noise, (7, CELLS_WIDTHWISE, CELLS_HEIGHTWISE, CELLS_DEPTHWISE), 1.0)
    return energy_stencil_factors[:, None, None, None] * warmth_grid * (1.0 + 0.1 * stochastic_nudge)


def plant(result, rng, least, top_value):
    longest = result.shape.index(max(result.shape))
    spots = []
    for shift in (0, 1):
        where = [jax.random.randint(jax.random.fold_in(rng, axis), (), 0, length) for axis, length in enumerate(result.shape)]
        where[longest] = (where[longest] + shift) % result.shape[longest]
        spots.append(tuple(where))
    return result.at[spots[0]].set(least).at[spots[1]].set(top_value)


def steps_of(own_key, shape, shards, least, high):
    def one(position, parts):
        steps = jax.random.uniform(jax.random.fold_in(jax.random.fold_in(own_key, 6), position), (parts,), jnp.float32, least / len(shards), high / len(shards))
        return jnp.repeat(jnp.exp(steps), shape[position] // parts).reshape((-1,) + (1,) * (len(shape) - position - 1))

    gain = one(*shards[0])
    for cut in shards[1:]:
        gain = gain * one(*cut)
    return gain


def gaussian(stream_key, extent, width, limit, pieces=(), held_as=jnp.bfloat16):
    level = steps_of(stream_key, extent, pieces, -0.22, 0.18) if pieces else 1.0
    values = jax.random.normal(stream_key, extent, jnp.float32) * width * level
    return jnp.minimum(jnp.maximum(values, -limit), limit).astype(held_as)


def setup_inputs(seed: int = 0) -> dict:
    seeds = jax.random.split(jax.random.key(seed), 8)
    return {
        "flow_populations": draw_flow_populations(jax.random.fold_in(seeds[7], 71), 0),
        "heat_populations": draw_heat_populations(jax.random.fold_in(seeds[7], 71), 0),
        "flow_weight": gaussian(seeds[2], (3, CELLS_WIDTHWISE, CELLS_HEIGHTWISE, CELLS_DEPTHWISE), 8.0, 48.0, ((1, 64), (3, 8)), jnp.float32),
        "heat_weight": gaussian(seeds[3], (CELLS_WIDTHWISE, CELLS_HEIGHTWISE, CELLS_DEPTHWISE), 32.0, 192.0, ((0, 64), (2, 8)), jnp.float32),
        "resistance": jnp.clip(jnp.exp(math.log(2.0) - 3.6888794 * jax.random.uniform(seeds[4], (CELLS_WIDTHWISE, CELLS_HEIGHTWISE, CELLS_DEPTHWISE), jnp.float32) ** steps_of(seeds[4], (CELLS_WIDTHWISE, CELLS_HEIGHTWISE, CELLS_DEPTHWISE), ((0, 64), (2, 8)), -0.2, 0.2)), 0.05, 2.0),
        "conductivity": jnp.clip(jnp.exp(math.log(2.0) - 1.3862944 * jax.random.uniform(seeds[5], (CELLS_WIDTHWISE, CELLS_HEIGHTWISE, CELLS_DEPTHWISE), jnp.float32) ** steps_of(seeds[5], (CELLS_WIDTHWISE, CELLS_HEIGHTWISE, CELLS_DEPTHWISE), ((0, 64), (2, 8)), -0.2, 0.2)), 0.5, 2.0),
        "solid_mask": plant((jax.random.randint(seeds[6], (CELLS_WIDTHWISE, CELLS_HEIGHTWISE, CELLS_DEPTHWISE), 0, 3) < 1).astype(jnp.int32), jax.random.fold_in(seeds[6], 1), 0, 1),
    }


GHOST_RATE = 1.2
HEAT_RATE = 1.4

def lattice_tables():
    velocity = np.array([[0, 0, 0], [1, 0, 0], [-1, 0, 0], [0, 1, 0], [0, -1, 0], [0, 0, 1], [0, 0, -1], [1, 1, 0], [-1, -1, 0], [1, -1, 0], [-1, 1, 0], [1, 0, 1], [-1, 0, -1], [1, 0, -1], [-1, 0, 1], [0, 1, 1], [0, -1, -1], [0, 1, -1], [0, -1, 1]], np.int64)
    weights = np.array([1.0 / 3.0] + [1.0 / 18.0] * 6 + [1.0 / 36.0] * 12, np.float32)
    energy_stencil_factors = np.array([0.25] + [0.125] * 6, np.float32)
    dot_table = (velocity @ velocity.T).astype(np.float32)
    lengths = np.sum(velocity * velocity, axis=1).astype(np.float32)
    stress_map = (4.5 * weights[:, None] * (dot_table * dot_table - lengths[None, :] / 3.0)).astype(np.float32)
    flux_map = (4.0 * energy_stencil_factors[:, None] * dot_table[:7, :7]).astype(np.float32)
    opposite = np.array([0, 2, 1, 4, 3, 6, 5, 8, 7, 10, 9, 12, 11, 14, 13, 16, 15, 18, 17])
    return (velocity, weights, energy_stencil_factors, stress_map, flux_map, opposite)

def full_velocity():
    velocity = lattice_tables()[0]
    return np.concatenate([velocity, velocity[:7]], axis=0)

def collide(flow_part, energy_share, resistance, conductivity, solid_cells):
    velocity, weights, energy_stencil_factors, stress_map, flux_map, opposite = lattice_tables()
    highest = lax.Precision.HIGHEST
    vel_float = velocity.astype(np.float32)
    momentum = jnp.einsum('qa,qxzy->axzy', vel_float, flow_part, precision=highest)
    density = lax.optimization_barrier(jnp.sum(flow_part, axis=0))
    warmth_grid = lax.optimization_barrier(jnp.sum(energy_share, axis=0))
    fluid_cells = 1.0 - solid_cells
    velocity_field = momentum * (fluid_cells / (1.0 + resistance))
    chosen_heading = jnp.einsum('qa,axzy->qxzy', vel_float, velocity_field, precision=highest)
    kinetic = lax.optimization_barrier(jnp.sum(velocity_field * velocity_field, axis=0))
    equilibrium = weights[:, None, None, None] * (density + 3.0 * chosen_heading + 4.5 * chosen_heading * chosen_heading - 1.5 * kinetic)
    excess = flow_part - equilibrium
    stress = jnp.einsum('iq,qxzy->ixzy', stress_map, excess, precision=highest)
    momentum_diffusivity = 0.1 * jnp.exp(-2.0 * (warmth_grid - 1.0))
    shear_rate = 1.0 / (0.5 + 3.0 * momentum_diffusivity)
    relaxed = equilibrium + (1.0 - shear_rate) * stress + (1.0 - GHOST_RATE) * (excess - stress)
    bounced = flow_part[opposite]
    flow_post = solid_cells * bounced + fluid_cells * relaxed
    energy_balanced_populations = energy_stencil_factors[:, None, None, None] * warmth_grid * (1.0 + 4.0 * chosen_heading[:7])
    heat_excess = energy_share - energy_balanced_populations
    heat_flux = jnp.einsum('iq,qxzy->ixzy', flux_map, heat_excess, precision=highest)
    flux_rate = 1.0 / (0.5 + 0.4 * conductivity)
    heat_post = energy_balanced_populations + (1.0 - flux_rate) * heat_flux + (1.0 - HEAT_RATE) * (heat_excess - heat_flux)
    return (flow_post, heat_post)

def stream(lattice_state, direction):
    velocity_table = full_velocity() * direction
    shifted = []
    for member in range(velocity_table.shape[0]):
        step_x, step_y, step_z = (int(entry_value) for entry_value in velocity_table[member])
        shifted.append(jnp.roll(lattice_state[member], (step_x, step_z, step_y), axis=(0, 1, 2)))
    return jnp.stack(shifted)

def objective_seed(flow_weight, heat_weight):
    vel_float = lattice_tables()[0].astype(np.float32)
    flow_seed = jnp.einsum('qa,axzy->qxzy', vel_float, flow_weight, precision=lax.Precision.HIGHEST)
    heat_seed = jnp.broadcast_to(heat_weight[None], (7,) + heat_weight.shape)
    return jnp.concatenate([flow_seed, heat_seed], axis=0)

def reference(flow_populations, heat_populations, flow_weight, heat_weight, resistance, conductivity, solid_mask):
    solid_cells = solid_mask.astype(jnp.float32)
    lattice_state = jnp.concatenate([flow_populations, heat_populations], axis=0)
    history = []
    for section_index in range(STEPS):
        history.append(lattice_state)
        if section_index + 1 < STEPS:
            flow_post, heat_post = collide(lattice_state[:19], lattice_state[19:], resistance, conductivity, solid_cells)
            lattice_state = stream(jnp.concatenate([flow_post, heat_post], axis=0), 1)
    adjoint = objective_seed(flow_weight, heat_weight)
    resistance_sensitivity = jnp.zeros_like(resistance)
    conductivity_sensitivity = jnp.zeros_like(conductivity)

    def local_step(flow_part, energy_share, resist_field, conduct_field):
        return collide(flow_part, energy_share, resist_field, conduct_field, solid_cells)
    for section_index in reversed(range(STEPS)):
        arrived = stream(adjoint, -1)
        saved_state = history[section_index]
        unused, pullback = jax.vjp(local_step, saved_state[:19], saved_state[19:], resistance, conductivity)
        flow_back, heat_back, resist_back, conduct_back = pullback((arrived[:19], arrived[19:]))
        adjoint = jnp.concatenate([flow_back, heat_back], axis=0)
        resistance_sensitivity = resistance_sensitivity + resist_back
        conductivity_sensitivity = conductivity_sensitivity + conduct_back
    return (resistance_sensitivity, conductivity_sensitivity)
```

```python
import jax
import jax.numpy as jnp
import numpy as np
from jax import lax
from jax.experimental import pallas as pl
from jax.experimental.pallas import tpu as pltpu
from jax.sharding import PartitionSpec as P

ZED = 16
LANES = 128
WIDE = 2 * LANES
EDGE = 4

FLOW_VELOCITY = [
    (0, 0, 0),
    (1, 0, 0),
    (-1, 0, 0),
    (0, 1, 0),
    (0, -1, 0),
    (0, 0, 1),
    (0, 0, -1),
    (1, 1, 0),
    (-1, -1, 0),
    (1, -1, 0),
    (-1, 1, 0),
    (1, 0, 1),
    (-1, 0, -1),
    (1, 0, -1),
    (-1, 0, 1),
    (0, 1, 1),
    (0, -1, -1),
    (0, 1, -1),
    (0, -1, 1),
]
VELOCITY = FLOW_VELOCITY + FLOW_VELOCITY[:7]
MEMBERS = len(VELOCITY)
RIGHTWARD = [q for q in range(MEMBERS) if VELOCITY[q][0] == 1]
LEFTWARD = [q for q in range(MEMBERS) if VELOCITY[q][0] == -1]
LEVEL = [q for q in range(MEMBERS) if VELOCITY[q][0] == 0]

MOBILITY, RATE, WEIGHT = MEMBERS, MEMBERS + 1, MEMBERS + 2
FIELDS = MEMBERS + 6

SLOTS = LANES // (2 * EDGE)
STRIP_ROWS = 2 * FIELDS // SLOTS
ADJ_ROWS = -(-MEMBERS // SLOTS)


def rows_of(entries):
    return {entry: row for row, entry in enumerate(entries)}


SIDE_FIELDS = list(range(MEMBERS, FIELDS))
TO_RIGHT = rows_of(
    [(q, 0) for q in RIGHTWARD] + [(q, 1) for q in RIGHTWARD + LEVEL] + [(k, 1) for k in SIDE_FIELDS]
)
TO_LEFT = rows_of(
    [(q, 1) for q in LEFTWARD] + [(q, 0) for q in LEFTWARD + LEVEL] + [(k, 0) for k in SIDE_FIELDS]
)
ADJ_TO_RIGHT = rows_of([(q, 0) for q in LEFTWARD] + [(q, 1) for q in LEFTWARD + LEVEL])
ADJ_TO_LEFT = rows_of([(q, 1) for q in RIGHTWARD] + [(q, 0) for q in RIGHTWARD + LEVEL])
BULK_ROWS = len(TO_RIGHT)
ADJ_BULK = len(ADJ_TO_RIGHT)


def pair_sums(f):
    total = [f[2 * k + 1] + f[2 * k + 2] for k in range(9)]
    gap = [f[2 * k + 1] - f[2 * k + 2] for k in range(9)]
    return total, gap


def flow_moments(f):
    s, d = pair_sums(f)
    xy, xz, yz = s[3] + s[4], s[5] + s[6], s[7] + s[8]
    rho = f[0] + (s[0] + s[1] + s[2]) + (xy + xz + yz)
    j = (
        d[0] + (d[3] + d[4]) + (d[5] + d[6]),
        d[1] + (d[3] - d[4]) + (d[7] + d[8]),
        d[2] + (d[5] - d[6]) + (d[7] - d[8]),
    )
    second = (s[0] + xy + xz, s[1] + xy + yz, s[2] + xz + yz, s[3] - s[4], s[5] - s[6], s[7] - s[8])
    return rho, j, second


def heat_moments(g):
    temperature = g[0] + (g[1] + g[2]) + (g[3] + g[4]) + (g[5] + g[6])
    return temperature, (g[1] - g[2], g[3] - g[4], g[5] - g[6])


def common(f, g, mobility):
    rho, j, second = flow_moments(f)
    temperature, flux = heat_moments(g)
    u = tuple(mobility * jk for jk in j)
    square = (u[0] * u[0], u[1] * u[1], u[2] * u[2])
    third = rho * (1.0 / 3.0)
    stress = (
        second[0] - third - square[0],
        second[1] - third - square[1],
        second[2] - third - square[2],
        second[3] - u[0] * u[1],
        second[4] - u[0] * u[2],
        second[5] - u[1] * u[2],
    )
    decay = jnp.exp(-2.0 * (temperature - 1.0))
    omega = 1.0 / (0.5 + 0.3 * decay)
    return rho, j, u, square, stress, temperature, flux, decay, omega


def collide(f, g, mobility, rate):
    rho, _, u, square, stress, temperature, flux, _, omega = common(f, g, mobility)
    solid = mobility == 0.0
    lam = 1.2 - omega
    trace = stress[0] + stress[1] + stress[2]
    base = 1.2 * rho - 1.8 * (square[0] + square[1] + square[2]) - (1.5 * lam) * trace
    scale = 4.5 * lam
    mxx = 5.4 * square[0] + scale * stress[0]
    myy = 5.4 * square[1] + scale * stress[1]
    mzz = 5.4 * square[2] + scale * stress[2]
    mxy = 2.0 * (5.4 * (u[0] * u[1]) + scale * stress[3])
    mxz = 2.0 * (5.4 * (u[0] * u[2]) + scale * stress[4])
    myz = 2.0 * (5.4 * (u[1] * u[2]) + scale * stress[5])
    bx, by, bz = base + mxx, base + myy, base + mzz
    sxy, sxz, syz = bx + myy, bx + mzz, by + mzz
    even = [bx, by, bz, sxy + mxy, sxy - mxy, sxz + mxz, sxz - mxz, syz + myz, syz - myz]
    odd = [u[0], u[1], u[2], u[0] + u[1], u[0] - u[1], u[0] + u[2], u[0] - u[2], u[1] + u[2], u[1] - u[2]]
    flow = [None] * 19
    flow[0] = jnp.where(solid, f[0], (1.0 / 3.0) * base - 0.2 * f[0])
    for k in range(9):
        a, b = 2 * k + 1, 2 * k + 2
        w = 1.0 / 18.0 if k < 3 else 1.0 / 36.0
        e, o = w * even[k], (3.6 * w) * odd[k]
        flow[a] = jnp.where(solid, f[b], (e + o) - 0.2 * f[a])
        flow[b] = jnp.where(solid, f[a], (e - o) - 0.2 * f[b])
    keep = 0.5 * (1.4 - rate)
    push = (0.5 * rate) * temperature
    warm = 0.175 * temperature
    heat = [0.35 * temperature - 0.4 * g[0]]
    for k in range(3):
        along = keep * flux[k] + push * u[k]
        heat.append((warm + along) - 0.4 * g[2 * k + 1])
        heat.append((warm - along) - 0.4 * g[2 * k + 2])
    return flow + heat


def pull_back(f, g, fa, ga, mobility, rate, wanted, sensitivity):
    rho, j, u, square, stress, temperature, flux, decay, omega = common(f, g, mobility)
    solid = mobility == 0.0
    lam = 1.2 - omega
    s, d = pair_sums(fa)
    w = 1.0 / 36.0
    xy, xz, yz = s[3] + s[4], s[5] + s[6], s[7] + s[8]
    s2 = (s[0] + s[0], s[1] + s[1], s[2] + s[2])
    mass = w * (12.0 * fa[0] + (s2[0] + s2[1] + s2[2]) + (xy + xz + yz))
    px = w * ((d[0] + d[0]) + (d[3] + d[4]) + (d[5] + d[6]))
    py = w * ((d[1] + d[1]) + (d[3] - d[4]) + (d[7] + d[8]))
    pz = w * ((d[2] + d[2]) + (d[5] - d[6]) + (d[7] - d[8]))
    rxx, ryy, rzz = w * (s2[0] + xy + xz), w * (s2[1] + xy + yz), w * (s2[2] + xz + yz)
    rxy, rxz, ryz = w * (s[3] - s[4]), w * (s[5] - s[6]), w * (s[7] - s[8])
    shift = 1.5 * mass
    dxx, dyy, dzz = 4.5 * rxx - shift, 4.5 * ryy - shift, 4.5 * rzz - shift
    dxy, dxz, dyz = 4.5 * rxy, 4.5 * rxz, 4.5 * ryz
    lam_bar = (
        dxx * stress[0]
        + dyy * stress[1]
        + dzz * stress[2]
        + 2.0 * (dxy * stress[3] + dxz * stress[4] + dyz * stress[5])
    )
    mix = 2.4 - 2.0 * lam
    b = ((ga[1] - ga[2]) * 0.125, (ga[3] - ga[4]) * 0.125, (ga[5] - ga[6]) * 0.125)
    push = (4.0 * rate) * temperature
    ux = 3.6 * px + mix * (dxx * u[0] + dxy * u[1] + dxz * u[2]) + push * b[0]
    uy = 3.6 * py + mix * (dxy * u[0] + dyy * u[1] + dyz * u[2]) + push * b[1]
    uz = 3.6 * pz + mix * (dxz * u[0] + dyz * u[1] + dzz * u[2]) + push * b[2]
    result = {}
    if wanted:
        rho_bar = 1.2 * mass - (1.5 * lam) * ((rxx + ryy + rzz) - mass)
        jx, jy, jz = mobility * ux, mobility * uy, mobility * uz
        ex, ey, ez = lam * dxx, lam * dyy, lam * dzz
        exy, exz, eyz = (2.0 * lam) * dxy, (2.0 * lam) * dxz, (2.0 * lam) * dyz
        hx, hy, hz = rho_bar + ex, rho_bar + ey, rho_bar + ez
        gxy, gxz, gyz = hx + ey, hx + ez, hy + ez
        even = [hx, hy, hz, gxy + exy, gxy - exy, gxz + exz, gxz - exz, gyz + eyz, gyz - eyz]
        odd = [jx, jy, jz, jx + jy, jx - jy, jx + jz, jx - jz, jy + jz, jy - jz]
        if 0 in wanted:
            result[0] = jnp.where(solid, fa[0], rho_bar - 0.2 * fa[0])
        for k in range(9):
            p, m = 2 * k + 1, 2 * k + 2
            if p in wanted:
                result[p] = jnp.where(solid, fa[m], (even[k] + odd[k]) - 0.2 * fa[p])
            if m in wanted:
                result[m] = jnp.where(solid, fa[p], (even[k] - odd[k]) - 0.2 * fa[m])
        warm = (
            0.35 * ga[0]
            + 0.175 * ((ga[1] + ga[2]) + (ga[3] + ga[4]) + (ga[5] + ga[6]))
            + (4.0 * rate) * (b[0] * u[0] + b[1] * u[1] + b[2] * u[2])
            - jnp.where(solid, 0.0, lam_bar * (0.6 * decay) * (omega * omega))
        )
        keep = 5.6 - 4.0 * rate
        if 19 in wanted:
            result[19] = warm - 0.4 * ga[0]
        for k in range(3):
            along = keep * b[k]
            p, m = 2 * k + 1, 2 * k + 2
            if 19 + p in wanted:
                result[19 + p] = (warm + along) - 0.4 * ga[p]
            if 19 + m in wanted:
                result[19 + m] = (warm - along) - 0.4 * ga[m]
    if sensitivity:
        by_resistance = -(mobility * mobility) * (ux * j[0] + uy * j[1] + uz * j[2])
        bent = (
            b[0] * (temperature * u[0] - flux[0])
            + b[1] * (temperature * u[1] - flux[1])
            + b[2] * (temperature * u[2] - flux[2])
        )
        by_conductivity = (-1.6 * (rate * rate)) * bent
        result["by"] = (by_resistance, by_conductivity)
    return result


def turn(value, by, axis):
    count = value.shape[axis]
    by %= count
    return pltpu.roll(value, by, axis) if by else value


def pack(value, slot):
    return turn(value, 2 * EDGE * slot + EDGE, 1)


def unpack(row, slot):
    return turn(row, -EDGE - 2 * EDGE * slot, 1)


def pack_rows(values):
    lane = lax.broadcasted_iota(jnp.int32, (ZED, LANES), 1)
    rows = []
    for start in range(0, len(values), SLOTS):
        row = None
        for slot, value in enumerate(values[start : start + SLOTS]):
            part = pack(value, slot)
            row = part if row is None else jnp.where(lane >= 2 * EDGE * slot, part, row)
        rows.append(row)
    return rows


def halves():
    return [pl.ds(0, 8), pl.ds(8, 8)]


def first_kernel(flow, heat, flow_weight, heat_weight, resistance, conductivity, solid, own, sides, right, left, strip):
    for c in range(2):
        for z in halves():
            mobility = jnp.where(solid[c, z, :] != 0, 0.0, 1.0 / (1.0 + resistance[c, z, :]))
            rate = 1.0 / (0.5 + 0.4 * conductivity[c, z, :])
            f = [flow[q, c, z, :] for q in range(19)]
            g = [heat[q, c, z, :] for q in range(7)]
            after = collide(f, g, mobility, rate)
            sides[0, c, z, :] = mobility
            sides[1, c, z, :] = rate
            more = [mobility, rate] + [flow_weight[k, c, z, :] for k in range(3)] + [heat_weight[c, z, :]]
            for k, value in enumerate(after + more):
                if k < MEMBERS:
                    own[k, c, z, :] = value
                if (k, c) in TO_RIGHT:
                    right[TO_RIGHT[k, c], z, :] = value
                if (k, c) in TO_LEFT:
                    left[TO_LEFT[k, c], z, :] = value
    values = []
    for c in range(2):
        values += [own[q, c] for q in range(MEMBERS)]
        values += [sides[0, c], sides[1, c]]
        values += [flow_weight[k, c] for k in range(3)] + [heat_weight[c]]
    for row, value in enumerate(pack_rows(values)):
        strip[row] = value


def merge_kernel(from_left, from_right, right_in, left_in, right, left, strip):
    del right_in, left_in
    lane = lax.broadcasted_iota(jnp.int32, (ZED, LANES), 1)
    low = lane % (2 * EDGE) < EDGE
    for row in range(STRIP_ROWS):
        value = jnp.where(low, from_left[row], from_right[row])
        right[row] = value
        left[row] = value
        strip[row] = value


def wide_field(k, column, own_value, strip, from_left, from_right):
    if column < 0:
        c, bulk, rows = column + 2, from_left, TO_RIGHT
        strips, start = from_left, BULK_ROWS
    elif column > 1:
        c, bulk, rows = column - 2, from_right, TO_LEFT
        strips, start = from_right, BULK_ROWS
    else:
        c, bulk, rows = column, None, None
        strips, start = strip, 0
    main = own_value(k, c) if bulk is None else bulk[rows[k, c]]
    place = c * FIELDS + k
    beside = unpack(strips[start + place // SLOTS], place % SLOTS)
    return jnp.concatenate([main, beside], axis=1)


def moved(value, velocity, way):
    _, step_y, step_z = velocity
    return turn(turn(value, way * step_z, 0), way * step_y, 1)


def tiles(lanes):
    return [(z, pl.ds(t, LANES)) for z in halves() for t in range(0, lanes, LANES)]


def second_kernel(
    own, sides, flow_weight, heat_weight, strip, from_left, from_right,
    state, wide_sides, adjoint, by_resistance, by_conductivity, right, left,
    after, later, seed,
):
    def own_value(k, c):
        if k < MEMBERS:
            return own[k, c]
        if k < WEIGHT:
            return sides[k - MOBILITY, c]
        return flow_weight[k - WEIGHT, c] if k < WEIGHT + 3 else heat_weight[c]

    def wide(k, column):
        return wide_field(k, column, own_value, strip, from_left, from_right)

    for column in range(-1, 3):
        i = column + 1
        wide_sides[0, i] = wide(MOBILITY, column)
        wide_sides[1, i] = wide(RATE, column)
        for q in range(MEMBERS):
            state[q, i] = moved(wide(q, column - VELOCITY[q][0]), VELOCITY[q], 1)
    for i in range(4):
        for z, y in tiles(WIDE):
            f = [state[q, i, z, y] for q in range(19)]
            g = [state[19 + q, i, z, y] for q in range(7)]
            result = collide(f, g, wide_sides[0, i, z, y], wide_sides[1, i, z, y])
            for q in range(MEMBERS):
                if 0 <= i - 1 + VELOCITY[q][0] <= 1:
                    after[q, i, z, y] = result[q]
    for c in range(2):
        for q in range(MEMBERS):
            later[q, c] = moved(after[q, c + 1 - VELOCITY[q][0]], VELOCITY[q], 1)
    for column in range(-1, 3):
        weights = [wide(WEIGHT + k, column) for k in range(4)]
        for q in range(1, MEMBERS):
            velocity = VELOCITY[q]
            c = column - velocity[0]
            if not 0 <= c <= 1:
                continue
            if q < 19:
                parts = [weights[k] if velocity[k] > 0 else -weights[k] for k in range(3) if velocity[k]]
                value = parts[0] if len(parts) == 1 else parts[0] + parts[1]
            else:
                value = weights[3]
            seed[q, c] = moved(value, velocity, -1)
    for c in range(2):
        for z, y in tiles(WIDE):
            f = [later[q, c, z, y] for q in range(19)]
            g = [later[19 + q, c, z, y] for q in range(7)]
            fa = [jnp.zeros((8, LANES), jnp.float32)] + [seed[q, c, z, y] for q in range(1, 19)]
            ga = [seed[19 + q, c, z, y] for q in range(7)]
            inner = y.start == 0
            result = pull_back(
                f, g, fa, ga, wide_sides[0, c + 1, z, y], wide_sides[1, c + 1, z, y], range(MEMBERS), inner
            )
            if inner:
                by_resistance[c, z, :], by_conductivity[c, z, :] = result["by"]
            for q in range(MEMBERS):
                adjoint[q, c, z, y] = result[q]
                if inner and (q, c) in ADJ_TO_RIGHT:
                    right[ADJ_TO_RIGHT[q, c], z, :] = result[q]
                if inner and (q, c) in ADJ_TO_LEFT:
                    left[ADJ_TO_LEFT[q, c], z, :] = result[q]
    for side, rows in ((right, ADJ_TO_RIGHT), (left, ADJ_TO_LEFT)):
        values = [adjoint[q, c, :, LANES:] for q, c in rows]
        for row, value in enumerate(pack_rows(values)):
            side[ADJ_BULK + row] = value


def third_kernel(
    flow, heat, state, wide_sides, adjoint, part_resistance, part_conductivity, from_left, from_right,
    by_resistance, by_conductivity,
    arrived, earlier, last,
):
    def wide(q, column):
        if 0 <= column <= 1:
            return adjoint[q, column]
        c, bulk, rows = (column + 2, from_left, ADJ_TO_RIGHT) if column < 0 else (column - 2, from_right, ADJ_TO_LEFT)
        place = rows[q, c]
        beside = unpack(bulk[ADJ_BULK + place // SLOTS], place % SLOTS)
        return jnp.concatenate([bulk[place], beside], axis=1)

    for column in range(-1, 3):
        for q in range(MEMBERS):
            arrived[q, column + 1] = moved(wide(q, column + VELOCITY[q][0]), VELOCITY[q], -1)
    for column in range(-1, 3):
        i = column + 1
        for z, y in tiles(WIDE):
            inner = y.start == 0
            own = 0 <= column <= 1
            wanted = [
                q
                for q in range(MEMBERS)
                if 0 <= column - VELOCITY[q][0] <= 1 and (inner or VELOCITY[q][1])
            ]
            f = [state[q, i, z, y] for q in range(19)]
            g = [state[19 + q, i, z, y] for q in range(7)]
            fa = [arrived[q, i, z, y] for q in range(19)]
            ga = [arrived[19 + q, i, z, y] for q in range(7)]
            result = pull_back(
                f, g, fa, ga, wide_sides[0, i, z, y], wide_sides[1, i, z, y], wanted, inner and own
            )
            for q in wanted:
                earlier[q, i, z, y] = result[q]
            if inner and own:
                by_resistance[column, z, :] = part_resistance[column, z, :] + result["by"][0]
                by_conductivity[column, z, :] = part_conductivity[column, z, :] + result["by"][1]
    for c in range(2):
        for q in range(MEMBERS):
            velocity = VELOCITY[q]
            source = earlier[q, c + 1 + velocity[0]] if velocity[1] else earlier[q, c + 1 + velocity[0], :, :LANES]
            last[q, c] = moved(source, velocity, -1)[:, :LANES]
    for c in range(2):
        for z in halves():
            f = [flow[q, c, z, :] for q in range(19)]
            g = [heat[q, c, z, :] for q in range(7)]
            fa = [last[q, c, z, :] for q in range(19)]
            ga = [last[19 + q, c, z, :] for q in range(7)]
            narrow = pl.ds(0, LANES)
            result = pull_back(
                f, g, fa, ga, wide_sides[0, c + 1, z, narrow], wide_sides[1, c + 1, z, narrow], (), True
            )
            by_resistance[c, z, :] += result["by"][0]
            by_conductivity[c, z, :] += result["by"][1]


def floats(*shape):
    return jax.ShapeDtypeStruct(shape, jnp.float32)


def neighbours(value, axis):
    count = lax.axis_size(axis)
    up = [(i, (i + 1) % count) for i in range(count)]
    return up, [(target, source) for source, target in up]


PARAMS = pltpu.CompilerParams(vmem_limit_bytes=24 * 1024 * 1024)


def on_device(flow, heat, flow_weight, heat_weight, resistance, conductivity, solid):
    own, sides, right, left, strip = pl.pallas_call(
        first_kernel,
        out_shape=(
            floats(MEMBERS, 2, ZED, LANES),
            floats(2, 2, ZED, LANES),
            floats(BULK_ROWS + STRIP_ROWS, ZED, LANES),
            floats(BULK_ROWS + STRIP_ROWS, ZED, LANES),
            floats(STRIP_ROWS, ZED, LANES),
        ),
        compiler_params=PARAMS,
        name="collide_own",
    )(flow, heat, flow_weight, heat_weight, resistance, conductivity, solid)

    up, down = neighbours(strip, "gy")
    strip_left = lax.ppermute(strip, "gy", up)
    strip_right = lax.ppermute(strip, "gy", down)

    whole = pl.BlockSpec((STRIP_ROWS, ZED, LANES), lambda i: (0, 0, 0))
    tail = pl.BlockSpec((STRIP_ROWS, ZED, LANES), lambda i: (BULK_ROWS // STRIP_ROWS, 0, 0))
    anywhere = pl.BlockSpec(memory_space=pl.ANY)
    right, left, strip = pl.pallas_call(
        merge_kernel,
        grid=(1,),
        in_specs=[whole, whole, anywhere, anywhere],
        out_specs=[tail, tail, whole],
        out_shape=(
            floats(BULK_ROWS + STRIP_ROWS, ZED, LANES),
            floats(BULK_ROWS + STRIP_ROWS, ZED, LANES),
            floats(STRIP_ROWS, ZED, LANES),
        ),
        input_output_aliases={2: 0, 3: 1},
        name="merge_strips",
    )(strip_left, strip_right, right, left)

    up, down = neighbours(right, "gx")
    from_left = lax.ppermute(right, "gx", up)
    from_right = lax.ppermute(left, "gx", down)

    state, wide_sides, adjoint, part_resistance, part_conductivity, right, left = pl.pallas_call(
        second_kernel,
        out_shape=(
            floats(MEMBERS, 4, ZED, WIDE),
            floats(2, 4, ZED, WIDE),
            floats(MEMBERS, 2, ZED, WIDE),
            floats(2, ZED, LANES),
            floats(2, ZED, LANES),
            floats(ADJ_BULK + ADJ_ROWS, ZED, LANES),
            floats(ADJ_BULK + ADJ_ROWS, ZED, LANES),
        ),
        scratch_shapes=[
            pltpu.VMEM((MEMBERS, 4, ZED, WIDE), jnp.float32),
            pltpu.VMEM((MEMBERS, 2, ZED, WIDE), jnp.float32),
            pltpu.VMEM((MEMBERS, 2, ZED, WIDE), jnp.float32),
        ],
        compiler_params=PARAMS,
        name="forward_and_seed",
    )(own, sides, flow_weight, heat_weight, strip, from_left, from_right)

    from_left = lax.ppermute(right, "gx", up)
    from_right = lax.ppermute(left, "gx", down)

    return pl.pallas_call(
        third_kernel,
        out_shape=(floats(2, ZED, LANES), floats(2, ZED, LANES)),
        scratch_shapes=[
            pltpu.VMEM((MEMBERS, 4, ZED, WIDE), jnp.float32),
            pltpu.VMEM((MEMBERS, 4, ZED, WIDE), jnp.float32),
            pltpu.VMEM((MEMBERS, 2, ZED, LANES), jnp.float32),
        ],
        compiler_params=PARAMS,
        name="adjoint_steps",
    )(flow, heat, state, wide_sides, adjoint, part_resistance, part_conductivity, from_left, from_right)


def solution(mesh):
    split = P("gx", None, "gy")
    stacked = P(None, "gx", None, "gy")
    return jax.shard_map(
        on_device,
        mesh=mesh,
        in_specs=(stacked, stacked, stacked, split, split, split, split),
        out_specs=(split, split),
        check_vma=False,
    )
```

```python
import jax
import jax.numpy as jnp
import numpy as np
from jax import lax
from jax.experimental import pallas as pl
from jax.experimental.pallas import tpu as pltpu
from jax.sharding import PartitionSpec as P

ZED = 16
LANES = 128
WIDE = 2 * LANES
EDGE = 4

FLOW_VELOCITY = [
    (0, 0, 0),
    (1, 0, 0),
    (-1, 0, 0),
    (0, 1, 0),
    (0, -1, 0),
    (0, 0, 1),
    (0, 0, -1),
    (1, 1, 0),
    (-1, -1, 0),
    (1, -1, 0),
    (-1, 1, 0),
    (1, 0, 1),
    (-1, 0, -1),
    (1, 0, -1),
    (-1, 0, 1),
    (0, 1, 1),
    (0, -1, -1),
    (0, 1, -1),
    (0, -1, 1),
]
VELOCITY = FLOW_VELOCITY + FLOW_VELOCITY[:7]
MEMBERS = len(VELOCITY)
RIGHTWARD = [q for q in range(MEMBERS) if VELOCITY[q][0] == 1]
LEFTWARD = [q for q in range(MEMBERS) if VELOCITY[q][0] == -1]
LEVEL = [q for q in range(MEMBERS) if VELOCITY[q][0] == 0]

MOBILITY, RATE, WEIGHT = MEMBERS, MEMBERS + 1, MEMBERS + 2
FIELDS = MEMBERS + 6

SLOTS = LANES // (2 * EDGE)
STRIP_ROWS = 2 * FIELDS // SLOTS
HALF_ROWS = STRIP_ROWS // 2
ADJ_ROWS = -(-MEMBERS // SLOTS)


def rows_of(entries):
    return {entry: row for row, entry in enumerate(entries)}


SIDE_FIELDS = list(range(MEMBERS, FIELDS))
TO_RIGHT = rows_of(
    [(q, 0) for q in RIGHTWARD] + [(q, 1) for q in RIGHTWARD + LEVEL] + [(k, 1) for k in SIDE_FIELDS]
)
TO_LEFT = rows_of(
    [(q, 1) for q in LEFTWARD] + [(q, 0) for q in LEFTWARD + LEVEL] + [(k, 0) for k in SIDE_FIELDS]
)
ADJ_TO_RIGHT = rows_of([(q, 0) for q in LEFTWARD] + [(q, 1) for q in LEFTWARD + LEVEL])
ADJ_TO_LEFT = rows_of([(q, 1) for q in RIGHTWARD] + [(q, 0) for q in RIGHTWARD + LEVEL])
BULK_ROWS = len(TO_RIGHT)
ADJ_BULK = len(ADJ_TO_RIGHT)


def pair_sums(f):
    total = [f[2 * k + 1] + f[2 * k + 2] for k in range(9)]
    gap = [f[2 * k + 1] - f[2 * k + 2] for k in range(9)]
    return total, gap


def flow_moments(f):
    s, d = pair_sums(f)
    xy, xz, yz = s[3] + s[4], s[5] + s[6], s[7] + s[8]
    rho = f[0] + (s[0] + s[1] + s[2]) + (xy + xz + yz)
    j = (
        d[0] + (d[3] + d[4]) + (d[5] + d[6]),
        d[1] + (d[3] - d[4]) + (d[7] + d[8]),
        d[2] + (d[5] - d[6]) + (d[7] - d[8]),
    )
    second = (s[0] + xy + xz, s[1] + xy + yz, s[2] + xz + yz, s[3] - s[4], s[5] - s[6], s[7] - s[8])
    return rho, j, second


def heat_moments(g):
    temperature = g[0] + (g[1] + g[2]) + (g[3] + g[4]) + (g[5] + g[6])
    return temperature, (g[1] - g[2], g[3] - g[4], g[5] - g[6])


def common(f, g, mobility):
    rho, j, second = flow_moments(f)
    temperature, flux = heat_moments(g)
    u = tuple(mobility * jk for jk in j)
    square = (u[0] * u[0], u[1] * u[1], u[2] * u[2])
    third = rho * (1.0 / 3.0)
    stress = (
        second[0] - third - square[0],
        second[1] - third - square[1],
        second[2] - third - square[2],
        second[3] - u[0] * u[1],
        second[4] - u[0] * u[2],
        second[5] - u[1] * u[2],
    )
    decay = jnp.exp(-2.0 * (temperature - 1.0))
    omega = 1.0 / (0.5 + 0.3 * decay)
    return rho, j, u, square, stress, temperature, flux, decay, omega


def collide(f, g, mobility, rate):
    rho, _, u, square, stress, temperature, flux, _, omega = common(f, g, mobility)
    solid = mobility == 0.0
    lam = 1.2 - omega
    trace = stress[0] + stress[1] + stress[2]
    base = 1.2 * rho - 1.8 * (square[0] + square[1] + square[2]) - (1.5 * lam) * trace
    scale = 4.5 * lam
    mxx = 5.4 * square[0] + scale * stress[0]
    myy = 5.4 * square[1] + scale * stress[1]
    mzz = 5.4 * square[2] + scale * stress[2]
    mxy = 2.0 * (5.4 * (u[0] * u[1]) + scale * stress[3])
    mxz = 2.0 * (5.4 * (u[0] * u[2]) + scale * stress[4])
    myz = 2.0 * (5.4 * (u[1] * u[2]) + scale * stress[5])
    bx, by, bz = base + mxx, base + myy, base + mzz
    sxy, sxz, syz = bx + myy, bx + mzz, by + mzz
    even = [bx, by, bz, sxy + mxy, sxy - mxy, sxz + mxz, sxz - mxz, syz + myz, syz - myz]
    odd = [u[0], u[1], u[2], u[0] + u[1], u[0] - u[1], u[0] + u[2], u[0] - u[2], u[1] + u[2], u[1] - u[2]]
    flow = [None] * 19
    flow[0] = jnp.where(solid, f[0], (1.0 / 3.0) * base - 0.2 * f[0])
    for k in range(9):
        a, b = 2 * k + 1, 2 * k + 2
        w = 1.0 / 18.0 if k < 3 else 1.0 / 36.0
        e, o = w * even[k], (3.6 * w) * odd[k]
        flow[a] = jnp.where(solid, f[b], (e + o) - 0.2 * f[a])
        flow[b] = jnp.where(solid, f[a], (e - o) - 0.2 * f[b])
    keep = 0.5 * (1.4 - rate)
    push = (0.5 * rate) * temperature
    warm = 0.175 * temperature
    heat = [0.35 * temperature - 0.4 * g[0]]
    for k in range(3):
        along = keep * flux[k] + push * u[k]
        heat.append((warm + along) - 0.4 * g[2 * k + 1])
        heat.append((warm - along) - 0.4 * g[2 * k + 2])
    return flow + heat


def pull_back(f, g, fa, ga, mobility, rate, wanted, sensitivity):
    rho, j, u, square, stress, temperature, flux, decay, omega = common(f, g, mobility)
    solid = mobility == 0.0
    lam = 1.2 - omega
    s, d = pair_sums(fa)
    w = 1.0 / 36.0
    xy, xz, yz = s[3] + s[4], s[5] + s[6], s[7] + s[8]
    s2 = (s[0] + s[0], s[1] + s[1], s[2] + s[2])
    mass = w * (12.0 * fa[0] + (s2[0] + s2[1] + s2[2]) + (xy + xz + yz))
    px = w * ((d[0] + d[0]) + (d[3] + d[4]) + (d[5] + d[6]))
    py = w * ((d[1] + d[1]) + (d[3] - d[4]) + (d[7] + d[8]))
    pz = w * ((d[2] + d[2]) + (d[5] - d[6]) + (d[7] - d[8]))
    rxx, ryy, rzz = w * (s2[0] + xy + xz), w * (s2[1] + xy + yz), w * (s2[2] + xz + yz)
    rxy, rxz, ryz = w * (s[3] - s[4]), w * (s[5] - s[6]), w * (s[7] - s[8])
    shift = 1.5 * mass
    dxx, dyy, dzz = 4.5 * rxx - shift, 4.5 * ryy - shift, 4.5 * rzz - shift
    dxy, dxz, dyz = 4.5 * rxy, 4.5 * rxz, 4.5 * ryz
    lam_bar = (
        dxx * stress[0]
        + dyy * stress[1]
        + dzz * stress[2]
        + 2.0 * (dxy * stress[3] + dxz * stress[4] + dyz * stress[5])
    )
    mix = 2.4 - 2.0 * lam
    b = ((ga[1] - ga[2]) * 0.125, (ga[3] - ga[4]) * 0.125, (ga[5] - ga[6]) * 0.125)
    push = (4.0 * rate) * temperature
    ux = 3.6 * px + mix * (dxx * u[0] + dxy * u[1] + dxz * u[2]) + push * b[0]
    uy = 3.6 * py + mix * (dxy * u[0] + dyy * u[1] + dyz * u[2]) + push * b[1]
    uz = 3.6 * pz + mix * (dxz * u[0] + dyz * u[1] + dzz * u[2]) + push * b[2]
    result = {}
    if wanted:
        rho_bar = 1.2 * mass - (1.5 * lam) * ((rxx + ryy + rzz) - mass)
        jx, jy, jz = mobility * ux, mobility * uy, mobility * uz
        ex, ey, ez = lam * dxx, lam * dyy, lam * dzz
        exy, exz, eyz = (2.0 * lam) * dxy, (2.0 * lam) * dxz, (2.0 * lam) * dyz
        hx, hy, hz = rho_bar + ex, rho_bar + ey, rho_bar + ez
        gxy, gxz, gyz = hx + ey, hx + ez, hy + ez
        even = [hx, hy, hz, gxy + exy, gxy - exy, gxz + exz, gxz - exz, gyz + eyz, gyz - eyz]
        odd = [jx, jy, jz, jx + jy, jx - jy, jx + jz, jx - jz, jy + jz, jy - jz]
        if 0 in wanted:
            result[0] = jnp.where(solid, fa[0], rho_bar - 0.2 * fa[0])
        for k in range(9):
            p, m = 2 * k + 1, 2 * k + 2
            if p in wanted:
                result[p] = jnp.where(solid, fa[m], (even[k] + odd[k]) - 0.2 * fa[p])
            if m in wanted:
                result[m] = jnp.where(solid, fa[p], (even[k] - odd[k]) - 0.2 * fa[m])
        warm = (
            0.35 * ga[0]
            + 0.175 * ((ga[1] + ga[2]) + (ga[3] + ga[4]) + (ga[5] + ga[6]))
            + (4.0 * rate) * (b[0] * u[0] + b[1] * u[1] + b[2] * u[2])
            - jnp.where(solid, 0.0, lam_bar * (0.6 * decay) * (omega * omega))
        )
        keep = 5.6 - 4.0 * rate
        if 19 in wanted:
            result[19] = warm - 0.4 * ga[0]
        for k in range(3):
            along = keep * b[k]
            p, m = 2 * k + 1, 2 * k + 2
            if 19 + p in wanted:
                result[19 + p] = (warm + along) - 0.4 * ga[p]
            if 19 + m in wanted:
                result[19 + m] = (warm - along) - 0.4 * ga[m]
    if sensitivity:
        by_resistance = -(mobility * mobility) * (ux * j[0] + uy * j[1] + uz * j[2])
        bent = (
            b[0] * (temperature * u[0] - flux[0])
            + b[1] * (temperature * u[1] - flux[1])
            + b[2] * (temperature * u[2] - flux[2])
        )
        by_conductivity = (-1.6 * (rate * rate)) * bent
        result["by"] = (by_resistance, by_conductivity)
    return result


def turn(value, by, axis):
    count = value.shape[axis]
    by %= count
    return pltpu.roll(value, by, axis) if by else value


def pack(value, slot):
    return turn(value, 2 * EDGE * slot + EDGE, 1)


def unpack(row, slot):
    return turn(row, -EDGE - 2 * EDGE * slot, 1)


def pack_rows(values):
    lane = lax.broadcasted_iota(jnp.int32, (ZED, LANES), 1)
    rows = []
    for start in range(0, len(values), SLOTS):
        row = None
        for slot, value in enumerate(values[start : start + SLOTS]):
            part = pack(value, slot)
            row = part if row is None else jnp.where(lane >= 2 * EDGE * slot, part, row)
        rows.append(row)
    return rows


def halves():
    return [pl.ds(0, 8), pl.ds(8, 8)]


def low_lanes():
    return lax.broadcasted_iota(jnp.int32, (ZED, LANES), 1) % (2 * EDGE) < EDGE


def ring_place(axis):
    count = lax.axis_size(axis)
    place = lax.axis_index(axis)
    return lax.rem(place + count - 1, count), lax.rem(place + 1, count)


def either_way(move):
    first = lax.rem(lax.axis_index("gx"), 2) == 0
    pl.when(first)(lambda: move(True))
    pl.when(jnp.logical_not(first))(lambda: move(False))


def copy_rows(target, source):
    for row in range(source.shape[0]):
        target[row] = source[row]


def first_kernel(
    flow_in, heat_in, flow_weight_in, heat_weight_in, resistance_in, conductivity_in, solid_in,
    own, far, near, strips,
    right, left, flow, heat, flow_weight, heat_weight, resistance, conductivity, solid, arrived,
):
    pairs = [
        (flow_in, flow),
        (heat_in, heat),
        (resistance_in, resistance),
        (conductivity_in, conductivity),
        (solid_in, solid),
        (flow_weight_in, flow_weight),
        (heat_weight_in, heat_weight),
    ]
    copies = [pltpu.make_async_copy(a, b, arrived.at[k]) for k, (a, b) in enumerate(pairs)]
    for copy in copies:
        copy.start()
    strips[...] = jnp.zeros(strips.shape, jnp.float32)
    for copy in copies:
        copy.wait()
    for c in range(2):
        for z in halves():
            mobility = jnp.where(solid[c, z, :] != 0, 0.0, 1.0 / (1.0 + resistance[c, z, :]))
            rate = 1.0 / (0.5 + 0.4 * conductivity[c, z, :])
            f = [flow[q, c, z, :] for q in range(19)]
            g = [heat[q, c, z, :] for q in range(7)]
            after = collide(f, g, mobility, rate)
            more = [mobility, rate] + [flow_weight[k, c, z, :] for k in range(3)] + [heat_weight[c, z, :]]
            for k, value in enumerate(after + more):
                if (k, c) in TO_RIGHT:
                    right[TO_RIGHT[k, c], z, :] = value
                else:
                    left[TO_LEFT[k, c], z, :] = value

    for k in range(BULK_ROWS):
        own[k] = right[k]
        own[k + BULK_ROWS] = left[k]

    def send(first):
        copy_rows(far, left if first else right)
        copy_rows(near, right if first else left)

    either_way(send)
    rows = pack_rows([right[k] for k in range(BULK_ROWS)] + [left[k] for k in range(BULK_ROWS)])
    low = low_lanes()
    below, above = ring_place("gy")
    for k in range(HALF_ROWS):
        strips[above, k] = jnp.where(low, rows[k], turn(rows[k + HALF_ROWS], EDGE, 1))
        strips[below, k] = jnp.where(low, turn(rows[k], -EDGE, 1), rows[k + HALF_ROWS])


def merge_kernel(strips, own_in, far_in, near_in, own, far, near, strip, sent):
    del own_in, far_in, near_in
    low = low_lanes()
    below, above = ring_place("gy")
    for k in range(HALF_ROWS):
        under, over = strips[below, k], strips[above, k]
        strip[k] = jnp.where(low, under, turn(over, EDGE, 1))
        strip[k + HALF_ROWS] = jnp.where(low, turn(under, -EDGE, 1), over)
    tail = pl.ds(BULK_ROWS, HALF_ROWS)
    rightward = HALF_ROWS * lax.rem(lax.axis_index("gx"), 2)
    copies = [
        pltpu.make_async_copy(strip.at[pl.ds(HALF_ROWS - rightward, HALF_ROWS)], far.at[tail], sent.at[0]),
        pltpu.make_async_copy(strip.at[pl.ds(rightward, HALF_ROWS)], near.at[tail], sent.at[1]),
        pltpu.make_async_copy(strip, own.at[pl.ds(2 * BULK_ROWS, STRIP_ROWS)], sent.at[2]),
    ]
    for copy in copies:
        copy.start()
    for copy in copies:
        copy.wait()


def wide_field(k, column, own, from_left, from_right):
    if column < 0:
        place = TO_RIGHT[k, column + 2]
        main, strips, start = from_left[place], from_left, BULK_ROWS
    elif column > 1:
        place = TO_LEFT[k, column - 2]
        main, strips, start = from_right[place], from_right, BULK_ROWS
    elif (k, column) in TO_RIGHT:
        place = TO_RIGHT[k, column]
        main, strips, start = own[place], own, 2 * BULK_ROWS
    else:
        place = TO_LEFT[k, column]
        main, strips, start = own[BULK_ROWS + place], own, 2 * BULK_ROWS + HALF_ROWS
    beside = unpack(strips[start + place // SLOTS], place % SLOTS)
    return jnp.concatenate([main, beside], axis=1)


def moved(value, velocity, way):
    _, step_y, step_z = velocity
    return turn(turn(value, way * step_z, 0), way * step_y, 1)


def tiles(lanes):
    return [(z, pl.ds(t, LANES)) for z in halves() for t in range(0, lanes, LANES)]


def second_kernel(
    own, from_far, from_near,
    state, wide_sides, adjoint, by_resistance, by_conductivity, far, near,
    from_left, from_right, after, later, seed, right, left,
):
    def receive(first):
        copy_rows(from_left, from_far if first else from_near)
        copy_rows(from_right, from_near if first else from_far)

    either_way(receive)

    def wide(k, column):
        return wide_field(k, column, own, from_left, from_right)

    for column in range(-1, 3):
        i = column + 1
        wide_sides[0, i] = wide(MOBILITY, column)
        wide_sides[1, i] = wide(RATE, column)
        for q in range(MEMBERS):
            state[q, i] = moved(wide(q, column - VELOCITY[q][0]), VELOCITY[q], 1)
    for i in range(4):
        for z, y in tiles(WIDE):
            f = [state[q, i, z, y] for q in range(19)]
            g = [state[19 + q, i, z, y] for q in range(7)]
            result = collide(f, g, wide_sides[0, i, z, y], wide_sides[1, i, z, y])
            for q in range(MEMBERS):
                if 0 <= i - 1 + VELOCITY[q][0] <= 1:
                    after[q, i, z, y] = result[q]
    for c in range(2):
        for q in range(MEMBERS):
            later[q, c] = moved(after[q, c + 1 - VELOCITY[q][0]], VELOCITY[q], 1)
    for column in range(-1, 3):
        weights = [wide(WEIGHT + k, column) for k in range(4)]
        for q in range(1, MEMBERS):
            velocity = VELOCITY[q]
            c = column - velocity[0]
            if not 0 <= c <= 1:
                continue
            if q < 19:
                parts = [weights[k] if velocity[k] > 0 else -weights[k] for k in range(3) if velocity[k]]
                value = parts[0] if len(parts) == 1 else parts[0] + parts[1]
            else:
                value = weights[3]
            seed[q, c] = moved(value, velocity, -1)
    for c in range(2):
        for z, y in tiles(WIDE):
            f = [later[q, c, z, y] for q in range(19)]
            g = [later[19 + q, c, z, y] for q in range(7)]
            fa = [jnp.zeros((8, LANES), jnp.float32)] + [seed[q, c, z, y] for q in range(1, 19)]
            ga = [seed[19 + q, c, z, y] for q in range(7)]
            inner = y.start == 0
            result = pull_back(
                f, g, fa, ga, wide_sides[0, c + 1, z, y], wide_sides[1, c + 1, z, y], range(MEMBERS), inner
            )
            if inner:
                by_resistance[c, z, :], by_conductivity[c, z, :] = result["by"]
            for q in range(MEMBERS):
                adjoint[q, c, z, y] = result[q]
                if inner and (q, c) in ADJ_TO_RIGHT:
                    right[ADJ_TO_RIGHT[q, c], z, :] = result[q]
                if inner and (q, c) in ADJ_TO_LEFT:
                    left[ADJ_TO_LEFT[q, c], z, :] = result[q]
    for side, rows in ((right, ADJ_TO_RIGHT), (left, ADJ_TO_LEFT)):
        values = [adjoint[q, c, :, LANES:] for q, c in rows]
        for row, value in enumerate(pack_rows(values)):
            side[ADJ_BULK + row] = value

    def send(first):
        copy_rows(far, left if first else right)
        copy_rows(near, right if first else left)

    either_way(send)


def third_kernel(
    flow, heat, state, wide_sides, adjoint, part_resistance, part_conductivity, from_far, from_near,
    by_resistance, by_conductivity,
    from_left, from_right, arrived, earlier, last,
):
    def receive(first):
        copy_rows(from_left, from_far if first else from_near)
        copy_rows(from_right, from_near if first else from_far)

    either_way(receive)

    def wide(q, column):
        if 0 <= column <= 1:
            return adjoint[q, column]
        c, bulk, rows = (column + 2, from_left, ADJ_TO_RIGHT) if column < 0 else (column - 2, from_right, ADJ_TO_LEFT)
        place = rows[q, c]
        beside = unpack(bulk[ADJ_BULK + place // SLOTS], place % SLOTS)
        return jnp.concatenate([bulk[place], beside], axis=1)

    for column in range(-1, 3):
        for q in range(MEMBERS):
            arrived[q, column + 1] = moved(wide(q, column + VELOCITY[q][0]), VELOCITY[q], -1)
    for column in range(-1, 3):
        i = column + 1
        for z, y in tiles(WIDE):
            inner = y.start == 0
            own = 0 <= column <= 1
            wanted = [
                q
                for q in range(MEMBERS)
                if 0 <= column - VELOCITY[q][0] <= 1 and (inner or VELOCITY[q][1])
            ]
            f = [state[q, i, z, y] for q in range(19)]
            g = [state[19 + q, i, z, y] for q in range(7)]
            fa = [arrived[q, i, z, y] for q in range(19)]
            ga = [arrived[19 + q, i, z, y] for q in range(7)]
            result = pull_back(
                f, g, fa, ga, wide_sides[0, i, z, y], wide_sides[1, i, z, y], wanted, inner and own
            )
            for q in wanted:
                earlier[q, i, z, y] = result[q]
            if inner and own:
                by_resistance[column, z, :] = part_resistance[column, z, :] + result["by"][0]
                by_conductivity[column, z, :] = part_conductivity[column, z, :] + result["by"][1]
    for c in range(2):
        for q in range(MEMBERS):
            velocity = VELOCITY[q]
            source = earlier[q, c + 1 + velocity[0]] if velocity[1] else earlier[q, c + 1 + velocity[0], :, :LANES]
            last[q, c] = moved(source, velocity, -1)[:, :LANES]
    for c in range(2):
        for z in halves():
            f = [flow[q, c, z, :] for q in range(19)]
            g = [heat[q, c, z, :] for q in range(7)]
            fa = [last[q, c, z, :] for q in range(19)]
            ga = [last[19 + q, c, z, :] for q in range(7)]
            narrow = pl.ds(0, LANES)
            result = pull_back(
                f, g, fa, ga, wide_sides[0, c + 1, z, narrow], wide_sides[1, c + 1, z, narrow], (), True
            )
            by_resistance[c, z, :] += result["by"][0]
            by_conductivity[c, z, :] += result["by"][1]


def floats(*shape):
    return jax.ShapeDtypeStruct(shape, jnp.float32)


def vmem(*shape):
    return pltpu.VMEM(shape, jnp.float32)


def swap_along_x(far, near):
    count = lax.axis_size("gx")
    across = [(i, (i + (1 if i % 2 else -1)) % count) for i in range(count)]
    within = [(i, i ^ 1) for i in range(count)]
    return lax.ppermute(far, "gx", across), lax.ppermute(near, "gx", within)


FIRST_PARAMS = pltpu.CompilerParams(vmem_limit_bytes=56 * 1024 * 1024)
PARAMS = pltpu.CompilerParams(vmem_limit_bytes=24 * 1024 * 1024)
SENT = BULK_ROWS + HALF_ROWS
OWN_ROWS = 2 * BULK_ROWS + STRIP_ROWS
ADJ_SENT = ADJ_BULK + ADJ_ROWS


def on_device(flow, heat, flow_weight, heat_weight, resistance, conductivity, solid):
    rings = lax.axis_size("gy")
    own, far, near, strips = pl.pallas_call(
        first_kernel,
        in_specs=[pl.BlockSpec(memory_space=pltpu.HBM)] * 7,
        out_shape=(
            floats(OWN_ROWS, ZED, LANES),
            floats(SENT, ZED, LANES),
            floats(SENT, ZED, LANES),
            floats(rings, HALF_ROWS, ZED, LANES),
        ),
        scratch_shapes=[
            vmem(BULK_ROWS, ZED, LANES),
            vmem(BULK_ROWS, ZED, LANES),
            vmem(19, 2, ZED, LANES),
            vmem(7, 2, ZED, LANES),
            vmem(3, 2, ZED, LANES),
            vmem(2, ZED, LANES),
            vmem(2, ZED, LANES),
            vmem(2, ZED, LANES),
            pltpu.VMEM((2, ZED, LANES), jnp.int32),
            pltpu.SemaphoreType.DMA((7,)),
        ],
        compiler_params=FIRST_PARAMS,
        name="collide_own",
    )(flow, heat, flow_weight, heat_weight, resistance, conductivity, solid)

    strips = lax.all_to_all(strips, "gy", 0, 0)

    in_place = pl.BlockSpec(memory_space=pltpu.HBM)
    own, far, near = pl.pallas_call(
        merge_kernel,
        in_specs=[pl.BlockSpec(memory_space=pltpu.VMEM), in_place, in_place, in_place],
        out_specs=[in_place, in_place, in_place],
        out_shape=(floats(OWN_ROWS, ZED, LANES), floats(SENT, ZED, LANES), floats(SENT, ZED, LANES)),
        scratch_shapes=[vmem(STRIP_ROWS, ZED, LANES), pltpu.SemaphoreType.DMA((3,))],
        input_output_aliases={1: 0, 2: 1, 3: 2},
        compiler_params=FIRST_PARAMS,
        name="merge_strips",
    )(strips, own, far, near)

    from_far, from_near = swap_along_x(far, near)

    state, wide_sides, adjoint, part_resistance, part_conductivity, far, near = pl.pallas_call(
        second_kernel,
        out_shape=(
            floats(MEMBERS, 4, ZED, WIDE),
            floats(2, 4, ZED, WIDE),
            floats(MEMBERS, 2, ZED, WIDE),
            floats(2, ZED, LANES),
            floats(2, ZED, LANES),
            floats(ADJ_SENT, ZED, LANES),
            floats(ADJ_SENT, ZED, LANES),
        ),
        scratch_shapes=[
            vmem(SENT, ZED, LANES),
            vmem(SENT, ZED, LANES),
            vmem(MEMBERS, 4, ZED, WIDE),
            vmem(MEMBERS, 2, ZED, WIDE),
            vmem(MEMBERS, 2, ZED, WIDE),
            vmem(ADJ_SENT, ZED, LANES),
            vmem(ADJ_SENT, ZED, LANES),
        ],
        compiler_params=PARAMS,
        name="forward_and_seed",
    )(own, from_far, from_near)

    from_far, from_near = swap_along_x(far, near)

    return pl.pallas_call(
        third_kernel,
        out_shape=(floats(2, ZED, LANES), floats(2, ZED, LANES)),
        scratch_shapes=[
            vmem(ADJ_SENT, ZED, LANES),
            vmem(ADJ_SENT, ZED, LANES),
            vmem(MEMBERS, 4, ZED, WIDE),
            vmem(MEMBERS, 4, ZED, WIDE),
            vmem(MEMBERS, 2, ZED, LANES),
        ],
        compiler_params=PARAMS,
        name="adjoint_steps",
    )(flow, heat, state, wide_sides, adjoint, part_resistance, part_conductivity, from_far, from_near)


def solution(mesh):
    split = P("gx", None, "gy")
    stacked = P(None, "gx", None, "gy")
    return jax.shard_map(
        on_device,
        mesh=mesh,
        in_specs=(stacked, stacked, stacked, split, split, split, split),
        out_specs=(split, split),
        check_vma=False,
    )
```

```python
import jax
import jax.numpy as jnp
import numpy as np
from jax import lax
from jax.experimental import pallas as pl
from jax.experimental.pallas import tpu as pltpu
from jax.sharding import PartitionSpec as P

ZED = 16
LANES = 128
WIDE = 2 * LANES
EDGE = 4

FLOW_VELOCITY = [
    (0, 0, 0),
    (1, 0, 0),
    (-1, 0, 0),
    (0, 1, 0),
    (0, -1, 0),
    (0, 0, 1),
    (0, 0, -1),
    (1, 1, 0),
    (-1, -1, 0),
    (1, -1, 0),
    (-1, 1, 0),
    (1, 0, 1),
    (-1, 0, -1),
    (1, 0, -1),
    (-1, 0, 1),
    (0, 1, 1),
    (0, -1, -1),
    (0, 1, -1),
    (0, -1, 1),
]
VELOCITY = FLOW_VELOCITY + FLOW_VELOCITY[:7]
MEMBERS = len(VELOCITY)
RIGHTWARD = [q for q in range(MEMBERS) if VELOCITY[q][0] == 1]
LEFTWARD = [q for q in range(MEMBERS) if VELOCITY[q][0] == -1]
LEVEL = [q for q in range(MEMBERS) if VELOCITY[q][0] == 0]

MOBILITY, RATE, WEIGHT = MEMBERS, MEMBERS + 1, MEMBERS + 2
FIELDS = MEMBERS + 6

SLOTS = LANES // (2 * EDGE)
STRIP_ROWS = 4 * FIELDS // SLOTS
HALF_ROWS = STRIP_ROWS // 2
ADJ_ROWS = -(-MEMBERS // SLOTS)


def rows_of(entries):
    return {entry: row for row, entry in enumerate(entries)}


SIDE_FIELDS = list(range(MEMBERS, FIELDS))
TO_RIGHT = rows_of(
    [(q, 0) for q in RIGHTWARD] + [(q, 1) for q in RIGHTWARD + LEVEL] + [(k, 1) for k in SIDE_FIELDS]
)
TO_LEFT = rows_of(
    [(q, 1) for q in LEFTWARD] + [(q, 0) for q in LEFTWARD + LEVEL] + [(k, 0) for k in SIDE_FIELDS]
)
ADJ_TO_RIGHT = rows_of([(q, 0) for q in LEFTWARD] + [(q, 1) for q in LEFTWARD + LEVEL])
ADJ_TO_LEFT = rows_of([(q, 1) for q in RIGHTWARD] + [(q, 0) for q in RIGHTWARD + LEVEL])
BULK_ROWS = len(TO_RIGHT)
ADJ_BULK = len(ADJ_TO_RIGHT)


def pair_sums(f):
    total = [f[2 * k + 1] + f[2 * k + 2] for k in range(9)]
    gap = [f[2 * k + 1] - f[2 * k + 2] for k in range(9)]
    return total, gap


def flow_moments(f):
    s, d = pair_sums(f)
    xy, xz, yz = s[3] + s[4], s[5] + s[6], s[7] + s[8]
    rho = f[0] + (s[0] + s[1] + s[2]) + (xy + xz + yz)
    j = (
        d[0] + (d[3] + d[4]) + (d[5] + d[6]),
        d[1] + (d[3] - d[4]) + (d[7] + d[8]),
        d[2] + (d[5] - d[6]) + (d[7] - d[8]),
    )
    second = (s[0] + xy + xz, s[1] + xy + yz, s[2] + xz + yz, s[3] - s[4], s[5] - s[6], s[7] - s[8])
    return rho, j, second


def heat_moments(g):
    temperature = g[0] + (g[1] + g[2]) + (g[3] + g[4]) + (g[5] + g[6])
    return temperature, (g[1] - g[2], g[3] - g[4], g[5] - g[6])


def common(f, g, mobility):
    rho, j, second = flow_moments(f)
    temperature, flux = heat_moments(g)
    u = tuple(mobility * jk for jk in j)
    square = (u[0] * u[0], u[1] * u[1], u[2] * u[2])
    third = rho * (1.0 / 3.0)
    stress = (
        second[0] - third - square[0],
        second[1] - third - square[1],
        second[2] - third - square[2],
        second[3] - u[0] * u[1],
        second[4] - u[0] * u[2],
        second[5] - u[1] * u[2],
    )
    decay = jnp.exp(-2.0 * (temperature - 1.0))
    omega = 1.0 / (0.5 + 0.3 * decay)
    return rho, j, u, square, stress, temperature, flux, decay, omega


def collide(f, g, mobility, rate):
    rho, _, u, square, stress, temperature, flux, _, omega = common(f, g, mobility)
    solid = mobility == 0.0
    lam = 1.2 - omega
    trace = stress[0] + stress[1] + stress[2]
    base = 1.2 * rho - 1.8 * (square[0] + square[1] + square[2]) - (1.5 * lam) * trace
    scale = 4.5 * lam
    mxx = 5.4 * square[0] + scale * stress[0]
    myy = 5.4 * square[1] + scale * stress[1]
    mzz = 5.4 * square[2] + scale * stress[2]
    mxy = 2.0 * (5.4 * (u[0] * u[1]) + scale * stress[3])
    mxz = 2.0 * (5.4 * (u[0] * u[2]) + scale * stress[4])
    myz = 2.0 * (5.4 * (u[1] * u[2]) + scale * stress[5])
    bx, by, bz = base + mxx, base + myy, base + mzz
    sxy, sxz, syz = bx + myy, bx + mzz, by + mzz
    even = [bx, by, bz, sxy + mxy, sxy - mxy, sxz + mxz, sxz - mxz, syz + myz, syz - myz]
    odd = [u[0], u[1], u[2], u[0] + u[1], u[0] - u[1], u[0] + u[2], u[0] - u[2], u[1] + u[2], u[1] - u[2]]
    flow = [None] * 19
    flow[0] = jnp.where(solid, f[0], (1.0 / 3.0) * base - 0.2 * f[0])
    for k in range(9):
        a, b = 2 * k + 1, 2 * k + 2
        w = 1.0 / 18.0 if k < 3 else 1.0 / 36.0
        e, o = w * even[k], (3.6 * w) * odd[k]
        flow[a] = jnp.where(solid, f[b], (e + o) - 0.2 * f[a])
        flow[b] = jnp.where(solid, f[a], (e - o) - 0.2 * f[b])
    keep = 0.5 * (1.4 - rate)
    push = (0.5 * rate) * temperature
    warm = 0.175 * temperature
    heat = [0.35 * temperature - 0.4 * g[0]]
    for k in range(3):
        along = keep * flux[k] + push * u[k]
        heat.append((warm + along) - 0.4 * g[2 * k + 1])
        heat.append((warm - along) - 0.4 * g[2 * k + 2])
    return flow + heat


def pull_back(f, g, fa, ga, mobility, rate, wanted, sensitivity):
    rho, j, u, square, stress, temperature, flux, decay, omega = common(f, g, mobility)
    solid = mobility == 0.0
    lam = 1.2 - omega
    s, d = pair_sums(fa)
    w = 1.0 / 36.0
    xy, xz, yz = s[3] + s[4], s[5] + s[6], s[7] + s[8]
    s2 = (s[0] + s[0], s[1] + s[1], s[2] + s[2])
    mass = w * (12.0 * fa[0] + (s2[0] + s2[1] + s2[2]) + (xy + xz + yz))
    px = w * ((d[0] + d[0]) + (d[3] + d[4]) + (d[5] + d[6]))
    py = w * ((d[1] + d[1]) + (d[3] - d[4]) + (d[7] + d[8]))
    pz = w * ((d[2] + d[2]) + (d[5] - d[6]) + (d[7] - d[8]))
    rxx, ryy, rzz = w * (s2[0] + xy + xz), w * (s2[1] + xy + yz), w * (s2[2] + xz + yz)
    rxy, rxz, ryz = w * (s[3] - s[4]), w * (s[5] - s[6]), w * (s[7] - s[8])
    shift = 1.5 * mass
    dxx, dyy, dzz = 4.5 * rxx - shift, 4.5 * ryy - shift, 4.5 * rzz - shift
    dxy, dxz, dyz = 4.5 * rxy, 4.5 * rxz, 4.5 * ryz
    lam_bar = (
        dxx * stress[0]
        + dyy * stress[1]
        + dzz * stress[2]
        + 2.0 * (dxy * stress[3] + dxz * stress[4] + dyz * stress[5])
    )
    mix = 2.4 - 2.0 * lam
    b = ((ga[1] - ga[2]) * 0.125, (ga[3] - ga[4]) * 0.125, (ga[5] - ga[6]) * 0.125)
    push = (4.0 * rate) * temperature
    ux = 3.6 * px + mix * (dxx * u[0] + dxy * u[1] + dxz * u[2]) + push * b[0]
    uy = 3.6 * py + mix * (dxy * u[0] + dyy * u[1] + dyz * u[2]) + push * b[1]
    uz = 3.6 * pz + mix * (dxz * u[0] + dyz * u[1] + dzz * u[2]) + push * b[2]
    result = {}
    if wanted:
        rho_bar = 1.2 * mass - (1.5 * lam) * ((rxx + ryy + rzz) - mass)
        jx, jy, jz = mobility * ux, mobility * uy, mobility * uz
        ex, ey, ez = lam * dxx, lam * dyy, lam * dzz
        exy, exz, eyz = (2.0 * lam) * dxy, (2.0 * lam) * dxz, (2.0 * lam) * dyz
        hx, hy, hz = rho_bar + ex, rho_bar + ey, rho_bar + ez
        gxy, gxz, gyz = hx + ey, hx + ez, hy + ez
        even = [hx, hy, hz, gxy + exy, gxy - exy, gxz + exz, gxz - exz, gyz + eyz, gyz - eyz]
        odd = [jx, jy, jz, jx + jy, jx - jy, jx + jz, jx - jz, jy + jz, jy - jz]
        if 0 in wanted:
            result[0] = jnp.where(solid, fa[0], rho_bar - 0.2 * fa[0])
        for k in range(9):
            p, m = 2 * k + 1, 2 * k + 2
            if p in wanted:
                result[p] = jnp.where(solid, fa[m], (even[k] + odd[k]) - 0.2 * fa[p])
            if m in wanted:
                result[m] = jnp.where(solid, fa[p], (even[k] - odd[k]) - 0.2 * fa[m])
        warm = (
            0.35 * ga[0]
            + 0.175 * ((ga[1] + ga[2]) + (ga[3] + ga[4]) + (ga[5] + ga[6]))
            + (4.0 * rate) * (b[0] * u[0] + b[1] * u[1] + b[2] * u[2])
            - jnp.where(solid, 0.0, lam_bar * (0.6 * decay) * (omega * omega))
        )
        keep = 5.6 - 4.0 * rate
        if 19 in wanted:
            result[19] = warm - 0.4 * ga[0]
        for k in range(3):
            along = keep * b[k]
            p, m = 2 * k + 1, 2 * k + 2
            if 19 + p in wanted:
                result[19 + p] = (warm + along) - 0.4 * ga[p]
            if 19 + m in wanted:
                result[19 + m] = (warm - along) - 0.4 * ga[m]
    if sensitivity:
        by_resistance = -(mobility * mobility) * (ux * j[0] + uy * j[1] + uz * j[2])
        bent = (
            b[0] * (temperature * u[0] - flux[0])
            + b[1] * (temperature * u[1] - flux[1])
            + b[2] * (temperature * u[2] - flux[2])
        )
        by_conductivity = (-1.6 * (rate * rate)) * bent
        result["by"] = (by_resistance, by_conductivity)
    return result


def turn(value, by, axis):
    count = value.shape[axis]
    by %= count
    return pltpu.roll(value, by, axis) if by else value


def pack(value, slot):
    return turn(value, 2 * EDGE * slot + EDGE, 1)


def pack_rows(values):
    lane = lax.broadcasted_iota(jnp.int32, (ZED, LANES), 1)
    rows = []
    for start in range(0, len(values), SLOTS):
        row = None
        for slot, value in enumerate(values[start : start + SLOTS]):
            part = pack(value, slot)
            row = part if row is None else jnp.where(lane >= 2 * EDGE * slot, part, row)
        rows.append(row)
    return rows


def halves():
    return [pl.ds(0, 8), pl.ds(8, 8)]


def low_lanes():
    return lax.broadcasted_iota(jnp.int32, (ZED, LANES), 1) % (2 * EDGE) < EDGE


def ring_place(axis):
    count = lax.axis_size(axis)
    place = lax.axis_index(axis)
    return lax.rem(place + count - 1, count), lax.rem(place + 1, count)


def either_way(move):
    first = lax.rem(lax.axis_index("gx"), 2) == 0
    pl.when(first)(lambda: move(True))
    pl.when(jnp.logical_not(first))(lambda: move(False))


def copy_rows(target, source):
    for row in range(source.shape[0]):
        target[row] = source[row]


def first_kernel(
    flow_in, heat_in, flow_weight_in, heat_weight_in, resistance_in, conductivity_in, solid_in,
    own, far, near,
    both, flow, heat, flow_weight, heat_weight, resistance, conductivity, solid, arrived, sent,
):
    pairs = [
        (flow_in, flow),
        (heat_in, heat),
        (resistance_in, resistance),
        (conductivity_in, conductivity),
        (solid_in, solid),
        (flow_weight_in, flow_weight),
        (heat_weight_in, heat_weight),
    ]
    copies = [pltpu.make_async_copy(a, b, arrived.at[k]) for k, (a, b) in enumerate(pairs)]
    for copy in copies:
        copy.start()
    for copy in copies:
        copy.wait()
    for c in range(2):
        for z in halves():
            mobility = jnp.where(solid[c, z, :] != 0, 0.0, 1.0 / (1.0 + resistance[c, z, :]))
            rate = 1.0 / (0.5 + 0.4 * conductivity[c, z, :])
            f = [flow[q, c, z, :] for q in range(19)]
            g = [heat[q, c, z, :] for q in range(7)]
            after = collide(f, g, mobility, rate)
            more = [mobility, rate] + [flow_weight[k, c, z, :] for k in range(3)] + [heat_weight[c, z, :]]
            for k, value in enumerate(after + more):
                both[TO_RIGHT[k, c] if (k, c) in TO_RIGHT else BULK_ROWS + TO_LEFT[k, c], z, :] = value
    odd = lax.rem(lax.axis_index("gx"), 2)
    copies = [
        pltpu.make_async_copy(both.at[pl.ds(BULK_ROWS * (1 - odd), BULK_ROWS)], far, sent.at[0]),
        pltpu.make_async_copy(both.at[pl.ds(BULK_ROWS * odd, BULK_ROWS)], near, sent.at[1]),
        pltpu.make_async_copy(both, own, sent.at[2]),
    ]
    for copy in copies:
        copy.start()
    for copy in copies:
        copy.wait()


def strip_kernel(own, from_far, from_near, strips, from_left, from_right):
    def receive(first):
        copy_rows(from_left, from_far if first else from_near)
        copy_rows(from_right, from_near if first else from_far)

    either_way(receive)
    strips[...] = jnp.zeros(strips.shape, jnp.float32)
    rows = pack_rows(
        [own[k] for k in range(2 * BULK_ROWS)]
        + [from_left[k] for k in range(BULK_ROWS)]
        + [from_right[k] for k in range(BULK_ROWS)]
    )
    low = low_lanes()
    below, above = ring_place("gy")
    for k in range(HALF_ROWS):
        strips[above, k] = jnp.where(low, rows[k], turn(rows[k + HALF_ROWS], EDGE, 1))
        strips[below, k] = jnp.where(low, turn(rows[k], -EDGE, 1), rows[k + HALF_ROWS])


def split(value):
    return value[:, :LANES], value[:, LANES:], 0


def beside(row, slot):
    return row, -EDGE - 2 * EDGE * slot


def moved(pair, velocity, way):
    main, extra, by = pair
    _, step_y, step_z = velocity
    step = way * step_y
    main, extra = turn(main, way * step_z, 0), turn(extra, way * step_z, 0)
    if not step:
        return main, turn(extra, by, 1)
    main, extra = turn(main, step, 1), turn(extra, by + step, 1)
    lane = lax.broadcasted_iota(jnp.int32, (ZED, LANES), 1)
    edge = lane == (0 if step == 1 else LANES - 1)
    return jnp.where(edge, extra, main), jnp.where(edge, main, extra)


def put(ref, q, i, pair):
    ref[q, i, :, :LANES], ref[q, i, :, LANES:] = pair


def tiles(lanes):
    return [(z, pl.ds(t, LANES)) for z in halves() for t in range(0, lanes, LANES)]


STILL = (0, 0, 0)


def second_kernel(
    own, from_left, from_right, strips,
    state, wide_sides, adjoint, by_resistance, by_conductivity, far, near,
    strip, after, later, seed, right, left,
):
    low = low_lanes()
    below, above = ring_place("gy")
    for k in range(HALF_ROWS):
        under, over = strips[below, k], strips[above, k]
        strip[k] = jnp.where(low, under, turn(over, EDGE, 1))
        strip[k + HALF_ROWS] = jnp.where(low, turn(under, -EDGE, 1), over)

    def wide(k, column):
        if column < 0:
            place = TO_RIGHT[k, column + 2]
            main, start = from_left[place], 2 * BULK_ROWS
        elif column > 1:
            place = TO_LEFT[k, column - 2]
            main, start = from_right[place], 3 * BULK_ROWS
        elif (k, column) in TO_RIGHT:
            place, start = TO_RIGHT[k, column], 0
            main = own[place]
        else:
            place, start = TO_LEFT[k, column], BULK_ROWS
            main = own[BULK_ROWS + place]
        return (main,) + beside(strip[(start + place) // SLOTS], place % SLOTS)

    for column in range(-1, 3):
        i = column + 1
        put(wide_sides, 0, i, moved(wide(MOBILITY, column), STILL, 1))
        put(wide_sides, 1, i, moved(wide(RATE, column), STILL, 1))
        for q in range(MEMBERS):
            put(state, q, i, moved(wide(q, column - VELOCITY[q][0]), VELOCITY[q], 1))
    for i in range(4):
        for z, y in tiles(WIDE):
            f = [state[q, i, z, y] for q in range(19)]
            g = [state[19 + q, i, z, y] for q in range(7)]
            result = collide(f, g, wide_sides[0, i, z, y], wide_sides[1, i, z, y])
            for q in range(MEMBERS):
                if 0 <= i - 1 + VELOCITY[q][0] <= 1:
                    after[q, i, z, y] = result[q]
    for c in range(2):
        for q in range(MEMBERS):
            put(later, q, c, moved(split(after[q, c + 1 - VELOCITY[q][0]]), VELOCITY[q], 1))
    for column in range(-1, 3):
        weights = [wide(WEIGHT + k, column) for k in range(3)]
        weights = [(main, turn(extra, by, 1)) for main, extra, by in weights]
        for q in range(1, MEMBERS):
            velocity = VELOCITY[q]
            c = column - velocity[0]
            if not 0 <= c <= 1:
                continue
            if q < 19:
                parts = [
                    tuple(value if velocity[k] > 0 else -value for value in weights[k]) for k in range(3) if velocity[k]
                ]
                pair = parts[0] if len(parts) == 1 else tuple(a + b for a, b in zip(*parts))
                pair += (0,)
            else:
                pair = wide(WEIGHT + 3, column)
            put(seed, q, c, moved(pair, velocity, -1))
    for c in range(2):
        for z, y in tiles(WIDE):
            f = [later[q, c, z, y] for q in range(19)]
            g = [later[19 + q, c, z, y] for q in range(7)]
            fa = [jnp.zeros((8, LANES), jnp.float32)] + [seed[q, c, z, y] for q in range(1, 19)]
            ga = [seed[19 + q, c, z, y] for q in range(7)]
            inner = y.start == 0
            result = pull_back(
                f, g, fa, ga, wide_sides[0, c + 1, z, y], wide_sides[1, c + 1, z, y], range(MEMBERS), inner
            )
            if inner:
                by_resistance[c, z, :], by_conductivity[c, z, :] = result["by"]
            for q in range(MEMBERS):
                adjoint[q, c, z, y] = result[q]
                if inner and (q, c) in ADJ_TO_RIGHT:
                    right[ADJ_TO_RIGHT[q, c], z, :] = result[q]
                if inner and (q, c) in ADJ_TO_LEFT:
                    left[ADJ_TO_LEFT[q, c], z, :] = result[q]
    for side, rows in ((right, ADJ_TO_RIGHT), (left, ADJ_TO_LEFT)):
        values = [adjoint[q, c, :, LANES:] for q, c in rows]
        for row, value in enumerate(pack_rows(values)):
            side[ADJ_BULK + row] = value

    def send(first):
        copy_rows(far, left if first else right)
        copy_rows(near, right if first else left)

    either_way(send)


def third_kernel(
    flow, heat, state, wide_sides, adjoint, part_resistance, part_conductivity, from_far, from_near,
    by_resistance, by_conductivity,
    from_left, from_right, arrived, earlier, last,
):
    def receive(first):
        copy_rows(from_left, from_far if first else from_near)
        copy_rows(from_right, from_near if first else from_far)

    either_way(receive)

    def wide(q, column):
        if 0 <= column <= 1:
            return split(adjoint[q, column])
        if column < 0:
            bulk, place = from_left, ADJ_TO_RIGHT[q, column + 2]
        else:
            bulk, place = from_right, ADJ_TO_LEFT[q, column - 2]
        return (bulk[place],) + beside(bulk[ADJ_BULK + place // SLOTS], place % SLOTS)

    for column in range(-1, 3):
        for q in range(MEMBERS):
            put(arrived, q, column + 1, moved(wide(q, column + VELOCITY[q][0]), VELOCITY[q], -1))
    for column in range(-1, 3):
        i = column + 1
        for z, y in tiles(WIDE):
            inner = y.start == 0
            own = 0 <= column <= 1
            wanted = [
                q
                for q in range(MEMBERS)
                if 0 <= column - VELOCITY[q][0] <= 1 and (inner or VELOCITY[q][1])
            ]
            f = [state[q, i, z, y] for q in range(19)]
            g = [state[19 + q, i, z, y] for q in range(7)]
            fa = [arrived[q, i, z, y] for q in range(19)]
            ga = [arrived[19 + q, i, z, y] for q in range(7)]
            result = pull_back(
                f, g, fa, ga, wide_sides[0, i, z, y], wide_sides[1, i, z, y], wanted, inner and own
            )
            for q in wanted:
                earlier[q, i, z, y] = result[q]
            if inner and own:
                by_resistance[column, z, :] = part_resistance[column, z, :] + result["by"][0]
                by_conductivity[column, z, :] = part_conductivity[column, z, :] + result["by"][1]
    for c in range(2):
        for q in range(MEMBERS):
            velocity = VELOCITY[q]
            i = c + 1 + velocity[0]
            if velocity[1]:
                last[q, c] = moved(split(earlier[q, i]), velocity, -1)[0]
            else:
                last[q, c] = turn(earlier[q, i, :, :LANES], -velocity[2], 0)
    for c in range(2):
        for z in halves():
            f = [flow[q, c, z, :] for q in range(19)]
            g = [heat[q, c, z, :] for q in range(7)]
            fa = [last[q, c, z, :] for q in range(19)]
            ga = [last[19 + q, c, z, :] for q in range(7)]
            narrow = pl.ds(0, LANES)
            result = pull_back(
                f, g, fa, ga, wide_sides[0, c + 1, z, narrow], wide_sides[1, c + 1, z, narrow], (), True
            )
            by_resistance[c, z, :] += result["by"][0]
            by_conductivity[c, z, :] += result["by"][1]


def floats(*shape):
    return jax.ShapeDtypeStruct(shape, jnp.float32)


def vmem(*shape):
    return pltpu.VMEM(shape, jnp.float32)


def swap_along_x(far, near):
    count = lax.axis_size("gx")
    across = [(i, (i + (1 if i % 2 else -1)) % count) for i in range(count)]
    within = [(i, i ^ 1) for i in range(count)]
    return lax.ppermute(far, "gx", across), lax.ppermute(near, "gx", within)


FIRST_PARAMS = pltpu.CompilerParams(vmem_limit_bytes=56 * 1024 * 1024)
PARAMS = pltpu.CompilerParams(vmem_limit_bytes=24 * 1024 * 1024)
ADJ_SENT = ADJ_BULK + ADJ_ROWS


def on_device(flow, heat, flow_weight, heat_weight, resistance, conductivity, solid):
    rings = lax.axis_size("gy")
    in_hbm = pl.BlockSpec(memory_space=pltpu.HBM)
    own, far, near = pl.pallas_call(
        first_kernel,
        in_specs=[in_hbm] * 7,
        out_specs=[in_hbm] * 3,
        out_shape=(
            floats(2 * BULK_ROWS, ZED, LANES),
            floats(BULK_ROWS, ZED, LANES),
            floats(BULK_ROWS, ZED, LANES),
        ),
        scratch_shapes=[
            vmem(2 * BULK_ROWS, ZED, LANES),
            vmem(19, 2, ZED, LANES),
            vmem(7, 2, ZED, LANES),
            vmem(3, 2, ZED, LANES),
            vmem(2, ZED, LANES),
            vmem(2, ZED, LANES),
            vmem(2, ZED, LANES),
            pltpu.VMEM((2, ZED, LANES), jnp.int32),
            pltpu.SemaphoreType.DMA((7,)),
            pltpu.SemaphoreType.DMA((3,)),
        ],
        compiler_params=FIRST_PARAMS,
        name="collide_own",
    )(flow, heat, flow_weight, heat_weight, resistance, conductivity, solid)

    from_far, from_near = swap_along_x(far, near)

    strips, from_left, from_right = pl.pallas_call(
        strip_kernel,
        out_shape=(
            floats(rings, HALF_ROWS, ZED, LANES),
            floats(BULK_ROWS, ZED, LANES),
            floats(BULK_ROWS, ZED, LANES),
        ),
        compiler_params=PARAMS,
        name="pack_strips",
    )(own, from_far, from_near)

    strips = lax.all_to_all(strips, "gy", 0, 0)

    state, wide_sides, adjoint, part_resistance, part_conductivity, far, near = pl.pallas_call(
        second_kernel,
        out_shape=(
            floats(MEMBERS, 4, ZED, WIDE),
            floats(2, 4, ZED, WIDE),
            floats(MEMBERS, 2, ZED, WIDE),
            floats(2, ZED, LANES),
            floats(2, ZED, LANES),
            floats(ADJ_SENT, ZED, LANES),
            floats(ADJ_SENT, ZED, LANES),
        ),
        scratch_shapes=[
            vmem(STRIP_ROWS, ZED, LANES),
            vmem(MEMBERS, 4, ZED, WIDE),
            vmem(MEMBERS, 2, ZED, WIDE),
            vmem(MEMBERS, 2, ZED, WIDE),
            vmem(ADJ_SENT, ZED, LANES),
            vmem(ADJ_SENT, ZED, LANES),
        ],
        compiler_params=PARAMS,
        name="forward_and_seed",
    )(own, from_left, from_right, strips)

    from_far, from_near = swap_along_x(far, near)

    return pl.pallas_call(
        third_kernel,
        out_shape=(floats(2, ZED, LANES), floats(2, ZED, LANES)),
        scratch_shapes=[
            vmem(ADJ_SENT, ZED, LANES),
            vmem(ADJ_SENT, ZED, LANES),
            vmem(MEMBERS, 4, ZED, WIDE),
            vmem(MEMBERS, 4, ZED, WIDE),
            vmem(MEMBERS, 2, ZED, LANES),
        ],
        compiler_params=PARAMS,
        name="adjoint_steps",
    )(flow, heat, state, wide_sides, adjoint, part_resistance, part_conductivity, from_far, from_near)


def solution(mesh):
    split = P("gx", None, "gy")
    stacked = P(None, "gx", None, "gy")
    return jax.shard_map(
        on_device,
        mesh=mesh,
        in_specs=(stacked, stacked, stacked, split, split, split, split),
        out_specs=(split, split),
        check_vma=False,
    )
```

```python
import jax
import jax.numpy as jnp
from jax import lax
from jax.experimental import pallas as pl
from jax.experimental.pallas import tpu as pltpu
from jax.sharding import PartitionSpec as P

ZED = 16
LANES = 128
WIDE = 2 * LANES
EDGE = 4

FLOW_VELOCITY = [
    (0, 0, 0),
    (1, 0, 0),
    (-1, 0, 0),
    (0, 1, 0),
    (0, -1, 0),
    (0, 0, 1),
    (0, 0, -1),
    (1, 1, 0),
    (-1, -1, 0),
    (1, -1, 0),
    (-1, 1, 0),
    (1, 0, 1),
    (-1, 0, -1),
    (1, 0, -1),
    (-1, 0, 1),
    (0, 1, 1),
    (0, -1, -1),
    (0, 1, -1),
    (0, -1, 1),
]
VELOCITY = FLOW_VELOCITY + FLOW_VELOCITY[:7]
STILL = (0, 0, 0)
MEMBERS = len(VELOCITY)
RIGHTWARD = [q for q in range(MEMBERS) if VELOCITY[q][0] == 1]
LEFTWARD = [q for q in range(MEMBERS) if VELOCITY[q][0] == -1]
LEVEL = [q for q in range(MEMBERS) if VELOCITY[q][0] == 0]

MOBILITY, RATE, WEIGHT = MEMBERS, MEMBERS + 1, MEMBERS + 2
FIELDS = MEMBERS + 6
SIDE_FIELDS = list(range(MEMBERS, FIELDS))

SUMS = 9
SUM_FIELDS = [FIELDS + k for k in range(SUMS)]

SLOTS = LANES // (2 * EDGE)
STRIP_ROWS = 2 * FIELDS // SLOTS
HALF_ROWS = STRIP_ROWS // 2


def rows_of(entries):
    return {entry: row for row, entry in enumerate(entries)}


TO_RIGHT = rows_of([(q, 0) for q in RIGHTWARD] + [(k, 1) for k in RIGHTWARD + SIDE_FIELDS + SUM_FIELDS])
TO_LEFT = rows_of([(q, 1) for q in LEFTWARD] + [(k, 0) for k in LEFTWARD + SIDE_FIELDS + SUM_FIELDS])
ADJ_TO_RIGHT = rows_of([(q, 0) for q in LEFTWARD] + [(k, 1) for k in LEFTWARD + SUM_FIELDS])
ADJ_TO_LEFT = rows_of([(q, 1) for q in RIGHTWARD] + [(k, 0) for k in RIGHTWARD + SUM_FIELDS])
BULK_ROWS, ADJ_BULK = len(TO_RIGHT), len(ADJ_TO_RIGHT)


def with_strips(bulk):
    return bulk + -(-bulk // SLOTS)


SENT, ADJ_SENT = with_strips(BULK_ROWS), with_strips(ADJ_BULK)


def level_sums(p):
    s1, s2, d1, d2 = p[3] + p[4], p[5] + p[6], p[3] - p[4], p[5] - p[6]
    s7, s8, d7, d8 = p[15] + p[16], p[17] + p[18], p[15] - p[16], p[17] - p[18]
    yz = s7 + s8
    mass = p[0] + (s1 + s2) + yz
    return [
        mass, d1 + (d7 + d8), d2 + (d7 - d8), s1 + yz, s2 + yz, s7 - s8,
        p[19] + (p[22] + p[23]) + (p[24] + p[25]), p[22] - p[23], p[24] - p[25],
    ]


def level_adjoint_sums(p):
    s1, s2, d1, d2 = p[3] + p[4], p[5] + p[6], p[3] - p[4], p[5] - p[6]
    s7, s8, d7, d8 = p[15] + p[16], p[17] + p[18], p[15] - p[16], p[17] - p[18]
    yz = s7 + s8
    t1, t2 = s1 + s1, s2 + s2
    mass = 12.0 * p[0] + (t1 + t2) + yz
    return [
        mass, (d1 + d1) + (d7 + d8), (d2 + d2) + (d7 - d8), t1 + yz, t2 + yz, s7 - s8,
        0.35 * p[19] + 0.175 * ((p[22] + p[23]) + (p[24] + p[25])),
        0.125 * (p[22] - p[23]), 0.125 * (p[24] - p[25]),
    ]


def cross_sums(p):
    pairs = [(1, 2), (7, 8), (9, 10), (11, 12), (13, 14)]
    return [p[a] + p[b] for a, b in pairs], [p[a] - p[b] for a, b in pairs]


def common(p, level, mobility):
    s, d = cross_sums(p)
    xy, xz = s[1] + s[2], s[3] + s[4]
    along = s[0] + xy + xz
    rho = level[0] + along
    j = (d[0] + (d[1] + d[2]) + (d[3] + d[4]), level[1] + (d[1] - d[2]), level[2] + (d[3] - d[4]))
    temperature = level[6] + (p[20] + p[21])
    flux = (p[20] - p[21], level[7], level[8])
    u = tuple(mobility * jk for jk in j)
    square = (u[0] * u[0], u[1] * u[1], u[2] * u[2])
    third = rho * (1.0 / 3.0)
    stress = (
        along - third - square[0],
        (level[3] + xy) - third - square[1],
        (level[4] + xz) - third - square[2],
        (s[1] - s[2]) - u[0] * u[1],
        (s[3] - s[4]) - u[0] * u[2],
        level[5] - u[1] * u[2],
    )
    decay = jnp.exp(-2.0 * (temperature - 1.0))
    omega = 1.0 / (0.5 + 0.3 * decay)
    return rho, j, u, square, stress, temperature, flux, decay, omega


def collide(p, level, mobility, rate, wanted):
    rho, _, u, square, stress, temperature, flux, _, omega = common(p, level, mobility)
    solid = mobility == 0.0
    lam = 1.2 - omega
    trace = stress[0] + stress[1] + stress[2]
    base = 1.2 * rho - 1.8 * (square[0] + square[1] + square[2]) - (1.5 * lam) * trace
    scale = 4.5 * lam
    mxx = 5.4 * square[0] + scale * stress[0]
    myy = 5.4 * square[1] + scale * stress[1]
    mzz = 5.4 * square[2] + scale * stress[2]
    mxy = 2.0 * (5.4 * (u[0] * u[1]) + scale * stress[3])
    mxz = 2.0 * (5.4 * (u[0] * u[2]) + scale * stress[4])
    myz = 2.0 * (5.4 * (u[1] * u[2]) + scale * stress[5])
    bx, by, bz = base + mxx, base + myy, base + mzz
    sxy, sxz, syz = bx + myy, bx + mzz, by + mzz
    even = [bx, by, bz, sxy + mxy, sxy - mxy, sxz + mxz, sxz - mxz, syz + myz, syz - myz]
    odd = [u[0], u[1], u[2], u[0] + u[1], u[0] - u[1], u[0] + u[2], u[0] - u[2], u[1] + u[2], u[1] - u[2]]
    result = {}
    if 0 in wanted:
        result[0] = jnp.where(solid, p[0], (1.0 / 3.0) * base - 0.2 * p[0])
    for k in range(9):
        a, b = 2 * k + 1, 2 * k + 2
        w = 1.0 / 18.0 if k < 3 else 1.0 / 36.0
        e, o = w * even[k], (3.6 * w) * odd[k]
        if a in wanted:
            result[a] = jnp.where(solid, p[b], (e + o) - 0.2 * p[a])
        if b in wanted:
            result[b] = jnp.where(solid, p[a], (e - o) - 0.2 * p[b])
    keep = 0.5 * (1.4 - rate)
    push = (0.5 * rate) * temperature
    warm = 0.175 * temperature
    if 19 in wanted:
        result[19] = 0.35 * temperature - 0.4 * p[19]
    for k in range(3):
        along = keep * flux[k] + push * u[k]
        a, b = 20 + 2 * k, 21 + 2 * k
        if a in wanted:
            result[a] = (warm + along) - 0.4 * p[a]
        if b in wanted:
            result[b] = (warm - along) - 0.4 * p[b]
    return result


def pull_back(p, level, pa, adjoint_level, mobility, rate, wanted, sensitivity):
    rho, j, u, square, stress, temperature, flux, decay, omega = common(p, level, mobility)
    solid = mobility == 0.0
    lam = 1.2 - omega
    s, d = cross_sums(pa)
    w = 1.0 / 36.0
    xy, xz = s[1] + s[2], s[3] + s[4]
    along = (s[0] + s[0]) + xy + xz
    mass = w * (adjoint_level[0] + along)
    px = w * ((d[0] + d[0]) + (d[1] + d[2]) + (d[3] + d[4]))
    py = w * (adjoint_level[1] + (d[1] - d[2]))
    pz = w * (adjoint_level[2] + (d[3] - d[4]))
    rxx, ryy, rzz = w * along, w * (adjoint_level[3] + xy), w * (adjoint_level[4] + xz)
    rxy, rxz, ryz = w * (s[1] - s[2]), w * (s[3] - s[4]), w * adjoint_level[5]
    shift = 1.5 * mass
    dxx, dyy, dzz = 4.5 * rxx - shift, 4.5 * ryy - shift, 4.5 * rzz - shift
    dxy, dxz, dyz = 4.5 * rxy, 4.5 * rxz, 4.5 * ryz
    mix = 2.4 - 2.0 * lam
    b = ((pa[20] - pa[21]) * 0.125, adjoint_level[7], adjoint_level[8])
    push = (4.0 * rate) * temperature
    ux = 3.6 * px + mix * (dxx * u[0] + dxy * u[1] + dxz * u[2]) + push * b[0]
    uy = 3.6 * py + mix * (dxy * u[0] + dyy * u[1] + dyz * u[2]) + push * b[1]
    uz = 3.6 * pz + mix * (dxz * u[0] + dyz * u[1] + dzz * u[2]) + push * b[2]
    result = {}
    if wanted:
        lam_bar = (
            dxx * stress[0]
            + dyy * stress[1]
            + dzz * stress[2]
            + 2.0 * (dxy * stress[3] + dxz * stress[4] + dyz * stress[5])
        )
        rho_bar = 1.2 * mass - (1.5 * lam) * ((rxx + ryy + rzz) - mass)
        jx, jy, jz = mobility * ux, mobility * uy, mobility * uz
        ex, ey, ez = lam * dxx, lam * dyy, lam * dzz
        exy, exz, eyz = (2.0 * lam) * dxy, (2.0 * lam) * dxz, (2.0 * lam) * dyz
        hx, hy, hz = rho_bar + ex, rho_bar + ey, rho_bar + ez
        gxy, gxz, gyz = hx + ey, hx + ez, hy + ez
        even = [hx, hy, hz, gxy + exy, gxy - exy, gxz + exz, gxz - exz, gyz + eyz, gyz - eyz]
        odd = [jx, jy, jz, jx + jy, jx - jy, jx + jz, jx - jz, jy + jz, jy - jz]
        if 0 in wanted:
            result[0] = jnp.where(solid, pa[0], rho_bar - 0.2 * pa[0])
        for k in range(9):
            a, m = 2 * k + 1, 2 * k + 2
            if a in wanted:
                result[a] = jnp.where(solid, pa[m], (even[k] + odd[k]) - 0.2 * pa[a])
            if m in wanted:
                result[m] = jnp.where(solid, pa[a], (even[k] - odd[k]) - 0.2 * pa[m])
        warm = (
            adjoint_level[6]
            + 0.175 * (pa[20] + pa[21])
            + (4.0 * rate) * (b[0] * u[0] + b[1] * u[1] + b[2] * u[2])
            - jnp.where(solid, 0.0, lam_bar * (0.6 * decay) * (omega * omega))
        )
        keep = 5.6 - 4.0 * rate
        if 19 in wanted:
            result[19] = warm - 0.4 * pa[19]
        for k in range(3):
            along = keep * b[k]
            a, m = 20 + 2 * k, 21 + 2 * k
            if a in wanted:
                result[a] = (warm + along) - 0.4 * pa[a]
            if m in wanted:
                result[m] = (warm - along) - 0.4 * pa[m]
    if sensitivity:
        by_resistance = -(mobility * mobility) * (ux * j[0] + uy * j[1] + uz * j[2])
        bent = (
            b[0] * (temperature * u[0] - flux[0])
            + b[1] * (temperature * u[1] - flux[1])
            + b[2] * (temperature * u[2] - flux[2])
        )
        by_conductivity = (-1.6 * (rate * rate)) * bent
        result["by"] = (by_resistance, by_conductivity)
    return result


def turn(value, by, axis):
    count = value.shape[axis]
    by %= count
    return pltpu.roll(value, by, axis) if by else value


def side_by_side(parts):
    lane = lax.broadcasted_iota(jnp.int32, (ZED, LANES), 1)
    row = None
    for slot, part in enumerate(parts):
        row = part if row is None else jnp.where(lane >= 2 * EDGE * slot, part, row)
    return row


def packed(value, slot):
    return turn(value, 2 * EDGE * slot + EDGE, 1)


def pack_rows(parts):
    return [
        side_by_side([part(slot) for slot, part in enumerate(parts[start : start + SLOTS])])
        for start in range(0, len(parts), SLOTS)
    ]


def halves():
    return [pl.ds(0, 8), pl.ds(8, 8)]


def low_lanes():
    return lax.broadcasted_iota(jnp.int32, (ZED, LANES), 1) % (2 * EDGE) < EDGE


def ring_place(axis):
    count = lax.axis_size(axis)
    place = lax.axis_index(axis)
    return lax.rem(place + count - 1, count), lax.rem(place + 1, count)


def either_way(move):
    first = lax.rem(lax.axis_index("gx"), 2) == 0
    pl.when(first)(lambda: move(True))
    pl.when(jnp.logical_not(first))(lambda: move(False))


def copy_rows(target, source):
    for row in range(source.shape[0]):
        target[row] = source[row]


def split(value):
    return value[:, :LANES], value[:, LANES:], 0


def beside(row, slot):
    return row, -EDGE - 2 * EDGE * slot


def moved(triple, velocity, way):
    main, extra, by = triple
    _, step_y, step_z = velocity
    step = way * step_y
    main, extra = turn(main, way * step_z, 0), turn(extra, way * step_z, 0)
    if not step:
        return main, turn(extra, by, 1)
    main, extra = turn(main, step, 1), turn(extra, by + step, 1)
    lane = lax.broadcasted_iota(jnp.int32, (ZED, LANES), 1)
    edge = lane == (0 if step == 1 else LANES - 1)
    return jnp.where(edge, extra, main), jnp.where(edge, main, extra)


def put(ref, q, i, pair):
    ref[q, i, :, :LANES], ref[q, i, :, LANES:] = pair


def tiles(lanes):
    return [(z, pl.ds(t, LANES)) for z in halves() for t in range(0, lanes, LANES)]


def own_row(k, c):
    return c * FIELDS + k


def own_value(own, strip, k, c):
    place = own_row(k, c)
    return (own[place],) + beside(strip[place // SLOTS], place % SLOTS)


def halo_value(buffer, bulk, place):
    return (buffer[place],) + beside(buffer[bulk + place // SLOTS], place % SLOTS)


def send_out(far, near, right, left):
    def send(first):
        copy_rows(far, left if first else right)
        copy_rows(near, right if first else left)

    either_way(send)


def take_in(from_left, from_right, from_far, from_near):
    def receive(first):
        copy_rows(from_left, from_far if first else from_near)
        copy_rows(from_right, from_near if first else from_far)

    either_way(receive)


def first_kernel(
    flow_in, heat_in, flow_weight_in, heat_weight_in, resistance_in, conductivity_in, solid_in,
    own_out, strips_out,
    own, strips, flow, heat, flow_weight, heat_weight, resistance, conductivity, solid, arrived, sent,
):
    pairs = [
        (flow_in, flow),
        (heat_in, heat),
        (resistance_in, resistance),
        (conductivity_in, conductivity),
        (solid_in, solid),
        (flow_weight_in, flow_weight),
        (heat_weight_in, heat_weight),
    ]
    copies = [pltpu.make_async_copy(a, b, arrived.at[k]) for k, (a, b) in enumerate(pairs)]
    for copy in copies:
        copy.start()
    strips[...] = jnp.zeros(strips.shape, jnp.float32)
    for copy in copies:
        copy.wait()
    for c in range(2):
        for z in halves():
            mobility = jnp.where(solid[c, z, :] != 0, 0.0, 1.0 / (1.0 + resistance[c, z, :]))
            rate = 1.0 / (0.5 + 0.4 * conductivity[c, z, :])
            p = [flow[q, c, z, :] for q in range(19)] + [heat[q, c, z, :] for q in range(7)]
            after = collide(p, level_sums(p), mobility, rate, range(MEMBERS))
            more = [mobility, rate] + [flow_weight[k, c, z, :] for k in range(3)] + [heat_weight[c, z, :]]
            for k, value in enumerate([after[q] for q in range(MEMBERS)] + more):
                own[own_row(k, c), z, :] = value
    copy_own = pltpu.make_async_copy(own, own_out, sent.at[0])
    copy_own.start()
    rows = pack_rows([lambda slot, k=k: packed(own[k], slot) for k in range(2 * FIELDS)])
    low = low_lanes()
    below, above = ring_place("gy")
    for k in range(HALF_ROWS):
        strips[above, k] = jnp.where(low, rows[k], turn(rows[k + HALF_ROWS], EDGE, 1))
        strips[below, k] = jnp.where(low, turn(rows[k], -EDGE, 1), rows[k + HALF_ROWS])
    copy_strips = pltpu.make_async_copy(strips, strips_out, sent.at[1])
    copy_strips.start()
    copy_own.wait()
    copy_strips.wait()


def halo_kernel(own, strips, far, near, strip, right, left):
    low = low_lanes()
    below, above = ring_place("gy")
    for k in range(HALF_ROWS):
        under, over = strips[below, k], strips[above, k]
        strip[k] = jnp.where(low, under, turn(over, EDGE, 1))
        strip[k + HALF_ROWS] = jnp.where(low, turn(under, -EDGE, 1), over)
    for side, rows, c in ((right, TO_RIGHT, 1), (left, TO_LEFT, 0)):
        level = {q: moved(own_value(own, strip, q, c), VELOCITY[q], 1) for q in LEVEL}
        sums = [level_sums({q: level[q][t] for q in LEVEL}) for t in range(2)]
        parts = []
        for (k, column), row in rows.items():
            if k >= FIELDS:
                side[row] = sums[0][k - FIELDS]
                parts.append(lambda slot, k=k: packed(sums[1][k - FIELDS], slot))
            else:
                place = own_row(k, column)
                side[row] = own[place]
                parts.append(
                    lambda slot, place=place: turn(
                        strip[place // SLOTS], 2 * EDGE * (slot - place % SLOTS), 1
                    )
                )
        for k, row in enumerate(pack_rows(parts)):
            side[BULK_ROWS + k] = row
    send_out(far, near, right, left)


def level_of(p, column, sums):
    return sums(p) if 0 <= column <= 1 else [p[q] for q in LEVEL[:SUMS]]


def second_kernel(
    own, strip, from_far, from_near,
    state, wide_sides, adjoint, by_resistance, by_conductivity, far, near,
    from_left, from_right, after, later, seed, right, left,
):
    take_in(from_left, from_right, from_far, from_near)

    def wide(k, column):
        if column < 0:
            return halo_value(from_left, BULK_ROWS, TO_RIGHT[k, column + 2])
        if column > 1:
            return halo_value(from_right, BULK_ROWS, TO_LEFT[k, column - 2])
        return own_value(own, strip, k, column)

    for column in range(-1, 3):
        i = column + 1
        put(wide_sides, 0, i, moved(wide(MOBILITY, column), STILL, 1))
        put(wide_sides, 1, i, moved(wide(RATE, column), STILL, 1))
        for q in range(MEMBERS):
            if 0 <= column <= 1 or q not in LEVEL:
                put(state, q, i, moved(wide(q, column - VELOCITY[q][0]), VELOCITY[q], 1))
            elif q in LEVEL[:SUMS]:
                put(state, q, i, moved(wide(SUM_FIELDS[LEVEL.index(q)], column), STILL, 1))
    for column in range(-1, 3):
        i = column + 1
        wanted = [q for q in range(MEMBERS) if 0 <= column + VELOCITY[q][0] <= 1]
        for z, y in tiles(WIDE):
            p = [state[q, i, z, y] for q in range(MEMBERS)]
            level = level_of(p, column, level_sums)
            result = collide(p, level, wide_sides[0, i, z, y], wide_sides[1, i, z, y], wanted)
            for q in wanted:
                after[q, i, z, y] = result[q]
    for c in range(2):
        for q in range(MEMBERS):
            put(later, q, c, moved(split(after[q, c + 1 - VELOCITY[q][0]]), VELOCITY[q], 1))
    for column in range(-1, 3):
        weights = [wide(WEIGHT + k, column) for k in range(3)]
        weights = [(main, turn(extra, by, 1)) for main, extra, by in weights]
        for q in range(1, MEMBERS):
            velocity = VELOCITY[q]
            c = column - velocity[0]
            if not 0 <= c <= 1:
                continue
            if q < 19:
                parts = [
                    tuple(value if velocity[k] > 0 else -value for value in weights[k]) for k in range(3) if velocity[k]
                ]
                pair = parts[0] if len(parts) == 1 else tuple(a + b for a, b in zip(*parts))
                pair += (0,)
            else:
                pair = wide(WEIGHT + 3, column)
            put(seed, q, c, moved(pair, velocity, -1))
    for c in range(2):
        for z, y in tiles(WIDE):
            p = [later[q, c, z, y] for q in range(MEMBERS)]
            pa = [jnp.zeros((8, LANES), jnp.float32)] + [seed[q, c, z, y] for q in range(1, MEMBERS)]
            inner = y.start == 0
            result = pull_back(
                p, level_sums(p), pa, level_adjoint_sums(pa),
                wide_sides[0, c + 1, z, y], wide_sides[1, c + 1, z, y], range(MEMBERS), inner,
            )
            if inner:
                by_resistance[c, z, :], by_conductivity[c, z, :] = result["by"]
            for q in range(MEMBERS):
                adjoint[q, c, z, y] = result[q]
    for side, rows, c in ((right, ADJ_TO_RIGHT, 1), (left, ADJ_TO_LEFT, 0)):
        level = {q: moved(split(adjoint[q, c]), VELOCITY[q], -1) for q in LEVEL}
        sums = [level_adjoint_sums({q: level[q][t] for q in LEVEL}) for t in range(2)]
        parts = []
        for (k, column), row in rows.items():
            if k >= FIELDS:
                side[row] = sums[0][k - FIELDS]
                parts.append(lambda slot, k=k: packed(sums[1][k - FIELDS], slot))
            else:
                side[row] = adjoint[k, column, :, :LANES]
                parts.append(lambda slot, k=k, column=column: packed(adjoint[k, column, :, LANES:], slot))
        for k, row in enumerate(pack_rows(parts)):
            side[ADJ_BULK + k] = row
    send_out(far, near, right, left)


def third_kernel(
    flow, heat, state, wide_sides, adjoint, part_resistance, part_conductivity, from_far, from_near,
    by_resistance, by_conductivity,
    from_left, from_right, arrived, earlier, last,
):
    take_in(from_left, from_right, from_far, from_near)

    def wide(k, column):
        if column < 0:
            return halo_value(from_left, ADJ_BULK, ADJ_TO_RIGHT[k, column + 2])
        if column > 1:
            return halo_value(from_right, ADJ_BULK, ADJ_TO_LEFT[k, column - 2])
        return split(adjoint[k, column])

    for column in range(-1, 3):
        i = column + 1
        for q in range(MEMBERS):
            if 0 <= column <= 1 or q not in LEVEL:
                put(arrived, q, i, moved(wide(q, column + VELOCITY[q][0]), VELOCITY[q], -1))
            elif q in LEVEL[:SUMS]:
                put(arrived, q, i, moved(wide(SUM_FIELDS[LEVEL.index(q)], column), STILL, 1))
    for column in range(-1, 3):
        i = column + 1
        own = 0 <= column <= 1
        for z, y in tiles(WIDE):
            inner = y.start == 0
            wanted = [
                q
                for q in range(MEMBERS)
                if 0 <= column - VELOCITY[q][0] <= 1 and (inner or VELOCITY[q][1])
            ]
            p = [state[q, i, z, y] for q in range(MEMBERS)]
            pa = [arrived[q, i, z, y] for q in range(MEMBERS)]
            result = pull_back(
                p, level_of(p, column, level_sums), pa, level_of(pa, column, level_adjoint_sums),
                wide_sides[0, i, z, y], wide_sides[1, i, z, y], wanted, inner and own,
            )
            for q in wanted:
                earlier[q, i, z, y] = result[q]
            if inner and own:
                by_resistance[column, z, :] = part_resistance[column, z, :] + result["by"][0]
                by_conductivity[column, z, :] = part_conductivity[column, z, :] + result["by"][1]
    for c in range(2):
        for q in range(MEMBERS):
            velocity = VELOCITY[q]
            i = c + 1 + velocity[0]
            if velocity[1]:
                last[q, c] = moved(split(earlier[q, i]), velocity, -1)[0]
            else:
                last[q, c] = turn(earlier[q, i, :, :LANES], -velocity[2], 0)
    narrow = pl.ds(0, LANES)
    for c in range(2):
        for z in halves():
            p = [flow[q, c, z, :] for q in range(19)] + [heat[q, c, z, :] for q in range(7)]
            pa = [last[q, c, z, :] for q in range(MEMBERS)]
            result = pull_back(
                p, level_sums(p), pa, level_adjoint_sums(pa),
                wide_sides[0, c + 1, z, narrow], wide_sides[1, c + 1, z, narrow], (), True,
            )
            by_resistance[c, z, :] += result["by"][0]
            by_conductivity[c, z, :] += result["by"][1]


def floats(*shape):
    return jax.ShapeDtypeStruct(shape, jnp.float32)


def vmem(*shape):
    return pltpu.VMEM(shape, jnp.float32)


def swap_along_x(far, near):
    count = lax.axis_size("gx")
    across = [(i, (i + (1 if i % 2 else -1)) % count) for i in range(count)]
    within = [(i, i ^ 1) for i in range(count)]
    return lax.ppermute(far, "gx", across), lax.ppermute(near, "gx", within)


FIRST_PARAMS = pltpu.CompilerParams(vmem_limit_bytes=56 * 1024 * 1024)
PARAMS = pltpu.CompilerParams(vmem_limit_bytes=24 * 1024 * 1024)


def on_device(flow, heat, flow_weight, heat_weight, resistance, conductivity, solid):
    rings = lax.axis_size("gy")
    in_hbm = pl.BlockSpec(memory_space=pltpu.HBM)
    own, strips = pl.pallas_call(
        first_kernel,
        in_specs=[in_hbm] * 7,
        out_specs=[in_hbm] * 2,
        out_shape=(floats(2 * FIELDS, ZED, LANES), floats(rings, HALF_ROWS, ZED, LANES)),
        scratch_shapes=[
            vmem(2 * FIELDS, ZED, LANES),
            vmem(rings, HALF_ROWS, ZED, LANES),
            vmem(19, 2, ZED, LANES),
            vmem(7, 2, ZED, LANES),
            vmem(3, 2, ZED, LANES),
            vmem(2, ZED, LANES),
            vmem(2, ZED, LANES),
            vmem(2, ZED, LANES),
            pltpu.VMEM((2, ZED, LANES), jnp.int32),
            pltpu.SemaphoreType.DMA((7,)),
            pltpu.SemaphoreType.DMA((2,)),
        ],
        compiler_params=FIRST_PARAMS,
        name="collide_own",
    )(flow, heat, flow_weight, heat_weight, resistance, conductivity, solid)

    strips = lax.all_to_all(strips, "gy", 0, 0)

    far, near, strip = pl.pallas_call(
        halo_kernel,
        out_shape=(floats(SENT, ZED, LANES), floats(SENT, ZED, LANES), floats(STRIP_ROWS, ZED, LANES)),
        scratch_shapes=[vmem(SENT, ZED, LANES), vmem(SENT, ZED, LANES)],
        compiler_params=PARAMS,
        name="halo_buffers",
    )(own, strips)

    from_far, from_near = swap_along_x(far, near)

    state, wide_sides, adjoint, part_resistance, part_conductivity, far, near = pl.pallas_call(
        second_kernel,
        out_shape=(
            floats(MEMBERS, 4, ZED, WIDE),
            floats(2, 4, ZED, WIDE),
            floats(MEMBERS, 2, ZED, WIDE),
            floats(2, ZED, LANES),
            floats(2, ZED, LANES),
            floats(ADJ_SENT, ZED, LANES),
            floats(ADJ_SENT, ZED, LANES),
        ),
        scratch_shapes=[
            vmem(SENT, ZED, LANES),
            vmem(SENT, ZED, LANES),
            vmem(MEMBERS, 4, ZED, WIDE),
            vmem(MEMBERS, 2, ZED, WIDE),
            vmem(MEMBERS, 2, ZED, WIDE),
            vmem(ADJ_SENT, ZED, LANES),
            vmem(ADJ_SENT, ZED, LANES),
        ],
        compiler_params=PARAMS,
        name="forward_and_seed",
    )(own, strip, from_far, from_near)

    from_far, from_near = swap_along_x(far, near)

    return pl.pallas_call(
        third_kernel,
        out_shape=(floats(2, ZED, LANES), floats(2, ZED, LANES)),
        scratch_shapes=[
            vmem(ADJ_SENT, ZED, LANES),
            vmem(ADJ_SENT, ZED, LANES),
            vmem(MEMBERS, 4, ZED, WIDE),
            vmem(MEMBERS, 4, ZED, WIDE),
            vmem(MEMBERS, 2, ZED, LANES),
        ],
        compiler_params=PARAMS,
        name="adjoint_steps",
    )(flow, heat, state, wide_sides, adjoint, part_resistance, part_conductivity, from_far, from_near)


def solution(mesh):
    split = P("gx", None, "gy")
    stacked = P(None, "gx", None, "gy")
    return jax.shard_map(
        on_device,
        mesh=mesh,
        in_specs=(stacked, stacked, stacked, split, split, split, split),
        out_specs=(split, split),
        check_vma=False,
    )
```

```python
import jax
import jax.numpy as jnp
from jax import lax
from jax.experimental import pallas as pl
from jax.experimental.pallas import tpu as pltpu
from jax.sharding import PartitionSpec as P

ZED = 16
LANES = 128
WIDE = 2 * LANES
EDGE = 4

FLOW_VELOCITY = [
    (0, 0, 0),
    (1, 0, 0),
    (-1, 0, 0),
    (0, 1, 0),
    (0, -1, 0),
    (0, 0, 1),
    (0, 0, -1),
    (1, 1, 0),
    (-1, -1, 0),
    (1, -1, 0),
    (-1, 1, 0),
    (1, 0, 1),
    (-1, 0, -1),
    (1, 0, -1),
    (-1, 0, 1),
    (0, 1, 1),
    (0, -1, -1),
    (0, 1, -1),
    (0, -1, 1),
]
VELOCITY = FLOW_VELOCITY + FLOW_VELOCITY[:7]
STILL = (0, 0, 0)
MEMBERS = len(VELOCITY)
RIGHTWARD = [q for q in range(MEMBERS) if VELOCITY[q][0] == 1]
LEFTWARD = [q for q in range(MEMBERS) if VELOCITY[q][0] == -1]
LEVEL = [q for q in range(MEMBERS) if VELOCITY[q][0] == 0]

MOBILITY, RATE, WEIGHT = MEMBERS, MEMBERS + 1, MEMBERS + 2
FIELDS = MEMBERS + 6
SIDE_FIELDS = list(range(MEMBERS, FIELDS))

SUMS = 9
SUM_FIELDS = [FIELDS + k for k in range(SUMS)]

SLOTS = LANES // (2 * EDGE)
STRIP_ROWS = 2 * FIELDS // SLOTS
HALF_ROWS = STRIP_ROWS // 2


def rows_of(entries):
    return {entry: row for row, entry in enumerate(entries)}


TO_RIGHT = rows_of([(q, 0) for q in RIGHTWARD] + [(k, 1) for k in RIGHTWARD + SIDE_FIELDS + SUM_FIELDS])
TO_LEFT = rows_of([(q, 1) for q in LEFTWARD] + [(k, 0) for k in LEFTWARD + SIDE_FIELDS + SUM_FIELDS])
ADJ_TO_RIGHT = rows_of([(q, 0) for q in LEFTWARD] + [(k, 1) for k in LEFTWARD + SUM_FIELDS])
ADJ_TO_LEFT = rows_of([(q, 1) for q in RIGHTWARD] + [(k, 0) for k in RIGHTWARD + SUM_FIELDS])
BULK_ROWS, ADJ_BULK = len(TO_RIGHT), len(ADJ_TO_RIGHT)


def with_strips(bulk):
    return bulk + -(-bulk // SLOTS)


SENT, ADJ_SENT = with_strips(BULK_ROWS), with_strips(ADJ_BULK)


def level_sums(p):
    s1, s2, d1, d2 = p[3] + p[4], p[5] + p[6], p[3] - p[4], p[5] - p[6]
    s7, s8, d7, d8 = p[15] + p[16], p[17] + p[18], p[15] - p[16], p[17] - p[18]
    yz = s7 + s8
    mass = p[0] + (s1 + s2) + yz
    return [
        mass, d1 + (d7 + d8), d2 + (d7 - d8), s1 + yz, s2 + yz, s7 - s8,
        p[19] + (p[22] + p[23]) + (p[24] + p[25]), p[22] - p[23], p[24] - p[25],
    ]


def level_adjoint_sums(p):
    s1, s2, d1, d2 = p[3] + p[4], p[5] + p[6], p[3] - p[4], p[5] - p[6]
    s7, s8, d7, d8 = p[15] + p[16], p[17] + p[18], p[15] - p[16], p[17] - p[18]
    yz = s7 + s8
    t1, t2 = s1 + s1, s2 + s2
    mass = 12.0 * p[0] + (t1 + t2) + yz
    return [
        mass, (d1 + d1) + (d7 + d8), (d2 + d2) + (d7 - d8), t1 + yz, t2 + yz, s7 - s8,
        0.35 * p[19] + 0.175 * ((p[22] + p[23]) + (p[24] + p[25])),
        0.125 * (p[22] - p[23]), 0.125 * (p[24] - p[25]),
    ]


def cross_sums(p):
    pairs = [(1, 2), (7, 8), (9, 10), (11, 12), (13, 14)]
    return [p[a] + p[b] for a, b in pairs], [p[a] - p[b] for a, b in pairs]


def common(p, level, mobility):
    s, d = cross_sums(p)
    xy, xz = s[1] + s[2], s[3] + s[4]
    along = s[0] + xy + xz
    rho = level[0] + along
    j = (d[0] + (d[1] + d[2]) + (d[3] + d[4]), level[1] + (d[1] - d[2]), level[2] + (d[3] - d[4]))
    temperature = level[6] + (p[20] + p[21])
    flux = (p[20] - p[21], level[7], level[8])
    u = tuple(mobility * jk for jk in j)
    square = (u[0] * u[0], u[1] * u[1], u[2] * u[2])
    third = rho * (1.0 / 3.0)
    stress = (
        along - third - square[0],
        (level[3] + xy) - third - square[1],
        (level[4] + xz) - third - square[2],
        (s[1] - s[2]) - u[0] * u[1],
        (s[3] - s[4]) - u[0] * u[2],
        level[5] - u[1] * u[2],
    )
    decay = jnp.exp(-2.0 * (temperature - 1.0))
    omega = 1.0 / (0.5 + 0.3 * decay)
    return rho, j, u, square, stress, temperature, flux, decay, omega


def collide(p, level, mobility, rate, wanted):
    rho, _, u, square, stress, temperature, flux, _, omega = common(p, level, mobility)
    solid = mobility == 0.0
    lam = 1.2 - omega
    trace = stress[0] + stress[1] + stress[2]
    base = 1.2 * rho - 1.8 * (square[0] + square[1] + square[2]) - (1.5 * lam) * trace
    scale = 4.5 * lam
    mxx = 5.4 * square[0] + scale * stress[0]
    myy = 5.4 * square[1] + scale * stress[1]
    mzz = 5.4 * square[2] + scale * stress[2]
    mxy = 2.0 * (5.4 * (u[0] * u[1]) + scale * stress[3])
    mxz = 2.0 * (5.4 * (u[0] * u[2]) + scale * stress[4])
    myz = 2.0 * (5.4 * (u[1] * u[2]) + scale * stress[5])
    bx, by, bz = base + mxx, base + myy, base + mzz
    sxy, sxz, syz = bx + myy, bx + mzz, by + mzz
    even = [bx, by, bz, sxy + mxy, sxy - mxy, sxz + mxz, sxz - mxz, syz + myz, syz - myz]
    odd = [u[0], u[1], u[2], u[0] + u[1], u[0] - u[1], u[0] + u[2], u[0] - u[2], u[1] + u[2], u[1] - u[2]]
    result = {}
    if 0 in wanted:
        result[0] = jnp.where(solid, p[0], (1.0 / 3.0) * base - 0.2 * p[0])
    for k in range(9):
        a, b = 2 * k + 1, 2 * k + 2
        w = 1.0 / 18.0 if k < 3 else 1.0 / 36.0
        e, o = w * even[k], (3.6 * w) * odd[k]
        if a in wanted:
            result[a] = jnp.where(solid, p[b], (e + o) - 0.2 * p[a])
        if b in wanted:
            result[b] = jnp.where(solid, p[a], (e - o) - 0.2 * p[b])
    keep = 0.5 * (1.4 - rate)
    push = (0.5 * rate) * temperature
    warm = 0.175 * temperature
    if 19 in wanted:
        result[19] = 0.35 * temperature - 0.4 * p[19]
    for k in range(3):
        along = keep * flux[k] + push * u[k]
        a, b = 20 + 2 * k, 21 + 2 * k
        if a in wanted:
            result[a] = (warm + along) - 0.4 * p[a]
        if b in wanted:
            result[b] = (warm - along) - 0.4 * p[b]
    return result


def pull_back(p, level, pa, adjoint_level, mobility, rate, wanted, sensitivity):
    rho, j, u, square, stress, temperature, flux, decay, omega = common(p, level, mobility)
    solid = mobility == 0.0
    lam = 1.2 - omega
    s, d = cross_sums(pa)
    w = 1.0 / 36.0
    xy, xz = s[1] + s[2], s[3] + s[4]
    along = (s[0] + s[0]) + xy + xz
    mass = w * (adjoint_level[0] + along)
    px = w * ((d[0] + d[0]) + (d[1] + d[2]) + (d[3] + d[4]))
    py = w * (adjoint_level[1] + (d[1] - d[2]))
    pz = w * (adjoint_level[2] + (d[3] - d[4]))
    rxx, ryy, rzz = w * along, w * (adjoint_level[3] + xy), w * (adjoint_level[4] + xz)
    rxy, rxz, ryz = w * (s[1] - s[2]), w * (s[3] - s[4]), w * adjoint_level[5]
    shift = 1.5 * mass
    dxx, dyy, dzz = 4.5 * rxx - shift, 4.5 * ryy - shift, 4.5 * rzz - shift
    dxy, dxz, dyz = 4.5 * rxy, 4.5 * rxz, 4.5 * ryz
    mix = 2.4 - 2.0 * lam
    b = ((pa[20] - pa[21]) * 0.125, adjoint_level[7], adjoint_level[8])
    push = (4.0 * rate) * temperature
    ux = 3.6 * px + mix * (dxx * u[0] + dxy * u[1] + dxz * u[2]) + push * b[0]
    uy = 3.6 * py + mix * (dxy * u[0] + dyy * u[1] + dyz * u[2]) + push * b[1]
    uz = 3.6 * pz + mix * (dxz * u[0] + dyz * u[1] + dzz * u[2]) + push * b[2]
    result = {}
    if wanted:
        lam_bar = (
            dxx * stress[0]
            + dyy * stress[1]
            + dzz * stress[2]
            + 2.0 * (dxy * stress[3] + dxz * stress[4] + dyz * stress[5])
        )
        rho_bar = 1.2 * mass - (1.5 * lam) * ((rxx + ryy + rzz) - mass)
        jx, jy, jz = mobility * ux, mobility * uy, mobility * uz
        ex, ey, ez = lam * dxx, lam * dyy, lam * dzz
        exy, exz, eyz = (2.0 * lam) * dxy, (2.0 * lam) * dxz, (2.0 * lam) * dyz
        hx, hy, hz = rho_bar + ex, rho_bar + ey, rho_bar + ez
        gxy, gxz, gyz = hx + ey, hx + ez, hy + ez
        even = [hx, hy, hz, gxy + exy, gxy - exy, gxz + exz, gxz - exz, gyz + eyz, gyz - eyz]
        odd = [jx, jy, jz, jx + jy, jx - jy, jx + jz, jx - jz, jy + jz, jy - jz]
        if 0 in wanted:
            result[0] = jnp.where(solid, pa[0], rho_bar - 0.2 * pa[0])
        for k in range(9):
            a, m = 2 * k + 1, 2 * k + 2
            if a in wanted:
                result[a] = jnp.where(solid, pa[m], (even[k] + odd[k]) - 0.2 * pa[a])
            if m in wanted:
                result[m] = jnp.where(solid, pa[a], (even[k] - odd[k]) - 0.2 * pa[m])
        warm = (
            adjoint_level[6]
            + 0.175 * (pa[20] + pa[21])
            + (4.0 * rate) * (b[0] * u[0] + b[1] * u[1] + b[2] * u[2])
            - jnp.where(solid, 0.0, lam_bar * (0.6 * decay) * (omega * omega))
        )
        keep = 5.6 - 4.0 * rate
        if 19 in wanted:
            result[19] = warm - 0.4 * pa[19]
        for k in range(3):
            along = keep * b[k]
            a, m = 20 + 2 * k, 21 + 2 * k
            if a in wanted:
                result[a] = (warm + along) - 0.4 * pa[a]
            if m in wanted:
                result[m] = (warm - along) - 0.4 * pa[m]
    if sensitivity:
        by_resistance = -(mobility * mobility) * (ux * j[0] + uy * j[1] + uz * j[2])
        bent = (
            b[0] * (temperature * u[0] - flux[0])
            + b[1] * (temperature * u[1] - flux[1])
            + b[2] * (temperature * u[2] - flux[2])
        )
        by_conductivity = (-1.6 * (rate * rate)) * bent
        result["by"] = (by_resistance, by_conductivity)
    return result


def turn(value, by, axis):
    count = value.shape[axis]
    by %= count
    return pltpu.roll(value, by, axis) if by else value


def side_by_side(parts):
    lane = lax.broadcasted_iota(jnp.int32, (ZED, LANES), 1)
    row = None
    for slot, part in enumerate(parts):
        row = part if row is None else jnp.where(lane >= 2 * EDGE * slot, part, row)
    return row


def packed(value, slot):
    return turn(value, 2 * EDGE * slot + EDGE, 1)


def pack_rows(parts):
    return [
        side_by_side([part(slot) for slot, part in enumerate(parts[start : start + SLOTS])])
        for start in range(0, len(parts), SLOTS)
    ]


def halves():
    return [pl.ds(0, 8), pl.ds(8, 8)]


def low_lanes():
    return lax.broadcasted_iota(jnp.int32, (ZED, LANES), 1) % (2 * EDGE) < EDGE


def either_way(move):
    first = lax.rem(lax.axis_index("gx"), 2) == 0
    pl.when(first)(lambda: move(True))
    pl.when(jnp.logical_not(first))(lambda: move(False))


def copy_rows(target, source):
    for row in range(source.shape[0]):
        target[row] = source[row]


def split(value):
    return value[:, :LANES], value[:, LANES:], 0


def beside(row, slot):
    return row, -EDGE - 2 * EDGE * slot


def moved(triple, velocity, way):
    main, extra, by = triple
    _, step_y, step_z = velocity
    step = way * step_y
    main, extra = turn(main, way * step_z, 0), turn(extra, way * step_z, 0)
    if not step:
        return main, turn(extra, by, 1)
    main, extra = turn(main, step, 1), turn(extra, by + step, 1)
    lane = lax.broadcasted_iota(jnp.int32, (ZED, LANES), 1)
    edge = lane == (0 if step == 1 else LANES - 1)
    return jnp.where(edge, extra, main), jnp.where(edge, main, extra)


def put(ref, q, i, pair):
    ref[q, i, :, :LANES], ref[q, i, :, LANES:] = pair


def tiles(lanes):
    return [(z, pl.ds(t, LANES)) for z in halves() for t in range(0, lanes, LANES)]


def own_row(k, c):
    return c * FIELDS + k


def own_value(own, strip, k, c):
    place = own_row(k, c)
    return (own[place],) + beside(strip[place // SLOTS], place % SLOTS)


def halo_value(buffer, bulk, place):
    return (buffer[place],) + beside(buffer[bulk + place // SLOTS], place % SLOTS)


def send_out(far, near, right, left):
    def send(first):
        copy_rows(far, left if first else right)
        copy_rows(near, right if first else left)

    either_way(send)


def take_in(from_left, from_right, from_far, from_near):
    def receive(first):
        copy_rows(from_left, from_far if first else from_near)
        copy_rows(from_right, from_near if first else from_far)

    either_way(receive)


def first_kernel(
    flow_in, heat_in, flow_weight_in, heat_weight_in, resistance_in, conductivity_in, solid_in,
    own_out, up_out, down_out,
    own, up, down, flow, heat, flow_weight, heat_weight, resistance, conductivity, solid, arrived, sent,
):
    pairs = [
        (flow_in, flow),
        (heat_in, heat),
        (resistance_in, resistance),
        (conductivity_in, conductivity),
        (solid_in, solid),
        (flow_weight_in, flow_weight),
        (heat_weight_in, heat_weight),
    ]
    copies = [pltpu.make_async_copy(a, b, arrived.at[k]) for k, (a, b) in enumerate(pairs)]
    for copy in copies:
        copy.start()
    for copy in copies:
        copy.wait()
    for c in range(2):
        for z in halves():
            mobility = jnp.where(solid[c, z, :] != 0, 0.0, 1.0 / (1.0 + resistance[c, z, :]))
            rate = 1.0 / (0.5 + 0.4 * conductivity[c, z, :])
            p = [flow[q, c, z, :] for q in range(19)] + [heat[q, c, z, :] for q in range(7)]
            after = collide(p, level_sums(p), mobility, rate, range(MEMBERS))
            more = [mobility, rate] + [flow_weight[k, c, z, :] for k in range(3)] + [heat_weight[c, z, :]]
            for k, value in enumerate([after[q] for q in range(MEMBERS)] + more):
                own[own_row(k, c), z, :] = value
    copy_own = pltpu.make_async_copy(own, own_out, sent.at[0])
    copy_own.start()
    rows = pack_rows([lambda slot, k=k: packed(own[k], slot) for k in range(2 * FIELDS)])
    low = low_lanes()
    for k in range(HALF_ROWS):
        up[k] = jnp.where(low, rows[k], turn(rows[k + HALF_ROWS], EDGE, 1))
        down[k] = jnp.where(low, turn(rows[k], -EDGE, 1), rows[k + HALF_ROWS])
    copies = [
        pltpu.make_async_copy(up, up_out, sent.at[1]),
        pltpu.make_async_copy(down, down_out, sent.at[2]),
    ]
    for copy in copies:
        copy.start()
    copy_own.wait()
    for copy in copies:
        copy.wait()


def stage_kernel(own, staged):
    copy_rows(staged, own)


def halo_kernel(own, from_below, from_above, far, near, strip, right, left):
    low = low_lanes()
    for k in range(HALF_ROWS):
        under, over = from_below[k], from_above[k]
        strip[k] = jnp.where(low, under, turn(over, EDGE, 1))
        strip[k + HALF_ROWS] = jnp.where(low, turn(under, -EDGE, 1), over)
    for side, rows, c in ((right, TO_RIGHT, 1), (left, TO_LEFT, 0)):
        level = {q: moved(own_value(own, strip, q, c), VELOCITY[q], 1) for q in LEVEL}
        sums = [level_sums({q: level[q][t] for q in LEVEL}) for t in range(2)]
        parts = []
        for (k, column), row in rows.items():
            if k >= FIELDS:
                side[row] = sums[0][k - FIELDS]
                parts.append(lambda slot, k=k: packed(sums[1][k - FIELDS], slot))
            else:
                place = own_row(k, column)
                side[row] = own[place]
                parts.append(
                    lambda slot, place=place: turn(
                        strip[place // SLOTS], 2 * EDGE * (slot - place % SLOTS), 1
                    )
                )
        for k, row in enumerate(pack_rows(parts)):
            side[BULK_ROWS + k] = row
    send_out(far, near, right, left)


def level_of(p, column, sums):
    return sums(p) if 0 <= column <= 1 else [p[q] for q in LEVEL[:SUMS]]


def second_kernel(
    own, strip, from_far, from_near,
    state, wide_sides, adjoint, by_resistance, by_conductivity, far, near,
    from_left, from_right, after, later, seed, right, left,
):
    take_in(from_left, from_right, from_far, from_near)

    def wide(k, column):
        if column < 0:
            return halo_value(from_left, BULK_ROWS, TO_RIGHT[k, column + 2])
        if column > 1:
            return halo_value(from_right, BULK_ROWS, TO_LEFT[k, column - 2])
        return own_value(own, strip, k, column)

    for column in range(-1, 3):
        i = column + 1
        put(wide_sides, 0, i, moved(wide(MOBILITY, column), STILL, 1))
        put(wide_sides, 1, i, moved(wide(RATE, column), STILL, 1))
        for q in range(MEMBERS):
            if 0 <= column <= 1 or q not in LEVEL:
                put(state, q, i, moved(wide(q, column - VELOCITY[q][0]), VELOCITY[q], 1))
            elif q in LEVEL[:SUMS]:
                put(state, q, i, moved(wide(SUM_FIELDS[LEVEL.index(q)], column), STILL, 1))
    for column in range(-1, 3):
        i = column + 1
        wanted = [q for q in range(MEMBERS) if 0 <= column + VELOCITY[q][0] <= 1]
        for z, y in tiles(WIDE):
            p = [state[q, i, z, y] for q in range(MEMBERS)]
            level = level_of(p, column, level_sums)
            result = collide(p, level, wide_sides[0, i, z, y], wide_sides[1, i, z, y], wanted)
            for q in wanted:
                after[q, i, z, y] = result[q]
    for c in range(2):
        for q in range(MEMBERS):
            put(later, q, c, moved(split(after[q, c + 1 - VELOCITY[q][0]]), VELOCITY[q], 1))
    for column in range(-1, 3):
        weights = [wide(WEIGHT + k, column) for k in range(3)]
        weights = [(main, turn(extra, by, 1)) for main, extra, by in weights]
        for q in range(1, MEMBERS):
            velocity = VELOCITY[q]
            c = column - velocity[0]
            if not 0 <= c <= 1:
                continue
            if q < 19:
                parts = [
                    tuple(value if velocity[k] > 0 else -value for value in weights[k]) for k in range(3) if velocity[k]
                ]
                pair = parts[0] if len(parts) == 1 else tuple(a + b for a, b in zip(*parts))
                pair += (0,)
            else:
                pair = wide(WEIGHT + 3, column)
            put(seed, q, c, moved(pair, velocity, -1))
    for c in range(2):
        for z, y in tiles(WIDE):
            p = [later[q, c, z, y] for q in range(MEMBERS)]
            pa = [jnp.zeros((8, LANES), jnp.float32)] + [seed[q, c, z, y] for q in range(1, MEMBERS)]
            inner = y.start == 0
            result = pull_back(
                p, level_sums(p), pa, level_adjoint_sums(pa),
                wide_sides[0, c + 1, z, y], wide_sides[1, c + 1, z, y], range(MEMBERS), inner,
            )
            if inner:
                by_resistance[c, z, :], by_conductivity[c, z, :] = result["by"]
            for q in range(MEMBERS):
                adjoint[q, c, z, y] = result[q]
    for side, rows, c in ((right, ADJ_TO_RIGHT, 1), (left, ADJ_TO_LEFT, 0)):
        level = {q: moved(split(adjoint[q, c]), VELOCITY[q], -1) for q in LEVEL}
        sums = [level_adjoint_sums({q: level[q][t] for q in LEVEL}) for t in range(2)]
        parts = []
        for (k, column), row in rows.items():
            if k >= FIELDS:
                side[row] = sums[0][k - FIELDS]
                parts.append(lambda slot, k=k: packed(sums[1][k - FIELDS], slot))
            else:
                side[row] = adjoint[k, column, :, :LANES]
                parts.append(lambda slot, k=k, column=column: packed(adjoint[k, column, :, LANES:], slot))
        for k, row in enumerate(pack_rows(parts)):
            side[ADJ_BULK + k] = row
    send_out(far, near, right, left)


def third_kernel(
    flow, heat, state, wide_sides, adjoint, part_resistance, part_conductivity, from_far, from_near,
    by_resistance, by_conductivity,
    from_left, from_right, arrived, earlier, last,
):
    take_in(from_left, from_right, from_far, from_near)

    def wide(k, column):
        if column < 0:
            return halo_value(from_left, ADJ_BULK, ADJ_TO_RIGHT[k, column + 2])
        if column > 1:
            return halo_value(from_right, ADJ_BULK, ADJ_TO_LEFT[k, column - 2])
        return split(adjoint[k, column])

    for column in range(-1, 3):
        i = column + 1
        for q in range(MEMBERS):
            if 0 <= column <= 1 or q not in LEVEL:
                put(arrived, q, i, moved(wide(q, column + VELOCITY[q][0]), VELOCITY[q], -1))
            elif q in LEVEL[:SUMS]:
                put(arrived, q, i, moved(wide(SUM_FIELDS[LEVEL.index(q)], column), STILL, 1))
    for column in range(-1, 3):
        i = column + 1
        own = 0 <= column <= 1
        for z, y in tiles(WIDE):
            inner = y.start == 0
            wanted = [
                q
                for q in range(MEMBERS)
                if 0 <= column - VELOCITY[q][0] <= 1 and (inner or VELOCITY[q][1])
            ]
            p = [state[q, i, z, y] for q in range(MEMBERS)]
            pa = [arrived[q, i, z, y] for q in range(MEMBERS)]
            result = pull_back(
                p, level_of(p, column, level_sums), pa, level_of(pa, column, level_adjoint_sums),
                wide_sides[0, i, z, y], wide_sides[1, i, z, y], wanted, inner and own,
            )
            for q in wanted:
                earlier[q, i, z, y] = result[q]
            if inner and own:
                by_resistance[column, z, :] = part_resistance[column, z, :] + result["by"][0]
                by_conductivity[column, z, :] = part_conductivity[column, z, :] + result["by"][1]
    for c in range(2):
        for q in range(MEMBERS):
            velocity = VELOCITY[q]
            i = c + 1 + velocity[0]
            if velocity[1]:
                last[q, c] = moved(split(earlier[q, i]), velocity, -1)[0]
            else:
                last[q, c] = turn(earlier[q, i, :, :LANES], -velocity[2], 0)
    narrow = pl.ds(0, LANES)
    for c in range(2):
        for z in halves():
            p = [flow[q, c, z, :] for q in range(19)] + [heat[q, c, z, :] for q in range(7)]
            pa = [last[q, c, z, :] for q in range(MEMBERS)]
            result = pull_back(
                p, level_sums(p), pa, level_adjoint_sums(pa),
                wide_sides[0, c + 1, z, narrow], wide_sides[1, c + 1, z, narrow], (), True,
            )
            by_resistance[c, z, :] += result["by"][0]
            by_conductivity[c, z, :] += result["by"][1]


def floats(*shape):
    return jax.ShapeDtypeStruct(shape, jnp.float32)


def vmem(*shape):
    return pltpu.VMEM(shape, jnp.float32)


def swap_along_x(far, near):
    count = lax.axis_size("gx")
    across = [(i, (i + (1 if i % 2 else -1)) % count) for i in range(count)]
    within = [(i, i ^ 1) for i in range(count)]
    return lax.ppermute(far, "gx", across), lax.ppermute(near, "gx", within)


FIRST_PARAMS = pltpu.CompilerParams(vmem_limit_bytes=56 * 1024 * 1024)
PARAMS = pltpu.CompilerParams(vmem_limit_bytes=24 * 1024 * 1024)


def on_device(flow, heat, flow_weight, heat_weight, resistance, conductivity, solid):
    in_hbm = pl.BlockSpec(memory_space=pltpu.HBM)
    own, up, down = pl.pallas_call(
        first_kernel,
        in_specs=[in_hbm] * 7,
        out_specs=[in_hbm] * 3,
        out_shape=(
            floats(2 * FIELDS, ZED, LANES),
            floats(HALF_ROWS, ZED, LANES),
            floats(HALF_ROWS, ZED, LANES),
        ),
        scratch_shapes=[
            vmem(2 * FIELDS, ZED, LANES),
            vmem(HALF_ROWS, ZED, LANES),
            vmem(HALF_ROWS, ZED, LANES),
            vmem(19, 2, ZED, LANES),
            vmem(7, 2, ZED, LANES),
            vmem(3, 2, ZED, LANES),
            vmem(2, ZED, LANES),
            vmem(2, ZED, LANES),
            vmem(2, ZED, LANES),
            pltpu.VMEM((2, ZED, LANES), jnp.int32),
            pltpu.SemaphoreType.DMA((7,)),
            pltpu.SemaphoreType.DMA((3,)),
        ],
        compiler_params=FIRST_PARAMS,
        name="collide_own",
    )(flow, heat, flow_weight, heat_weight, resistance, conductivity, solid)

    count = lax.axis_size("gy")
    upward = [(i, (i + 1) % count) for i in range(count)]
    from_below = lax.ppermute(up, "gy", upward)
    from_above = lax.ppermute(down, "gy", [(target, source) for source, target in upward])

    own = pl.pallas_call(
        stage_kernel,
        out_shape=floats(2 * FIELDS, ZED, LANES),
        compiler_params=PARAMS,
        cost_estimate=pl.CostEstimate(flops=10**7, bytes_accessed=10**6, transcendentals=0),
        name="stage_own",
    )(own)

    far, near, strip = pl.pallas_call(
        halo_kernel,
        out_shape=(floats(SENT, ZED, LANES), floats(SENT, ZED, LANES), floats(STRIP_ROWS, ZED, LANES)),
        scratch_shapes=[vmem(SENT, ZED, LANES), vmem(SENT, ZED, LANES)],
        compiler_params=PARAMS,
        name="halo_buffers",
    )(own, from_below, from_above)

    from_far, from_near = swap_along_x(far, near)

    state, wide_sides, adjoint, part_resistance, part_conductivity, far, near = pl.pallas_call(
        second_kernel,
        out_shape=(
            floats(MEMBERS, 4, ZED, WIDE),
            floats(2, 4, ZED, WIDE),
            floats(MEMBERS, 2, ZED, WIDE),
            floats(2, ZED, LANES),
            floats(2, ZED, LANES),
            floats(ADJ_SENT, ZED, LANES),
            floats(ADJ_SENT, ZED, LANES),
        ),
        scratch_shapes=[
            vmem(SENT, ZED, LANES),
            vmem(SENT, ZED, LANES),
            vmem(MEMBERS, 4, ZED, WIDE),
            vmem(MEMBERS, 2, ZED, WIDE),
            vmem(MEMBERS, 2, ZED, WIDE),
            vmem(ADJ_SENT, ZED, LANES),
            vmem(ADJ_SENT, ZED, LANES),
        ],
        compiler_params=PARAMS,
        name="forward_and_seed",
    )(own, strip, from_far, from_near)

    from_far, from_near = swap_along_x(far, near)

    return pl.pallas_call(
        third_kernel,
        out_shape=(floats(2, ZED, LANES), floats(2, ZED, LANES)),
        scratch_shapes=[
            vmem(ADJ_SENT, ZED, LANES),
            vmem(ADJ_SENT, ZED, LANES),
            vmem(MEMBERS, 4, ZED, WIDE),
            vmem(MEMBERS, 4, ZED, WIDE),
            vmem(MEMBERS, 2, ZED, LANES),
        ],
        compiler_params=PARAMS,
        name="adjoint_steps",
    )(flow, heat, state, wide_sides, adjoint, part_resistance, part_conductivity, from_far, from_near)


def solution(mesh):
    split = P("gx", None, "gy")
    stacked = P(None, "gx", None, "gy")
    return jax.shard_map(
        on_device,
        mesh=mesh,
        in_specs=(stacked, stacked, stacked, split, split, split, split),
        out_specs=(split, split),
        check_vma=False,
    )
```

```python
import jax
import jax.numpy as jnp
from jax import lax
from jax.experimental import pallas as pl
from jax.experimental.pallas import tpu as pltpu
from jax.sharding import PartitionSpec as P

ZED = 16
LANES = 128
WIDE = 2 * LANES
EDGE = 4

FLOW_VELOCITY = [
    (0, 0, 0),
    (1, 0, 0),
    (-1, 0, 0),
    (0, 1, 0),
    (0, -1, 0),
    (0, 0, 1),
    (0, 0, -1),
    (1, 1, 0),
    (-1, -1, 0),
    (1, -1, 0),
    (-1, 1, 0),
    (1, 0, 1),
    (-1, 0, -1),
    (1, 0, -1),
    (-1, 0, 1),
    (0, 1, 1),
    (0, -1, -1),
    (0, 1, -1),
    (0, -1, 1),
]
VELOCITY = FLOW_VELOCITY + FLOW_VELOCITY[:7]
STILL = (0, 0, 0)
MEMBERS = len(VELOCITY)
RIGHTWARD = [q for q in range(MEMBERS) if VELOCITY[q][0] == 1]
LEFTWARD = [q for q in range(MEMBERS) if VELOCITY[q][0] == -1]
LEVEL = [q for q in range(MEMBERS) if VELOCITY[q][0] == 0]

MOBILITY, RATE, WEIGHT = MEMBERS, MEMBERS + 1, MEMBERS + 2
FIELDS = MEMBERS + 6
SIDE_FIELDS = list(range(MEMBERS, FIELDS))

SUMS = 9
SUM_FIELDS = [FIELDS + k for k in range(SUMS)]

SLOTS = LANES // (2 * EDGE)
STRIP_ROWS = 2 * FIELDS // SLOTS
HALF_ROWS = STRIP_ROWS // 2


def rows_of(entries):
    return {entry: row for row, entry in enumerate(entries)}


TO_RIGHT = rows_of([(q, 0) for q in RIGHTWARD] + [(k, 1) for k in RIGHTWARD + SIDE_FIELDS + SUM_FIELDS])
TO_LEFT = rows_of([(q, 1) for q in LEFTWARD] + [(k, 0) for k in LEFTWARD + SIDE_FIELDS + SUM_FIELDS])
ADJ_TO_RIGHT = rows_of([(q, 0) for q in LEFTWARD] + [(k, 1) for k in LEFTWARD + SUM_FIELDS])
ADJ_TO_LEFT = rows_of([(q, 1) for q in RIGHTWARD] + [(k, 0) for k in RIGHTWARD + SUM_FIELDS])
BULK_ROWS, ADJ_BULK = len(TO_RIGHT), len(ADJ_TO_RIGHT)


def with_strips(bulk):
    return bulk + -(-bulk // SLOTS)


SENT, ADJ_SENT = with_strips(BULK_ROWS), with_strips(ADJ_BULK)


def level_sums(p):
    s1, s2, d1, d2 = p[3] + p[4], p[5] + p[6], p[3] - p[4], p[5] - p[6]
    s7, s8, d7, d8 = p[15] + p[16], p[17] + p[18], p[15] - p[16], p[17] - p[18]
    yz = s7 + s8
    mass = p[0] + (s1 + s2) + yz
    return [
        mass, d1 + (d7 + d8), d2 + (d7 - d8), s1 + yz, s2 + yz, s7 - s8,
        p[19] + (p[22] + p[23]) + (p[24] + p[25]), p[22] - p[23], p[24] - p[25],
    ]


def level_adjoint_sums(p):
    s1, s2, d1, d2 = p[3] + p[4], p[5] + p[6], p[3] - p[4], p[5] - p[6]
    s7, s8, d7, d8 = p[15] + p[16], p[17] + p[18], p[15] - p[16], p[17] - p[18]
    yz = s7 + s8
    t1, t2 = s1 + s1, s2 + s2
    mass = 12.0 * p[0] + (t1 + t2) + yz
    return [
        mass, (d1 + d1) + (d7 + d8), (d2 + d2) + (d7 - d8), t1 + yz, t2 + yz, s7 - s8,
        0.35 * p[19] + 0.175 * ((p[22] + p[23]) + (p[24] + p[25])),
        0.125 * (p[22] - p[23]), 0.125 * (p[24] - p[25]),
    ]


def cross_sums(p):
    pairs = [(1, 2), (7, 8), (9, 10), (11, 12), (13, 14)]
    return [p[a] + p[b] for a, b in pairs], [p[a] - p[b] for a, b in pairs]


def common(p, level, mobility):
    s, d = cross_sums(p)
    xy, xz = s[1] + s[2], s[3] + s[4]
    along = s[0] + xy + xz
    rho = level[0] + along
    j = (d[0] + (d[1] + d[2]) + (d[3] + d[4]), level[1] + (d[1] - d[2]), level[2] + (d[3] - d[4]))
    temperature = level[6] + (p[20] + p[21])
    flux = (p[20] - p[21], level[7], level[8])
    u = tuple(mobility * jk for jk in j)
    square = (u[0] * u[0], u[1] * u[1], u[2] * u[2])
    third = rho * (1.0 / 3.0)
    stress = (
        along - third - square[0],
        (level[3] + xy) - third - square[1],
        (level[4] + xz) - third - square[2],
        (s[1] - s[2]) - u[0] * u[1],
        (s[3] - s[4]) - u[0] * u[2],
        level[5] - u[1] * u[2],
    )
    decay = jnp.exp(-2.0 * (temperature - 1.0))
    omega = 1.0 / (0.5 + 0.3 * decay)
    return rho, j, u, square, stress, temperature, flux, decay, omega


def collide(p, level, mobility, rate, wanted):
    rho, _, u, square, stress, temperature, flux, _, omega = common(p, level, mobility)
    solid = mobility == 0.0
    lam = 1.2 - omega
    trace = stress[0] + stress[1] + stress[2]
    base = 1.2 * rho - 1.8 * (square[0] + square[1] + square[2]) - (1.5 * lam) * trace
    scale = 4.5 * lam
    mxx = 5.4 * square[0] + scale * stress[0]
    myy = 5.4 * square[1] + scale * stress[1]
    mzz = 5.4 * square[2] + scale * stress[2]
    mxy = 2.0 * (5.4 * (u[0] * u[1]) + scale * stress[3])
    mxz = 2.0 * (5.4 * (u[0] * u[2]) + scale * stress[4])
    myz = 2.0 * (5.4 * (u[1] * u[2]) + scale * stress[5])
    bx, by, bz = base + mxx, base + myy, base + mzz
    sxy, sxz, syz = bx + myy, bx + mzz, by + mzz
    even = [bx, by, bz, sxy + mxy, sxy - mxy, sxz + mxz, sxz - mxz, syz + myz, syz - myz]
    odd = [u[0], u[1], u[2], u[0] + u[1], u[0] - u[1], u[0] + u[2], u[0] - u[2], u[1] + u[2], u[1] - u[2]]
    result = {}
    if 0 in wanted:
        result[0] = jnp.where(solid, p[0], (1.0 / 3.0) * base - 0.2 * p[0])
    for k in range(9):
        a, b = 2 * k + 1, 2 * k + 2
        w = 1.0 / 18.0 if k < 3 else 1.0 / 36.0
        e, o = w * even[k], (3.6 * w) * odd[k]
        if a in wanted:
            result[a] = jnp.where(solid, p[b], (e + o) - 0.2 * p[a])
        if b in wanted:
            result[b] = jnp.where(solid, p[a], (e - o) - 0.2 * p[b])
    keep = 0.5 * (1.4 - rate)
    push = (0.5 * rate) * temperature
    warm = 0.175 * temperature
    if 19 in wanted:
        result[19] = 0.35 * temperature - 0.4 * p[19]
    for k in range(3):
        along = keep * flux[k] + push * u[k]
        a, b = 20 + 2 * k, 21 + 2 * k
        if a in wanted:
            result[a] = (warm + along) - 0.4 * p[a]
        if b in wanted:
            result[b] = (warm - along) - 0.4 * p[b]
    return result


def pull_back(p, level, pa, adjoint_level, mobility, rate, wanted, sensitivity):
    rho, j, u, square, stress, temperature, flux, decay, omega = common(p, level, mobility)
    solid = mobility == 0.0
    lam = 1.2 - omega
    s, d = cross_sums(pa)
    w = 1.0 / 36.0
    xy, xz = s[1] + s[2], s[3] + s[4]
    along = (s[0] + s[0]) + xy + xz
    mass = w * (adjoint_level[0] + along)
    px = w * ((d[0] + d[0]) + (d[1] + d[2]) + (d[3] + d[4]))
    py = w * (adjoint_level[1] + (d[1] - d[2]))
    pz = w * (adjoint_level[2] + (d[3] - d[4]))
    rxx, ryy, rzz = w * along, w * (adjoint_level[3] + xy), w * (adjoint_level[4] + xz)
    rxy, rxz, ryz = w * (s[1] - s[2]), w * (s[3] - s[4]), w * adjoint_level[5]
    shift = 1.5 * mass
    dxx, dyy, dzz = 4.5 * rxx - shift, 4.5 * ryy - shift, 4.5 * rzz - shift
    dxy, dxz, dyz = 4.5 * rxy, 4.5 * rxz, 4.5 * ryz
    mix = 2.4 - 2.0 * lam
    b = ((pa[20] - pa[21]) * 0.125, adjoint_level[7], adjoint_level[8])
    push = (4.0 * rate) * temperature
    ux = 3.6 * px + mix * (dxx * u[0] + dxy * u[1] + dxz * u[2]) + push * b[0]
    uy = 3.6 * py + mix * (dxy * u[0] + dyy * u[1] + dyz * u[2]) + push * b[1]
    uz = 3.6 * pz + mix * (dxz * u[0] + dyz * u[1] + dzz * u[2]) + push * b[2]
    result = {}
    if wanted:
        lam_bar = (
            dxx * stress[0]
            + dyy * stress[1]
            + dzz * stress[2]
            + 2.0 * (dxy * stress[3] + dxz * stress[4] + dyz * stress[5])
        )
        rho_bar = 1.2 * mass - (1.5 * lam) * ((rxx + ryy + rzz) - mass)
        jx, jy, jz = mobility * ux, mobility * uy, mobility * uz
        ex, ey, ez = lam * dxx, lam * dyy, lam * dzz
        exy, exz, eyz = (2.0 * lam) * dxy, (2.0 * lam) * dxz, (2.0 * lam) * dyz
        hx, hy, hz = rho_bar + ex, rho_bar + ey, rho_bar + ez
        gxy, gxz, gyz = hx + ey, hx + ez, hy + ez
        even = [hx, hy, hz, gxy + exy, gxy - exy, gxz + exz, gxz - exz, gyz + eyz, gyz - eyz]
        odd = [jx, jy, jz, jx + jy, jx - jy, jx + jz, jx - jz, jy + jz, jy - jz]
        if 0 in wanted:
            result[0] = jnp.where(solid, pa[0], rho_bar - 0.2 * pa[0])
        for k in range(9):
            a, m = 2 * k + 1, 2 * k + 2
            if a in wanted:
                result[a] = jnp.where(solid, pa[m], (even[k] + odd[k]) - 0.2 * pa[a])
            if m in wanted:
                result[m] = jnp.where(solid, pa[a], (even[k] - odd[k]) - 0.2 * pa[m])
        warm = (
            adjoint_level[6]
            + 0.175 * (pa[20] + pa[21])
            + (4.0 * rate) * (b[0] * u[0] + b[1] * u[1] + b[2] * u[2])
            - jnp.where(solid, 0.0, lam_bar * (0.6 * decay) * (omega * omega))
        )
        keep = 5.6 - 4.0 * rate
        if 19 in wanted:
            result[19] = warm - 0.4 * pa[19]
        for k in range(3):
            along = keep * b[k]
            a, m = 20 + 2 * k, 21 + 2 * k
            if a in wanted:
                result[a] = (warm + along) - 0.4 * pa[a]
            if m in wanted:
                result[m] = (warm - along) - 0.4 * pa[m]
    if sensitivity:
        by_resistance = -(mobility * mobility) * (ux * j[0] + uy * j[1] + uz * j[2])
        bent = (
            b[0] * (temperature * u[0] - flux[0])
            + b[1] * (temperature * u[1] - flux[1])
            + b[2] * (temperature * u[2] - flux[2])
        )
        by_conductivity = (-1.6 * (rate * rate)) * bent
        result["by"] = (by_resistance, by_conductivity)
    return result


def turn(value, by, axis):
    count = value.shape[axis]
    by %= count
    return pltpu.roll(value, by, axis) if by else value


def side_by_side(parts):
    lane = lax.broadcasted_iota(jnp.int32, (ZED, LANES), 1)
    row = None
    for slot, part in enumerate(parts):
        row = part if row is None else jnp.where(lane >= 2 * EDGE * slot, part, row)
    return row


def packed(value, slot):
    return turn(value, 2 * EDGE * slot + EDGE, 1)


def pack_rows(parts):
    return [
        side_by_side([part(slot) for slot, part in enumerate(parts[start : start + SLOTS])])
        for start in range(0, len(parts), SLOTS)
    ]


def halves():
    return [pl.ds(0, 8), pl.ds(8, 8)]


def low_lanes():
    return lax.broadcasted_iota(jnp.int32, (ZED, LANES), 1) % (2 * EDGE) < EDGE


def either_way(move):
    first = lax.rem(lax.axis_index("gx"), 2) == 0
    pl.when(first)(lambda: move(True))
    pl.when(jnp.logical_not(first))(lambda: move(False))


def copy_rows(target, source):
    for row in range(source.shape[0]):
        target[row] = source[row]


def split(value):
    return value[:, :LANES], value[:, LANES:], 0


def beside(row, slot):
    return row, -EDGE - 2 * EDGE * slot


def moved(triple, velocity, way):
    main, extra, by = triple
    _, step_y, step_z = velocity
    step = way * step_y
    main, extra = turn(main, way * step_z, 0), turn(extra, way * step_z, 0)
    if not step:
        return main, turn(extra, by, 1)
    main, extra = turn(main, step, 1), turn(extra, by + step, 1)
    lane = lax.broadcasted_iota(jnp.int32, (ZED, LANES), 1)
    edge = lane == (0 if step == 1 else LANES - 1)
    return jnp.where(edge, extra, main), jnp.where(edge, main, extra)


def put(ref, q, i, pair):
    ref[q, i, :, :LANES], ref[q, i, :, LANES:] = pair


def tiles(lanes):
    return [(z, pl.ds(t, LANES)) for z in halves() for t in range(0, lanes, LANES)]


def own_row(k, c):
    return c * FIELDS + k


def own_value(own, strip, k, c):
    place = own_row(k, c)
    return (own[place],) + beside(strip[place // SLOTS], place % SLOTS)


def halo_value(buffer, bulk, place):
    return (buffer[place],) + beside(buffer[bulk + place // SLOTS], place % SLOTS)


def send_out(far, near, right, left):
    def send(first):
        copy_rows(far, left if first else right)
        copy_rows(near, right if first else left)

    either_way(send)


def take_in(from_left, from_right, from_far, from_near):
    def receive(first):
        copy_rows(from_left, from_far if first else from_near)
        copy_rows(from_right, from_near if first else from_far)

    either_way(receive)


def first_kernel(
    flow_in, heat_in, flow_weight_in, heat_weight_in, resistance_in, conductivity_in, solid_in,
    own_out, up_out, down_out,
    own, up, down, flow, heat, flow_weight, heat_weight, resistance, conductivity, solid, arrived, sent,
):
    pairs = [
        (flow_in, flow),
        (heat_in, heat),
        (resistance_in, resistance),
        (conductivity_in, conductivity),
        (solid_in, solid),
        (flow_weight_in, flow_weight),
        (heat_weight_in, heat_weight),
    ]
    copies = [pltpu.make_async_copy(a, b, arrived.at[k]) for k, (a, b) in enumerate(pairs)]
    for copy in copies:
        copy.start()
    for copy in copies:
        copy.wait()
    for c in range(2):
        for z in halves():
            mobility = jnp.where(solid[c, z, :] != 0, 0.0, 1.0 / (1.0 + resistance[c, z, :]))
            rate = 1.0 / (0.5 + 0.4 * conductivity[c, z, :])
            p = [flow[q, c, z, :] for q in range(19)] + [heat[q, c, z, :] for q in range(7)]
            after = collide(p, level_sums(p), mobility, rate, range(MEMBERS))
            more = [mobility, rate] + [flow_weight[k, c, z, :] for k in range(3)] + [heat_weight[c, z, :]]
            for k, value in enumerate([after[q] for q in range(MEMBERS)] + more):
                own[own_row(k, c), z, :] = value
    copy_own = pltpu.make_async_copy(own, own_out, sent.at[0])
    copy_own.start()
    rows = pack_rows([lambda slot, k=k: packed(own[k], slot) for k in range(2 * FIELDS)])
    low = low_lanes()
    for k in range(HALF_ROWS):
        up[k] = jnp.where(low, rows[k], turn(rows[k + HALF_ROWS], EDGE, 1))
        down[k] = jnp.where(low, turn(rows[k], -EDGE, 1), rows[k + HALF_ROWS])
    copies = [
        pltpu.make_async_copy(up, up_out, sent.at[1]),
        pltpu.make_async_copy(down, down_out, sent.at[2]),
    ]
    for copy in copies:
        copy.start()
    copy_own.wait()
    for copy in copies:
        copy.wait()


def stage_kernel(own, staged):
    copy_rows(staged, own)


def halo_kernel(own, from_below, from_above, far, near, strip, right, left):
    low = low_lanes()
    for k in range(HALF_ROWS):
        under, over = from_below[k], from_above[k]
        strip[k] = jnp.where(low, under, turn(over, EDGE, 1))
        strip[k + HALF_ROWS] = jnp.where(low, turn(under, -EDGE, 1), over)
    for side, rows, c in ((right, TO_RIGHT, 1), (left, TO_LEFT, 0)):
        level = {q: moved(own_value(own, strip, q, c), VELOCITY[q], 1) for q in LEVEL}
        sums = [level_sums({q: level[q][t] for q in LEVEL}) for t in range(2)]
        parts = []
        for (k, column), row in rows.items():
            if k >= FIELDS:
                side[row] = sums[0][k - FIELDS]
                parts.append(lambda slot, k=k: packed(sums[1][k - FIELDS], slot))
            else:
                place = own_row(k, column)
                side[row] = own[place]
                parts.append(
                    lambda slot, place=place: turn(
                        strip[place // SLOTS], 2 * EDGE * (slot - place % SLOTS), 1
                    )
                )
        for k, row in enumerate(pack_rows(parts)):
            side[BULK_ROWS + k] = row
    send_out(far, near, right, left)


def level_of(p, column, sums):
    return sums(p) if 0 <= column <= 1 else [p[q] for q in LEVEL[:SUMS]]


def second_kernel(
    own, strip, from_far, from_near,
    state, wide_sides, adjoint, by_resistance, by_conductivity, right, left,
    from_left, from_right, after, later, seed,
):
    take_in(from_left, from_right, from_far, from_near)

    def wide(k, column):
        if column < 0:
            return halo_value(from_left, BULK_ROWS, TO_RIGHT[k, column + 2])
        if column > 1:
            return halo_value(from_right, BULK_ROWS, TO_LEFT[k, column - 2])
        return own_value(own, strip, k, column)

    for column in range(-1, 3):
        i = column + 1
        put(wide_sides, 0, i, moved(wide(MOBILITY, column), STILL, 1))
        put(wide_sides, 1, i, moved(wide(RATE, column), STILL, 1))
        for q in range(MEMBERS):
            if 0 <= column <= 1 or q not in LEVEL:
                put(state, q, i, moved(wide(q, column - VELOCITY[q][0]), VELOCITY[q], 1))
            elif q in LEVEL[:SUMS]:
                put(state, q, i, moved(wide(SUM_FIELDS[LEVEL.index(q)], column), STILL, 1))
    for column in range(-1, 3):
        i = column + 1
        wanted = [q for q in range(MEMBERS) if 0 <= column + VELOCITY[q][0] <= 1]
        for z, y in tiles(WIDE):
            p = [state[q, i, z, y] for q in range(MEMBERS)]
            level = level_of(p, column, level_sums)
            result = collide(p, level, wide_sides[0, i, z, y], wide_sides[1, i, z, y], wanted)
            for q in wanted:
                after[q, i, z, y] = result[q]
    for c in range(2):
        for q in range(MEMBERS):
            put(later, q, c, moved(split(after[q, c + 1 - VELOCITY[q][0]]), VELOCITY[q], 1))
    for column in range(-1, 3):
        weights = [wide(WEIGHT + k, column) for k in range(3)]
        weights = [(main, turn(extra, by, 1)) for main, extra, by in weights]
        for q in range(1, MEMBERS):
            velocity = VELOCITY[q]
            c = column - velocity[0]
            if not 0 <= c <= 1:
                continue
            if q < 19:
                parts = [
                    tuple(value if velocity[k] > 0 else -value for value in weights[k]) for k in range(3) if velocity[k]
                ]
                pair = parts[0] if len(parts) == 1 else tuple(a + b for a, b in zip(*parts))
                pair += (0,)
            else:
                pair = wide(WEIGHT + 3, column)
            put(seed, q, c, moved(pair, velocity, -1))
    for c in range(2):
        for z, y in tiles(WIDE):
            p = [later[q, c, z, y] for q in range(MEMBERS)]
            pa = [jnp.zeros((8, LANES), jnp.float32)] + [seed[q, c, z, y] for q in range(1, MEMBERS)]
            inner = y.start == 0
            result = pull_back(
                p, level_sums(p), pa, level_adjoint_sums(pa),
                wide_sides[0, c + 1, z, y], wide_sides[1, c + 1, z, y], range(MEMBERS), inner,
            )
            if inner:
                by_resistance[c, z, :], by_conductivity[c, z, :] = result["by"]
            for q in range(MEMBERS):
                adjoint[q, c, z, y] = result[q]
    for side, rows, c in ((right, ADJ_TO_RIGHT, 1), (left, ADJ_TO_LEFT, 0)):
        level = {q: moved(split(adjoint[q, c]), VELOCITY[q], -1) for q in LEVEL}
        sums = [level_adjoint_sums({q: level[q][t] for q in LEVEL}) for t in range(2)]
        parts = []
        for (k, column), row in rows.items():
            if k >= FIELDS:
                side[row] = sums[0][k - FIELDS]
                parts.append(lambda slot, k=k: packed(sums[1][k - FIELDS], slot))
            else:
                side[row] = adjoint[k, column, :, :LANES]
                parts.append(lambda slot, k=k, column=column: packed(adjoint[k, column, :, LANES:], slot))
        for k, row in enumerate(pack_rows(parts)):
            side[ADJ_BULK + k] = row


def third_kernel(
    flow, heat, state, wide_sides, adjoint, part_resistance, part_conductivity, from_left, from_right,
    by_resistance, by_conductivity,
    arrived, earlier, last,
):
    def wide(k, column):
        if column < 0:
            return halo_value(from_left, ADJ_BULK, ADJ_TO_RIGHT[k, column + 2])
        if column > 1:
            return halo_value(from_right, ADJ_BULK, ADJ_TO_LEFT[k, column - 2])
        return split(adjoint[k, column])

    for column in range(-1, 3):
        i = column + 1
        for q in range(MEMBERS):
            if 0 <= column <= 1 or q not in LEVEL:
                put(arrived, q, i, moved(wide(q, column + VELOCITY[q][0]), VELOCITY[q], -1))
            elif q in LEVEL[:SUMS]:
                put(arrived, q, i, moved(wide(SUM_FIELDS[LEVEL.index(q)], column), STILL, 1))
    for column in range(-1, 3):
        i = column + 1
        own = 0 <= column <= 1
        for z, y in tiles(WIDE):
            inner = y.start == 0
            wanted = [
                q
                for q in range(MEMBERS)
                if 0 <= column - VELOCITY[q][0] <= 1 and (inner or VELOCITY[q][1])
            ]
            p = [state[q, i, z, y] for q in range(MEMBERS)]
            pa = [arrived[q, i, z, y] for q in range(MEMBERS)]
            result = pull_back(
                p, level_of(p, column, level_sums), pa, level_of(pa, column, level_adjoint_sums),
                wide_sides[0, i, z, y], wide_sides[1, i, z, y], wanted, inner and own,
            )
            for q in wanted:
                earlier[q, i, z, y] = result[q]
            if inner and own:
                by_resistance[column, z, :] = part_resistance[column, z, :] + result["by"][0]
                by_conductivity[column, z, :] = part_conductivity[column, z, :] + result["by"][1]
    for c in range(2):
        for q in range(MEMBERS):
            velocity = VELOCITY[q]
            i = c + 1 + velocity[0]
            if velocity[1]:
                last[q, c] = moved(split(earlier[q, i]), velocity, -1)[0]
            else:
                last[q, c] = turn(earlier[q, i, :, :LANES], -velocity[2], 0)
    narrow = pl.ds(0, LANES)
    for c in range(2):
        for z in halves():
            p = [flow[q, c, z, :] for q in range(19)] + [heat[q, c, z, :] for q in range(7)]
            pa = [last[q, c, z, :] for q in range(MEMBERS)]
            result = pull_back(
                p, level_sums(p), pa, level_adjoint_sums(pa),
                wide_sides[0, c + 1, z, narrow], wide_sides[1, c + 1, z, narrow], (), True,
            )
            by_resistance[c, z, :] += result["by"][0]
            by_conductivity[c, z, :] += result["by"][1]


def floats(*shape):
    return jax.ShapeDtypeStruct(shape, jnp.float32)


def vmem(*shape):
    return pltpu.VMEM(shape, jnp.float32)


def swap_along_x(far, near):
    count = lax.axis_size("gx")
    across = [(i, (i + (1 if i % 2 else -1)) % count) for i in range(count)]
    within = [(i, i ^ 1) for i in range(count)]
    return lax.ppermute(far, "gx", across), lax.ppermute(near, "gx", within)


FIRST_PARAMS = pltpu.CompilerParams(vmem_limit_bytes=56 * 1024 * 1024)
PARAMS = pltpu.CompilerParams(vmem_limit_bytes=24 * 1024 * 1024)


def on_device(flow, heat, flow_weight, heat_weight, resistance, conductivity, solid):
    in_hbm = pl.BlockSpec(memory_space=pltpu.HBM)
    own, up, down = pl.pallas_call(
        first_kernel,
        in_specs=[in_hbm] * 7,
        out_specs=[in_hbm] * 3,
        out_shape=(
            floats(2 * FIELDS, ZED, LANES),
            floats(HALF_ROWS, ZED, LANES),
            floats(HALF_ROWS, ZED, LANES),
        ),
        scratch_shapes=[
            vmem(2 * FIELDS, ZED, LANES),
            vmem(HALF_ROWS, ZED, LANES),
            vmem(HALF_ROWS, ZED, LANES),
            vmem(19, 2, ZED, LANES),
            vmem(7, 2, ZED, LANES),
            vmem(3, 2, ZED, LANES),
            vmem(2, ZED, LANES),
            vmem(2, ZED, LANES),
            vmem(2, ZED, LANES),
            pltpu.VMEM((2, ZED, LANES), jnp.int32),
            pltpu.SemaphoreType.DMA((7,)),
            pltpu.SemaphoreType.DMA((3,)),
        ],
        compiler_params=FIRST_PARAMS,
        name="collide_own",
    )(flow, heat, flow_weight, heat_weight, resistance, conductivity, solid)

    count = lax.axis_size("gy")
    upward = [(i, (i + 1) % count) for i in range(count)]
    from_below = lax.ppermute(up, "gy", upward)
    from_above = lax.ppermute(down, "gy", [(target, source) for source, target in upward])

    own = pl.pallas_call(
        stage_kernel,
        out_shape=floats(2 * FIELDS, ZED, LANES),
        compiler_params=PARAMS,
        cost_estimate=pl.CostEstimate(flops=10**7, bytes_accessed=10**6, transcendentals=0),
        name="stage_own",
    )(own)

    far, near, strip = pl.pallas_call(
        halo_kernel,
        out_shape=(floats(SENT, ZED, LANES), floats(SENT, ZED, LANES), floats(STRIP_ROWS, ZED, LANES)),
        scratch_shapes=[vmem(SENT, ZED, LANES), vmem(SENT, ZED, LANES)],
        compiler_params=PARAMS,
        name="halo_buffers",
    )(own, from_below, from_above)

    from_far, from_near = swap_along_x(far, near)

    state, wide_sides, adjoint, part_resistance, part_conductivity, right, left = pl.pallas_call(
        second_kernel,
        out_shape=(
            floats(MEMBERS, 4, ZED, WIDE),
            floats(2, 4, ZED, WIDE),
            floats(MEMBERS, 2, ZED, WIDE),
            floats(2, ZED, LANES),
            floats(2, ZED, LANES),
            floats(ADJ_SENT, ZED, LANES),
            floats(ADJ_SENT, ZED, LANES),
        ),
        scratch_shapes=[
            vmem(SENT, ZED, LANES),
            vmem(SENT, ZED, LANES),
            vmem(MEMBERS, 4, ZED, WIDE),
            vmem(MEMBERS, 2, ZED, WIDE),
            vmem(MEMBERS, 2, ZED, WIDE),
        ],
        compiler_params=PARAMS,
        name="forward_and_seed",
    )(own, strip, from_far, from_near)

    count = lax.axis_size("gx")
    rightward = [(i, (i + 1) % count) for i in range(count)]
    from_left = lax.ppermute(right, "gx", rightward)
    from_right = lax.ppermute(left, "gx", [(target, source) for source, target in rightward])

    return pl.pallas_call(
        third_kernel,
        out_shape=(floats(2, ZED, LANES), floats(2, ZED, LANES)),
        scratch_shapes=[
            vmem(MEMBERS, 4, ZED, WIDE),
            vmem(MEMBERS, 4, ZED, WIDE),
            vmem(MEMBERS, 2, ZED, LANES),
        ],
        compiler_params=PARAMS,
        name="adjoint_steps",
    )(flow, heat, state, wide_sides, adjoint, part_resistance, part_conductivity, from_left, from_right)


def solution(mesh):
    split = P("gx", None, "gy")
    stacked = P(None, "gx", None, "gy")
    return jax.shard_map(
        on_device,
        mesh=mesh,
        in_specs=(stacked, stacked, stacked, split, split, split, split),
        out_specs=(split, split),
        check_vma=False,
    )
```

```python
import jax
import jax.numpy as jnp
from jax import lax
from jax.experimental import pallas as pl
from jax.experimental.pallas import tpu as pltpu
from jax.sharding import PartitionSpec as P

ZED = 16
LANES = 128
WIDE = 2 * LANES
EDGE = 4

FLOW_VELOCITY = [
    (0, 0, 0),
    (1, 0, 0),
    (-1, 0, 0),
    (0, 1, 0),
    (0, -1, 0),
    (0, 0, 1),
    (0, 0, -1),
    (1, 1, 0),
    (-1, -1, 0),
    (1, -1, 0),
    (-1, 1, 0),
    (1, 0, 1),
    (-1, 0, -1),
    (1, 0, -1),
    (-1, 0, 1),
    (0, 1, 1),
    (0, -1, -1),
    (0, 1, -1),
    (0, -1, 1),
]
VELOCITY = FLOW_VELOCITY + FLOW_VELOCITY[:7]
STILL = (0, 0, 0)
MEMBERS = len(VELOCITY)
RIGHTWARD = [q for q in range(MEMBERS) if VELOCITY[q][0] == 1]
LEFTWARD = [q for q in range(MEMBERS) if VELOCITY[q][0] == -1]
LEVEL = [q for q in range(MEMBERS) if VELOCITY[q][0] == 0]


def mirrored(q):
    x, y, z = VELOCITY[q]
    start = 0 if q < 19 else 19
    return start + FLOW_VELOCITY.index((-x, y, z))


MOBILITY, RATE, WEIGHT = MEMBERS, MEMBERS + 1, MEMBERS + 2
FIELDS = MEMBERS + 6
SIDE_FIELDS = list(range(MEMBERS, FIELDS))

SUMS = 9
SUM_FIELDS = [FIELDS + k for k in range(SUMS)]

SLOTS = LANES // (2 * EDGE)
STRIP_ROWS = 2 * FIELDS // SLOTS
HALF_ROWS = STRIP_ROWS // 2


def rows_of(entries):
    return {entry: row for row, entry in enumerate(entries)}


TO_NEAR = rows_of([(q, 0) for q in RIGHTWARD] + [(k, 1) for k in RIGHTWARD + SIDE_FIELDS + SUM_FIELDS])
TO_FAR = rows_of([(q, 1) for q in LEFTWARD] + [(k, 0) for k in LEFTWARD + SIDE_FIELDS + SUM_FIELDS])
ADJ_TO_NEAR = rows_of([(q, 0) for q in LEFTWARD] + [(k, 1) for k in LEFTWARD + SUM_FIELDS])
ADJ_TO_FAR = rows_of([(q, 1) for q in RIGHTWARD] + [(k, 0) for k in RIGHTWARD + SUM_FIELDS])
BULK_ROWS, ADJ_BULK = len(TO_NEAR), len(ADJ_TO_NEAR)


def with_strips(bulk):
    return bulk + -(-bulk // SLOTS)


SENT, ADJ_SENT = with_strips(BULK_ROWS), with_strips(ADJ_BULK)


def level_sums(p):
    s1, s2, d1, d2 = p[3] + p[4], p[5] + p[6], p[3] - p[4], p[5] - p[6]
    s7, s8, d7, d8 = p[15] + p[16], p[17] + p[18], p[15] - p[16], p[17] - p[18]
    yz = s7 + s8
    mass = p[0] + (s1 + s2) + yz
    return [
        mass, d1 + (d7 + d8), d2 + (d7 - d8), s1 + yz, s2 + yz, s7 - s8,
        p[19] + (p[22] + p[23]) + (p[24] + p[25]), p[22] - p[23], p[24] - p[25],
    ]


def level_adjoint_sums(p):
    s1, s2, d1, d2 = p[3] + p[4], p[5] + p[6], p[3] - p[4], p[5] - p[6]
    s7, s8, d7, d8 = p[15] + p[16], p[17] + p[18], p[15] - p[16], p[17] - p[18]
    yz = s7 + s8
    t1, t2 = s1 + s1, s2 + s2
    mass = 12.0 * p[0] + (t1 + t2) + yz
    return [
        mass, (d1 + d1) + (d7 + d8), (d2 + d2) + (d7 - d8), t1 + yz, t2 + yz, s7 - s8,
        0.35 * p[19] + 0.175 * ((p[22] + p[23]) + (p[24] + p[25])),
        0.125 * (p[22] - p[23]), 0.125 * (p[24] - p[25]),
    ]


def cross_sums(p):
    pairs = [(1, 2), (7, 8), (9, 10), (11, 12), (13, 14)]
    return [p[a] + p[b] for a, b in pairs], [p[a] - p[b] for a, b in pairs]


def common(p, level, mobility):
    s, d = cross_sums(p)
    xy, xz = s[1] + s[2], s[3] + s[4]
    along = s[0] + xy + xz
    rho = level[0] + along
    j = (d[0] + (d[1] + d[2]) + (d[3] + d[4]), level[1] + (d[1] - d[2]), level[2] + (d[3] - d[4]))
    temperature = level[6] + (p[20] + p[21])
    flux = (p[20] - p[21], level[7], level[8])
    u = tuple(mobility * jk for jk in j)
    square = (u[0] * u[0], u[1] * u[1], u[2] * u[2])
    third = rho * (1.0 / 3.0)
    stress = (
        along - third - square[0],
        (level[3] + xy) - third - square[1],
        (level[4] + xz) - third - square[2],
        (s[1] - s[2]) - u[0] * u[1],
        (s[3] - s[4]) - u[0] * u[2],
        level[5] - u[1] * u[2],
    )
    decay = jnp.exp(-2.0 * (temperature - 1.0))
    omega = 1.0 / (0.5 + 0.3 * decay)
    return rho, j, u, square, stress, temperature, flux, decay, omega


def collide(p, level, mobility, rate, wanted):
    rho, _, u, square, stress, temperature, flux, _, omega = common(p, level, mobility)
    solid = mobility == 0.0
    lam = 1.2 - omega
    trace = stress[0] + stress[1] + stress[2]
    base = 1.2 * rho - 1.8 * (square[0] + square[1] + square[2]) - (1.5 * lam) * trace
    scale = 4.5 * lam
    mxx = 5.4 * square[0] + scale * stress[0]
    myy = 5.4 * square[1] + scale * stress[1]
    mzz = 5.4 * square[2] + scale * stress[2]
    mxy = 2.0 * (5.4 * (u[0] * u[1]) + scale * stress[3])
    mxz = 2.0 * (5.4 * (u[0] * u[2]) + scale * stress[4])
    myz = 2.0 * (5.4 * (u[1] * u[2]) + scale * stress[5])
    bx, by, bz = base + mxx, base + myy, base + mzz
    sxy, sxz, syz = bx + myy, bx + mzz, by + mzz
    even = [bx, by, bz, sxy + mxy, sxy - mxy, sxz + mxz, sxz - mxz, syz + myz, syz - myz]
    odd = [u[0], u[1], u[2], u[0] + u[1], u[0] - u[1], u[0] + u[2], u[0] - u[2], u[1] + u[2], u[1] - u[2]]
    result = {}
    if 0 in wanted:
        result[0] = jnp.where(solid, p[0], (1.0 / 3.0) * base - 0.2 * p[0])
    for k in range(9):
        a, b = 2 * k + 1, 2 * k + 2
        w = 1.0 / 18.0 if k < 3 else 1.0 / 36.0
        e, o = w * even[k], (3.6 * w) * odd[k]
        if a in wanted:
            result[a] = jnp.where(solid, p[b], (e + o) - 0.2 * p[a])
        if b in wanted:
            result[b] = jnp.where(solid, p[a], (e - o) - 0.2 * p[b])
    keep = 0.5 * (1.4 - rate)
    push = (0.5 * rate) * temperature
    warm = 0.175 * temperature
    if 19 in wanted:
        result[19] = 0.35 * temperature - 0.4 * p[19]
    for k in range(3):
        along = keep * flux[k] + push * u[k]
        a, b = 20 + 2 * k, 21 + 2 * k
        if a in wanted:
            result[a] = (warm + along) - 0.4 * p[a]
        if b in wanted:
            result[b] = (warm - along) - 0.4 * p[b]
    return result


def pull_back(p, level, pa, adjoint_level, mobility, rate, wanted, sensitivity):
    rho, j, u, square, stress, temperature, flux, decay, omega = common(p, level, mobility)
    solid = mobility == 0.0
    lam = 1.2 - omega
    s, d = cross_sums(pa)
    w = 1.0 / 36.0
    xy, xz = s[1] + s[2], s[3] + s[4]
    along = (s[0] + s[0]) + xy + xz
    mass = w * (adjoint_level[0] + along)
    px = w * ((d[0] + d[0]) + (d[1] + d[2]) + (d[3] + d[4]))
    py = w * (adjoint_level[1] + (d[1] - d[2]))
    pz = w * (adjoint_level[2] + (d[3] - d[4]))
    rxx, ryy, rzz = w * along, w * (adjoint_level[3] + xy), w * (adjoint_level[4] + xz)
    rxy, rxz, ryz = w * (s[1] - s[2]), w * (s[3] - s[4]), w * adjoint_level[5]
    shift = 1.5 * mass
    dxx, dyy, dzz = 4.5 * rxx - shift, 4.5 * ryy - shift, 4.5 * rzz - shift
    dxy, dxz, dyz = 4.5 * rxy, 4.5 * rxz, 4.5 * ryz
    mix = 2.4 - 2.0 * lam
    b = ((pa[20] - pa[21]) * 0.125, adjoint_level[7], adjoint_level[8])
    push = (4.0 * rate) * temperature
    ux = 3.6 * px + mix * (dxx * u[0] + dxy * u[1] + dxz * u[2]) + push * b[0]
    uy = 3.6 * py + mix * (dxy * u[0] + dyy * u[1] + dyz * u[2]) + push * b[1]
    uz = 3.6 * pz + mix * (dxz * u[0] + dyz * u[1] + dzz * u[2]) + push * b[2]
    result = {}
    if wanted:
        lam_bar = (
            dxx * stress[0]
            + dyy * stress[1]
            + dzz * stress[2]
            + 2.0 * (dxy * stress[3] + dxz * stress[4] + dyz * stress[5])
        )
        rho_bar = 1.2 * mass - (1.5 * lam) * ((rxx + ryy + rzz) - mass)
        jx, jy, jz = mobility * ux, mobility * uy, mobility * uz
        ex, ey, ez = lam * dxx, lam * dyy, lam * dzz
        exy, exz, eyz = (2.0 * lam) * dxy, (2.0 * lam) * dxz, (2.0 * lam) * dyz
        hx, hy, hz = rho_bar + ex, rho_bar + ey, rho_bar + ez
        gxy, gxz, gyz = hx + ey, hx + ez, hy + ez
        even = [hx, hy, hz, gxy + exy, gxy - exy, gxz + exz, gxz - exz, gyz + eyz, gyz - eyz]
        odd = [jx, jy, jz, jx + jy, jx - jy, jx + jz, jx - jz, jy + jz, jy - jz]
        if 0 in wanted:
            result[0] = jnp.where(solid, pa[0], rho_bar - 0.2 * pa[0])
        for k in range(9):
            a, m = 2 * k + 1, 2 * k + 2
            if a in wanted:
                result[a] = jnp.where(solid, pa[m], (even[k] + odd[k]) - 0.2 * pa[a])
            if m in wanted:
                result[m] = jnp.where(solid, pa[a], (even[k] - odd[k]) - 0.2 * pa[m])
        warm = (
            adjoint_level[6]
            + 0.175 * (pa[20] + pa[21])
            + (4.0 * rate) * (b[0] * u[0] + b[1] * u[1] + b[2] * u[2])
            - jnp.where(solid, 0.0, lam_bar * (0.6 * decay) * (omega * omega))
        )
        keep = 5.6 - 4.0 * rate
        if 19 in wanted:
            result[19] = warm - 0.4 * pa[19]
        for k in range(3):
            along = keep * b[k]
            a, m = 20 + 2 * k, 21 + 2 * k
            if a in wanted:
                result[a] = (warm + along) - 0.4 * pa[a]
            if m in wanted:
                result[m] = (warm - along) - 0.4 * pa[m]
    if sensitivity:
        by_resistance = -(mobility * mobility) * (ux * j[0] + uy * j[1] + uz * j[2])
        bent = (
            b[0] * (temperature * u[0] - flux[0])
            + b[1] * (temperature * u[1] - flux[1])
            + b[2] * (temperature * u[2] - flux[2])
        )
        by_conductivity = (-1.6 * (rate * rate)) * bent
        result["by"] = (by_resistance, by_conductivity)
    return result


def turn(value, by, axis):
    count = value.shape[axis]
    by %= count
    return pltpu.roll(value, by, axis) if by else value


def side_by_side(parts):
    lane = lax.broadcasted_iota(jnp.int32, (ZED, LANES), 1)
    row = None
    for slot, part in enumerate(parts):
        row = part if row is None else jnp.where(lane >= 2 * EDGE * slot, part, row)
    return row


def packed(value, slot):
    return turn(value, 2 * EDGE * slot + EDGE, 1)


def pack_rows(parts):
    return [
        side_by_side([part(slot) for slot, part in enumerate(parts[start : start + SLOTS])])
        for start in range(0, len(parts), SLOTS)
    ]


def halves():
    return [pl.ds(0, 8), pl.ds(8, 8)]


def low_lanes():
    return lax.broadcasted_iota(jnp.int32, (ZED, LANES), 1) % (2 * EDGE) < EDGE


def second_core():
    return lax.rem(lax.axis_index("gx"), 2)


def framed(q, odd):
    return q + odd * (mirrored(q) - q)


def copy_rows(target, source):
    for row in range(source.shape[0]):
        target[row] = source[row]


def split(value):
    return value[:, :LANES], value[:, LANES:], 0


def beside(row, slot):
    return row, -EDGE - 2 * EDGE * slot


def moved(triple, velocity, way):
    main, extra, by = triple
    _, step_y, step_z = velocity
    step = way * step_y
    main, extra = turn(main, way * step_z, 0), turn(extra, way * step_z, 0)
    if not step:
        return main, turn(extra, by, 1)
    main, extra = turn(main, step, 1), turn(extra, by + step, 1)
    lane = lax.broadcasted_iota(jnp.int32, (ZED, LANES), 1)
    edge = lane == (0 if step == 1 else LANES - 1)
    return jnp.where(edge, extra, main), jnp.where(edge, main, extra)


def put(ref, q, i, pair):
    ref[q, i, :, :LANES], ref[q, i, :, LANES:] = pair


def tiles(lanes):
    return [(z, pl.ds(t, LANES)) for z in halves() for t in range(0, lanes, LANES)]


def own_row(k, c):
    return c * FIELDS + k


def own_value(own, strip, k, c):
    place = own_row(k, c)
    return (own[place],) + beside(strip[place // SLOTS], place % SLOTS)


def halo_value(buffer, bulk, place):
    return (buffer[place],) + beside(buffer[bulk + place // SLOTS], place % SLOTS)


def given_state(flow, heat, odd, c, z):
    i = c + odd * (1 - 2 * c)
    return [flow[framed(q, odd), i, z, :] for q in range(19)] + [
        heat[framed(q, odd) - 19, i, z, :] for q in range(19, MEMBERS)
    ]


def first_kernel(
    flow_in, heat_in, flow_weight_in, heat_weight_in, resistance_in, conductivity_in, solid_in,
    own_out, up_out, down_out,
    own, up, down, flow, heat, flow_weight, heat_weight, resistance, conductivity, solid, arrived, sent,
):
    pairs = [
        (flow_in, flow),
        (heat_in, heat),
        (resistance_in, resistance),
        (conductivity_in, conductivity),
        (solid_in, solid),
        (flow_weight_in, flow_weight),
        (heat_weight_in, heat_weight),
    ]
    copies = [pltpu.make_async_copy(a, b, arrived.at[k]) for k, (a, b) in enumerate(pairs)]
    for copy in copies:
        copy.start()
    for copy in copies:
        copy.wait()
    odd = second_core()
    sign = (1 - 2 * odd).astype(jnp.float32)
    for c in range(2):
        i = c + odd * (1 - 2 * c)
        for z in halves():
            mobility = jnp.where(solid[i, z, :] != 0, 0.0, 1.0 / (1.0 + resistance[i, z, :]))
            rate = 1.0 / (0.5 + 0.4 * conductivity[i, z, :])
            p = given_state(flow, heat, odd, c, z)
            after = collide(p, level_sums(p), mobility, rate, range(MEMBERS))
            more = [mobility, rate, sign * flow_weight[0, i, z, :]]
            more += [flow_weight[1, i, z, :], flow_weight[2, i, z, :], heat_weight[i, z, :]]
            for k, value in enumerate([after[q] for q in range(MEMBERS)] + more):
                own[own_row(k, c), z, :] = value
    copy_own = pltpu.make_async_copy(own, own_out, sent.at[0])
    copy_own.start()
    rows = pack_rows([lambda slot, k=k: packed(own[k], slot) for k in range(2 * FIELDS)])
    low = low_lanes()
    for k in range(HALF_ROWS):
        up[k] = jnp.where(low, rows[k], turn(rows[k + HALF_ROWS], EDGE, 1))
        down[k] = jnp.where(low, turn(rows[k], -EDGE, 1), rows[k + HALF_ROWS])
    copies = [
        pltpu.make_async_copy(up, up_out, sent.at[1]),
        pltpu.make_async_copy(down, down_out, sent.at[2]),
    ]
    for copy in copies:
        copy.start()
    copy_own.wait()
    for copy in copies:
        copy.wait()


def stage_kernel(own, staged):
    copy_rows(staged, own)


def halo_kernel(own, from_below, from_above, far, near, strip):
    low = low_lanes()
    for k in range(HALF_ROWS):
        under, over = from_below[k], from_above[k]
        strip[k] = jnp.where(low, under, turn(over, EDGE, 1))
        strip[k + HALF_ROWS] = jnp.where(low, turn(under, -EDGE, 1), over)
    for side, rows, c in ((near, TO_NEAR, 1), (far, TO_FAR, 0)):
        level = {q: moved(own_value(own, strip, q, c), VELOCITY[q], 1) for q in LEVEL}
        sums = [level_sums({q: level[q][t] for q in LEVEL}) for t in range(2)]
        parts = []
        for (k, column), row in rows.items():
            if k >= FIELDS:
                side[row] = sums[0][k - FIELDS]
                parts.append(lambda slot, k=k: packed(sums[1][k - FIELDS], slot))
            else:
                place = own_row(k, column)
                side[row] = own[place]
                parts.append(
                    lambda slot, place=place: turn(
                        strip[place // SLOTS], 2 * EDGE * (slot - place % SLOTS), 1
                    )
                )
        for k, row in enumerate(pack_rows(parts)):
            side[BULK_ROWS + k] = row


def level_of(p, column, sums):
    return sums(p) if 0 <= column <= 1 else [p[q] for q in LEVEL[:SUMS]]


def near_place(rows, k, column):
    return rows[mirrored(k) if k < MEMBERS else k, 3 - column]


def far_place(rows, k, column):
    return rows[mirrored(k) if k < MEMBERS else k, -1 - column]


def own_fed(q, column):
    return 0 <= column <= 1 and 0 <= column - VELOCITY[q][0] <= 1


def state_of(own_state, state, first, column, z, y):
    return [
        own_state[q, column, z, y] if own_fed(q, column) else state[q, column - first, z, y]
        for q in range(MEMBERS)
    ]


def first_state(wide, column, state, sides, i):
    put(sides, 0, i, moved(wide(MOBILITY, column), STILL, 1))
    put(sides, 1, i, moved(wide(RATE, column), STILL, 1))
    for q in range(MEMBERS):
        if own_fed(q, column):
            continue
        if 0 <= column <= 1 or q not in LEVEL:
            put(state, q, i, moved(wide(q, column - VELOCITY[q][0]), VELOCITY[q], 1))
        elif q in LEVEL[:SUMS]:
            put(state, q, i, moved(wide(SUM_FIELDS[LEVEL.index(q)], column), STILL, 1))


def first_collision(column, own_state, state, sides, after, first):
    i = column - first
    wanted = [q for q in range(MEMBERS) if 0 <= column + VELOCITY[q][0] <= 1]
    for z, y in tiles(WIDE):
        p = state_of(own_state, state, first, column, z, y)
        level = level_of(p, column, level_sums)
        result = collide(p, level, sides[0, i, z, y], sides[1, i, z, y], wanted)
        for q in wanted:
            after[q, i, z, y] = result[q]


def seeds(wide, column, seed):
    weights = [wide(WEIGHT + k, column) for k in range(3)]
    weights = [(main, turn(extra, by, 1)) for main, extra, by in weights]
    if not 0 <= column <= 1:
        weights[0] = tuple(-value for value in weights[0])
    for q in range(1, MEMBERS):
        velocity = VELOCITY[q]
        c = column - velocity[0]
        if not 0 <= c <= 1:
            continue
        if q < 19:
            parts = [
                tuple(value if velocity[k] > 0 else -value for value in weights[k]) for k in range(3) if velocity[k]
            ]
            pair = parts[0] if len(parts) == 1 else tuple(a + b for a, b in zip(*parts))
            pair += (0,)
        else:
            pair = wide(WEIGHT + 3, column)
        put(seed, q, c, moved(pair, velocity, -1))


def own_step_kernel(own, strip, own_state, own_seed):
    def wide(k, column):
        return own_value(own, strip, k, column)

    for column in (0, 1):
        for q in range(MEMBERS):
            if own_fed(q, column):
                put(own_state, q, column, moved(wide(q, column - VELOCITY[q][0]), VELOCITY[q], 1))
        seeds(wide, column, own_seed)


def step_kernel(
    own, strip, own_state, own_seed, from_far, from_near,
    far_state, far_sides, near_state, near_sides, adjoint, by_resistance, by_conductivity, far, near,
    after, near_after, later, halo_seed,
):
    def wide(k, column):
        if column < 0:
            return halo_value(from_far, BULK_ROWS, far_place(TO_FAR, k, column))
        if column > 1:
            return halo_value(from_near, BULK_ROWS, near_place(TO_NEAR, k, column))
        return own_value(own, strip, k, column)

    for column in (-1, 0):
        first_state(wide, column, far_state, far_sides, column + 1)
        first_collision(column, own_state, far_state, far_sides, after, -1)
    for column in (1, 2):
        first_state(wide, column, near_state, near_sides, column - 1)
        first_collision(column, own_state, near_state, near_sides, near_after, 1)
    for column in (-1, 2):
        seeds(wide, column, halo_seed)
    for c in range(2):
        for q in range(MEMBERS):
            column = c - VELOCITY[q][0]
            source = near_after[q, column - 1] if column >= 1 else after[q, column + 1]
            put(later, q, c, moved(split(source), VELOCITY[q], 1))
    for c in range(2):
        for z, y in tiles(WIDE):
            p = [later[q, c, z, y] for q in range(MEMBERS)]
            pa = [jnp.zeros((8, LANES), jnp.float32)]
            pa += [
                (own_seed if 0 <= c + VELOCITY[q][0] <= 1 else halo_seed)[q, c, z, y] for q in range(1, MEMBERS)
            ]
            inner = y.start == 0
            mobility, rate = [near_sides[k, 0, z, y] if c else far_sides[k, 1, z, y] for k in range(2)]
            result = pull_back(
                p, level_sums(p), pa, level_adjoint_sums(pa), mobility, rate, range(MEMBERS), inner
            )
            if inner:
                by_resistance[c, z, :], by_conductivity[c, z, :] = result["by"]
            for q in range(MEMBERS):
                adjoint[q, c, z, y] = result[q]
    for side, rows, c in ((near, ADJ_TO_NEAR, 1), (far, ADJ_TO_FAR, 0)):
        level = {q: moved(split(adjoint[q, c]), VELOCITY[q], -1) for q in LEVEL}
        sums = [level_adjoint_sums({q: level[q][t] for q in LEVEL}) for t in range(2)]
        parts = []
        for (k, column), row in rows.items():
            if k >= FIELDS:
                side[row] = sums[0][k - FIELDS]
                parts.append(lambda slot, k=k: packed(sums[1][k - FIELDS], slot))
            else:
                side[row] = adjoint[k, column, :, :LANES]
                parts.append(lambda slot, k=k, column=column: packed(adjoint[k, column, :, LANES:], slot))
        for k, row in enumerate(pack_rows(parts)):
            side[ADJ_BULK + k] = row


def adjoint_step(wide, column, own_state, state, sides, arrived, earlier, first, keep):
    own = 0 <= column <= 1
    i = column - first
    for q in range(MEMBERS):
        if own or q not in LEVEL:
            put(arrived, q, i, moved(wide(q, column + VELOCITY[q][0]), VELOCITY[q], -1))
        elif q in LEVEL[:SUMS]:
            put(arrived, q, i, moved(wide(SUM_FIELDS[LEVEL.index(q)], column), STILL, 1))
    for z, y in tiles(WIDE):
        inner = y.start == 0
        wanted = [
            q for q in range(MEMBERS) if 0 <= column - VELOCITY[q][0] <= 1 and (inner or VELOCITY[q][1])
        ]
        p = state_of(own_state, state, first, column, z, y)
        pa = [arrived[q, i, z, y] for q in range(MEMBERS)]
        result = pull_back(
            p, level_of(p, column, level_sums), pa, level_of(pa, column, level_adjoint_sums),
            sides[0, i, z, y], sides[1, i, z, y], wanted, inner and own,
        )
        for q in wanted:
            earlier[q, i, z, y] = result[q]
        if inner and own:
            keep(z, *result["by"])


def far_adjoint_kernel(
    own_state, state, sides, adjoint, part_resistance, part_conductivity, from_far,
    earlier, by_resistance, by_conductivity,
    arrived,
):
    def wide(k, column):
        if column < 0:
            return halo_value(from_far, ADJ_BULK, far_place(ADJ_TO_FAR, k, column))
        return split(adjoint[k, column])

    def keep(z, resistance, conductivity):
        by_resistance[0, z, :] = part_resistance[0, z, :] + resistance
        by_conductivity[0, z, :] = part_conductivity[0, z, :] + conductivity

    for column in (-1, 0):
        adjoint_step(wide, column, own_state, state, sides, arrived, earlier, -1, keep)
    by_resistance[1] = part_resistance[1]
    by_conductivity[1] = part_conductivity[1]


def near_adjoint_kernel(
    flow, heat, own_state, state, sides, far_sides, adjoint, far_earlier, part_resistance, part_conductivity, from_near,
    by_resistance, by_conductivity,
    arrived, earlier, last, sums,
):
    def wide(k, column):
        if column > 1:
            return halo_value(from_near, ADJ_BULK, near_place(ADJ_TO_NEAR, k, column))
        return split(adjoint[k, column])

    def keep(z, resistance, conductivity):
        sums[0, z, :] = part_resistance[1, z, :] + resistance
        sums[1, z, :] = part_conductivity[1, z, :] + conductivity

    for column in (1, 2):
        adjoint_step(wide, column, own_state, state, sides, arrived, earlier, 1, keep)
    for c in range(2):
        for q in range(MEMBERS):
            velocity = VELOCITY[q]
            column = c + velocity[0]
            source, i = (earlier, column - 1) if column >= 1 else (far_earlier, column + 1)
            if velocity[1]:
                last[q, c] = moved(split(source[q, i]), velocity, -1)[0]
            else:
                last[q, c] = turn(source[q, i, :, :LANES], -velocity[2], 0)
    narrow = pl.ds(0, LANES)
    odd = second_core()
    for c in range(2):
        i = c + odd * (1 - 2 * c)
        for z in halves():
            p = given_state(flow, heat, odd, c, z)
            pa = [last[q, c, z, :] for q in range(MEMBERS)]
            mobility, rate = [(sides[k, 0, z, narrow] if c else far_sides[k, 1, z, narrow]) for k in range(2)]
            result = pull_back(p, level_sums(p), pa, level_adjoint_sums(pa), mobility, rate, (), True)
            resistance, conductivity = result["by"]
            by_resistance[i, z, :] = resistance + (sums[0, z, :] if c else part_resistance[0, z, :])
            by_conductivity[i, z, :] = conductivity + (sums[1, z, :] if c else part_conductivity[0, z, :])


def floats(*shape):
    return jax.ShapeDtypeStruct(shape, jnp.float32)


def vmem(*shape):
    return pltpu.VMEM(shape, jnp.float32)


def swap_along_x(far, near):
    count = lax.axis_size("gx")
    across = [(i, (i + (1 if i % 2 else -1)) % count) for i in range(count)]
    within = [(i, i ^ 1) for i in range(count)]
    return lax.ppermute(far, "gx", across), lax.ppermute(near, "gx", within)


FIRST_PARAMS = pltpu.CompilerParams(vmem_limit_bytes=56 * 1024 * 1024)
PARAMS = pltpu.CompilerParams(vmem_limit_bytes=24 * 1024 * 1024)


def on_device(flow, heat, flow_weight, heat_weight, resistance, conductivity, solid):
    in_hbm = pl.BlockSpec(memory_space=pltpu.HBM)
    own, up, down = pl.pallas_call(
        first_kernel,
        in_specs=[in_hbm] * 7,
        out_specs=[in_hbm] * 3,
        out_shape=(
            floats(2 * FIELDS, ZED, LANES),
            floats(HALF_ROWS, ZED, LANES),
            floats(HALF_ROWS, ZED, LANES),
        ),
        scratch_shapes=[
            vmem(2 * FIELDS, ZED, LANES),
            vmem(HALF_ROWS, ZED, LANES),
            vmem(HALF_ROWS, ZED, LANES),
            vmem(19, 2, ZED, LANES),
            vmem(7, 2, ZED, LANES),
            vmem(3, 2, ZED, LANES),
            vmem(2, ZED, LANES),
            vmem(2, ZED, LANES),
            vmem(2, ZED, LANES),
            pltpu.VMEM((2, ZED, LANES), jnp.int32),
            pltpu.SemaphoreType.DMA((7,)),
            pltpu.SemaphoreType.DMA((3,)),
        ],
        compiler_params=FIRST_PARAMS,
        name="collide_own",
    )(flow, heat, flow_weight, heat_weight, resistance, conductivity, solid)

    count = lax.axis_size("gy")
    upward = [(i, (i + 1) % count) for i in range(count)]
    from_below = lax.ppermute(up, "gy", upward)
    from_above = lax.ppermute(down, "gy", [(target, source) for source, target in upward])

    own = pl.pallas_call(
        stage_kernel,
        out_shape=floats(2 * FIELDS, ZED, LANES),
        compiler_params=PARAMS,
        cost_estimate=pl.CostEstimate(flops=10**7, bytes_accessed=10**6, transcendentals=0),
        name="stage_own",
    )(own)

    far, near, strip = pl.pallas_call(
        halo_kernel,
        out_shape=(floats(SENT, ZED, LANES), floats(SENT, ZED, LANES), floats(STRIP_ROWS, ZED, LANES)),
        compiler_params=PARAMS,
        name="halo_buffers",
    )(own, from_below, from_above)

    from_far, from_near = swap_along_x(far, near)

    columns = floats(MEMBERS, 2, ZED, WIDE)
    side_columns = floats(2, 2, ZED, WIDE)
    cells = floats(2, ZED, LANES)
    held = vmem(MEMBERS, 2, ZED, WIDE)
    busy = pl.CostEstimate(flops=10**7, bytes_accessed=10**6, transcendentals=0)

    own_state, own_seed = pl.pallas_call(
        own_step_kernel,
        out_shape=(columns, columns),
        compiler_params=PARAMS,
        cost_estimate=busy,
        name="own_step",
    )(own, strip)

    far_state, far_sides, near_state, near_sides, adjoint, part_resistance, part_conductivity, far, near = (
        pl.pallas_call(
            step_kernel,
            out_shape=(
                columns, side_columns, columns, side_columns, columns, cells, cells,
                floats(ADJ_SENT, ZED, LANES), floats(ADJ_SENT, ZED, LANES),
            ),
            scratch_shapes=[held, held, held, held],
            compiler_params=PARAMS,
            name="two_steps",
        )(own, strip, own_state, own_seed, from_far, from_near)
    )

    from_far, from_near = swap_along_x(far, near)

    far_earlier, part_resistance, part_conductivity = pl.pallas_call(
        far_adjoint_kernel,
        out_shape=(columns, cells, cells),
        scratch_shapes=[held],
        compiler_params=PARAMS,
        cost_estimate=busy,
        name="far_adjoint",
    )(own_state, far_state, far_sides, adjoint, part_resistance, part_conductivity, from_far)

    return pl.pallas_call(
        near_adjoint_kernel,
        out_shape=(cells, cells),
        scratch_shapes=[held, held, vmem(MEMBERS, 2, ZED, LANES), vmem(2, ZED, LANES)],
        compiler_params=PARAMS,
        name="near_adjoint",
    )(
        flow, heat, own_state, near_state, near_sides, far_sides, adjoint, far_earlier,
        part_resistance, part_conductivity, from_near,
    )


def solution(mesh):
    split = P("gx", None, "gy")
    stacked = P(None, "gx", None, "gy")
    return jax.shard_map(
        on_device,
        mesh=mesh,
        in_specs=(stacked, stacked, stacked, split, split, split, split),
        out_specs=(split, split),
        check_vma=False,
    )
```

```python
import jax
import jax.numpy as jnp
from jax import lax
from jax.experimental import pallas as pl
from jax.experimental.pallas import tpu as pltpu
from jax.sharding import PartitionSpec as P

ZED = 16
LANES = 128
WIDE = 2 * LANES
EDGE = 4

FLOW_VELOCITY = [
    (0, 0, 0),
    (1, 0, 0),
    (-1, 0, 0),
    (0, 1, 0),
    (0, -1, 0),
    (0, 0, 1),
    (0, 0, -1),
    (1, 1, 0),
    (-1, -1, 0),
    (1, -1, 0),
    (-1, 1, 0),
    (1, 0, 1),
    (-1, 0, -1),
    (1, 0, -1),
    (-1, 0, 1),
    (0, 1, 1),
    (0, -1, -1),
    (0, 1, -1),
    (0, -1, 1),
]
VELOCITY = FLOW_VELOCITY + FLOW_VELOCITY[:7]
STILL = (0, 0, 0)
MEMBERS = len(VELOCITY)
RIGHTWARD = [q for q in range(MEMBERS) if VELOCITY[q][0] == 1]
LEFTWARD = [q for q in range(MEMBERS) if VELOCITY[q][0] == -1]
LEVEL = [q for q in range(MEMBERS) if VELOCITY[q][0] == 0]


def mirrored(q):
    x, y, z = VELOCITY[q]
    start = 0 if q < 19 else 19
    return start + FLOW_VELOCITY.index((-x, y, z))


MOBILITY, RATE, WEIGHT = MEMBERS, MEMBERS + 1, MEMBERS + 2
FIELDS = MEMBERS + 6
SIDE_FIELDS = list(range(MEMBERS, FIELDS))

SUMS = 9
SUM_FIELDS = [FIELDS + k for k in range(SUMS)]

SLOTS = LANES // (2 * EDGE)
STRIP_ROWS = 2 * FIELDS // SLOTS
HALF_ROWS = STRIP_ROWS // 2


def rows_of(entries):
    return {entry: row for row, entry in enumerate(entries)}


TO_NEAR = rows_of([(q, 0) for q in RIGHTWARD] + [(k, 1) for k in RIGHTWARD + SIDE_FIELDS + SUM_FIELDS])
TO_FAR = rows_of([(q, 1) for q in LEFTWARD] + [(k, 0) for k in LEFTWARD + SIDE_FIELDS + SUM_FIELDS])
ADJ_TO_NEAR = rows_of([(q, 0) for q in LEFTWARD] + [(k, 1) for k in LEFTWARD + SUM_FIELDS])
ADJ_TO_FAR = rows_of([(q, 1) for q in RIGHTWARD] + [(k, 0) for k in RIGHTWARD + SUM_FIELDS])
BULK_ROWS, ADJ_BULK = len(TO_NEAR), len(ADJ_TO_NEAR)


def with_strips(bulk):
    return bulk + -(-bulk // SLOTS)


SENT, ADJ_SENT = with_strips(BULK_ROWS), with_strips(ADJ_BULK)


def level_sums(p):
    s1, s2, d1, d2 = p[3] + p[4], p[5] + p[6], p[3] - p[4], p[5] - p[6]
    s7, s8, d7, d8 = p[15] + p[16], p[17] + p[18], p[15] - p[16], p[17] - p[18]
    yz = s7 + s8
    mass = p[0] + (s1 + s2) + yz
    return [
        mass, d1 + (d7 + d8), d2 + (d7 - d8), s1 + yz, s2 + yz, s7 - s8,
        p[19] + (p[22] + p[23]) + (p[24] + p[25]), p[22] - p[23], p[24] - p[25],
    ]


def level_adjoint_sums(p):
    s1, s2, d1, d2 = p[3] + p[4], p[5] + p[6], p[3] - p[4], p[5] - p[6]
    s7, s8, d7, d8 = p[15] + p[16], p[17] + p[18], p[15] - p[16], p[17] - p[18]
    yz = s7 + s8
    t1, t2 = s1 + s1, s2 + s2
    mass = 12.0 * p[0] + (t1 + t2) + yz
    return [
        mass, (d1 + d1) + (d7 + d8), (d2 + d2) + (d7 - d8), t1 + yz, t2 + yz, s7 - s8,
        0.35 * p[19] + 0.175 * ((p[22] + p[23]) + (p[24] + p[25])),
        0.125 * (p[22] - p[23]), 0.125 * (p[24] - p[25]),
    ]


def cross_sums(p):
    pairs = [(1, 2), (7, 8), (9, 10), (11, 12), (13, 14)]
    return [p[a] + p[b] for a, b in pairs], [p[a] - p[b] for a, b in pairs]


def common(p, level, mobility):
    s, d = cross_sums(p)
    xy, xz = s[1] + s[2], s[3] + s[4]
    along = s[0] + xy + xz
    rho = level[0] + along
    j = (d[0] + (d[1] + d[2]) + (d[3] + d[4]), level[1] + (d[1] - d[2]), level[2] + (d[3] - d[4]))
    temperature = level[6] + (p[20] + p[21])
    flux = (p[20] - p[21], level[7], level[8])
    u = tuple(mobility * jk for jk in j)
    square = (u[0] * u[0], u[1] * u[1], u[2] * u[2])
    third = rho * (1.0 / 3.0)
    stress = (
        along - third - square[0],
        (level[3] + xy) - third - square[1],
        (level[4] + xz) - third - square[2],
        (s[1] - s[2]) - u[0] * u[1],
        (s[3] - s[4]) - u[0] * u[2],
        level[5] - u[1] * u[2],
    )
    decay = jnp.exp(-2.0 * (temperature - 1.0))
    omega = 1.0 / (0.5 + 0.3 * decay)
    return rho, j, u, square, stress, temperature, flux, decay, omega


def collide(p, level, mobility, rate, wanted):
    rho, _, u, square, stress, temperature, flux, _, omega = common(p, level, mobility)
    solid = mobility == 0.0
    lam = 1.2 - omega
    trace = stress[0] + stress[1] + stress[2]
    base = 1.2 * rho - 1.8 * (square[0] + square[1] + square[2]) - (1.5 * lam) * trace
    scale = 4.5 * lam
    mxx = 5.4 * square[0] + scale * stress[0]
    myy = 5.4 * square[1] + scale * stress[1]
    mzz = 5.4 * square[2] + scale * stress[2]
    mxy = 2.0 * (5.4 * (u[0] * u[1]) + scale * stress[3])
    mxz = 2.0 * (5.4 * (u[0] * u[2]) + scale * stress[4])
    myz = 2.0 * (5.4 * (u[1] * u[2]) + scale * stress[5])
    bx, by, bz = base + mxx, base + myy, base + mzz
    sxy, sxz, syz = bx + myy, bx + mzz, by + mzz
    even = [bx, by, bz, sxy + mxy, sxy - mxy, sxz + mxz, sxz - mxz, syz + myz, syz - myz]
    odd = [u[0], u[1], u[2], u[0] + u[1], u[0] - u[1], u[0] + u[2], u[0] - u[2], u[1] + u[2], u[1] - u[2]]
    result = {}
    if 0 in wanted:
        result[0] = jnp.where(solid, p[0], (1.0 / 3.0) * base - 0.2 * p[0])
    for k in range(9):
        a, b = 2 * k + 1, 2 * k + 2
        w = 1.0 / 18.0 if k < 3 else 1.0 / 36.0
        e, o = w * even[k], (3.6 * w) * odd[k]
        if a in wanted:
            result[a] = jnp.where(solid, p[b], (e + o) - 0.2 * p[a])
        if b in wanted:
            result[b] = jnp.where(solid, p[a], (e - o) - 0.2 * p[b])
    keep = 0.5 * (1.4 - rate)
    push = (0.5 * rate) * temperature
    warm = 0.175 * temperature
    if 19 in wanted:
        result[19] = 0.35 * temperature - 0.4 * p[19]
    for k in range(3):
        along = keep * flux[k] + push * u[k]
        a, b = 20 + 2 * k, 21 + 2 * k
        if a in wanted:
            result[a] = (warm + along) - 0.4 * p[a]
        if b in wanted:
            result[b] = (warm - along) - 0.4 * p[b]
    return result


def pull_back(p, level, pa, adjoint_level, mobility, rate, wanted, sensitivity):
    rho, j, u, square, stress, temperature, flux, decay, omega = common(p, level, mobility)
    solid = mobility == 0.0
    lam = 1.2 - omega
    s, d = cross_sums(pa)
    w = 1.0 / 36.0
    xy, xz = s[1] + s[2], s[3] + s[4]
    along = (s[0] + s[0]) + xy + xz
    mass = w * (adjoint_level[0] + along)
    px = w * ((d[0] + d[0]) + (d[1] + d[2]) + (d[3] + d[4]))
    py = w * (adjoint_level[1] + (d[1] - d[2]))
    pz = w * (adjoint_level[2] + (d[3] - d[4]))
    rxx, ryy, rzz = w * along, w * (adjoint_level[3] + xy), w * (adjoint_level[4] + xz)
    rxy, rxz, ryz = w * (s[1] - s[2]), w * (s[3] - s[4]), w * adjoint_level[5]
    shift = 1.5 * mass
    dxx, dyy, dzz = 4.5 * rxx - shift, 4.5 * ryy - shift, 4.5 * rzz - shift
    dxy, dxz, dyz = 4.5 * rxy, 4.5 * rxz, 4.5 * ryz
    mix = 2.4 - 2.0 * lam
    b = ((pa[20] - pa[21]) * 0.125, adjoint_level[7], adjoint_level[8])
    push = (4.0 * rate) * temperature
    ux = 3.6 * px + mix * (dxx * u[0] + dxy * u[1] + dxz * u[2]) + push * b[0]
    uy = 3.6 * py + mix * (dxy * u[0] + dyy * u[1] + dyz * u[2]) + push * b[1]
    uz = 3.6 * pz + mix * (dxz * u[0] + dyz * u[1] + dzz * u[2]) + push * b[2]
    result = {}
    if wanted:
        lam_bar = (
            dxx * stress[0]
            + dyy * stress[1]
            + dzz * stress[2]
            + 2.0 * (dxy * stress[3] + dxz * stress[4] + dyz * stress[5])
        )
        rho_bar = 1.2 * mass - (1.5 * lam) * ((rxx + ryy + rzz) - mass)
        jx, jy, jz = mobility * ux, mobility * uy, mobility * uz
        ex, ey, ez = lam * dxx, lam * dyy, lam * dzz
        exy, exz, eyz = (2.0 * lam) * dxy, (2.0 * lam) * dxz, (2.0 * lam) * dyz
        hx, hy, hz = rho_bar + ex, rho_bar + ey, rho_bar + ez
        gxy, gxz, gyz = hx + ey, hx + ez, hy + ez
        even = [hx, hy, hz, gxy + exy, gxy - exy, gxz + exz, gxz - exz, gyz + eyz, gyz - eyz]
        odd = [jx, jy, jz, jx + jy, jx - jy, jx + jz, jx - jz, jy + jz, jy - jz]
        if 0 in wanted:
            result[0] = jnp.where(solid, pa[0], rho_bar - 0.2 * pa[0])
        for k in range(9):
            a, m = 2 * k + 1, 2 * k + 2
            if a in wanted:
                result[a] = jnp.where(solid, pa[m], (even[k] + odd[k]) - 0.2 * pa[a])
            if m in wanted:
                result[m] = jnp.where(solid, pa[a], (even[k] - odd[k]) - 0.2 * pa[m])
        warm = (
            adjoint_level[6]
            + 0.175 * (pa[20] + pa[21])
            + (4.0 * rate) * (b[0] * u[0] + b[1] * u[1] + b[2] * u[2])
            - jnp.where(solid, 0.0, lam_bar * (0.6 * decay) * (omega * omega))
        )
        keep = 5.6 - 4.0 * rate
        if 19 in wanted:
            result[19] = warm - 0.4 * pa[19]
        for k in range(3):
            along = keep * b[k]
            a, m = 20 + 2 * k, 21 + 2 * k
            if a in wanted:
                result[a] = (warm + along) - 0.4 * pa[a]
            if m in wanted:
                result[m] = (warm - along) - 0.4 * pa[m]
    if sensitivity:
        by_resistance = -(mobility * mobility) * (ux * j[0] + uy * j[1] + uz * j[2])
        bent = (
            b[0] * (temperature * u[0] - flux[0])
            + b[1] * (temperature * u[1] - flux[1])
            + b[2] * (temperature * u[2] - flux[2])
        )
        by_conductivity = (-1.6 * (rate * rate)) * bent
        result["by"] = (by_resistance, by_conductivity)
    return result


BEGIN = 8


def begin_terms(p, mobility, rate):
    _, _, u, _, _, temperature, flux, _, omega = common(p, level_sums(p), mobility)
    bent = [temperature * u[k] - flux[k] for k in range(3)]
    return list(u) + bent + [2.4 - 2.0 * (1.2 - omega), (4.0 * rate) * temperature]


def end_terms(terms, pa, mobility, rate):
    u, bent, mix, push = terms[:3], terms[3:6], terms[6], terms[7]
    level = level_adjoint_sums(pa)
    s, d = cross_sums(pa)
    w = 1.0 / 36.0
    xy, xz = s[1] + s[2], s[3] + s[4]
    along = (s[0] + s[0]) + xy + xz
    shift = (1.5 * w) * (level[0] + along)
    v = 4.5 * w
    dxx, dyy, dzz = v * along - shift, v * (level[3] + xy) - shift, v * (level[4] + xz) - shift
    dxy, dxz, dyz = v * (s[1] - s[2]), v * (s[3] - s[4]), v * level[5]
    px = (d[0] + d[0]) + (d[1] + d[2]) + (d[3] + d[4])
    py = level[1] + (d[1] - d[2])
    pz = level[2] + (d[3] - d[4])
    b = ((pa[20] - pa[21]) * 0.125, level[7], level[8])
    ux = (3.6 * w) * px + mix * (dxx * u[0] + dxy * u[1] + dxz * u[2]) + push * b[0]
    uy = (3.6 * w) * py + mix * (dxy * u[0] + dyy * u[1] + dyz * u[2]) + push * b[1]
    uz = (3.6 * w) * pz + mix * (dxz * u[0] + dyz * u[1] + dzz * u[2]) + push * b[2]
    by_resistance = -mobility * (ux * u[0] + uy * u[1] + uz * u[2])
    by_conductivity = (-1.6 * (rate * rate)) * (b[0] * bent[0] + b[1] * bent[1] + b[2] * bent[2])
    return by_resistance, by_conductivity


def turn(value, by, axis):
    count = value.shape[axis]
    by %= count
    return pltpu.roll(value, by, axis) if by else value


def side_by_side(parts):
    lane = lax.broadcasted_iota(jnp.int32, (ZED, LANES), 1)
    row = None
    for slot, part in enumerate(parts):
        row = part if row is None else jnp.where(lane >= 2 * EDGE * slot, part, row)
    return row


def packed(value, slot):
    return turn(value, 2 * EDGE * slot + EDGE, 1)


def pack_rows(parts):
    return [
        side_by_side([part(slot) for slot, part in enumerate(parts[start : start + SLOTS])])
        for start in range(0, len(parts), SLOTS)
    ]


def halves():
    return [pl.ds(0, 8), pl.ds(8, 8)]


def low_lanes():
    return lax.broadcasted_iota(jnp.int32, (ZED, LANES), 1) % (2 * EDGE) < EDGE


def second_core():
    return lax.rem(lax.axis_index("gx"), 2)


def odd_along_y():
    return lax.rem(lax.axis_index("gy"), 2)


def framed(q, odd):
    return q + odd * (mirrored(q) - q)


def copy_rows(target, source):
    for row in range(source.shape[0]):
        target[row] = source[row]


def split(value):
    return value[:, :LANES], value[:, LANES:], 0


def beside(row, slot):
    return row, -EDGE - 2 * EDGE * slot


def moved(triple, velocity, way):
    main, extra, by = triple
    _, step_y, step_z = velocity
    step = way * step_y
    main, extra = turn(main, way * step_z, 0), turn(extra, way * step_z, 0)
    if not step:
        return main, turn(extra, by, 1)
    main, extra = turn(main, step, 1), turn(extra, by + step, 1)
    lane = lax.broadcasted_iota(jnp.int32, (ZED, LANES), 1)
    edge = lane == (0 if step == 1 else LANES - 1)
    return jnp.where(edge, extra, main), jnp.where(edge, main, extra)


def put(ref, q, i, pair):
    ref[q, i, :, :LANES], ref[q, i, :, LANES:] = pair


def tiles(lanes):
    return [(z, pl.ds(t, LANES)) for z in halves() for t in range(0, lanes, LANES)]


def own_row(k, c):
    return c * FIELDS + k


def own_value(own, strip, k, c):
    place = own_row(k, c)
    return (own[place],) + beside(strip[place // SLOTS], place % SLOTS)


def halo_value(buffer, bulk, place):
    return (buffer[place],) + beside(buffer[bulk + place // SLOTS], place % SLOTS)


def given_state(flow, heat, odd, c, z):
    i = c + odd * (1 - 2 * c)
    return [flow[framed(q, odd), i, z, :] for q in range(19)] + [
        heat[framed(q, odd) - 19, i, z, :] for q in range(19, MEMBERS)
    ]


def first_kernel(
    flow_in, heat_in, flow_weight_in, heat_weight_in, resistance_in, conductivity_in, solid_in,
    own_out, outer_out, inner_out,
    own, strips, flow, heat, flow_weight, heat_weight, resistance, conductivity, solid, arrived, sent,
):
    pairs = [
        (flow_in, flow),
        (heat_in, heat),
        (resistance_in, resistance),
        (conductivity_in, conductivity),
        (solid_in, solid),
        (flow_weight_in, flow_weight),
        (heat_weight_in, heat_weight),
    ]
    copies = [pltpu.make_async_copy(a, b, arrived.at[k]) for k, (a, b) in enumerate(pairs)]
    for copy in copies:
        copy.start()
    for copy in copies:
        copy.wait()
    odd = second_core()
    sign = (1 - 2 * odd).astype(jnp.float32)
    for c in range(2):
        i = c + odd * (1 - 2 * c)
        for z in halves():
            mobility = jnp.where(solid[i, z, :] != 0, 0.0, 1.0 / (1.0 + resistance[i, z, :]))
            rate = 1.0 / (0.5 + 0.4 * conductivity[i, z, :])
            p = given_state(flow, heat, odd, c, z)
            after = collide(p, level_sums(p), mobility, rate, range(MEMBERS))
            more = [mobility, rate, sign * flow_weight[0, i, z, :]]
            more += [flow_weight[1, i, z, :], flow_weight[2, i, z, :], heat_weight[i, z, :]]
            for k, value in enumerate([after[q] for q in range(MEMBERS)] + more):
                own[own_row(k, c), z, :] = value
    copy_own = pltpu.make_async_copy(own, own_out, sent.at[0])
    copy_own.start()
    rows = pack_rows([lambda slot, k=k: packed(own[k], slot) for k in range(2 * FIELDS)])
    low = low_lanes()
    for k in range(HALF_ROWS):
        strips[k] = jnp.where(low, rows[k], turn(rows[k + HALF_ROWS], EDGE, 1))
        strips[k + HALF_ROWS] = jnp.where(low, turn(rows[k], -EDGE, 1), rows[k + HALF_ROWS])
    above = HALF_ROWS * (1 - odd_along_y())
    copies = [
        pltpu.make_async_copy(strips.at[pl.ds(above, HALF_ROWS)], outer_out, sent.at[1]),
        pltpu.make_async_copy(strips.at[pl.ds(HALF_ROWS - above, HALF_ROWS)], inner_out, sent.at[2]),
    ]
    for copy in copies:
        copy.start()
    copy_own.wait()
    for copy in copies:
        copy.wait()


def stage_kernel(own, staged):
    copy_rows(staged, own)


def halo_kernel(own, from_outer, from_inner, far, near, strip):
    low = low_lanes()
    odd = odd_along_y() == 1
    for k in range(HALF_ROWS):
        outer, inner = from_outer[k], from_inner[k]
        under, over = jnp.where(odd, inner, outer), jnp.where(odd, outer, inner)
        strip[k] = jnp.where(low, under, turn(over, EDGE, 1))
        strip[k + HALF_ROWS] = jnp.where(low, turn(under, -EDGE, 1), over)
    for side, rows, c in ((near, TO_NEAR, 1), (far, TO_FAR, 0)):
        level = {q: moved(own_value(own, strip, q, c), VELOCITY[q], 1) for q in LEVEL}
        sums = [level_sums({q: level[q][t] for q in LEVEL}) for t in range(2)]
        parts = []
        for (k, column), row in rows.items():
            if k >= FIELDS:
                side[row] = sums[0][k - FIELDS]
                parts.append(lambda slot, k=k: packed(sums[1][k - FIELDS], slot))
            else:
                place = own_row(k, column)
                side[row] = own[place]
                parts.append(
                    lambda slot, place=place: turn(
                        strip[place // SLOTS], 2 * EDGE * (slot - place % SLOTS), 1
                    )
                )
        for k, row in enumerate(pack_rows(parts)):
            side[BULK_ROWS + k] = row


def level_of(p, column, sums):
    return sums(p) if 0 <= column <= 1 else [p[q] for q in LEVEL[:SUMS]]


def near_place(rows, k, column):
    return rows[mirrored(k) if k < MEMBERS else k, 3 - column]


def far_place(rows, k, column):
    return rows[mirrored(k) if k < MEMBERS else k, -1 - column]


def own_fed(q, column):
    return 0 <= column <= 1 and 0 <= column - VELOCITY[q][0] <= 1


def state_of(own_state, state, first, column, z, y):
    return [
        own_state[q, column, z, y] if own_fed(q, column) else state[q, column - first, z, y]
        for q in range(MEMBERS)
    ]


def first_state(wide, column, state, sides, i):
    put(sides, 0, i, moved(wide(MOBILITY, column), STILL, 1))
    put(sides, 1, i, moved(wide(RATE, column), STILL, 1))
    for q in range(MEMBERS):
        if own_fed(q, column):
            continue
        if 0 <= column <= 1 or q not in LEVEL:
            put(state, q, i, moved(wide(q, column - VELOCITY[q][0]), VELOCITY[q], 1))
        elif q in LEVEL[:SUMS]:
            put(state, q, i, moved(wide(SUM_FIELDS[LEVEL.index(q)], column), STILL, 1))


def first_collision(column, own_state, state, sides, after, first):
    i = column - first
    wanted = [q for q in range(MEMBERS) if 0 <= column + VELOCITY[q][0] <= 1]
    for z, y in tiles(WIDE):
        p = state_of(own_state, state, first, column, z, y)
        level = level_of(p, column, level_sums)
        result = collide(p, level, sides[0, i, z, y], sides[1, i, z, y], wanted)
        for q in wanted:
            after[q, i, z, y] = result[q]


def seeds(wide, column, seed):
    weights = [wide(WEIGHT + k, column) for k in range(3)]
    weights = [(main, turn(extra, by, 1)) for main, extra, by in weights]
    if not 0 <= column <= 1:
        weights[0] = tuple(-value for value in weights[0])
    for q in range(1, MEMBERS):
        velocity = VELOCITY[q]
        c = column - velocity[0]
        if not 0 <= c <= 1:
            continue
        if q < 19:
            parts = [
                tuple(value if velocity[k] > 0 else -value for value in weights[k]) for k in range(3) if velocity[k]
            ]
            pair = parts[0] if len(parts) == 1 else tuple(a + b for a, b in zip(*parts))
            pair += (0,)
        else:
            pair = wide(WEIGHT + 3, column)
        put(seed, q, c, moved(pair, velocity, -1))


def own_step_kernel(flow, heat, own, strip, own_state, own_seed, begin):
    def wide(k, column):
        return own_value(own, strip, k, column)

    for column in (0, 1):
        for q in range(MEMBERS):
            if own_fed(q, column):
                put(own_state, q, column, moved(wide(q, column - VELOCITY[q][0]), VELOCITY[q], 1))
        seeds(wide, column, own_seed)
    odd = second_core()
    for c in range(2):
        for z in halves():
            terms = begin_terms(
                given_state(flow, heat, odd, c, z), own[own_row(MOBILITY, c), z, :], own[own_row(RATE, c), z, :]
            )
            for k, value in enumerate(terms):
                begin[k, c, z, :] = value


def step_kernel(
    own, strip, own_state, own_seed, from_far, from_near,
    far_state, far_sides, near_state, near_sides, adjoint, by_resistance, by_conductivity, far, near,
    after, near_after, later, halo_seed,
):
    def wide(k, column):
        if column < 0:
            return halo_value(from_far, BULK_ROWS, far_place(TO_FAR, k, column))
        if column > 1:
            return halo_value(from_near, BULK_ROWS, near_place(TO_NEAR, k, column))
        return own_value(own, strip, k, column)

    for column in (-1, 0):
        first_state(wide, column, far_state, far_sides, column + 1)
        first_collision(column, own_state, far_state, far_sides, after, -1)
    for column in (1, 2):
        first_state(wide, column, near_state, near_sides, column - 1)
        first_collision(column, own_state, near_state, near_sides, near_after, 1)
    for column in (-1, 2):
        seeds(wide, column, halo_seed)
    for c in range(2):
        for q in range(MEMBERS):
            column = c - VELOCITY[q][0]
            source = near_after[q, column - 1] if column >= 1 else after[q, column + 1]
            put(later, q, c, moved(split(source), VELOCITY[q], 1))
    for c in range(2):
        for z, y in tiles(WIDE):
            p = [later[q, c, z, y] for q in range(MEMBERS)]
            pa = [jnp.zeros((8, LANES), jnp.float32)]
            pa += [
                (own_seed if 0 <= c + VELOCITY[q][0] <= 1 else halo_seed)[q, c, z, y] for q in range(1, MEMBERS)
            ]
            inner = y.start == 0
            mobility, rate = [near_sides[k, 0, z, y] if c else far_sides[k, 1, z, y] for k in range(2)]
            result = pull_back(
                p, level_sums(p), pa, level_adjoint_sums(pa), mobility, rate, range(MEMBERS), inner
            )
            if inner:
                by_resistance[c, z, :], by_conductivity[c, z, :] = result["by"]
            for q in range(MEMBERS):
                adjoint[q, c, z, y] = result[q]
    for side, rows, c in ((near, ADJ_TO_NEAR, 1), (far, ADJ_TO_FAR, 0)):
        level = {q: moved(split(adjoint[q, c]), VELOCITY[q], -1) for q in LEVEL}
        sums = [level_adjoint_sums({q: level[q][t] for q in LEVEL}) for t in range(2)]
        parts = []
        for (k, column), row in rows.items():
            if k >= FIELDS:
                side[row] = sums[0][k - FIELDS]
                parts.append(lambda slot, k=k: packed(sums[1][k - FIELDS], slot))
            else:
                side[row] = adjoint[k, column, :, :LANES]
                parts.append(lambda slot, k=k, column=column: packed(adjoint[k, column, :, LANES:], slot))
        for k, row in enumerate(pack_rows(parts)):
            side[ADJ_BULK + k] = row


def adjoint_step(wide, column, own_state, state, sides, arrived, earlier, first, keep):
    own = 0 <= column <= 1
    i = column - first
    for q in range(MEMBERS):
        if own or q not in LEVEL:
            put(arrived, q, i, moved(wide(q, column + VELOCITY[q][0]), VELOCITY[q], -1))
        elif q in LEVEL[:SUMS]:
            put(arrived, q, i, moved(wide(SUM_FIELDS[LEVEL.index(q)], column), STILL, 1))
    for z, y in tiles(WIDE):
        inner = y.start == 0
        wanted = [
            q for q in range(MEMBERS) if 0 <= column - VELOCITY[q][0] <= 1 and (inner or VELOCITY[q][1])
        ]
        p = state_of(own_state, state, first, column, z, y)
        pa = [arrived[q, i, z, y] for q in range(MEMBERS)]
        result = pull_back(
            p, level_of(p, column, level_sums), pa, level_of(pa, column, level_adjoint_sums),
            sides[0, i, z, y], sides[1, i, z, y], wanted, inner and own,
        )
        for q in wanted:
            earlier[q, i, z, y] = result[q]
        if inner and own:
            keep(z, *result["by"])


def far_adjoint_kernel(
    own_state, state, sides, adjoint, part_resistance, part_conductivity, from_far,
    earlier, by_resistance, by_conductivity,
    arrived,
):
    def wide(k, column):
        if column < 0:
            return halo_value(from_far, ADJ_BULK, far_place(ADJ_TO_FAR, k, column))
        return split(adjoint[k, column])

    def keep(z, resistance, conductivity):
        by_resistance[0, z, :] = part_resistance[0, z, :] + resistance
        by_conductivity[0, z, :] = part_conductivity[0, z, :] + conductivity

    for column in (-1, 0):
        adjoint_step(wide, column, own_state, state, sides, arrived, earlier, -1, keep)
    by_resistance[1] = part_resistance[1]
    by_conductivity[1] = part_conductivity[1]


def near_adjoint_kernel(
    begin, own_state, state, sides, far_sides, adjoint, far_earlier, part_resistance, part_conductivity, from_near,
    by_resistance, by_conductivity,
    arrived, earlier, last, sums,
):
    def wide(k, column):
        if column > 1:
            return halo_value(from_near, ADJ_BULK, near_place(ADJ_TO_NEAR, k, column))
        return split(adjoint[k, column])

    def keep(z, resistance, conductivity):
        sums[0, z, :] = part_resistance[1, z, :] + resistance
        sums[1, z, :] = part_conductivity[1, z, :] + conductivity

    for column in (1, 2):
        adjoint_step(wide, column, own_state, state, sides, arrived, earlier, 1, keep)
    for c in range(2):
        for q in range(MEMBERS):
            velocity = VELOCITY[q]
            column = c + velocity[0]
            source, i = (earlier, column - 1) if column >= 1 else (far_earlier, column + 1)
            if velocity[1]:
                last[q, c] = moved(split(source[q, i]), velocity, -1)[0]
            else:
                last[q, c] = turn(source[q, i, :, :LANES], -velocity[2], 0)
    narrow = pl.ds(0, LANES)
    odd = second_core()
    for c in range(2):
        i = c + odd * (1 - 2 * c)
        for z in halves():
            pa = [last[q, c, z, :] for q in range(MEMBERS)]
            mobility, rate = [(sides[k, 0, z, narrow] if c else far_sides[k, 1, z, narrow]) for k in range(2)]
            terms = [begin[k, c, z, :] for k in range(BEGIN)]
            resistance, conductivity = end_terms(terms, pa, mobility, rate)
            by_resistance[i, z, :] = resistance + (sums[0, z, :] if c else part_resistance[0, z, :])
            by_conductivity[i, z, :] = conductivity + (sums[1, z, :] if c else part_conductivity[0, z, :])


def floats(*shape):
    return jax.ShapeDtypeStruct(shape, jnp.float32)


def vmem(*shape):
    return pltpu.VMEM(shape, jnp.float32)


def swap(outer, inner, axis):
    count = lax.axis_size(axis)
    across = [(i, (i + (1 if i % 2 else -1)) % count) for i in range(count)]
    within = [(i, i ^ 1) for i in range(count)]
    return lax.ppermute(outer, axis, across), lax.ppermute(inner, axis, within)


FIRST_PARAMS = pltpu.CompilerParams(vmem_limit_bytes=56 * 1024 * 1024)
PARAMS = pltpu.CompilerParams(vmem_limit_bytes=24 * 1024 * 1024)


def on_device(flow, heat, flow_weight, heat_weight, resistance, conductivity, solid):
    in_hbm = pl.BlockSpec(memory_space=pltpu.HBM)
    own, outer, inner = pl.pallas_call(
        first_kernel,
        in_specs=[in_hbm] * 7,
        out_specs=[in_hbm] * 3,
        out_shape=(
            floats(2 * FIELDS, ZED, LANES),
            floats(HALF_ROWS, ZED, LANES),
            floats(HALF_ROWS, ZED, LANES),
        ),
        scratch_shapes=[
            vmem(2 * FIELDS, ZED, LANES),
            vmem(STRIP_ROWS, ZED, LANES),
            vmem(19, 2, ZED, LANES),
            vmem(7, 2, ZED, LANES),
            vmem(3, 2, ZED, LANES),
            vmem(2, ZED, LANES),
            vmem(2, ZED, LANES),
            vmem(2, ZED, LANES),
            pltpu.VMEM((2, ZED, LANES), jnp.int32),
            pltpu.SemaphoreType.DMA((7,)),
            pltpu.SemaphoreType.DMA((3,)),
        ],
        compiler_params=FIRST_PARAMS,
        name="collide_own",
    )(flow, heat, flow_weight, heat_weight, resistance, conductivity, solid)

    from_outer, from_inner = swap(outer, inner, "gy")

    own = pl.pallas_call(
        stage_kernel,
        out_shape=floats(2 * FIELDS, ZED, LANES),
        compiler_params=PARAMS,
        cost_estimate=pl.CostEstimate(flops=10**7, bytes_accessed=10**6, transcendentals=0),
        name="stage_own",
    )(own)

    far, near, strip = pl.pallas_call(
        halo_kernel,
        out_shape=(floats(SENT, ZED, LANES), floats(SENT, ZED, LANES), floats(STRIP_ROWS, ZED, LANES)),
        compiler_params=PARAMS,
        name="halo_buffers",
    )(own, from_outer, from_inner)

    from_far, from_near = swap(far, near, "gx")

    columns = floats(MEMBERS, 2, ZED, WIDE)
    side_columns = floats(2, 2, ZED, WIDE)
    cells = floats(2, ZED, LANES)
    held = vmem(MEMBERS, 2, ZED, WIDE)
    busy = pl.CostEstimate(flops=10**7, bytes_accessed=10**6, transcendentals=0)

    own_state, own_seed, begin = pl.pallas_call(
        own_step_kernel,
        out_shape=(columns, columns, floats(BEGIN, 2, ZED, LANES)),
        compiler_params=PARAMS,
        cost_estimate=busy,
        name="own_step",
    )(flow, heat, own, strip)

    far_state, far_sides, near_state, near_sides, adjoint, part_resistance, part_conductivity, far, near = (
        pl.pallas_call(
            step_kernel,
            out_shape=(
                columns, side_columns, columns, side_columns, columns, cells, cells,
                floats(ADJ_SENT, ZED, LANES), floats(ADJ_SENT, ZED, LANES),
            ),
            scratch_shapes=[held, held, held, held],
            compiler_params=PARAMS,
            name="two_steps",
        )(own, strip, own_state, own_seed, from_far, from_near)
    )

    from_far, from_near = swap(far, near, "gx")

    far_earlier, part_resistance, part_conductivity = pl.pallas_call(
        far_adjoint_kernel,
        out_shape=(columns, cells, cells),
        scratch_shapes=[held],
        compiler_params=PARAMS,
        cost_estimate=busy,
        name="far_adjoint",
    )(own_state, far_state, far_sides, adjoint, part_resistance, part_conductivity, from_far)

    return pl.pallas_call(
        near_adjoint_kernel,
        out_shape=(cells, cells),
        scratch_shapes=[held, held, vmem(MEMBERS, 2, ZED, LANES), vmem(2, ZED, LANES)],
        compiler_params=PARAMS,
        name="near_adjoint",
    )(
        begin, own_state, near_state, near_sides, far_sides, adjoint, far_earlier,
        part_resistance, part_conductivity, from_near,
    )


def solution(mesh):
    split = P("gx", None, "gy")
    stacked = P(None, "gx", None, "gy")
    return jax.shard_map(
        on_device,
        mesh=mesh,
        in_specs=(stacked, stacked, stacked, split, split, split, split),
        out_specs=(split, split),
        check_vma=False,
    )
```

```python
import jax
import jax.numpy as jnp
from jax import lax
from jax.experimental import pallas as pl
from jax.experimental.pallas import tpu as pltpu
from jax.sharding import PartitionSpec as P

ZED = 16
LANES = 128
WIDE = 2 * LANES
EDGE = 4

FLOW_VELOCITY = [
    (0, 0, 0),
    (1, 0, 0),
    (-1, 0, 0),
    (0, 1, 0),
    (0, -1, 0),
    (0, 0, 1),
    (0, 0, -1),
    (1, 1, 0),
    (-1, -1, 0),
    (1, -1, 0),
    (-1, 1, 0),
    (1, 0, 1),
    (-1, 0, -1),
    (1, 0, -1),
    (-1, 0, 1),
    (0, 1, 1),
    (0, -1, -1),
    (0, 1, -1),
    (0, -1, 1),
]
VELOCITY = FLOW_VELOCITY + FLOW_VELOCITY[:7]
STILL = (0, 0, 0)
MEMBERS = len(VELOCITY)
RIGHTWARD = [q for q in range(MEMBERS) if VELOCITY[q][0] == 1]
LEFTWARD = [q for q in range(MEMBERS) if VELOCITY[q][0] == -1]
LEVEL = [q for q in range(MEMBERS) if VELOCITY[q][0] == 0]


def mirrored(q):
    x, y, z = VELOCITY[q]
    start = 0 if q < 19 else 19
    return start + FLOW_VELOCITY.index((-x, y, z))


MOBILITY, RATE, WEIGHT = MEMBERS, MEMBERS + 1, MEMBERS + 2
FIELDS = MEMBERS + 6
SIDE_FIELDS = list(range(MEMBERS, FIELDS))

SUMS = 9
SUM_FIELDS = [FIELDS + k for k in range(SUMS)]

SLOTS = LANES // (2 * EDGE)
STRIP_ROWS = 2 * FIELDS // SLOTS
HALF_ROWS = STRIP_ROWS // 2


def rows_of(entries):
    return {entry: row for row, entry in enumerate(entries)}


TO_NEAR = rows_of([(q, 0) for q in RIGHTWARD] + [(k, 1) for k in RIGHTWARD + SIDE_FIELDS + SUM_FIELDS])
TO_FAR = rows_of([(q, 1) for q in LEFTWARD] + [(k, 0) for k in LEFTWARD + SIDE_FIELDS + SUM_FIELDS])
ADJ_TO_NEAR = rows_of([(q, 0) for q in LEFTWARD] + [(k, 1) for k in LEFTWARD + SUM_FIELDS])
ADJ_TO_FAR = rows_of([(q, 1) for q in RIGHTWARD] + [(k, 0) for k in RIGHTWARD + SUM_FIELDS])
BULK_ROWS, ADJ_BULK = len(TO_NEAR), len(ADJ_TO_NEAR)


def with_strips(bulk):
    return bulk + -(-bulk // SLOTS)


SENT, ADJ_SENT = with_strips(BULK_ROWS), with_strips(ADJ_BULK)


def level_sums(p):
    s1, s2, d1, d2 = p[3] + p[4], p[5] + p[6], p[3] - p[4], p[5] - p[6]
    s7, s8, d7, d8 = p[15] + p[16], p[17] + p[18], p[15] - p[16], p[17] - p[18]
    yz = s7 + s8
    mass = p[0] + (s1 + s2) + yz
    return [
        mass, d1 + (d7 + d8), d2 + (d7 - d8), s1 + yz, s2 + yz, s7 - s8,
        p[19] + (p[22] + p[23]) + (p[24] + p[25]), p[22] - p[23], p[24] - p[25],
    ]


def level_adjoint_sums(p):
    s1, s2, d1, d2 = p[3] + p[4], p[5] + p[6], p[3] - p[4], p[5] - p[6]
    s7, s8, d7, d8 = p[15] + p[16], p[17] + p[18], p[15] - p[16], p[17] - p[18]
    yz = s7 + s8
    t1, t2 = s1 + s1, s2 + s2
    mass = 12.0 * p[0] + (t1 + t2) + yz
    return [
        mass, (d1 + d1) + (d7 + d8), (d2 + d2) + (d7 - d8), t1 + yz, t2 + yz, s7 - s8,
        0.35 * p[19] + 0.175 * ((p[22] + p[23]) + (p[24] + p[25])),
        0.125 * (p[22] - p[23]), 0.125 * (p[24] - p[25]),
    ]


def cross_sums(p):
    pairs = [(1, 2), (7, 8), (9, 10), (11, 12), (13, 14)]
    return [p[a] + p[b] for a, b in pairs], [p[a] - p[b] for a, b in pairs]


def common(p, level, mobility):
    s, d = cross_sums(p)
    xy, xz = s[1] + s[2], s[3] + s[4]
    along = s[0] + xy + xz
    rho = level[0] + along
    j = (d[0] + (d[1] + d[2]) + (d[3] + d[4]), level[1] + (d[1] - d[2]), level[2] + (d[3] - d[4]))
    temperature = level[6] + (p[20] + p[21])
    flux = (p[20] - p[21], level[7], level[8])
    u = tuple(mobility * jk for jk in j)
    square = (u[0] * u[0], u[1] * u[1], u[2] * u[2])
    third = rho * (1.0 / 3.0)
    stress = (
        along - third - square[0],
        (level[3] + xy) - third - square[1],
        (level[4] + xz) - third - square[2],
        (s[1] - s[2]) - u[0] * u[1],
        (s[3] - s[4]) - u[0] * u[2],
        level[5] - u[1] * u[2],
    )
    decay = jnp.exp(-2.0 * (temperature - 1.0))
    omega = 1.0 / (0.5 + 0.3 * decay)
    return rho, j, u, square, stress, temperature, flux, decay, omega


def collide(p, level, mobility, rate, wanted):
    rho, _, u, square, stress, temperature, flux, _, omega = common(p, level, mobility)
    solid = mobility == 0.0
    lam = 1.2 - omega
    trace = stress[0] + stress[1] + stress[2]
    base = 1.2 * rho - 1.8 * (square[0] + square[1] + square[2]) - (1.5 * lam) * trace
    scale = 4.5 * lam
    mxx = 5.4 * square[0] + scale * stress[0]
    myy = 5.4 * square[1] + scale * stress[1]
    mzz = 5.4 * square[2] + scale * stress[2]
    mxy = 2.0 * (5.4 * (u[0] * u[1]) + scale * stress[3])
    mxz = 2.0 * (5.4 * (u[0] * u[2]) + scale * stress[4])
    myz = 2.0 * (5.4 * (u[1] * u[2]) + scale * stress[5])
    bx, by, bz = base + mxx, base + myy, base + mzz
    sxy, sxz, syz = bx + myy, bx + mzz, by + mzz
    even = [bx, by, bz, sxy + mxy, sxy - mxy, sxz + mxz, sxz - mxz, syz + myz, syz - myz]
    odd = [u[0], u[1], u[2], u[0] + u[1], u[0] - u[1], u[0] + u[2], u[0] - u[2], u[1] + u[2], u[1] - u[2]]
    result = {}
    if 0 in wanted:
        result[0] = jnp.where(solid, p[0], (1.0 / 3.0) * base - 0.2 * p[0])
    for k in range(9):
        a, b = 2 * k + 1, 2 * k + 2
        w = 1.0 / 18.0 if k < 3 else 1.0 / 36.0
        e, o = w * even[k], (3.6 * w) * odd[k]
        if a in wanted:
            result[a] = jnp.where(solid, p[b], (e + o) - 0.2 * p[a])
        if b in wanted:
            result[b] = jnp.where(solid, p[a], (e - o) - 0.2 * p[b])
    keep = 0.5 * (1.4 - rate)
    push = (0.5 * rate) * temperature
    warm = 0.175 * temperature
    if 19 in wanted:
        result[19] = 0.35 * temperature - 0.4 * p[19]
    for k in range(3):
        along = keep * flux[k] + push * u[k]
        a, b = 20 + 2 * k, 21 + 2 * k
        if a in wanted:
            result[a] = (warm + along) - 0.4 * p[a]
        if b in wanted:
            result[b] = (warm - along) - 0.4 * p[b]
    return result


def pull_back(p, level, pa, adjoint_level, mobility, rate, wanted, sensitivity):
    rho, j, u, square, stress, temperature, flux, decay, omega = common(p, level, mobility)
    solid = mobility == 0.0
    lam = 1.2 - omega
    s, d = cross_sums(pa)
    w = 1.0 / 36.0
    xy, xz = s[1] + s[2], s[3] + s[4]
    along = (s[0] + s[0]) + xy + xz
    mass = w * (adjoint_level[0] + along)
    px = w * ((d[0] + d[0]) + (d[1] + d[2]) + (d[3] + d[4]))
    py = w * (adjoint_level[1] + (d[1] - d[2]))
    pz = w * (adjoint_level[2] + (d[3] - d[4]))
    rxx, ryy, rzz = w * along, w * (adjoint_level[3] + xy), w * (adjoint_level[4] + xz)
    rxy, rxz, ryz = w * (s[1] - s[2]), w * (s[3] - s[4]), w * adjoint_level[5]
    shift = 1.5 * mass
    dxx, dyy, dzz = 4.5 * rxx - shift, 4.5 * ryy - shift, 4.5 * rzz - shift
    dxy, dxz, dyz = 4.5 * rxy, 4.5 * rxz, 4.5 * ryz
    mix = 2.4 - 2.0 * lam
    b = ((pa[20] - pa[21]) * 0.125, adjoint_level[7], adjoint_level[8])
    push = (4.0 * rate) * temperature
    ux = 3.6 * px + mix * (dxx * u[0] + dxy * u[1] + dxz * u[2]) + push * b[0]
    uy = 3.6 * py + mix * (dxy * u[0] + dyy * u[1] + dyz * u[2]) + push * b[1]
    uz = 3.6 * pz + mix * (dxz * u[0] + dyz * u[1] + dzz * u[2]) + push * b[2]
    result = {}
    if wanted:
        lam_bar = (
            dxx * stress[0]
            + dyy * stress[1]
            + dzz * stress[2]
            + 2.0 * (dxy * stress[3] + dxz * stress[4] + dyz * stress[5])
        )
        rho_bar = 1.2 * mass - (1.5 * lam) * ((rxx + ryy + rzz) - mass)
        jx, jy, jz = mobility * ux, mobility * uy, mobility * uz
        ex, ey, ez = lam * dxx, lam * dyy, lam * dzz
        exy, exz, eyz = (2.0 * lam) * dxy, (2.0 * lam) * dxz, (2.0 * lam) * dyz
        hx, hy, hz = rho_bar + ex, rho_bar + ey, rho_bar + ez
        gxy, gxz, gyz = hx + ey, hx + ez, hy + ez
        even = [hx, hy, hz, gxy + exy, gxy - exy, gxz + exz, gxz - exz, gyz + eyz, gyz - eyz]
        odd = [jx, jy, jz, jx + jy, jx - jy, jx + jz, jx - jz, jy + jz, jy - jz]
        if 0 in wanted:
            result[0] = jnp.where(solid, pa[0], rho_bar - 0.2 * pa[0])
        for k in range(9):
            a, m = 2 * k + 1, 2 * k + 2
            if a in wanted:
                result[a] = jnp.where(solid, pa[m], (even[k] + odd[k]) - 0.2 * pa[a])
            if m in wanted:
                result[m] = jnp.where(solid, pa[a], (even[k] - odd[k]) - 0.2 * pa[m])
        warm = (
            adjoint_level[6]
            + 0.175 * (pa[20] + pa[21])
            + (4.0 * rate) * (b[0] * u[0] + b[1] * u[1] + b[2] * u[2])
            - jnp.where(solid, 0.0, lam_bar * (0.6 * decay) * (omega * omega))
        )
        keep = 5.6 - 4.0 * rate
        if 19 in wanted:
            result[19] = warm - 0.4 * pa[19]
        for k in range(3):
            along = keep * b[k]
            a, m = 20 + 2 * k, 21 + 2 * k
            if a in wanted:
                result[a] = (warm + along) - 0.4 * pa[a]
            if m in wanted:
                result[m] = (warm - along) - 0.4 * pa[m]
    if sensitivity:
        by_resistance = -(mobility * mobility) * (ux * j[0] + uy * j[1] + uz * j[2])
        bent = (
            b[0] * (temperature * u[0] - flux[0])
            + b[1] * (temperature * u[1] - flux[1])
            + b[2] * (temperature * u[2] - flux[2])
        )
        by_conductivity = (-1.6 * (rate * rate)) * bent
        result["by"] = (by_resistance, by_conductivity)
    return result


BEGIN = 8


def begin_terms(p, mobility, rate):
    _, _, u, _, _, temperature, flux, _, omega = common(p, level_sums(p), mobility)
    bent = [temperature * u[k] - flux[k] for k in range(3)]
    return list(u) + bent + [2.4 - 2.0 * (1.2 - omega), (4.0 * rate) * temperature]


def end_terms(terms, pa, mobility, rate):
    u, bent, mix, push = terms[:3], terms[3:6], terms[6], terms[7]
    level = level_adjoint_sums(pa)
    s, d = cross_sums(pa)
    w = 1.0 / 36.0
    xy, xz = s[1] + s[2], s[3] + s[4]
    along = (s[0] + s[0]) + xy + xz
    shift = (1.5 * w) * (level[0] + along)
    v = 4.5 * w
    dxx, dyy, dzz = v * along - shift, v * (level[3] + xy) - shift, v * (level[4] + xz) - shift
    dxy, dxz, dyz = v * (s[1] - s[2]), v * (s[3] - s[4]), v * level[5]
    px = (d[0] + d[0]) + (d[1] + d[2]) + (d[3] + d[4])
    py = level[1] + (d[1] - d[2])
    pz = level[2] + (d[3] - d[4])
    b = ((pa[20] - pa[21]) * 0.125, level[7], level[8])
    ux = (3.6 * w) * px + mix * (dxx * u[0] + dxy * u[1] + dxz * u[2]) + push * b[0]
    uy = (3.6 * w) * py + mix * (dxy * u[0] + dyy * u[1] + dyz * u[2]) + push * b[1]
    uz = (3.6 * w) * pz + mix * (dxz * u[0] + dyz * u[1] + dzz * u[2]) + push * b[2]
    by_resistance = -mobility * (ux * u[0] + uy * u[1] + uz * u[2])
    by_conductivity = (-1.6 * (rate * rate)) * (b[0] * bent[0] + b[1] * bent[1] + b[2] * bent[2])
    return by_resistance, by_conductivity


def turn(value, by, axis):
    count = value.shape[axis]
    by %= count
    return pltpu.roll(value, by, axis) if by else value


def side_by_side(parts):
    lane = lax.broadcasted_iota(jnp.int32, (ZED, LANES), 1)
    row = None
    for slot, part in enumerate(parts):
        row = part if row is None else jnp.where(lane >= 2 * EDGE * slot, part, row)
    return row


def packed(value, slot):
    return turn(value, 2 * EDGE * slot + EDGE, 1)


def pack_rows(parts):
    return [
        side_by_side([part(slot) for slot, part in enumerate(parts[start : start + SLOTS])])
        for start in range(0, len(parts), SLOTS)
    ]


def halves():
    return [pl.ds(0, 8), pl.ds(8, 8)]


def low_lanes():
    return lax.broadcasted_iota(jnp.int32, (ZED, LANES), 1) % (2 * EDGE) < EDGE


def second_core():
    return lax.rem(lax.axis_index("gx"), 2)


def framed(q, odd):
    return q + odd * (mirrored(q) - q)


def copy_rows(target, source):
    for row in range(source.shape[0]):
        target[row] = source[row]


def split(value):
    return value[:, :LANES], value[:, LANES:], 0


def beside(row, slot):
    return row, -EDGE - 2 * EDGE * slot


def moved(triple, velocity, way):
    main, extra, by = triple
    _, step_y, step_z = velocity
    step = way * step_y
    main, extra = turn(main, way * step_z, 0), turn(extra, way * step_z, 0)
    if not step:
        return main, turn(extra, by, 1)
    main, extra = turn(main, step, 1), turn(extra, by + step, 1)
    lane = lax.broadcasted_iota(jnp.int32, (ZED, LANES), 1)
    edge = lane == (0 if step == 1 else LANES - 1)
    return jnp.where(edge, extra, main), jnp.where(edge, main, extra)


def put(ref, q, i, pair):
    ref[q, i, :, :LANES], ref[q, i, :, LANES:] = pair


def tiles(lanes):
    return [(z, pl.ds(t, LANES)) for z in halves() for t in range(0, lanes, LANES)]


def own_row(k, c):
    return c * FIELDS + k


def own_value(own, strip, k, c):
    place = own_row(k, c)
    return (own[place],) + beside(strip[place // SLOTS], place % SLOTS)


def halo_value(buffer, bulk, place):
    return (buffer[place],) + beside(buffer[bulk + place // SLOTS], place % SLOTS)


def given_state(flow, heat, odd, c, z):
    i = c + odd * (1 - 2 * c)
    return [flow[framed(q, odd), i, z, :] for q in range(19)] + [
        heat[framed(q, odd) - 19, i, z, :] for q in range(19, MEMBERS)
    ]


def first_kernel(
    flow_in, heat_in, flow_weight_in, heat_weight_in, resistance_in, conductivity_in, solid_in,
    own_out, up_out, down_out,
    own, strips, flow, heat, flow_weight, heat_weight, resistance, conductivity, solid, arrived, sent,
):
    pairs = [
        (flow_in, flow),
        (heat_in, heat),
        (resistance_in, resistance),
        (conductivity_in, conductivity),
        (solid_in, solid),
        (flow_weight_in, flow_weight),
        (heat_weight_in, heat_weight),
    ]
    copies = [pltpu.make_async_copy(a, b, arrived.at[k]) for k, (a, b) in enumerate(pairs)]
    for copy in copies:
        copy.start()
    for copy in copies:
        copy.wait()
    odd = second_core()
    sign = (1 - 2 * odd).astype(jnp.float32)
    for c in range(2):
        i = c + odd * (1 - 2 * c)
        for z in halves():
            mobility = jnp.where(solid[i, z, :] != 0, 0.0, 1.0 / (1.0 + resistance[i, z, :]))
            rate = 1.0 / (0.5 + 0.4 * conductivity[i, z, :])
            p = given_state(flow, heat, odd, c, z)
            after = collide(p, level_sums(p), mobility, rate, range(MEMBERS))
            more = [mobility, rate, sign * flow_weight[0, i, z, :]]
            more += [flow_weight[1, i, z, :], flow_weight[2, i, z, :], heat_weight[i, z, :]]
            for k, value in enumerate([after[q] for q in range(MEMBERS)] + more):
                own[own_row(k, c), z, :] = value
    copy_own = pltpu.make_async_copy(own, own_out, sent.at[0])
    copy_own.start()
    rows = pack_rows([lambda slot, k=k: packed(own[k], slot) for k in range(2 * FIELDS)])
    low = low_lanes()
    for k in range(HALF_ROWS):
        strips[k] = jnp.where(low, rows[k], turn(rows[k + HALF_ROWS], EDGE, 1))
        strips[k + HALF_ROWS] = jnp.where(low, turn(rows[k], -EDGE, 1), rows[k + HALF_ROWS])
    copies = [
        pltpu.make_async_copy(strips.at[pl.ds(0, HALF_ROWS)], up_out, sent.at[1]),
        pltpu.make_async_copy(strips.at[pl.ds(HALF_ROWS, HALF_ROWS)], down_out, sent.at[2]),
    ]
    for copy in copies:
        copy.start()
    copy_own.wait()
    for copy in copies:
        copy.wait()


def stage_kernel(own, staged):
    copy_rows(staged, own)


def halo_kernel(own, from_below, from_above, far, near, strip):
    low = low_lanes()
    for k in range(HALF_ROWS):
        under, over = from_below[k], from_above[k]
        strip[k] = jnp.where(low, under, turn(over, EDGE, 1))
        strip[k + HALF_ROWS] = jnp.where(low, turn(under, -EDGE, 1), over)
    for side, rows, c in ((near, TO_NEAR, 1), (far, TO_FAR, 0)):
        level = {q: moved(own_value(own, strip, q, c), VELOCITY[q], 1) for q in LEVEL}
        sums = [level_sums({q: level[q][t] for q in LEVEL}) for t in range(2)]
        parts = []
        for (k, column), row in rows.items():
            if k >= FIELDS:
                side[row] = sums[0][k - FIELDS]
                parts.append(lambda slot, k=k: packed(sums[1][k - FIELDS], slot))
            else:
                place = own_row(k, column)
                side[row] = own[place]
                parts.append(
                    lambda slot, place=place: turn(
                        strip[place // SLOTS], 2 * EDGE * (slot - place % SLOTS), 1
                    )
                )
        for k, row in enumerate(pack_rows(parts)):
            side[BULK_ROWS + k] = row


def level_of(p, column, sums):
    return sums(p) if 0 <= column <= 1 else [p[q] for q in LEVEL[:SUMS]]


def near_place(rows, k, column):
    return rows[mirrored(k) if k < MEMBERS else k, 3 - column]


def far_place(rows, k, column):
    return rows[mirrored(k) if k < MEMBERS else k, -1 - column]


def own_fed(q, column):
    return 0 <= column <= 1 and 0 <= column - VELOCITY[q][0] <= 1


def state_of(own_state, state, first, column, z, y):
    return [
        own_state[q, column, z, y] if own_fed(q, column) else state[q, column - first, z, y]
        for q in range(MEMBERS)
    ]


def first_state(wide, column, state, sides, i):
    put(sides, 0, i, moved(wide(MOBILITY, column), STILL, 1))
    put(sides, 1, i, moved(wide(RATE, column), STILL, 1))
    for q in range(MEMBERS):
        if own_fed(q, column):
            continue
        if 0 <= column <= 1 or q not in LEVEL:
            put(state, q, i, moved(wide(q, column - VELOCITY[q][0]), VELOCITY[q], 1))
        elif q in LEVEL[:SUMS]:
            put(state, q, i, moved(wide(SUM_FIELDS[LEVEL.index(q)], column), STILL, 1))


def first_collision(column, own_state, state, sides, after, first):
    i = column - first
    wanted = [q for q in range(MEMBERS) if 0 <= column + VELOCITY[q][0] <= 1]
    for z, y in tiles(WIDE):
        p = state_of(own_state, state, first, column, z, y)
        level = level_of(p, column, level_sums)
        result = collide(p, level, sides[0, i, z, y], sides[1, i, z, y], wanted)
        for q in wanted:
            after[q, i, z, y] = result[q]


def seeds(wide, column, seed):
    weights = [wide(WEIGHT + k, column) for k in range(3)]
    weights = [(main, turn(extra, by, 1)) for main, extra, by in weights]
    if not 0 <= column <= 1:
        weights[0] = tuple(-value for value in weights[0])
    for q in range(1, MEMBERS):
        velocity = VELOCITY[q]
        c = column - velocity[0]
        if not 0 <= c <= 1:
            continue
        if q < 19:
            parts = [
                tuple(value if velocity[k] > 0 else -value for value in weights[k]) for k in range(3) if velocity[k]
            ]
            pair = parts[0] if len(parts) == 1 else tuple(a + b for a, b in zip(*parts))
            pair += (0,)
        else:
            pair = wide(WEIGHT + 3, column)
        put(seed, q, c, moved(pair, velocity, -1))


def own_step_kernel(flow, heat, own, strip, own_state, own_seed, begin):
    def wide(k, column):
        return own_value(own, strip, k, column)

    for column in (0, 1):
        for q in range(MEMBERS):
            if own_fed(q, column):
                put(own_state, q, column, moved(wide(q, column - VELOCITY[q][0]), VELOCITY[q], 1))
        seeds(wide, column, own_seed)
    odd = second_core()
    for c in range(2):
        for z in halves():
            terms = begin_terms(
                given_state(flow, heat, odd, c, z), own[own_row(MOBILITY, c), z, :], own[own_row(RATE, c), z, :]
            )
            for k, value in enumerate(terms):
                begin[k, c, z, :] = value


def step_kernel(
    own, strip, own_state, own_seed, from_far, from_near,
    far_state, far_sides, near_state, near_sides, adjoint, by_resistance, by_conductivity, far, near,
    after, near_after, later, halo_seed,
):
    def wide(k, column):
        if column < 0:
            return halo_value(from_far, BULK_ROWS, far_place(TO_FAR, k, column))
        if column > 1:
            return halo_value(from_near, BULK_ROWS, near_place(TO_NEAR, k, column))
        return own_value(own, strip, k, column)

    for column in (-1, 0):
        first_state(wide, column, far_state, far_sides, column + 1)
        first_collision(column, own_state, far_state, far_sides, after, -1)
    for column in (1, 2):
        first_state(wide, column, near_state, near_sides, column - 1)
        first_collision(column, own_state, near_state, near_sides, near_after, 1)
    for column in (-1, 2):
        seeds(wide, column, halo_seed)
    for c in range(2):
        for q in range(MEMBERS):
            column = c - VELOCITY[q][0]
            source = near_after[q, column - 1] if column >= 1 else after[q, column + 1]
            put(later, q, c, moved(split(source), VELOCITY[q], 1))
    for c in range(2):
        for z, y in tiles(WIDE):
            p = [later[q, c, z, y] for q in range(MEMBERS)]
            pa = [jnp.zeros((8, LANES), jnp.float32)]
            pa += [
                (own_seed if 0 <= c + VELOCITY[q][0] <= 1 else halo_seed)[q, c, z, y] for q in range(1, MEMBERS)
            ]
            inner = y.start == 0
            mobility, rate = [near_sides[k, 0, z, y] if c else far_sides[k, 1, z, y] for k in range(2)]
            result = pull_back(
                p, level_sums(p), pa, level_adjoint_sums(pa), mobility, rate, range(MEMBERS), inner
            )
            if inner:
                by_resistance[c, z, :], by_conductivity[c, z, :] = result["by"]
            for q in range(MEMBERS):
                adjoint[q, c, z, y] = result[q]
    for side, rows, c in ((near, ADJ_TO_NEAR, 1), (far, ADJ_TO_FAR, 0)):
        level = {q: moved(split(adjoint[q, c]), VELOCITY[q], -1) for q in LEVEL}
        sums = [level_adjoint_sums({q: level[q][t] for q in LEVEL}) for t in range(2)]
        parts = []
        for (k, column), row in rows.items():
            if k >= FIELDS:
                side[row] = sums[0][k - FIELDS]
                parts.append(lambda slot, k=k: packed(sums[1][k - FIELDS], slot))
            else:
                side[row] = adjoint[k, column, :, :LANES]
                parts.append(lambda slot, k=k, column=column: packed(adjoint[k, column, :, LANES:], slot))
        for k, row in enumerate(pack_rows(parts)):
            side[ADJ_BULK + k] = row


def adjoint_step(wide, column, own_state, state, sides, arrived, earlier, first, keep):
    own = 0 <= column <= 1
    i = column - first
    for q in range(MEMBERS):
        if own or q not in LEVEL:
            put(arrived, q, i, moved(wide(q, column + VELOCITY[q][0]), VELOCITY[q], -1))
        elif q in LEVEL[:SUMS]:
            put(arrived, q, i, moved(wide(SUM_FIELDS[LEVEL.index(q)], column), STILL, 1))
    for z, y in tiles(WIDE):
        inner = y.start == 0
        wanted = [
            q for q in range(MEMBERS) if 0 <= column - VELOCITY[q][0] <= 1 and (inner or VELOCITY[q][1])
        ]
        p = state_of(own_state, state, first, column, z, y)
        pa = [arrived[q, i, z, y] for q in range(MEMBERS)]
        result = pull_back(
            p, level_of(p, column, level_sums), pa, level_of(pa, column, level_adjoint_sums),
            sides[0, i, z, y], sides[1, i, z, y], wanted, inner and own,
        )
        for q in wanted:
            earlier[q, i, z, y] = result[q]
        if inner and own:
            keep(z, *result["by"])


def far_adjoint_kernel(
    own_state, state, sides, adjoint, part_resistance, part_conductivity, from_far,
    earlier, by_resistance, by_conductivity,
    arrived,
):
    def wide(k, column):
        if column < 0:
            return halo_value(from_far, ADJ_BULK, far_place(ADJ_TO_FAR, k, column))
        return split(adjoint[k, column])

    def keep(z, resistance, conductivity):
        by_resistance[0, z, :] = part_resistance[0, z, :] + resistance
        by_conductivity[0, z, :] = part_conductivity[0, z, :] + conductivity

    for column in (-1, 0):
        adjoint_step(wide, column, own_state, state, sides, arrived, earlier, -1, keep)
    by_resistance[1] = part_resistance[1]
    by_conductivity[1] = part_conductivity[1]


def near_adjoint_kernel(
    begin, own_state, state, sides, far_sides, adjoint, far_earlier, part_resistance, part_conductivity, from_near,
    by_resistance, by_conductivity,
    arrived, earlier, last, sums,
):
    def wide(k, column):
        if column > 1:
            return halo_value(from_near, ADJ_BULK, near_place(ADJ_TO_NEAR, k, column))
        return split(adjoint[k, column])

    def keep(z, resistance, conductivity):
        sums[0, z, :] = part_resistance[1, z, :] + resistance
        sums[1, z, :] = part_conductivity[1, z, :] + conductivity

    for column in (1, 2):
        adjoint_step(wide, column, own_state, state, sides, arrived, earlier, 1, keep)
    for c in range(2):
        for q in range(MEMBERS):
            velocity = VELOCITY[q]
            column = c + velocity[0]
            source, i = (earlier, column - 1) if column >= 1 else (far_earlier, column + 1)
            if velocity[1]:
                last[q, c] = moved(split(source[q, i]), velocity, -1)[0]
            else:
                last[q, c] = turn(source[q, i, :, :LANES], -velocity[2], 0)
    narrow = pl.ds(0, LANES)
    odd = second_core()
    for c in range(2):
        i = c + odd * (1 - 2 * c)
        for z in halves():
            pa = [last[q, c, z, :] for q in range(MEMBERS)]
            mobility, rate = [(sides[k, 0, z, narrow] if c else far_sides[k, 1, z, narrow]) for k in range(2)]
            terms = [begin[k, c, z, :] for k in range(BEGIN)]
            resistance, conductivity = end_terms(terms, pa, mobility, rate)
            by_resistance[i, z, :] = resistance + (sums[0, z, :] if c else part_resistance[0, z, :])
            by_conductivity[i, z, :] = conductivity + (sums[1, z, :] if c else part_conductivity[0, z, :])


def floats(*shape):
    return jax.ShapeDtypeStruct(shape, jnp.float32)


def vmem(*shape):
    return pltpu.VMEM(shape, jnp.float32)


def swap_along_x(far, near):
    count = lax.axis_size("gx")
    across = [(i, (i + (1 if i % 2 else -1)) % count) for i in range(count)]
    within = [(i, i ^ 1) for i in range(count)]
    return lax.ppermute(far, "gx", across), lax.ppermute(near, "gx", within)


FIRST_PARAMS = pltpu.CompilerParams(vmem_limit_bytes=56 * 1024 * 1024)
PARAMS = pltpu.CompilerParams(vmem_limit_bytes=24 * 1024 * 1024)


def on_device(flow, heat, flow_weight, heat_weight, resistance, conductivity, solid):
    in_hbm = pl.BlockSpec(memory_space=pltpu.HBM)
    own, up, down = pl.pallas_call(
        first_kernel,
        in_specs=[in_hbm] * 7,
        out_specs=[in_hbm] * 3,
        out_shape=(
            floats(2 * FIELDS, ZED, LANES),
            floats(HALF_ROWS, ZED, LANES),
            floats(HALF_ROWS, ZED, LANES),
        ),
        scratch_shapes=[
            vmem(2 * FIELDS, ZED, LANES),
            vmem(STRIP_ROWS, ZED, LANES),
            vmem(19, 2, ZED, LANES),
            vmem(7, 2, ZED, LANES),
            vmem(3, 2, ZED, LANES),
            vmem(2, ZED, LANES),
            vmem(2, ZED, LANES),
            vmem(2, ZED, LANES),
            pltpu.VMEM((2, ZED, LANES), jnp.int32),
            pltpu.SemaphoreType.DMA((7,)),
            pltpu.SemaphoreType.DMA((3,)),
        ],
        compiler_params=FIRST_PARAMS,
        name="collide_own",
    )(flow, heat, flow_weight, heat_weight, resistance, conductivity, solid)

    count = lax.axis_size("gy")
    upward = [(i, (i + 1) % count) for i in range(count)]
    from_below = lax.ppermute(up, "gy", upward)
    from_above = lax.ppermute(down, "gy", [(target, source) for source, target in upward])

    own = pl.pallas_call(
        stage_kernel,
        out_shape=floats(2 * FIELDS, ZED, LANES),
        compiler_params=PARAMS,
        cost_estimate=pl.CostEstimate(flops=10**7, bytes_accessed=10**6, transcendentals=0),
        name="stage_own",
    )(own)

    far, near, strip = pl.pallas_call(
        halo_kernel,
        out_shape=(floats(SENT, ZED, LANES), floats(SENT, ZED, LANES), floats(STRIP_ROWS, ZED, LANES)),
        compiler_params=PARAMS,
        name="halo_buffers",
    )(own, from_below, from_above)

    from_far, from_near = swap_along_x(far, near)

    columns = floats(MEMBERS, 2, ZED, WIDE)
    side_columns = floats(2, 2, ZED, WIDE)
    cells = floats(2, ZED, LANES)
    held = vmem(MEMBERS, 2, ZED, WIDE)
    busy = pl.CostEstimate(flops=10**7, bytes_accessed=10**6, transcendentals=0)

    own_state, own_seed, begin = pl.pallas_call(
        own_step_kernel,
        out_shape=(columns, columns, floats(BEGIN, 2, ZED, LANES)),
        compiler_params=PARAMS,
        cost_estimate=busy,
        name="own_step",
    )(flow, heat, own, strip)

    far_state, far_sides, near_state, near_sides, adjoint, part_resistance, part_conductivity, far, near = (
        pl.pallas_call(
            step_kernel,
            out_shape=(
                columns, side_columns, columns, side_columns, columns, cells, cells,
                floats(ADJ_SENT, ZED, LANES), floats(ADJ_SENT, ZED, LANES),
            ),
            scratch_shapes=[held, held, held, held],
            compiler_params=PARAMS,
            name="two_steps",
        )(own, strip, own_state, own_seed, from_far, from_near)
    )

    from_far, from_near = swap_along_x(far, near)

    far_earlier, part_resistance, part_conductivity = pl.pallas_call(
        far_adjoint_kernel,
        out_shape=(columns, cells, cells),
        scratch_shapes=[held],
        compiler_params=PARAMS,
        cost_estimate=busy,
        name="far_adjoint",
    )(own_state, far_state, far_sides, adjoint, part_resistance, part_conductivity, from_far)

    return pl.pallas_call(
        near_adjoint_kernel,
        out_shape=(cells, cells),
        scratch_shapes=[held, held, vmem(MEMBERS, 2, ZED, LANES), vmem(2, ZED, LANES)],
        compiler_params=PARAMS,
        name="near_adjoint",
    )(
        begin, own_state, near_state, near_sides, far_sides, adjoint, far_earlier,
        part_resistance, part_conductivity, from_near,
    )


def solution(mesh):
    split = P("gx", None, "gy")
    stacked = P(None, "gx", None, "gy")
    return jax.shard_map(
        on_device,
        mesh=mesh,
        in_specs=(stacked, stacked, stacked, split, split, split, split),
        out_specs=(split, split),
        check_vma=False,
    )
```

```python
import jax
import jax.numpy as jnp
from jax import lax
from jax.experimental import pallas as pl
from jax.experimental.pallas import tpu as pltpu
from jax.sharding import PartitionSpec as P

ZED = 16
LANES = 128
WIDE = 2 * LANES
EDGE = 4

FLOW_VELOCITY = [
    (0, 0, 0),
    (1, 0, 0),
    (-1, 0, 0),
    (0, 1, 0),
    (0, -1, 0),
    (0, 0, 1),
    (0, 0, -1),
    (1, 1, 0),
    (-1, -1, 0),
    (1, -1, 0),
    (-1, 1, 0),
    (1, 0, 1),
    (-1, 0, -1),
    (1, 0, -1),
    (-1, 0, 1),
    (0, 1, 1),
    (0, -1, -1),
    (0, 1, -1),
    (0, -1, 1),
]
VELOCITY = FLOW_VELOCITY + FLOW_VELOCITY[:7]
STILL = (0, 0, 0)
MEMBERS = len(VELOCITY)
RIGHTWARD = [q for q in range(MEMBERS) if VELOCITY[q][0] == 1]
LEFTWARD = [q for q in range(MEMBERS) if VELOCITY[q][0] == -1]
LEVEL = [q for q in range(MEMBERS) if VELOCITY[q][0] == 0]


def mirrored(q):
    x, y, z = VELOCITY[q]
    start = 0 if q < 19 else 19
    return start + FLOW_VELOCITY.index((-x, y, z))


MOBILITY, RATE, WEIGHT = MEMBERS, MEMBERS + 1, MEMBERS + 2
FIELDS = MEMBERS + 6
SIDE_FIELDS = list(range(MEMBERS, FIELDS))

SUMS = 9
SUM_FIELDS = [FIELDS + k for k in range(SUMS)]

SLOTS = LANES // (2 * EDGE)
STRIP_ROWS = 2 * FIELDS // SLOTS
HALF_ROWS = STRIP_ROWS // 2


def rows_of(entries):
    return {entry: row for row, entry in enumerate(entries)}


TO_NEAR = rows_of([(q, 0) for q in RIGHTWARD] + [(k, 1) for k in RIGHTWARD + SIDE_FIELDS + SUM_FIELDS])
TO_FAR = rows_of([(q, 1) for q in LEFTWARD] + [(k, 0) for k in LEFTWARD + SIDE_FIELDS + SUM_FIELDS])
ADJ_TO_NEAR = rows_of([(q, 0) for q in LEFTWARD] + [(k, 1) for k in LEFTWARD + SUM_FIELDS])
ADJ_TO_FAR = rows_of([(q, 1) for q in RIGHTWARD] + [(k, 0) for k in RIGHTWARD + SUM_FIELDS])
BULK_ROWS, ADJ_BULK = len(TO_NEAR), len(ADJ_TO_NEAR)


def with_strips(bulk):
    return bulk + -(-bulk // SLOTS)


SENT, ADJ_SENT = with_strips(BULK_ROWS), with_strips(ADJ_BULK)


def level_sums(p):
    s1, s2, d1, d2 = p[3] + p[4], p[5] + p[6], p[3] - p[4], p[5] - p[6]
    s7, s8, d7, d8 = p[15] + p[16], p[17] + p[18], p[15] - p[16], p[17] - p[18]
    yz = s7 + s8
    mass = p[0] + (s1 + s2) + yz
    return [
        mass, d1 + (d7 + d8), d2 + (d7 - d8), s1 + yz, s2 + yz, s7 - s8,
        p[19] + (p[22] + p[23]) + (p[24] + p[25]), p[22] - p[23], p[24] - p[25],
    ]


def level_adjoint_sums(p):
    s1, s2, d1, d2 = p[3] + p[4], p[5] + p[6], p[3] - p[4], p[5] - p[6]
    s7, s8, d7, d8 = p[15] + p[16], p[17] + p[18], p[15] - p[16], p[17] - p[18]
    yz = s7 + s8
    t1, t2 = s1 + s1, s2 + s2
    mass = 12.0 * p[0] + (t1 + t2) + yz
    return [
        mass, (d1 + d1) + (d7 + d8), (d2 + d2) + (d7 - d8), t1 + yz, t2 + yz, s7 - s8,
        0.35 * p[19] + 0.175 * ((p[22] + p[23]) + (p[24] + p[25])),
        0.125 * (p[22] - p[23]), 0.125 * (p[24] - p[25]),
    ]


def cross_sums(p):
    pairs = [(1, 2), (7, 8), (9, 10), (11, 12), (13, 14)]
    return [p[a] + p[b] for a, b in pairs], [p[a] - p[b] for a, b in pairs]


def common(p, level, mobility):
    s, d = cross_sums(p)
    xy, xz = s[1] + s[2], s[3] + s[4]
    along = s[0] + xy + xz
    rho = level[0] + along
    j = (d[0] + (d[1] + d[2]) + (d[3] + d[4]), level[1] + (d[1] - d[2]), level[2] + (d[3] - d[4]))
    temperature = level[6] + (p[20] + p[21])
    flux = (p[20] - p[21], level[7], level[8])
    u = tuple(mobility * jk for jk in j)
    square = (u[0] * u[0], u[1] * u[1], u[2] * u[2])
    third = rho * (1.0 / 3.0)
    stress = (
        along - third - square[0],
        (level[3] + xy) - third - square[1],
        (level[4] + xz) - third - square[2],
        (s[1] - s[2]) - u[0] * u[1],
        (s[3] - s[4]) - u[0] * u[2],
        level[5] - u[1] * u[2],
    )
    decay = jnp.exp(-2.0 * (temperature - 1.0))
    omega = 1.0 / (0.5 + 0.3 * decay)
    return rho, j, u, square, stress, temperature, flux, decay, omega


def collide(p, level, mobility, rate, wanted):
    rho, _, u, square, stress, temperature, flux, _, omega = common(p, level, mobility)
    solid = mobility == 0.0
    lam = 1.2 - omega
    trace = stress[0] + stress[1] + stress[2]
    base = 1.2 * rho - 1.8 * (square[0] + square[1] + square[2]) - (1.5 * lam) * trace
    scale = 4.5 * lam
    mxx = 5.4 * square[0] + scale * stress[0]
    myy = 5.4 * square[1] + scale * stress[1]
    mzz = 5.4 * square[2] + scale * stress[2]
    mxy = 2.0 * (5.4 * (u[0] * u[1]) + scale * stress[3])
    mxz = 2.0 * (5.4 * (u[0] * u[2]) + scale * stress[4])
    myz = 2.0 * (5.4 * (u[1] * u[2]) + scale * stress[5])
    bx, by, bz = base + mxx, base + myy, base + mzz
    sxy, sxz, syz = bx + myy, bx + mzz, by + mzz
    even = [bx, by, bz, sxy + mxy, sxy - mxy, sxz + mxz, sxz - mxz, syz + myz, syz - myz]
    odd = [u[0], u[1], u[2], u[0] + u[1], u[0] - u[1], u[0] + u[2], u[0] - u[2], u[1] + u[2], u[1] - u[2]]
    result = {}
    if 0 in wanted:
        result[0] = jnp.where(solid, p[0], (1.0 / 3.0) * base - 0.2 * p[0])
    for k in range(9):
        a, b = 2 * k + 1, 2 * k + 2
        w = 1.0 / 18.0 if k < 3 else 1.0 / 36.0
        e, o = w * even[k], (3.6 * w) * odd[k]
        if a in wanted:
            result[a] = jnp.where(solid, p[b], (e + o) - 0.2 * p[a])
        if b in wanted:
            result[b] = jnp.where(solid, p[a], (e - o) - 0.2 * p[b])
    keep = 0.5 * (1.4 - rate)
    push = (0.5 * rate) * temperature
    warm = 0.175 * temperature
    if 19 in wanted:
        result[19] = 0.35 * temperature - 0.4 * p[19]
    for k in range(3):
        along = keep * flux[k] + push * u[k]
        a, b = 20 + 2 * k, 21 + 2 * k
        if a in wanted:
            result[a] = (warm + along) - 0.4 * p[a]
        if b in wanted:
            result[b] = (warm - along) - 0.4 * p[b]
    return result


def state_terms(p, level, mobility, rate, full):
    _, _, u, _, stress, temperature, flux, decay, omega = common(p, level, mobility)
    slope = jnp.where(mobility == 0.0, 0.0, (0.6 * decay) * (omega * omega))
    terms = list(u) + list(stress) + [1.2 - omega, (4.0 * rate) * temperature, slope]
    return terms + [temperature * u[k] - flux[k] for k in range(3)] if full else terms


def pull_back(terms, pa, adjoint_level, mobility, rate, wanted, sensitivity):
    u, stress, lam, push, slope, bent = terms[:3], terms[3:9], terms[9], terms[10], terms[11], terms[12:]
    solid = mobility == 0.0
    s, d = cross_sums(pa)
    w = 1.0 / 36.0
    xy, xz = s[1] + s[2], s[3] + s[4]
    along = (s[0] + s[0]) + xy + xz
    mass = w * (adjoint_level[0] + along)
    px = w * ((d[0] + d[0]) + (d[1] + d[2]) + (d[3] + d[4]))
    py = w * (adjoint_level[1] + (d[1] - d[2]))
    pz = w * (adjoint_level[2] + (d[3] - d[4]))
    rxx, ryy, rzz = w * along, w * (adjoint_level[3] + xy), w * (adjoint_level[4] + xz)
    rxy, rxz, ryz = w * (s[1] - s[2]), w * (s[3] - s[4]), w * adjoint_level[5]
    shift = 1.5 * mass
    dxx, dyy, dzz = 4.5 * rxx - shift, 4.5 * ryy - shift, 4.5 * rzz - shift
    dxy, dxz, dyz = 4.5 * rxy, 4.5 * rxz, 4.5 * ryz
    mix = 2.4 - 2.0 * lam
    b = ((pa[20] - pa[21]) * 0.125, adjoint_level[7], adjoint_level[8])
    ux = 3.6 * px + mix * (dxx * u[0] + dxy * u[1] + dxz * u[2]) + push * b[0]
    uy = 3.6 * py + mix * (dxy * u[0] + dyy * u[1] + dyz * u[2]) + push * b[1]
    uz = 3.6 * pz + mix * (dxz * u[0] + dyz * u[1] + dzz * u[2]) + push * b[2]
    result = {}
    if wanted:
        lam_bar = (
            dxx * stress[0]
            + dyy * stress[1]
            + dzz * stress[2]
            + 2.0 * (dxy * stress[3] + dxz * stress[4] + dyz * stress[5])
        )
        rho_bar = 1.2 * mass - (1.5 * lam) * ((rxx + ryy + rzz) - mass)
        jx, jy, jz = mobility * ux, mobility * uy, mobility * uz
        ex, ey, ez = lam * dxx, lam * dyy, lam * dzz
        exy, exz, eyz = (2.0 * lam) * dxy, (2.0 * lam) * dxz, (2.0 * lam) * dyz
        hx, hy, hz = rho_bar + ex, rho_bar + ey, rho_bar + ez
        gxy, gxz, gyz = hx + ey, hx + ez, hy + ez
        even = [hx, hy, hz, gxy + exy, gxy - exy, gxz + exz, gxz - exz, gyz + eyz, gyz - eyz]
        odd = [jx, jy, jz, jx + jy, jx - jy, jx + jz, jx - jz, jy + jz, jy - jz]
        if 0 in wanted:
            result[0] = jnp.where(solid, pa[0], rho_bar - 0.2 * pa[0])
        for k in range(9):
            a, m = 2 * k + 1, 2 * k + 2
            if a in wanted:
                result[a] = jnp.where(solid, pa[m], (even[k] + odd[k]) - 0.2 * pa[a])
            if m in wanted:
                result[m] = jnp.where(solid, pa[a], (even[k] - odd[k]) - 0.2 * pa[m])
        warm = (
            adjoint_level[6]
            + 0.175 * (pa[20] + pa[21])
            + (4.0 * rate) * (b[0] * u[0] + b[1] * u[1] + b[2] * u[2])
            - lam_bar * slope
        )
        keep = 5.6 - 4.0 * rate
        if 19 in wanted:
            result[19] = warm - 0.4 * pa[19]
        for k in range(3):
            along = keep * b[k]
            a, m = 20 + 2 * k, 21 + 2 * k
            if a in wanted:
                result[a] = (warm + along) - 0.4 * pa[a]
            if m in wanted:
                result[m] = (warm - along) - 0.4 * pa[m]
    if sensitivity:
        by_resistance = -mobility * (ux * u[0] + uy * u[1] + uz * u[2])
        by_conductivity = (-1.6 * (rate * rate)) * (b[0] * bent[0] + b[1] * bent[1] + b[2] * bent[2])
        result["by"] = (by_resistance, by_conductivity)
    return result


BEGIN = 8


def begin_terms(p, mobility, rate):
    _, _, u, _, _, temperature, flux, _, omega = common(p, level_sums(p), mobility)
    bent = [temperature * u[k] - flux[k] for k in range(3)]
    return list(u) + bent + [2.4 - 2.0 * (1.2 - omega), (4.0 * rate) * temperature]


def end_terms(terms, pa, mobility, rate):
    u, bent, mix, push = terms[:3], terms[3:6], terms[6], terms[7]
    level = level_adjoint_sums(pa)
    s, d = cross_sums(pa)
    w = 1.0 / 36.0
    xy, xz = s[1] + s[2], s[3] + s[4]
    along = (s[0] + s[0]) + xy + xz
    shift = (1.5 * w) * (level[0] + along)
    v = 4.5 * w
    dxx, dyy, dzz = v * along - shift, v * (level[3] + xy) - shift, v * (level[4] + xz) - shift
    dxy, dxz, dyz = v * (s[1] - s[2]), v * (s[3] - s[4]), v * level[5]
    px = (d[0] + d[0]) + (d[1] + d[2]) + (d[3] + d[4])
    py = level[1] + (d[1] - d[2])
    pz = level[2] + (d[3] - d[4])
    b = ((pa[20] - pa[21]) * 0.125, level[7], level[8])
    ux = (3.6 * w) * px + mix * (dxx * u[0] + dxy * u[1] + dxz * u[2]) + push * b[0]
    uy = (3.6 * w) * py + mix * (dxy * u[0] + dyy * u[1] + dyz * u[2]) + push * b[1]
    uz = (3.6 * w) * pz + mix * (dxz * u[0] + dyz * u[1] + dzz * u[2]) + push * b[2]
    by_resistance = -mobility * (ux * u[0] + uy * u[1] + uz * u[2])
    by_conductivity = (-1.6 * (rate * rate)) * (b[0] * bent[0] + b[1] * bent[1] + b[2] * bent[2])
    return by_resistance, by_conductivity


def turn(value, by, axis):
    count = value.shape[axis]
    by %= count
    return pltpu.roll(value, by, axis) if by else value


def side_by_side(parts):
    lane = lax.broadcasted_iota(jnp.int32, (ZED, LANES), 1)
    row = None
    for slot, part in enumerate(parts):
        row = part if row is None else jnp.where(lane >= 2 * EDGE * slot, part, row)
    return row


def packed(value, slot):
    return turn(value, 2 * EDGE * slot + EDGE, 1)


def pack_rows(parts):
    return [
        side_by_side([part(slot) for slot, part in enumerate(parts[start : start + SLOTS])])
        for start in range(0, len(parts), SLOTS)
    ]


def halves():
    return [pl.ds(0, 8), pl.ds(8, 8)]


def low_lanes():
    return lax.broadcasted_iota(jnp.int32, (ZED, LANES), 1) % (2 * EDGE) < EDGE


def second_core():
    return lax.rem(lax.axis_index("gx"), 2)


def framed(q, odd):
    return q + odd * (mirrored(q) - q)


def copy_rows(target, source):
    for row in range(source.shape[0]):
        target[row] = source[row]


def split(value):
    return value[:, :LANES], value[:, LANES:], 0


def beside(row, slot):
    return row, -EDGE - 2 * EDGE * slot


def moved(triple, velocity, way):
    main, extra, by = triple
    _, step_y, step_z = velocity
    step = way * step_y
    main, extra = turn(main, way * step_z, 0), turn(extra, way * step_z, 0)
    if not step:
        return main, turn(extra, by, 1)
    main, extra = turn(main, step, 1), turn(extra, by + step, 1)
    lane = lax.broadcasted_iota(jnp.int32, (ZED, LANES), 1)
    edge = lane == (0 if step == 1 else LANES - 1)
    return jnp.where(edge, extra, main), jnp.where(edge, main, extra)


def put(ref, q, i, pair):
    ref[q, i, :, :LANES], ref[q, i, :, LANES:] = pair


def tiles(lanes):
    return [(z, pl.ds(t, LANES)) for z in halves() for t in range(0, lanes, LANES)]


def own_row(k, c):
    return c * FIELDS + k


def own_value(own, strip, k, c):
    place = own_row(k, c)
    return (own[place],) + beside(strip[place // SLOTS], place % SLOTS)


def halo_value(buffer, bulk, place):
    return (buffer[place],) + beside(buffer[bulk + place // SLOTS], place % SLOTS)


def given_state(flow, heat, odd, c, z):
    i = c + odd * (1 - 2 * c)
    return [flow[framed(q, odd), i, z, :] for q in range(19)] + [
        heat[framed(q, odd) - 19, i, z, :] for q in range(19, MEMBERS)
    ]


def first_kernel(
    flow_in, heat_in, flow_weight_in, heat_weight_in, resistance_in, conductivity_in, solid_in,
    own_out, up_out, down_out,
    own, strips, flow, heat, flow_weight, heat_weight, resistance, conductivity, solid, arrived, sent,
):
    pairs = [
        (flow_in, flow),
        (heat_in, heat),
        (resistance_in, resistance),
        (conductivity_in, conductivity),
        (solid_in, solid),
        (flow_weight_in, flow_weight),
        (heat_weight_in, heat_weight),
    ]
    copies = [pltpu.make_async_copy(a, b, arrived.at[k]) for k, (a, b) in enumerate(pairs)]
    for copy in copies:
        copy.start()
    for copy in copies:
        copy.wait()
    odd = second_core()
    sign = (1 - 2 * odd).astype(jnp.float32)
    for c in range(2):
        i = c + odd * (1 - 2 * c)
        for z in halves():
            mobility = jnp.where(solid[i, z, :] != 0, 0.0, 1.0 / (1.0 + resistance[i, z, :]))
            rate = 1.0 / (0.5 + 0.4 * conductivity[i, z, :])
            p = given_state(flow, heat, odd, c, z)
            after = collide(p, level_sums(p), mobility, rate, range(MEMBERS))
            more = [mobility, rate, sign * flow_weight[0, i, z, :]]
            more += [flow_weight[1, i, z, :], flow_weight[2, i, z, :], heat_weight[i, z, :]]
            for k, value in enumerate([after[q] for q in range(MEMBERS)] + more):
                own[own_row(k, c), z, :] = value
    copy_own = pltpu.make_async_copy(own, own_out, sent.at[0])
    copy_own.start()
    rows = pack_rows([lambda slot, k=k: packed(own[k], slot) for k in range(2 * FIELDS)])
    low = low_lanes()
    for k in range(HALF_ROWS):
        strips[k] = jnp.where(low, rows[k], turn(rows[k + HALF_ROWS], EDGE, 1))
        strips[k + HALF_ROWS] = jnp.where(low, turn(rows[k], -EDGE, 1), rows[k + HALF_ROWS])
    copies = [
        pltpu.make_async_copy(strips.at[pl.ds(0, HALF_ROWS)], up_out, sent.at[1]),
        pltpu.make_async_copy(strips.at[pl.ds(HALF_ROWS, HALF_ROWS)], down_out, sent.at[2]),
    ]
    for copy in copies:
        copy.start()
    copy_own.wait()
    for copy in copies:
        copy.wait()


def stage_kernel(own, staged):
    copy_rows(staged, own)


def halo_kernel(own, from_below, from_above, far, near, strip):
    low = low_lanes()
    for k in range(HALF_ROWS):
        under, over = from_below[k], from_above[k]
        strip[k] = jnp.where(low, under, turn(over, EDGE, 1))
        strip[k + HALF_ROWS] = jnp.where(low, turn(under, -EDGE, 1), over)
    for side, rows, c in ((near, TO_NEAR, 1), (far, TO_FAR, 0)):
        level = {q: moved(own_value(own, strip, q, c), VELOCITY[q], 1) for q in LEVEL}
        sums = [level_sums({q: level[q][t] for q in LEVEL}) for t in range(2)]
        parts = []
        for (k, column), row in rows.items():
            if k >= FIELDS:
                side[row] = sums[0][k - FIELDS]
                parts.append(lambda slot, k=k: packed(sums[1][k - FIELDS], slot))
            else:
                place = own_row(k, column)
                side[row] = own[place]
                parts.append(
                    lambda slot, place=place: turn(
                        strip[place // SLOTS], 2 * EDGE * (slot - place % SLOTS), 1
                    )
                )
        for k, row in enumerate(pack_rows(parts)):
            side[BULK_ROWS + k] = row


def level_of(p, column, sums):
    return sums(p) if 0 <= column <= 1 else [p[q] for q in LEVEL[:SUMS]]


def near_place(rows, k, column):
    return rows[mirrored(k) if k < MEMBERS else k, 3 - column]


def far_place(rows, k, column):
    return rows[mirrored(k) if k < MEMBERS else k, -1 - column]


def own_fed(q, column):
    return 0 <= column <= 1 and 0 <= column - VELOCITY[q][0] <= 1


def state_of(own_state, state, first, column, z, y):
    return [
        own_state[q, column, z, y] if own_fed(q, column) else state[q, column - first, z, y]
        for q in range(MEMBERS)
    ]


def first_state(wide, column, state, sides, i):
    put(sides, 0, i, moved(wide(MOBILITY, column), STILL, 1))
    put(sides, 1, i, moved(wide(RATE, column), STILL, 1))
    for q in range(MEMBERS):
        if own_fed(q, column):
            continue
        if 0 <= column <= 1 or q not in LEVEL:
            put(state, q, i, moved(wide(q, column - VELOCITY[q][0]), VELOCITY[q], 1))
        elif q in LEVEL[:SUMS]:
            put(state, q, i, moved(wide(SUM_FIELDS[LEVEL.index(q)], column), STILL, 1))


def first_collision(column, own_state, state, sides, after, first):
    i = column - first
    wanted = [q for q in range(MEMBERS) if 0 <= column + VELOCITY[q][0] <= 1]
    for z, y in tiles(WIDE):
        p = state_of(own_state, state, first, column, z, y)
        level = level_of(p, column, level_sums)
        result = collide(p, level, sides[0, i, z, y], sides[1, i, z, y], wanted)
        for q in wanted:
            after[q, i, z, y] = result[q]


def seeds(wide, column, seed):
    weights = [wide(WEIGHT + k, column) for k in range(3)]
    weights = [(main, turn(extra, by, 1)) for main, extra, by in weights]
    if not 0 <= column <= 1:
        weights[0] = tuple(-value for value in weights[0])
    for q in range(1, MEMBERS):
        velocity = VELOCITY[q]
        c = column - velocity[0]
        if not 0 <= c <= 1:
            continue
        if q < 19:
            parts = [
                tuple(value if velocity[k] > 0 else -value for value in weights[k]) for k in range(3) if velocity[k]
            ]
            pair = parts[0] if len(parts) == 1 else tuple(a + b for a, b in zip(*parts))
            pair += (0,)
        else:
            pair = wide(WEIGHT + 3, column)
        put(seed, q, c, moved(pair, velocity, -1))


def own_step_kernel(flow, heat, own, strip, own_state, own_seed, begin):
    def wide(k, column):
        return own_value(own, strip, k, column)

    for column in (0, 1):
        for q in range(MEMBERS):
            if own_fed(q, column):
                put(own_state, q, column, moved(wide(q, column - VELOCITY[q][0]), VELOCITY[q], 1))
        seeds(wide, column, own_seed)
    odd = second_core()
    for c in range(2):
        for z in halves():
            terms = begin_terms(
                given_state(flow, heat, odd, c, z), own[own_row(MOBILITY, c), z, :], own[own_row(RATE, c), z, :]
            )
            for k, value in enumerate(terms):
                begin[k, c, z, :] = value


def step_kernel(
    own, strip, own_state, own_seed, from_far, from_near,
    far_state, far_sides, near_state, near_sides, adjoint, by_resistance, by_conductivity, far, near,
    after, near_after, later, halo_seed,
):
    def wide(k, column):
        if column < 0:
            return halo_value(from_far, BULK_ROWS, far_place(TO_FAR, k, column))
        if column > 1:
            return halo_value(from_near, BULK_ROWS, near_place(TO_NEAR, k, column))
        return own_value(own, strip, k, column)

    for column in (-1, 0):
        first_state(wide, column, far_state, far_sides, column + 1)
        first_collision(column, own_state, far_state, far_sides, after, -1)
    for column in (1, 2):
        first_state(wide, column, near_state, near_sides, column - 1)
        first_collision(column, own_state, near_state, near_sides, near_after, 1)
    for column in (-1, 2):
        seeds(wide, column, halo_seed)
    for c in range(2):
        for q in range(MEMBERS):
            column = c - VELOCITY[q][0]
            source = near_after[q, column - 1] if column >= 1 else after[q, column + 1]
            put(later, q, c, moved(split(source), VELOCITY[q], 1))
    for c in range(2):
        for z, y in tiles(WIDE):
            p = [later[q, c, z, y] for q in range(MEMBERS)]
            pa = [jnp.zeros((8, LANES), jnp.float32)]
            pa += [
                (own_seed if 0 <= c + VELOCITY[q][0] <= 1 else halo_seed)[q, c, z, y] for q in range(1, MEMBERS)
            ]
            inner = y.start == 0
            mobility, rate = [near_sides[k, 0, z, y] if c else far_sides[k, 1, z, y] for k in range(2)]
            terms = state_terms(p, level_sums(p), mobility, rate, inner)
            result = pull_back(terms, pa, level_adjoint_sums(pa), mobility, rate, range(MEMBERS), inner)
            if inner:
                by_resistance[c, z, :], by_conductivity[c, z, :] = result["by"]
            for q in range(MEMBERS):
                adjoint[q, c, z, y] = result[q]
    for side, rows, c in ((near, ADJ_TO_NEAR, 1), (far, ADJ_TO_FAR, 0)):
        level = {q: moved(split(adjoint[q, c]), VELOCITY[q], -1) for q in LEVEL}
        sums = [level_adjoint_sums({q: level[q][t] for q in LEVEL}) for t in range(2)]
        parts = []
        for (k, column), row in rows.items():
            if k >= FIELDS:
                side[row] = sums[0][k - FIELDS]
                parts.append(lambda slot, k=k: packed(sums[1][k - FIELDS], slot))
            else:
                side[row] = adjoint[k, column, :, :LANES]
                parts.append(lambda slot, k=k, column=column: packed(adjoint[k, column, :, LANES:], slot))
        for k, row in enumerate(pack_rows(parts)):
            side[ADJ_BULK + k] = row


TERMS = 15


def prepare_kernel(
    own_state, far_state, far_sides, near_state, near_sides, adjoint,
    terms, own_arrived, own_sums,
):
    for column in range(-1, 3):
        first, state, sides = (1, near_state, near_sides) if column >= 1 else (-1, far_state, far_sides)
        for z, y in tiles(WIDE):
            p = state_of(own_state, state, first, column, z, y)
            mobility, rate = sides[0, column - first, z, y], sides[1, column - first, z, y]
            full = y.start == 0 and 0 <= column <= 1
            values = state_terms(p, level_of(p, column, level_sums), mobility, rate, full)
            for k, value in enumerate(values):
                terms[k, column + 1, z, y] = value
    for column in range(-1, 3):
        level = {}
        for q in range(MEMBERS):
            if 0 <= column + VELOCITY[q][0] <= 1:
                pair = moved(split(adjoint[q, column + VELOCITY[q][0]]), VELOCITY[q], -1)
                put(own_arrived, q, column + 1, pair)
                if q in LEVEL:
                    level[q] = pair
        if 0 <= column <= 1:
            sums = [level_adjoint_sums({q: level[q][t] for q in LEVEL}) for t in range(2)]
            for k in range(SUMS):
                put(own_sums, k, column, (sums[0][k], sums[1][k]))


def adjoint_step(halo, column, terms, own_arrived, own_sums, sides, arrived, earlier, first, keep):
    own = 0 <= column <= 1
    i = column - first
    for q in range(MEMBERS):
        if 0 <= column + VELOCITY[q][0] <= 1:
            continue
        if q not in LEVEL:
            put(arrived, q, i, moved(halo(q, column + VELOCITY[q][0]), VELOCITY[q], -1))
        elif q in LEVEL[:SUMS]:
            put(arrived, q, i, moved(halo(SUM_FIELDS[LEVEL.index(q)], column), STILL, 1))
    for z, y in tiles(WIDE):
        inner = y.start == 0
        wanted = [
            q for q in range(MEMBERS) if 0 <= column - VELOCITY[q][0] <= 1 and (inner or VELOCITY[q][1])
        ]
        pa = [
            own_arrived[q, column + 1, z, y] if 0 <= column + VELOCITY[q][0] <= 1 else arrived[q, i, z, y]
            for q in range(MEMBERS)
        ]
        if own:
            level = [own_sums[k, column, z, y] for k in range(SUMS)]
        else:
            level = [pa[q] for q in LEVEL[:SUMS]]
        held_terms = [terms[k, column + 1, z, y] for k in range(TERMS if inner and own else TERMS - 3)]
        result = pull_back(
            held_terms, pa, level, sides[0, i, z, y], sides[1, i, z, y], wanted, inner and own
        )
        for q in wanted:
            earlier[q, i, z, y] = result[q]
        if inner and own:
            keep(z, *result["by"])


def far_adjoint_kernel(
    terms, own_arrived, own_sums, sides, part_resistance, part_conductivity, from_far,
    earlier, by_resistance, by_conductivity,
    arrived,
):
    def halo(k, column):
        return halo_value(from_far, ADJ_BULK, far_place(ADJ_TO_FAR, k, column))

    def keep(z, resistance, conductivity):
        by_resistance[0, z, :] = part_resistance[0, z, :] + resistance
        by_conductivity[0, z, :] = part_conductivity[0, z, :] + conductivity

    for column in (-1, 0):
        adjoint_step(halo, column, terms, own_arrived, own_sums, sides, arrived, earlier, -1, keep)
    by_resistance[1] = part_resistance[1]
    by_conductivity[1] = part_conductivity[1]


def near_adjoint_kernel(
    begin, terms, own_arrived, own_sums, sides, far_sides, far_earlier,
    part_resistance, part_conductivity, from_near,
    by_resistance, by_conductivity,
    arrived, earlier, last, sums,
):
    def halo(k, column):
        return halo_value(from_near, ADJ_BULK, near_place(ADJ_TO_NEAR, k, column))

    def keep(z, resistance, conductivity):
        sums[0, z, :] = part_resistance[1, z, :] + resistance
        sums[1, z, :] = part_conductivity[1, z, :] + conductivity

    for column in (1, 2):
        adjoint_step(halo, column, terms, own_arrived, own_sums, sides, arrived, earlier, 1, keep)
    for c in range(2):
        for q in range(MEMBERS):
            velocity = VELOCITY[q]
            column = c + velocity[0]
            source, i = (earlier, column - 1) if column >= 1 else (far_earlier, column + 1)
            if velocity[1]:
                last[q, c] = moved(split(source[q, i]), velocity, -1)[0]
            else:
                last[q, c] = turn(source[q, i, :, :LANES], -velocity[2], 0)
    narrow = pl.ds(0, LANES)
    odd = second_core()
    for c in range(2):
        i = c + odd * (1 - 2 * c)
        for z in halves():
            pa = [last[q, c, z, :] for q in range(MEMBERS)]
            mobility, rate = [(sides[k, 0, z, narrow] if c else far_sides[k, 1, z, narrow]) for k in range(2)]
            terms = [begin[k, c, z, :] for k in range(BEGIN)]
            resistance, conductivity = end_terms(terms, pa, mobility, rate)
            by_resistance[i, z, :] = resistance + (sums[0, z, :] if c else part_resistance[0, z, :])
            by_conductivity[i, z, :] = conductivity + (sums[1, z, :] if c else part_conductivity[0, z, :])


def floats(*shape):
    return jax.ShapeDtypeStruct(shape, jnp.float32)


def vmem(*shape):
    return pltpu.VMEM(shape, jnp.float32)


def swap_along_x(far, near):
    count = lax.axis_size("gx")
    across = [(i, (i + (1 if i % 2 else -1)) % count) for i in range(count)]
    within = [(i, i ^ 1) for i in range(count)]
    return lax.ppermute(far, "gx", across), lax.ppermute(near, "gx", within)


FIRST_PARAMS = pltpu.CompilerParams(vmem_limit_bytes=56 * 1024 * 1024)
PARAMS = pltpu.CompilerParams(vmem_limit_bytes=24 * 1024 * 1024)


def on_device(flow, heat, flow_weight, heat_weight, resistance, conductivity, solid):
    in_hbm = pl.BlockSpec(memory_space=pltpu.HBM)
    own, up, down = pl.pallas_call(
        first_kernel,
        in_specs=[in_hbm] * 7,
        out_specs=[in_hbm] * 3,
        out_shape=(
            floats(2 * FIELDS, ZED, LANES),
            floats(HALF_ROWS, ZED, LANES),
            floats(HALF_ROWS, ZED, LANES),
        ),
        scratch_shapes=[
            vmem(2 * FIELDS, ZED, LANES),
            vmem(STRIP_ROWS, ZED, LANES),
            vmem(19, 2, ZED, LANES),
            vmem(7, 2, ZED, LANES),
            vmem(3, 2, ZED, LANES),
            vmem(2, ZED, LANES),
            vmem(2, ZED, LANES),
            vmem(2, ZED, LANES),
            pltpu.VMEM((2, ZED, LANES), jnp.int32),
            pltpu.SemaphoreType.DMA((7,)),
            pltpu.SemaphoreType.DMA((3,)),
        ],
        compiler_params=FIRST_PARAMS,
        name="collide_own",
    )(flow, heat, flow_weight, heat_weight, resistance, conductivity, solid)

    count = lax.axis_size("gy")
    upward = [(i, (i + 1) % count) for i in range(count)]
    from_below = lax.ppermute(up, "gy", upward)
    from_above = lax.ppermute(down, "gy", [(target, source) for source, target in upward])

    own = pl.pallas_call(
        stage_kernel,
        out_shape=floats(2 * FIELDS, ZED, LANES),
        compiler_params=PARAMS,
        cost_estimate=pl.CostEstimate(flops=10**7, bytes_accessed=10**6, transcendentals=0),
        name="stage_own",
    )(own)

    far, near, strip = pl.pallas_call(
        halo_kernel,
        out_shape=(floats(SENT, ZED, LANES), floats(SENT, ZED, LANES), floats(STRIP_ROWS, ZED, LANES)),
        compiler_params=PARAMS,
        name="halo_buffers",
    )(own, from_below, from_above)

    from_far, from_near = swap_along_x(far, near)

    columns = floats(MEMBERS, 2, ZED, WIDE)
    side_columns = floats(2, 2, ZED, WIDE)
    cells = floats(2, ZED, LANES)
    held = vmem(MEMBERS, 2, ZED, WIDE)
    busy = pl.CostEstimate(flops=10**7, bytes_accessed=10**6, transcendentals=0)

    own_state, own_seed, begin = pl.pallas_call(
        own_step_kernel,
        out_shape=(columns, columns, floats(BEGIN, 2, ZED, LANES)),
        compiler_params=PARAMS,
        cost_estimate=busy,
        name="own_step",
    )(flow, heat, own, strip)

    far_state, far_sides, near_state, near_sides, adjoint, part_resistance, part_conductivity, far, near = (
        pl.pallas_call(
            step_kernel,
            out_shape=(
                columns, side_columns, columns, side_columns, columns, cells, cells,
                floats(ADJ_SENT, ZED, LANES), floats(ADJ_SENT, ZED, LANES),
            ),
            scratch_shapes=[held, held, held, held],
            compiler_params=PARAMS,
            name="two_steps",
        )(own, strip, own_state, own_seed, from_far, from_near)
    )

    from_far, from_near = swap_along_x(far, near)

    terms, own_arrived, own_sums = pl.pallas_call(
        prepare_kernel,
        out_shape=(
            floats(TERMS, 4, ZED, WIDE), floats(MEMBERS, 4, ZED, WIDE), floats(SUMS, 2, ZED, WIDE),
        ),
        compiler_params=PARAMS,
        cost_estimate=busy,
        name="prepare",
    )(own_state, far_state, far_sides, near_state, near_sides, adjoint)

    far_earlier, part_resistance, part_conductivity = pl.pallas_call(
        far_adjoint_kernel,
        out_shape=(columns, cells, cells),
        scratch_shapes=[held],
        compiler_params=PARAMS,
        cost_estimate=busy,
        name="far_adjoint",
    )(terms, own_arrived, own_sums, far_sides, part_resistance, part_conductivity, from_far)

    return pl.pallas_call(
        near_adjoint_kernel,
        out_shape=(cells, cells),
        scratch_shapes=[held, held, vmem(MEMBERS, 2, ZED, LANES), vmem(2, ZED, LANES)],
        compiler_params=PARAMS,
        name="near_adjoint",
    )(
        begin, terms, own_arrived, own_sums, near_sides, far_sides, far_earlier,
        part_resistance, part_conductivity, from_near,
    )


def solution(mesh):
    split = P("gx", None, "gy")
    stacked = P(None, "gx", None, "gy")
    return jax.shard_map(
        on_device,
        mesh=mesh,
        in_specs=(stacked, stacked, stacked, split, split, split, split),
        out_specs=(split, split),
        check_vma=False,
    )
```

```python
import jax
import jax.numpy as jnp
from jax import lax
from jax.experimental import pallas as pl
from jax.experimental.pallas import tpu as pltpu
from jax.sharding import PartitionSpec as P

ZED = 16
LANES = 128
WIDE = 2 * LANES
EDGE = 4

FLOW_VELOCITY = [
    (0, 0, 0),
    (1, 0, 0),
    (-1, 0, 0),
    (0, 1, 0),
    (0, -1, 0),
    (0, 0, 1),
    (0, 0, -1),
    (1, 1, 0),
    (-1, -1, 0),
    (1, -1, 0),
    (-1, 1, 0),
    (1, 0, 1),
    (-1, 0, -1),
    (1, 0, -1),
    (-1, 0, 1),
    (0, 1, 1),
    (0, -1, -1),
    (0, 1, -1),
    (0, -1, 1),
]
VELOCITY = FLOW_VELOCITY + FLOW_VELOCITY[:7]
STILL = (0, 0, 0)
MEMBERS = len(VELOCITY)
RIGHTWARD = [q for q in range(MEMBERS) if VELOCITY[q][0] == 1]
LEFTWARD = [q for q in range(MEMBERS) if VELOCITY[q][0] == -1]
LEVEL = [q for q in range(MEMBERS) if VELOCITY[q][0] == 0]


def mirrored(q):
    x, y, z = VELOCITY[q]
    start = 0 if q < 19 else 19
    return start + FLOW_VELOCITY.index((-x, y, z))


MOBILITY, RATE, WEIGHT = MEMBERS, MEMBERS + 1, MEMBERS + 2
FIELDS = MEMBERS + 6
SIDE_FIELDS = list(range(MEMBERS, FIELDS))

SUMS = 9
SUM_FIELDS = [FIELDS + k for k in range(SUMS)]

ADJ_EDGE = 2
SLOTS = LANES // (2 * EDGE)
STRIP_ROWS = 2 * FIELDS // SLOTS
HALF_ROWS = STRIP_ROWS // 2


def rows_of(entries):
    return {entry: row for row, entry in enumerate(entries)}


TO_NEAR = rows_of([(q, 0) for q in RIGHTWARD] + [(k, 1) for k in RIGHTWARD + SIDE_FIELDS + SUM_FIELDS])
TO_FAR = rows_of([(q, 1) for q in LEFTWARD] + [(k, 0) for k in LEFTWARD + SIDE_FIELDS + SUM_FIELDS])
ADJ_TO_NEAR = rows_of([(q, 0) for q in LEFTWARD] + [(k, 1) for k in LEFTWARD + SUM_FIELDS])
ADJ_TO_FAR = rows_of([(q, 1) for q in RIGHTWARD] + [(k, 0) for k in RIGHTWARD + SUM_FIELDS])
BULK_ROWS, ADJ_BULK = len(TO_NEAR), len(ADJ_TO_NEAR)


def with_strips(bulk, edge):
    return bulk + -(-bulk * 2 * edge // LANES)


SENT, ADJ_SENT = with_strips(BULK_ROWS, EDGE), with_strips(ADJ_BULK, ADJ_EDGE)


def level_sums(p):
    s1, s2, d1, d2 = p[3] + p[4], p[5] + p[6], p[3] - p[4], p[5] - p[6]
    s7, s8, d7, d8 = p[15] + p[16], p[17] + p[18], p[15] - p[16], p[17] - p[18]
    yz = s7 + s8
    mass = p[0] + (s1 + s2) + yz
    return [
        mass, d1 + (d7 + d8), d2 + (d7 - d8), s1 + yz, s2 + yz, s7 - s8,
        p[19] + (p[22] + p[23]) + (p[24] + p[25]), p[22] - p[23], p[24] - p[25],
    ]


def level_adjoint_sums(p):
    s1, s2, d1, d2 = p[3] + p[4], p[5] + p[6], p[3] - p[4], p[5] - p[6]
    s7, s8, d7, d8 = p[15] + p[16], p[17] + p[18], p[15] - p[16], p[17] - p[18]
    yz = s7 + s8
    t1, t2 = s1 + s1, s2 + s2
    mass = 12.0 * p[0] + (t1 + t2) + yz
    return [
        mass, (d1 + d1) + (d7 + d8), (d2 + d2) + (d7 - d8), t1 + yz, t2 + yz, s7 - s8,
        0.35 * p[19] + 0.175 * ((p[22] + p[23]) + (p[24] + p[25])),
        0.125 * (p[22] - p[23]), 0.125 * (p[24] - p[25]),
    ]


def cross_sums(p):
    pairs = [(1, 2), (7, 8), (9, 10), (11, 12), (13, 14)]
    return [p[a] + p[b] for a, b in pairs], [p[a] - p[b] for a, b in pairs]


def common(p, level, mobility):
    s, d = cross_sums(p)
    xy, xz = s[1] + s[2], s[3] + s[4]
    along = s[0] + xy + xz
    rho = level[0] + along
    j = (d[0] + (d[1] + d[2]) + (d[3] + d[4]), level[1] + (d[1] - d[2]), level[2] + (d[3] - d[4]))
    temperature = level[6] + (p[20] + p[21])
    flux = (p[20] - p[21], level[7], level[8])
    u = tuple(mobility * jk for jk in j)
    square = (u[0] * u[0], u[1] * u[1], u[2] * u[2])
    third = rho * (1.0 / 3.0)
    stress = (
        along - third - square[0],
        (level[3] + xy) - third - square[1],
        (level[4] + xz) - third - square[2],
        (s[1] - s[2]) - u[0] * u[1],
        (s[3] - s[4]) - u[0] * u[2],
        level[5] - u[1] * u[2],
    )
    decay = jnp.exp(-2.0 * (temperature - 1.0))
    omega = 1.0 / (0.5 + 0.3 * decay)
    return rho, j, u, square, stress, temperature, flux, decay, omega


def collide(p, level, mobility, rate, wanted):
    rho, _, u, square, stress, temperature, flux, _, omega = common(p, level, mobility)
    solid = mobility == 0.0
    lam = 1.2 - omega
    trace = stress[0] + stress[1] + stress[2]
    base = 1.2 * rho - 1.8 * (square[0] + square[1] + square[2]) - (1.5 * lam) * trace
    scale = 4.5 * lam
    mxx = 5.4 * square[0] + scale * stress[0]
    myy = 5.4 * square[1] + scale * stress[1]
    mzz = 5.4 * square[2] + scale * stress[2]
    mxy = 2.0 * (5.4 * (u[0] * u[1]) + scale * stress[3])
    mxz = 2.0 * (5.4 * (u[0] * u[2]) + scale * stress[4])
    myz = 2.0 * (5.4 * (u[1] * u[2]) + scale * stress[5])
    bx, by, bz = base + mxx, base + myy, base + mzz
    sxy, sxz, syz = bx + myy, bx + mzz, by + mzz
    even = [bx, by, bz, sxy + mxy, sxy - mxy, sxz + mxz, sxz - mxz, syz + myz, syz - myz]
    odd = [u[0], u[1], u[2], u[0] + u[1], u[0] - u[1], u[0] + u[2], u[0] - u[2], u[1] + u[2], u[1] - u[2]]
    result = {}
    if 0 in wanted:
        result[0] = jnp.where(solid, p[0], (1.0 / 3.0) * base - 0.2 * p[0])
    for k in range(9):
        a, b = 2 * k + 1, 2 * k + 2
        w = 1.0 / 18.0 if k < 3 else 1.0 / 36.0
        e, o = w * even[k], (3.6 * w) * odd[k]
        if a in wanted:
            result[a] = jnp.where(solid, p[b], (e + o) - 0.2 * p[a])
        if b in wanted:
            result[b] = jnp.where(solid, p[a], (e - o) - 0.2 * p[b])
    keep = 0.5 * (1.4 - rate)
    push = (0.5 * rate) * temperature
    warm = 0.175 * temperature
    if 19 in wanted:
        result[19] = 0.35 * temperature - 0.4 * p[19]
    for k in range(3):
        along = keep * flux[k] + push * u[k]
        a, b = 20 + 2 * k, 21 + 2 * k
        if a in wanted:
            result[a] = (warm + along) - 0.4 * p[a]
        if b in wanted:
            result[b] = (warm - along) - 0.4 * p[b]
    return result


def state_terms(p, level, mobility, rate, full):
    _, _, u, _, stress, temperature, flux, decay, omega = common(p, level, mobility)
    slope = jnp.where(mobility == 0.0, 0.0, (0.6 * decay) * (omega * omega))
    terms = list(u) + list(stress) + [1.2 - omega, (4.0 * rate) * temperature, slope]
    return terms + [temperature * u[k] - flux[k] for k in range(3)] if full else terms


def pull_back(terms, pa, adjoint_level, mobility, rate, wanted, sensitivity):
    u, stress, lam, push, slope, bent = terms[:3], terms[3:9], terms[9], terms[10], terms[11], terms[12:]
    solid = mobility == 0.0
    s, d = cross_sums(pa)
    w = 1.0 / 36.0
    xy, xz = s[1] + s[2], s[3] + s[4]
    along = (s[0] + s[0]) + xy + xz
    mass = w * (adjoint_level[0] + along)
    px = w * ((d[0] + d[0]) + (d[1] + d[2]) + (d[3] + d[4]))
    py = w * (adjoint_level[1] + (d[1] - d[2]))
    pz = w * (adjoint_level[2] + (d[3] - d[4]))
    rxx, ryy, rzz = w * along, w * (adjoint_level[3] + xy), w * (adjoint_level[4] + xz)
    rxy, rxz, ryz = w * (s[1] - s[2]), w * (s[3] - s[4]), w * adjoint_level[5]
    shift = 1.5 * mass
    dxx, dyy, dzz = 4.5 * rxx - shift, 4.5 * ryy - shift, 4.5 * rzz - shift
    dxy, dxz, dyz = 4.5 * rxy, 4.5 * rxz, 4.5 * ryz
    mix = 2.4 - 2.0 * lam
    b = ((pa[20] - pa[21]) * 0.125, adjoint_level[7], adjoint_level[8])
    ux = 3.6 * px + mix * (dxx * u[0] + dxy * u[1] + dxz * u[2]) + push * b[0]
    uy = 3.6 * py + mix * (dxy * u[0] + dyy * u[1] + dyz * u[2]) + push * b[1]
    uz = 3.6 * pz + mix * (dxz * u[0] + dyz * u[1] + dzz * u[2]) + push * b[2]
    result = {}
    if wanted:
        lam_bar = (
            dxx * stress[0]
            + dyy * stress[1]
            + dzz * stress[2]
            + 2.0 * (dxy * stress[3] + dxz * stress[4] + dyz * stress[5])
        )
        rho_bar = 1.2 * mass - (1.5 * lam) * ((rxx + ryy + rzz) - mass)
        jx, jy, jz = mobility * ux, mobility * uy, mobility * uz
        ex, ey, ez = lam * dxx, lam * dyy, lam * dzz
        exy, exz, eyz = (2.0 * lam) * dxy, (2.0 * lam) * dxz, (2.0 * lam) * dyz
        hx, hy, hz = rho_bar + ex, rho_bar + ey, rho_bar + ez
        gxy, gxz, gyz = hx + ey, hx + ez, hy + ez
        even = [hx, hy, hz, gxy + exy, gxy - exy, gxz + exz, gxz - exz, gyz + eyz, gyz - eyz]
        odd = [jx, jy, jz, jx + jy, jx - jy, jx + jz, jx - jz, jy + jz, jy - jz]
        if 0 in wanted:
            result[0] = jnp.where(solid, pa[0], rho_bar - 0.2 * pa[0])
        for k in range(9):
            a, m = 2 * k + 1, 2 * k + 2
            if a in wanted:
                result[a] = jnp.where(solid, pa[m], (even[k] + odd[k]) - 0.2 * pa[a])
            if m in wanted:
                result[m] = jnp.where(solid, pa[a], (even[k] - odd[k]) - 0.2 * pa[m])
        warm = (
            adjoint_level[6]
            + 0.175 * (pa[20] + pa[21])
            + (4.0 * rate) * (b[0] * u[0] + b[1] * u[1] + b[2] * u[2])
            - lam_bar * slope
        )
        keep = 5.6 - 4.0 * rate
        if 19 in wanted:
            result[19] = warm - 0.4 * pa[19]
        for k in range(3):
            along = keep * b[k]
            a, m = 20 + 2 * k, 21 + 2 * k
            if a in wanted:
                result[a] = (warm + along) - 0.4 * pa[a]
            if m in wanted:
                result[m] = (warm - along) - 0.4 * pa[m]
    if sensitivity:
        by_resistance = -mobility * (ux * u[0] + uy * u[1] + uz * u[2])
        by_conductivity = (-1.6 * (rate * rate)) * (b[0] * bent[0] + b[1] * bent[1] + b[2] * bent[2])
        result["by"] = (by_resistance, by_conductivity)
    return result


BEGIN = 8


def begin_terms(p, mobility, rate):
    _, _, u, _, _, temperature, flux, _, omega = common(p, level_sums(p), mobility)
    bent = [temperature * u[k] - flux[k] for k in range(3)]
    return list(u) + bent + [2.4 - 2.0 * (1.2 - omega), (4.0 * rate) * temperature]


def end_terms(terms, pa, mobility, rate):
    u, bent, mix, push = terms[:3], terms[3:6], terms[6], terms[7]
    level = level_adjoint_sums(pa)
    s, d = cross_sums(pa)
    w = 1.0 / 36.0
    xy, xz = s[1] + s[2], s[3] + s[4]
    along = (s[0] + s[0]) + xy + xz
    shift = (1.5 * w) * (level[0] + along)
    v = 4.5 * w
    dxx, dyy, dzz = v * along - shift, v * (level[3] + xy) - shift, v * (level[4] + xz) - shift
    dxy, dxz, dyz = v * (s[1] - s[2]), v * (s[3] - s[4]), v * level[5]
    px = (d[0] + d[0]) + (d[1] + d[2]) + (d[3] + d[4])
    py = level[1] + (d[1] - d[2])
    pz = level[2] + (d[3] - d[4])
    b = ((pa[20] - pa[21]) * 0.125, level[7], level[8])
    ux = (3.6 * w) * px + mix * (dxx * u[0] + dxy * u[1] + dxz * u[2]) + push * b[0]
    uy = (3.6 * w) * py + mix * (dxy * u[0] + dyy * u[1] + dyz * u[2]) + push * b[1]
    uz = (3.6 * w) * pz + mix * (dxz * u[0] + dyz * u[1] + dzz * u[2]) + push * b[2]
    by_resistance = -mobility * (ux * u[0] + uy * u[1] + uz * u[2])
    by_conductivity = (-1.6 * (rate * rate)) * (b[0] * bent[0] + b[1] * bent[1] + b[2] * bent[2])
    return by_resistance, by_conductivity


def turn(value, by, axis):
    count = value.shape[axis]
    by %= count
    return pltpu.roll(value, by, axis) if by else value


def side_by_side(parts, edge):
    lane = lax.broadcasted_iota(jnp.int32, (ZED, LANES), 1)
    row = None
    for slot, part in enumerate(parts):
        row = part if row is None else jnp.where(lane >= 2 * edge * slot, part, row)
    return row


def packed(value, slot, edge=EDGE):
    return turn(value, 2 * edge * slot + edge, 1)


def pack_rows(parts, edge=EDGE):
    slots = LANES // (2 * edge)
    return [
        side_by_side([part(slot) for slot, part in enumerate(parts[start : start + slots])], edge)
        for start in range(0, len(parts), slots)
    ]


def halves():
    return [pl.ds(0, 8), pl.ds(8, 8)]


def low_lanes():
    return lax.broadcasted_iota(jnp.int32, (ZED, LANES), 1) % (2 * EDGE) < EDGE


def second_core():
    return lax.rem(lax.axis_index("gx"), 2)


def framed(q, odd):
    return q + odd * (mirrored(q) - q)


def copy_rows(target, source):
    for row in range(source.shape[0]):
        target[row] = source[row]


def split(value):
    return value[:, :LANES], value[:, LANES:], 0


def beside(row, slot, edge=EDGE):
    return row, -edge - 2 * edge * slot


def moved(triple, velocity, way):
    main, extra, by = triple
    _, step_y, step_z = velocity
    step = way * step_y
    main, extra = turn(main, way * step_z, 0), turn(extra, way * step_z, 0)
    if not step:
        return main, turn(extra, by, 1)
    main, extra = turn(main, step, 1), turn(extra, by + step, 1)
    lane = lax.broadcasted_iota(jnp.int32, (ZED, LANES), 1)
    edge = lane == (0 if step == 1 else LANES - 1)
    return jnp.where(edge, extra, main), jnp.where(edge, main, extra)


def put(ref, q, i, pair):
    ref[q, i, :, :LANES], ref[q, i, :, LANES:] = pair


def tiles(lanes):
    return [(z, pl.ds(t, LANES)) for z in halves() for t in range(0, lanes, LANES)]


def own_row(k, c):
    return c * FIELDS + k


def own_value(own, strip, k, c):
    place = own_row(k, c)
    return (own[place],) + beside(strip[place // SLOTS], place % SLOTS)


def halo_value(buffer, bulk, place, edge=EDGE):
    slots = LANES // (2 * edge)
    return (buffer[place],) + beside(buffer[bulk + place // slots], place % slots, edge)


def given_state(flow, heat, odd, c, z):
    i = c + odd * (1 - 2 * c)
    return [flow[framed(q, odd), i, z, :] for q in range(19)] + [
        heat[framed(q, odd) - 19, i, z, :] for q in range(19, MEMBERS)
    ]


def first_kernel(
    flow_in, heat_in, flow_weight_in, heat_weight_in, resistance_in, conductivity_in, solid_in,
    own_out, up_out, down_out,
    own, strips, flow, heat, flow_weight, heat_weight, resistance, conductivity, solid, arrived, sent,
):
    pairs = [
        (flow_in, flow),
        (heat_in, heat),
        (resistance_in, resistance),
        (conductivity_in, conductivity),
        (solid_in, solid),
        (flow_weight_in, flow_weight),
        (heat_weight_in, heat_weight),
    ]
    copies = [pltpu.make_async_copy(a, b, arrived.at[k]) for k, (a, b) in enumerate(pairs)]
    for copy in copies:
        copy.start()
    for copy in copies:
        copy.wait()
    odd = second_core()
    sign = (1 - 2 * odd).astype(jnp.float32)
    for c in range(2):
        i = c + odd * (1 - 2 * c)
        for z in halves():
            mobility = jnp.where(solid[i, z, :] != 0, 0.0, 1.0 / (1.0 + resistance[i, z, :]))
            rate = 1.0 / (0.5 + 0.4 * conductivity[i, z, :])
            p = given_state(flow, heat, odd, c, z)
            after = collide(p, level_sums(p), mobility, rate, range(MEMBERS))
            more = [mobility, rate, sign * flow_weight[0, i, z, :]]
            more += [flow_weight[1, i, z, :], flow_weight[2, i, z, :], heat_weight[i, z, :]]
            for k, value in enumerate([after[q] for q in range(MEMBERS)] + more):
                own[own_row(k, c), z, :] = value
    copy_own = pltpu.make_async_copy(own, own_out, sent.at[0])
    copy_own.start()
    rows = pack_rows([lambda slot, k=k: packed(own[k], slot) for k in range(2 * FIELDS)])
    low = low_lanes()
    for k in range(HALF_ROWS):
        strips[k] = jnp.where(low, rows[k], turn(rows[k + HALF_ROWS], EDGE, 1))
        strips[k + HALF_ROWS] = jnp.where(low, turn(rows[k], -EDGE, 1), rows[k + HALF_ROWS])
    copies = [
        pltpu.make_async_copy(strips.at[pl.ds(0, HALF_ROWS)], up_out, sent.at[1]),
        pltpu.make_async_copy(strips.at[pl.ds(HALF_ROWS, HALF_ROWS)], down_out, sent.at[2]),
    ]
    for copy in copies:
        copy.start()
    copy_own.wait()
    for copy in copies:
        copy.wait()


def stage_kernel(own, staged):
    copy_rows(staged, own)


def halo_kernel(own, from_below, from_above, far, near, strip):
    low = low_lanes()
    for k in range(HALF_ROWS):
        under, over = from_below[k], from_above[k]
        strip[k] = jnp.where(low, under, turn(over, EDGE, 1))
        strip[k + HALF_ROWS] = jnp.where(low, turn(under, -EDGE, 1), over)
    for side, rows, c in ((near, TO_NEAR, 1), (far, TO_FAR, 0)):
        level = {q: moved(own_value(own, strip, q, c), VELOCITY[q], 1) for q in LEVEL}
        sums = [level_sums({q: level[q][t] for q in LEVEL}) for t in range(2)]
        parts = []
        for (k, column), row in rows.items():
            if k >= FIELDS:
                side[row] = sums[0][k - FIELDS]
                parts.append(lambda slot, k=k: packed(sums[1][k - FIELDS], slot))
            else:
                place = own_row(k, column)
                side[row] = own[place]
                parts.append(
                    lambda slot, place=place: turn(
                        strip[place // SLOTS], 2 * EDGE * (slot - place % SLOTS), 1
                    )
                )
        for k, row in enumerate(pack_rows(parts)):
            side[BULK_ROWS + k] = row


def level_of(p, column, sums):
    return sums(p) if 0 <= column <= 1 else [p[q] for q in LEVEL[:SUMS]]


def near_place(rows, k, column):
    return rows[mirrored(k) if k < MEMBERS else k, 3 - column]


def far_place(rows, k, column):
    return rows[mirrored(k) if k < MEMBERS else k, -1 - column]


def own_fed(q, column):
    return 0 <= column <= 1 and 0 <= column - VELOCITY[q][0] <= 1


def state_of(own_state, state, first, column, z, y):
    return [
        own_state[q, column, z, y] if own_fed(q, column) else state[q, column - first, z, y]
        for q in range(MEMBERS)
    ]


def first_state(wide, column, state, sides, i):
    put(sides, 0, i, moved(wide(MOBILITY, column), STILL, 1))
    put(sides, 1, i, moved(wide(RATE, column), STILL, 1))
    for q in range(MEMBERS):
        if own_fed(q, column):
            continue
        if 0 <= column <= 1 or q not in LEVEL:
            put(state, q, i, moved(wide(q, column - VELOCITY[q][0]), VELOCITY[q], 1))
        elif q in LEVEL[:SUMS]:
            put(state, q, i, moved(wide(SUM_FIELDS[LEVEL.index(q)], column), STILL, 1))


def first_collision(column, own_state, state, sides, after, first):
    i = column - first
    wanted = [q for q in range(MEMBERS) if 0 <= column + VELOCITY[q][0] <= 1]
    for z, y in tiles(WIDE):
        p = state_of(own_state, state, first, column, z, y)
        level = level_of(p, column, level_sums)
        result = collide(p, level, sides[0, i, z, y], sides[1, i, z, y], wanted)
        for q in wanted:
            after[q, i, z, y] = result[q]


def seeds(wide, column, seed):
    weights = [wide(WEIGHT + k, column) for k in range(3)]
    weights = [(main, turn(extra, by, 1)) for main, extra, by in weights]
    if not 0 <= column <= 1:
        weights[0] = tuple(-value for value in weights[0])
    for q in range(1, MEMBERS):
        velocity = VELOCITY[q]
        c = column - velocity[0]
        if not 0 <= c <= 1:
            continue
        if q < 19:
            parts = [
                tuple(value if velocity[k] > 0 else -value for value in weights[k]) for k in range(3) if velocity[k]
            ]
            pair = parts[0] if len(parts) == 1 else tuple(a + b for a, b in zip(*parts))
            pair += (0,)
        else:
            pair = wide(WEIGHT + 3, column)
        put(seed, q, c, moved(pair, velocity, -1))


def own_step_kernel(flow, heat, own, strip, own_state, own_seed, begin):
    def wide(k, column):
        return own_value(own, strip, k, column)

    for column in (0, 1):
        for q in range(MEMBERS):
            if own_fed(q, column):
                put(own_state, q, column, moved(wide(q, column - VELOCITY[q][0]), VELOCITY[q], 1))
        seeds(wide, column, own_seed)
    odd = second_core()
    for c in range(2):
        for z in halves():
            terms = begin_terms(
                given_state(flow, heat, odd, c, z), own[own_row(MOBILITY, c), z, :], own[own_row(RATE, c), z, :]
            )
            for k, value in enumerate(terms):
                begin[k, c, z, :] = value


def step_kernel(
    own, strip, own_state, own_seed, from_far, from_near,
    far_state, far_sides, near_state, near_sides, adjoint, by_resistance, by_conductivity, far, near,
    after, near_after, later, halo_seed,
):
    def wide(k, column):
        if column < 0:
            return halo_value(from_far, BULK_ROWS, far_place(TO_FAR, k, column))
        if column > 1:
            return halo_value(from_near, BULK_ROWS, near_place(TO_NEAR, k, column))
        return own_value(own, strip, k, column)

    for column in (-1, 0):
        first_state(wide, column, far_state, far_sides, column + 1)
        first_collision(column, own_state, far_state, far_sides, after, -1)
    for column in (1, 2):
        first_state(wide, column, near_state, near_sides, column - 1)
        first_collision(column, own_state, near_state, near_sides, near_after, 1)
    for column in (-1, 2):
        seeds(wide, column, halo_seed)
    for c in range(2):
        for q in range(MEMBERS):
            column = c - VELOCITY[q][0]
            source = near_after[q, column - 1] if column >= 1 else after[q, column + 1]
            put(later, q, c, moved(split(source), VELOCITY[q], 1))
    for c in range(2):
        for z, y in tiles(WIDE):
            p = [later[q, c, z, y] for q in range(MEMBERS)]
            pa = [jnp.zeros((8, LANES), jnp.float32)]
            pa += [
                (own_seed if 0 <= c + VELOCITY[q][0] <= 1 else halo_seed)[q, c, z, y] for q in range(1, MEMBERS)
            ]
            inner = y.start == 0
            mobility, rate = [near_sides[k, 0, z, y] if c else far_sides[k, 1, z, y] for k in range(2)]
            terms = state_terms(p, level_sums(p), mobility, rate, inner)
            result = pull_back(terms, pa, level_adjoint_sums(pa), mobility, rate, range(MEMBERS), inner)
            if inner:
                by_resistance[c, z, :], by_conductivity[c, z, :] = result["by"]
            for q in range(MEMBERS):
                adjoint[q, c, z, y] = result[q]
    for side, rows, c in ((near, ADJ_TO_NEAR, 1), (far, ADJ_TO_FAR, 0)):
        level = {q: moved(split(adjoint[q, c]), VELOCITY[q], -1) for q in LEVEL}
        sums = [level_adjoint_sums({q: level[q][t] for q in LEVEL}) for t in range(2)]
        parts = []
        for (k, column), row in rows.items():
            if k >= FIELDS:
                side[row] = sums[0][k - FIELDS]
                parts.append(lambda slot, k=k: packed(sums[1][k - FIELDS], slot, ADJ_EDGE))
            else:
                side[row] = adjoint[k, column, :, :LANES]
                parts.append(lambda slot, k=k, column=column: packed(adjoint[k, column, :, LANES:], slot, ADJ_EDGE))
        for k, row in enumerate(pack_rows(parts, ADJ_EDGE)):
            side[ADJ_BULK + k] = row


TERMS = 15


def prepare_kernel(
    own_state, far_state, far_sides, near_state, near_sides, adjoint,
    terms, own_arrived, own_sums,
):
    for column in range(-1, 3):
        first, state, sides = (1, near_state, near_sides) if column >= 1 else (-1, far_state, far_sides)
        for z, y in tiles(WIDE):
            p = state_of(own_state, state, first, column, z, y)
            mobility, rate = sides[0, column - first, z, y], sides[1, column - first, z, y]
            full = y.start == 0 and 0 <= column <= 1
            values = state_terms(p, level_of(p, column, level_sums), mobility, rate, full)
            for k, value in enumerate(values):
                terms[k, column + 1, z, y] = value
    for column in range(-1, 3):
        level = {}
        for q in range(MEMBERS):
            if 0 <= column + VELOCITY[q][0] <= 1:
                pair = moved(split(adjoint[q, column + VELOCITY[q][0]]), VELOCITY[q], -1)
                put(own_arrived, q, column + 1, pair)
                if q in LEVEL:
                    level[q] = pair
        if 0 <= column <= 1:
            sums = [level_adjoint_sums({q: level[q][t] for q in LEVEL}) for t in range(2)]
            for k in range(SUMS):
                put(own_sums, k, column, (sums[0][k], sums[1][k]))


def adjoint_step(halo, column, terms, own_arrived, own_sums, sides, arrived, earlier, first, keep):
    own = 0 <= column <= 1
    i = column - first
    for q in range(MEMBERS):
        if 0 <= column + VELOCITY[q][0] <= 1:
            continue
        if q not in LEVEL:
            put(arrived, q, i, moved(halo(q, column + VELOCITY[q][0]), VELOCITY[q], -1))
        elif q in LEVEL[:SUMS]:
            put(arrived, q, i, moved(halo(SUM_FIELDS[LEVEL.index(q)], column), STILL, 1))
    for z, y in tiles(WIDE):
        inner = y.start == 0
        wanted = [
            q for q in range(MEMBERS) if 0 <= column - VELOCITY[q][0] <= 1 and (inner or VELOCITY[q][1])
        ]
        pa = [
            own_arrived[q, column + 1, z, y] if 0 <= column + VELOCITY[q][0] <= 1 else arrived[q, i, z, y]
            for q in range(MEMBERS)
        ]
        if own:
            level = [own_sums[k, column, z, y] for k in range(SUMS)]
        else:
            level = [pa[q] for q in LEVEL[:SUMS]]
        held_terms = [terms[k, column + 1, z, y] for k in range(TERMS if inner and own else TERMS - 3)]
        result = pull_back(
            held_terms, pa, level, sides[0, i, z, y], sides[1, i, z, y], wanted, inner and own
        )
        for q in wanted:
            earlier[q, i, z, y] = result[q]
        if inner and own:
            keep(z, *result["by"])


def far_adjoint_kernel(
    terms, own_arrived, own_sums, sides, part_resistance, part_conductivity, from_far,
    earlier, by_resistance, by_conductivity,
    arrived,
):
    def halo(k, column):
        return halo_value(from_far, ADJ_BULK, far_place(ADJ_TO_FAR, k, column), ADJ_EDGE)

    def keep(z, resistance, conductivity):
        by_resistance[0, z, :] = part_resistance[0, z, :] + resistance
        by_conductivity[0, z, :] = part_conductivity[0, z, :] + conductivity

    for column in (-1, 0):
        adjoint_step(halo, column, terms, own_arrived, own_sums, sides, arrived, earlier, -1, keep)
    by_resistance[1] = part_resistance[1]
    by_conductivity[1] = part_conductivity[1]


def near_adjoint_kernel(
    begin, terms, own_arrived, own_sums, sides, far_sides, far_earlier,
    part_resistance, part_conductivity, from_near,
    by_resistance, by_conductivity,
    arrived, earlier, last, sums,
):
    def halo(k, column):
        return halo_value(from_near, ADJ_BULK, near_place(ADJ_TO_NEAR, k, column), ADJ_EDGE)

    def keep(z, resistance, conductivity):
        sums[0, z, :] = part_resistance[1, z, :] + resistance
        sums[1, z, :] = part_conductivity[1, z, :] + conductivity

    for column in (1, 2):
        adjoint_step(halo, column, terms, own_arrived, own_sums, sides, arrived, earlier, 1, keep)
    for c in range(2):
        for q in range(MEMBERS):
            velocity = VELOCITY[q]
            column = c + velocity[0]
            source, i = (earlier, column - 1) if column >= 1 else (far_earlier, column + 1)
            if velocity[1]:
                last[q, c] = moved(split(source[q, i]), velocity, -1)[0]
            else:
                last[q, c] = turn(source[q, i, :, :LANES], -velocity[2], 0)
    narrow = pl.ds(0, LANES)
    odd = second_core()
    for c in range(2):
        i = c + odd * (1 - 2 * c)
        for z in halves():
            pa = [last[q, c, z, :] for q in range(MEMBERS)]
            mobility, rate = [(sides[k, 0, z, narrow] if c else far_sides[k, 1, z, narrow]) for k in range(2)]
            terms = [begin[k, c, z, :] for k in range(BEGIN)]
            resistance, conductivity = end_terms(terms, pa, mobility, rate)
            by_resistance[i, z, :] = resistance + (sums[0, z, :] if c else part_resistance[0, z, :])
            by_conductivity[i, z, :] = conductivity + (sums[1, z, :] if c else part_conductivity[0, z, :])


def floats(*shape):
    return jax.ShapeDtypeStruct(shape, jnp.float32)


def vmem(*shape):
    return pltpu.VMEM(shape, jnp.float32)


def swap_along_x(far, near):
    count = lax.axis_size("gx")
    across = [(i, (i + (1 if i % 2 else -1)) % count) for i in range(count)]
    within = [(i, i ^ 1) for i in range(count)]
    return lax.ppermute(far, "gx", across), lax.ppermute(near, "gx", within)


FIRST_PARAMS = pltpu.CompilerParams(vmem_limit_bytes=56 * 1024 * 1024)
PARAMS = pltpu.CompilerParams(vmem_limit_bytes=24 * 1024 * 1024)


def on_device(flow, heat, flow_weight, heat_weight, resistance, conductivity, solid):
    in_hbm = pl.BlockSpec(memory_space=pltpu.HBM)
    own, up, down = pl.pallas_call(
        first_kernel,
        in_specs=[in_hbm] * 7,
        out_specs=[in_hbm] * 3,
        out_shape=(
            floats(2 * FIELDS, ZED, LANES),
            floats(HALF_ROWS, ZED, LANES),
            floats(HALF_ROWS, ZED, LANES),
        ),
        scratch_shapes=[
            vmem(2 * FIELDS, ZED, LANES),
            vmem(STRIP_ROWS, ZED, LANES),
            vmem(19, 2, ZED, LANES),
            vmem(7, 2, ZED, LANES),
            vmem(3, 2, ZED, LANES),
            vmem(2, ZED, LANES),
            vmem(2, ZED, LANES),
            vmem(2, ZED, LANES),
            pltpu.VMEM((2, ZED, LANES), jnp.int32),
            pltpu.SemaphoreType.DMA((7,)),
            pltpu.SemaphoreType.DMA((3,)),
        ],
        compiler_params=FIRST_PARAMS,
        name="collide_own",
    )(flow, heat, flow_weight, heat_weight, resistance, conductivity, solid)

    count = lax.axis_size("gy")
    upward = [(i, (i + 1) % count) for i in range(count)]
    from_below = lax.ppermute(up, "gy", upward)
    from_above = lax.ppermute(down, "gy", [(target, source) for source, target in upward])

    own = pl.pallas_call(
        stage_kernel,
        out_shape=floats(2 * FIELDS, ZED, LANES),
        compiler_params=PARAMS,
        cost_estimate=pl.CostEstimate(flops=10**7, bytes_accessed=10**6, transcendentals=0),
        name="stage_own",
    )(own)

    far, near, strip = pl.pallas_call(
        halo_kernel,
        out_shape=(floats(SENT, ZED, LANES), floats(SENT, ZED, LANES), floats(STRIP_ROWS, ZED, LANES)),
        compiler_params=PARAMS,
        name="halo_buffers",
    )(own, from_below, from_above)

    from_far, from_near = swap_along_x(far, near)

    columns = floats(MEMBERS, 2, ZED, WIDE)
    side_columns = floats(2, 2, ZED, WIDE)
    cells = floats(2, ZED, LANES)
    held = vmem(MEMBERS, 2, ZED, WIDE)
    busy = pl.CostEstimate(flops=10**7, bytes_accessed=10**6, transcendentals=0)

    own_state, own_seed, begin = pl.pallas_call(
        own_step_kernel,
        out_shape=(columns, columns, floats(BEGIN, 2, ZED, LANES)),
        compiler_params=PARAMS,
        cost_estimate=busy,
        name="own_step",
    )(flow, heat, own, strip)

    far_state, far_sides, near_state, near_sides, adjoint, part_resistance, part_conductivity, far, near = (
        pl.pallas_call(
            step_kernel,
            out_shape=(
                columns, side_columns, columns, side_columns, columns, cells, cells,
                floats(ADJ_SENT, ZED, LANES), floats(ADJ_SENT, ZED, LANES),
            ),
            scratch_shapes=[held, held, held, held],
            compiler_params=PARAMS,
            name="two_steps",
        )(own, strip, own_state, own_seed, from_far, from_near)
    )

    from_far, from_near = swap_along_x(far, near)

    terms, own_arrived, own_sums = pl.pallas_call(
        prepare_kernel,
        out_shape=(
            floats(TERMS, 4, ZED, WIDE), floats(MEMBERS, 4, ZED, WIDE), floats(SUMS, 2, ZED, WIDE),
        ),
        compiler_params=PARAMS,
        cost_estimate=busy,
        name="prepare",
    )(own_state, far_state, far_sides, near_state, near_sides, adjoint)

    far_earlier, part_resistance, part_conductivity = pl.pallas_call(
        far_adjoint_kernel,
        out_shape=(columns, cells, cells),
        scratch_shapes=[held],
        compiler_params=PARAMS,
        cost_estimate=busy,
        name="far_adjoint",
    )(terms, own_arrived, own_sums, far_sides, part_resistance, part_conductivity, from_far)

    return pl.pallas_call(
        near_adjoint_kernel,
        out_shape=(cells, cells),
        scratch_shapes=[held, held, vmem(MEMBERS, 2, ZED, LANES), vmem(2, ZED, LANES)],
        compiler_params=PARAMS,
        name="near_adjoint",
    )(
        begin, terms, own_arrived, own_sums, near_sides, far_sides, far_earlier,
        part_resistance, part_conductivity, from_near,
    )


def solution(mesh):
    split = P("gx", None, "gy")
    stacked = P(None, "gx", None, "gy")
    return jax.shard_map(
        on_device,
        mesh=mesh,
        in_specs=(stacked, stacked, stacked, split, split, split, split),
        out_specs=(split, split),
        check_vma=False,
    )
```

```python
import jax
import jax.numpy as jnp
from jax import lax
from jax.experimental import pallas as pl
from jax.experimental.pallas import tpu as pltpu
from jax.sharding import PartitionSpec as P

ZED = 16
LANES = 128
WIDE = 2 * LANES
EDGE = 4

FLOW_VELOCITY = [
    (0, 0, 0),
    (1, 0, 0),
    (-1, 0, 0),
    (0, 1, 0),
    (0, -1, 0),
    (0, 0, 1),
    (0, 0, -1),
    (1, 1, 0),
    (-1, -1, 0),
    (1, -1, 0),
    (-1, 1, 0),
    (1, 0, 1),
    (-1, 0, -1),
    (1, 0, -1),
    (-1, 0, 1),
    (0, 1, 1),
    (0, -1, -1),
    (0, 1, -1),
    (0, -1, 1),
]
VELOCITY = FLOW_VELOCITY + FLOW_VELOCITY[:7]
STILL = (0, 0, 0)
MEMBERS = len(VELOCITY)
RIGHTWARD = [q for q in range(MEMBERS) if VELOCITY[q][0] == 1]
LEFTWARD = [q for q in range(MEMBERS) if VELOCITY[q][0] == -1]
LEVEL = [q for q in range(MEMBERS) if VELOCITY[q][0] == 0]


def mirrored(q):
    x, y, z = VELOCITY[q]
    start = 0 if q < 19 else 19
    return start + FLOW_VELOCITY.index((-x, y, z))


MOBILITY, RATE, WEIGHT = MEMBERS, MEMBERS + 1, MEMBERS + 2
FIELDS = MEMBERS + 6
SIDE_FIELDS = list(range(MEMBERS, FIELDS))

SUMS = 9
SUM_FIELDS = [FIELDS + k for k in range(SUMS)]

ADJ_EDGE = 2
SLOTS = LANES // (2 * EDGE)
STRIP_ROWS = 2 * FIELDS // SLOTS
HALF_ROWS = STRIP_ROWS // 2


def rows_of(entries):
    return {entry: row for row, entry in enumerate(entries)}


TO_NEAR = rows_of([(q, 0) for q in RIGHTWARD] + [(k, 1) for k in RIGHTWARD + SIDE_FIELDS + SUM_FIELDS])
TO_FAR = rows_of([(q, 1) for q in LEFTWARD] + [(k, 0) for k in LEFTWARD + SIDE_FIELDS + SUM_FIELDS])
ADJ_TO_NEAR = rows_of([(q, 0) for q in LEFTWARD] + [(k, 1) for k in LEFTWARD + SUM_FIELDS])
ADJ_TO_FAR = rows_of([(q, 1) for q in RIGHTWARD] + [(k, 0) for k in RIGHTWARD + SUM_FIELDS])
BULK_ROWS, ADJ_BULK = len(TO_NEAR), len(ADJ_TO_NEAR)


def with_strips(bulk, edge):
    return bulk + -(-bulk * 2 * edge // LANES)


SENT, ADJ_SENT = with_strips(BULK_ROWS, EDGE), with_strips(ADJ_BULK, ADJ_EDGE)


def level_sums(p):
    s1, s2, d1, d2 = p[3] + p[4], p[5] + p[6], p[3] - p[4], p[5] - p[6]
    s7, s8, d7, d8 = p[15] + p[16], p[17] + p[18], p[15] - p[16], p[17] - p[18]
    yz = s7 + s8
    mass = p[0] + (s1 + s2) + yz
    return [
        mass, d1 + (d7 + d8), d2 + (d7 - d8), s1 + yz, s2 + yz, s7 - s8,
        p[19] + (p[22] + p[23]) + (p[24] + p[25]), p[22] - p[23], p[24] - p[25],
    ]


def level_adjoint_sums(p):
    s1, s2, d1, d2 = p[3] + p[4], p[5] + p[6], p[3] - p[4], p[5] - p[6]
    s7, s8, d7, d8 = p[15] + p[16], p[17] + p[18], p[15] - p[16], p[17] - p[18]
    yz = s7 + s8
    t1, t2 = s1 + s1, s2 + s2
    mass = 12.0 * p[0] + (t1 + t2) + yz
    return [
        mass, (d1 + d1) + (d7 + d8), (d2 + d2) + (d7 - d8), t1 + yz, t2 + yz, s7 - s8,
        0.35 * p[19] + 0.175 * ((p[22] + p[23]) + (p[24] + p[25])),
        0.125 * (p[22] - p[23]), 0.125 * (p[24] - p[25]),
    ]


def cross_sums(p):
    pairs = [(1, 2), (7, 8), (9, 10), (11, 12), (13, 14)]
    return [p[a] + p[b] for a, b in pairs], [p[a] - p[b] for a, b in pairs]


def common(p, level, mobility):
    s, d = cross_sums(p)
    xy, xz = s[1] + s[2], s[3] + s[4]
    along = s[0] + xy + xz
    rho = level[0] + along
    j = (d[0] + (d[1] + d[2]) + (d[3] + d[4]), level[1] + (d[1] - d[2]), level[2] + (d[3] - d[4]))
    temperature = level[6] + (p[20] + p[21])
    flux = (p[20] - p[21], level[7], level[8])
    u = tuple(mobility * jk for jk in j)
    square = (u[0] * u[0], u[1] * u[1], u[2] * u[2])
    third = rho * (1.0 / 3.0)
    stress = (
        along - third - square[0],
        (level[3] + xy) - third - square[1],
        (level[4] + xz) - third - square[2],
        (s[1] - s[2]) - u[0] * u[1],
        (s[3] - s[4]) - u[0] * u[2],
        level[5] - u[1] * u[2],
    )
    decay = jnp.exp(-2.0 * (temperature - 1.0))
    omega = 1.0 / (0.5 + 0.3 * decay)
    return rho, j, u, square, stress, temperature, flux, decay, omega


def collide(p, level, mobility, rate, wanted):
    rho, _, u, square, stress, temperature, flux, _, omega = common(p, level, mobility)
    solid = mobility == 0.0
    lam = 1.2 - omega
    trace = stress[0] + stress[1] + stress[2]
    base = 1.2 * rho - 1.8 * (square[0] + square[1] + square[2]) - (1.5 * lam) * trace
    scale = 4.5 * lam
    mxx = 5.4 * square[0] + scale * stress[0]
    myy = 5.4 * square[1] + scale * stress[1]
    mzz = 5.4 * square[2] + scale * stress[2]
    mxy = 2.0 * (5.4 * (u[0] * u[1]) + scale * stress[3])
    mxz = 2.0 * (5.4 * (u[0] * u[2]) + scale * stress[4])
    myz = 2.0 * (5.4 * (u[1] * u[2]) + scale * stress[5])
    bx, by, bz = base + mxx, base + myy, base + mzz
    sxy, sxz, syz = bx + myy, bx + mzz, by + mzz
    even = [bx, by, bz, sxy + mxy, sxy - mxy, sxz + mxz, sxz - mxz, syz + myz, syz - myz]
    odd = [u[0], u[1], u[2], u[0] + u[1], u[0] - u[1], u[0] + u[2], u[0] - u[2], u[1] + u[2], u[1] - u[2]]
    result = {}
    if 0 in wanted:
        result[0] = jnp.where(solid, p[0], (1.0 / 3.0) * base - 0.2 * p[0])
    for k in range(9):
        a, b = 2 * k + 1, 2 * k + 2
        w = 1.0 / 18.0 if k < 3 else 1.0 / 36.0
        e, o = w * even[k], (3.6 * w) * odd[k]
        if a in wanted:
            result[a] = jnp.where(solid, p[b], (e + o) - 0.2 * p[a])
        if b in wanted:
            result[b] = jnp.where(solid, p[a], (e - o) - 0.2 * p[b])
    keep = 0.5 * (1.4 - rate)
    push = (0.5 * rate) * temperature
    warm = 0.175 * temperature
    if 19 in wanted:
        result[19] = 0.35 * temperature - 0.4 * p[19]
    for k in range(3):
        along = keep * flux[k] + push * u[k]
        a, b = 20 + 2 * k, 21 + 2 * k
        if a in wanted:
            result[a] = (warm + along) - 0.4 * p[a]
        if b in wanted:
            result[b] = (warm - along) - 0.4 * p[b]
    return result


def state_terms(p, level, mobility, rate, full):
    _, _, u, _, stress, temperature, flux, decay, omega = common(p, level, mobility)
    slope = jnp.where(mobility == 0.0, 0.0, (0.6 * decay) * (omega * omega))
    terms = list(u) + list(stress) + [1.2 - omega, (4.0 * rate) * temperature, slope]
    return terms + [temperature * u[k] - flux[k] for k in range(3)] if full else terms


def pull_back(terms, pa, adjoint_level, mobility, rate, wanted, sensitivity):
    u, stress, lam, push, slope, bent = terms[:3], terms[3:9], terms[9], terms[10], terms[11], terms[12:]
    solid = mobility == 0.0
    s, d = cross_sums(pa)
    w = 1.0 / 36.0
    xy, xz = s[1] + s[2], s[3] + s[4]
    along = (s[0] + s[0]) + xy + xz
    mass = w * (adjoint_level[0] + along)
    px = w * ((d[0] + d[0]) + (d[1] + d[2]) + (d[3] + d[4]))
    py = w * (adjoint_level[1] + (d[1] - d[2]))
    pz = w * (adjoint_level[2] + (d[3] - d[4]))
    rxx, ryy, rzz = w * along, w * (adjoint_level[3] + xy), w * (adjoint_level[4] + xz)
    rxy, rxz, ryz = w * (s[1] - s[2]), w * (s[3] - s[4]), w * adjoint_level[5]
    shift = 1.5 * mass
    dxx, dyy, dzz = 4.5 * rxx - shift, 4.5 * ryy - shift, 4.5 * rzz - shift
    dxy, dxz, dyz = 4.5 * rxy, 4.5 * rxz, 4.5 * ryz
    mix = 2.4 - 2.0 * lam
    b = ((pa[20] - pa[21]) * 0.125, adjoint_level[7], adjoint_level[8])
    ux = 3.6 * px + mix * (dxx * u[0] + dxy * u[1] + dxz * u[2]) + push * b[0]
    uy = 3.6 * py + mix * (dxy * u[0] + dyy * u[1] + dyz * u[2]) + push * b[1]
    uz = 3.6 * pz + mix * (dxz * u[0] + dyz * u[1] + dzz * u[2]) + push * b[2]
    result = {}
    if wanted:
        lam_bar = (
            dxx * stress[0]
            + dyy * stress[1]
            + dzz * stress[2]
            + 2.0 * (dxy * stress[3] + dxz * stress[4] + dyz * stress[5])
        )
        rho_bar = 1.2 * mass - (1.5 * lam) * ((rxx + ryy + rzz) - mass)
        jx, jy, jz = mobility * ux, mobility * uy, mobility * uz
        ex, ey, ez = lam * dxx, lam * dyy, lam * dzz
        exy, exz, eyz = (2.0 * lam) * dxy, (2.0 * lam) * dxz, (2.0 * lam) * dyz
        hx, hy, hz = rho_bar + ex, rho_bar + ey, rho_bar + ez
        gxy, gxz, gyz = hx + ey, hx + ez, hy + ez
        even = [hx, hy, hz, gxy + exy, gxy - exy, gxz + exz, gxz - exz, gyz + eyz, gyz - eyz]
        odd = [jx, jy, jz, jx + jy, jx - jy, jx + jz, jx - jz, jy + jz, jy - jz]
        if 0 in wanted:
            result[0] = jnp.where(solid, pa[0], rho_bar - 0.2 * pa[0])
        for k in range(9):
            a, m = 2 * k + 1, 2 * k + 2
            if a in wanted:
                result[a] = jnp.where(solid, pa[m], (even[k] + odd[k]) - 0.2 * pa[a])
            if m in wanted:
                result[m] = jnp.where(solid, pa[a], (even[k] - odd[k]) - 0.2 * pa[m])
        warm = (
            adjoint_level[6]
            + 0.175 * (pa[20] + pa[21])
            + (4.0 * rate) * (b[0] * u[0] + b[1] * u[1] + b[2] * u[2])
            - lam_bar * slope
        )
        keep = 5.6 - 4.0 * rate
        if 19 in wanted:
            result[19] = warm - 0.4 * pa[19]
        for k in range(3):
            along = keep * b[k]
            a, m = 20 + 2 * k, 21 + 2 * k
            if a in wanted:
                result[a] = (warm + along) - 0.4 * pa[a]
            if m in wanted:
                result[m] = (warm - along) - 0.4 * pa[m]
    if sensitivity:
        by_resistance = -mobility * (ux * u[0] + uy * u[1] + uz * u[2])
        by_conductivity = (-1.6 * (rate * rate)) * (b[0] * bent[0] + b[1] * bent[1] + b[2] * bent[2])
        result["by"] = (by_resistance, by_conductivity)
    return result


BEGIN = 8


def begin_terms(p, mobility, rate):
    _, _, u, _, _, temperature, flux, _, omega = common(p, level_sums(p), mobility)
    bent = [temperature * u[k] - flux[k] for k in range(3)]
    return list(u) + bent + [2.4 - 2.0 * (1.2 - omega), (4.0 * rate) * temperature]


def end_terms(terms, pa, mobility, rate):
    u, bent, mix, push = terms[:3], terms[3:6], terms[6], terms[7]
    level = level_adjoint_sums(pa)
    s, d = cross_sums(pa)
    w = 1.0 / 36.0
    xy, xz = s[1] + s[2], s[3] + s[4]
    along = (s[0] + s[0]) + xy + xz
    shift = (1.5 * w) * (level[0] + along)
    v = 4.5 * w
    dxx, dyy, dzz = v * along - shift, v * (level[3] + xy) - shift, v * (level[4] + xz) - shift
    dxy, dxz, dyz = v * (s[1] - s[2]), v * (s[3] - s[4]), v * level[5]
    px = (d[0] + d[0]) + (d[1] + d[2]) + (d[3] + d[4])
    py = level[1] + (d[1] - d[2])
    pz = level[2] + (d[3] - d[4])
    b = ((pa[20] - pa[21]) * 0.125, level[7], level[8])
    ux = (3.6 * w) * px + mix * (dxx * u[0] + dxy * u[1] + dxz * u[2]) + push * b[0]
    uy = (3.6 * w) * py + mix * (dxy * u[0] + dyy * u[1] + dyz * u[2]) + push * b[1]
    uz = (3.6 * w) * pz + mix * (dxz * u[0] + dyz * u[1] + dzz * u[2]) + push * b[2]
    by_resistance = -mobility * (ux * u[0] + uy * u[1] + uz * u[2])
    by_conductivity = (-1.6 * (rate * rate)) * (b[0] * bent[0] + b[1] * bent[1] + b[2] * bent[2])
    return by_resistance, by_conductivity


def turn(value, by, axis):
    count = value.shape[axis]
    by %= count
    return pltpu.roll(value, by, axis) if by else value


def side_by_side(parts, edge):
    lane = lax.broadcasted_iota(jnp.int32, (ZED, LANES), 1)
    row = None
    for slot, part in enumerate(parts):
        row = part if row is None else jnp.where(lane >= 2 * edge * slot, part, row)
    return row


def packed(value, slot, edge=EDGE):
    return turn(value, 2 * edge * slot + edge, 1)


def pack_rows(parts, edge=EDGE):
    slots = LANES // (2 * edge)
    return [
        side_by_side([part(slot) for slot, part in enumerate(parts[start : start + slots])], edge)
        for start in range(0, len(parts), slots)
    ]


def halves():
    return [pl.ds(0, 8), pl.ds(8, 8)]


def low_lanes():
    return lax.broadcasted_iota(jnp.int32, (ZED, LANES), 1) % (2 * EDGE) < EDGE


def second_core():
    return lax.rem(lax.axis_index("gx"), 2)


def framed(q, odd):
    return q + odd * (mirrored(q) - q)


def copy_rows(target, source):
    for row in range(source.shape[0]):
        target[row] = source[row]


def split(value):
    return value[:, :LANES], value[:, LANES:], 0


def beside(row, slot, edge=EDGE):
    return row, -edge - 2 * edge * slot


def moved(triple, velocity, way):
    main, extra, by = triple
    _, step_y, step_z = velocity
    step = way * step_y
    main, extra = turn(main, way * step_z, 0), turn(extra, way * step_z, 0)
    if not step:
        return main, turn(extra, by, 1)
    main, extra = turn(main, step, 1), turn(extra, by + step, 1)
    lane = lax.broadcasted_iota(jnp.int32, (ZED, LANES), 1)
    edge = lane == (0 if step == 1 else LANES - 1)
    return jnp.where(edge, extra, main), jnp.where(edge, main, extra)


def put(ref, q, i, pair):
    ref[q, i, :, :LANES], ref[q, i, :, LANES:] = pair


def tiles(lanes):
    return [(z, pl.ds(t, LANES)) for z in halves() for t in range(0, lanes, LANES)]


def own_row(k, c):
    return c * FIELDS + k


def own_value(own, strip, k, c):
    place = own_row(k, c)
    return (own[place],) + beside(strip[place // SLOTS], place % SLOTS)


def halo_value(buffer, bulk, place, edge=EDGE):
    slots = LANES // (2 * edge)
    return (buffer[place],) + beside(buffer[bulk + place // slots], place % slots, edge)


def given_state(flow, heat, odd, c, z):
    i = c + odd * (1 - 2 * c)
    return [flow[framed(q, odd), i, z, :] for q in range(19)] + [
        heat[framed(q, odd) - 19, i, z, :] for q in range(19, MEMBERS)
    ]


def first_kernel(
    flow_in, heat_in, flow_weight_in, heat_weight_in, resistance_in, conductivity_in, solid_in,
    own_out, up_out, down_out,
    own, strips, flow, heat, flow_weight, heat_weight, resistance, conductivity, solid, arrived, sent,
):
    pairs = [
        (flow_in, flow),
        (heat_in, heat),
        (resistance_in, resistance),
        (conductivity_in, conductivity),
        (solid_in, solid),
        (flow_weight_in, flow_weight),
        (heat_weight_in, heat_weight),
    ]
    copies = [pltpu.make_async_copy(a, b, arrived.at[k]) for k, (a, b) in enumerate(pairs)]
    for copy in copies:
        copy.start()
    for copy in copies:
        copy.wait()
    odd = second_core()
    sign = (1 - 2 * odd).astype(jnp.float32)
    for c in range(2):
        i = c + odd * (1 - 2 * c)
        for z in halves():
            mobility = jnp.where(solid[i, z, :] != 0, 0.0, 1.0 / (1.0 + resistance[i, z, :]))
            rate = 1.0 / (0.5 + 0.4 * conductivity[i, z, :])
            p = given_state(flow, heat, odd, c, z)
            after = collide(p, level_sums(p), mobility, rate, range(MEMBERS))
            more = [mobility, rate, sign * flow_weight[0, i, z, :]]
            more += [flow_weight[1, i, z, :], flow_weight[2, i, z, :], heat_weight[i, z, :]]
            for k, value in enumerate([after[q] for q in range(MEMBERS)] + more):
                own[own_row(k, c), z, :] = value
    copy_own = pltpu.make_async_copy(own, own_out, sent.at[0])
    copy_own.start()
    rows = pack_rows([lambda slot, k=k: packed(own[k], slot) for k in range(2 * FIELDS)])
    low = low_lanes()
    for k in range(HALF_ROWS):
        strips[k] = jnp.where(low, rows[k], turn(rows[k + HALF_ROWS], EDGE, 1))
        strips[k + HALF_ROWS] = jnp.where(low, turn(rows[k], -EDGE, 1), rows[k + HALF_ROWS])
    copies = [
        pltpu.make_async_copy(strips.at[pl.ds(0, HALF_ROWS)], up_out, sent.at[1]),
        pltpu.make_async_copy(strips.at[pl.ds(HALF_ROWS, HALF_ROWS)], down_out, sent.at[2]),
    ]
    for copy in copies:
        copy.start()
    copy_own.wait()
    for copy in copies:
        copy.wait()


def stage_kernel(own, staged):
    copy_rows(staged, own)


def halo_buffer(own, strip, side, rows, c):
    level = {q: moved(own_value(own, strip, q, c), VELOCITY[q], 1) for q in LEVEL}
    sums = [level_sums({q: level[q][t] for q in LEVEL}) for t in range(2)]
    parts = []
    for (k, column), row in rows.items():
        if k >= FIELDS:
            side[row] = sums[0][k - FIELDS]
            parts.append(lambda slot, k=k: packed(sums[1][k - FIELDS], slot))
        else:
            place = own_row(k, column)
            side[row] = own[place]
            parts.append(
                lambda slot, place=place: turn(
                    strip[place // SLOTS], 2 * EDGE * (slot - place % SLOTS), 1
                )
            )
    for k, row in enumerate(pack_rows(parts)):
        side[BULK_ROWS + k] = row


def far_halo_kernel(own, from_below, from_above, far, strip):
    low = low_lanes()
    for k in range(HALF_ROWS):
        under, over = from_below[k], from_above[k]
        strip[k] = jnp.where(low, under, turn(over, EDGE, 1))
        strip[k + HALF_ROWS] = jnp.where(low, turn(under, -EDGE, 1), over)
    halo_buffer(own, strip, far, TO_FAR, 0)


def near_halo_kernel(own, strip, near):
    halo_buffer(own, strip, near, TO_NEAR, 1)


def level_of(p, column, sums):
    return sums(p) if 0 <= column <= 1 else [p[q] for q in LEVEL[:SUMS]]


def near_place(rows, k, column):
    return rows[mirrored(k) if k < MEMBERS else k, 3 - column]


def far_place(rows, k, column):
    return rows[mirrored(k) if k < MEMBERS else k, -1 - column]


def own_fed(q, column):
    return 0 <= column <= 1 and 0 <= column - VELOCITY[q][0] <= 1


def state_of(own_state, state, first, column, z, y):
    return [
        own_state[q, column, z, y] if own_fed(q, column) else state[q, column - first, z, y]
        for q in range(MEMBERS)
    ]


def first_state(wide, column, state, sides, i):
    put(sides, 0, i, moved(wide(MOBILITY, column), STILL, 1))
    put(sides, 1, i, moved(wide(RATE, column), STILL, 1))
    for q in range(MEMBERS):
        if own_fed(q, column):
            continue
        if 0 <= column <= 1 or q not in LEVEL:
            put(state, q, i, moved(wide(q, column - VELOCITY[q][0]), VELOCITY[q], 1))
        elif q in LEVEL[:SUMS]:
            put(state, q, i, moved(wide(SUM_FIELDS[LEVEL.index(q)], column), STILL, 1))


def first_collision(column, own_state, state, sides, after, first):
    i = column - first
    wanted = [q for q in range(MEMBERS) if 0 <= column + VELOCITY[q][0] <= 1]
    for z, y in tiles(WIDE):
        p = state_of(own_state, state, first, column, z, y)
        level = level_of(p, column, level_sums)
        result = collide(p, level, sides[0, i, z, y], sides[1, i, z, y], wanted)
        for q in wanted:
            after[q, i, z, y] = result[q]


def seeds(wide, column, seed):
    weights = [wide(WEIGHT + k, column) for k in range(3)]
    weights = [(main, turn(extra, by, 1)) for main, extra, by in weights]
    if not 0 <= column <= 1:
        weights[0] = tuple(-value for value in weights[0])
    for q in range(1, MEMBERS):
        velocity = VELOCITY[q]
        c = column - velocity[0]
        if not 0 <= c <= 1:
            continue
        if q < 19:
            parts = [
                tuple(value if velocity[k] > 0 else -value for value in weights[k]) for k in range(3) if velocity[k]
            ]
            pair = parts[0] if len(parts) == 1 else tuple(a + b for a, b in zip(*parts))
            pair += (0,)
        else:
            pair = wide(WEIGHT + 3, column)
        put(seed, q, c, moved(pair, velocity, -1))


def own_step_kernel(flow, heat, own, strip, own_state, own_seed, begin):
    def wide(k, column):
        return own_value(own, strip, k, column)

    for column in (0, 1):
        for q in range(MEMBERS):
            if own_fed(q, column):
                put(own_state, q, column, moved(wide(q, column - VELOCITY[q][0]), VELOCITY[q], 1))
        seeds(wide, column, own_seed)
    odd = second_core()
    for c in range(2):
        for z in halves():
            terms = begin_terms(
                given_state(flow, heat, odd, c, z), own[own_row(MOBILITY, c), z, :], own[own_row(RATE, c), z, :]
            )
            for k, value in enumerate(terms):
                begin[k, c, z, :] = value


def step_kernel(
    own, strip, own_state, own_seed, from_far, from_near,
    far_state, far_sides, near_state, near_sides, adjoint, by_resistance, by_conductivity, far,
    after, near_after, later, halo_seed,
):
    def wide(k, column):
        if column < 0:
            return halo_value(from_far, BULK_ROWS, far_place(TO_FAR, k, column))
        if column > 1:
            return halo_value(from_near, BULK_ROWS, near_place(TO_NEAR, k, column))
        return own_value(own, strip, k, column)

    for column in (-1, 0):
        first_state(wide, column, far_state, far_sides, column + 1)
        first_collision(column, own_state, far_state, far_sides, after, -1)
    for column in (1, 2):
        first_state(wide, column, near_state, near_sides, column - 1)
        first_collision(column, own_state, near_state, near_sides, near_after, 1)
    for column in (-1, 2):
        seeds(wide, column, halo_seed)
    for c in range(2):
        for q in range(MEMBERS):
            column = c - VELOCITY[q][0]
            source = near_after[q, column - 1] if column >= 1 else after[q, column + 1]
            put(later, q, c, moved(split(source), VELOCITY[q], 1))
    for c in range(2):
        for z, y in tiles(WIDE):
            p = [later[q, c, z, y] for q in range(MEMBERS)]
            pa = [jnp.zeros((8, LANES), jnp.float32)]
            pa += [
                (own_seed if 0 <= c + VELOCITY[q][0] <= 1 else halo_seed)[q, c, z, y] for q in range(1, MEMBERS)
            ]
            inner = y.start == 0
            mobility, rate = [near_sides[k, 0, z, y] if c else far_sides[k, 1, z, y] for k in range(2)]
            terms = state_terms(p, level_sums(p), mobility, rate, inner)
            result = pull_back(terms, pa, level_adjoint_sums(pa), mobility, rate, range(MEMBERS), inner)
            if inner:
                by_resistance[c, z, :], by_conductivity[c, z, :] = result["by"]
            for q in range(MEMBERS):
                adjoint[q, c, z, y] = result[q]
    adjoint_buffer(adjoint, far, ADJ_TO_FAR, 0)


def adjoint_buffer(adjoint, side, rows, c):
    level = {q: moved(split(adjoint[q, c]), VELOCITY[q], -1) for q in LEVEL}
    sums = [level_adjoint_sums({q: level[q][t] for q in LEVEL}) for t in range(2)]
    parts = []
    for (k, column), row in rows.items():
        if k >= FIELDS:
            side[row] = sums[0][k - FIELDS]
            parts.append(lambda slot, k=k: packed(sums[1][k - FIELDS], slot, ADJ_EDGE))
        else:
            side[row] = adjoint[k, column, :, :LANES]
            parts.append(lambda slot, k=k, column=column: packed(adjoint[k, column, :, LANES:], slot, ADJ_EDGE))
    for k, row in enumerate(pack_rows(parts, ADJ_EDGE)):
        side[ADJ_BULK + k] = row


def near_buffer_kernel(adjoint, near):
    adjoint_buffer(adjoint, near, ADJ_TO_NEAR, 1)


TERMS = 15


def prepare_kernel(
    own_state, far_state, far_sides, near_state, near_sides, adjoint,
    terms, own_arrived, own_sums,
):
    for column in range(-1, 3):
        first, state, sides = (1, near_state, near_sides) if column >= 1 else (-1, far_state, far_sides)
        for z, y in tiles(WIDE):
            p = state_of(own_state, state, first, column, z, y)
            mobility, rate = sides[0, column - first, z, y], sides[1, column - first, z, y]
            full = y.start == 0 and 0 <= column <= 1
            values = state_terms(p, level_of(p, column, level_sums), mobility, rate, full)
            for k, value in enumerate(values):
                terms[k, column + 1, z, y] = value
    for column in range(-1, 3):
        level = {}
        for q in range(MEMBERS):
            if 0 <= column + VELOCITY[q][0] <= 1:
                pair = moved(split(adjoint[q, column + VELOCITY[q][0]]), VELOCITY[q], -1)
                put(own_arrived, q, column + 1, pair)
                if q in LEVEL:
                    level[q] = pair
        if 0 <= column <= 1:
            sums = [level_adjoint_sums({q: level[q][t] for q in LEVEL}) for t in range(2)]
            for k in range(SUMS):
                put(own_sums, k, column, (sums[0][k], sums[1][k]))


def adjoint_step(halo, column, terms, own_arrived, own_sums, sides, arrived, earlier, first, keep):
    own = 0 <= column <= 1
    i = column - first
    for q in range(MEMBERS):
        if 0 <= column + VELOCITY[q][0] <= 1:
            continue
        if q not in LEVEL:
            put(arrived, q, i, moved(halo(q, column + VELOCITY[q][0]), VELOCITY[q], -1))
        elif q in LEVEL[:SUMS]:
            put(arrived, q, i, moved(halo(SUM_FIELDS[LEVEL.index(q)], column), STILL, 1))
    for z, y in tiles(WIDE):
        inner = y.start == 0
        wanted = [
            q for q in range(MEMBERS) if 0 <= column - VELOCITY[q][0] <= 1 and (inner or VELOCITY[q][1])
        ]
        pa = [
            own_arrived[q, column + 1, z, y] if 0 <= column + VELOCITY[q][0] <= 1 else arrived[q, i, z, y]
            for q in range(MEMBERS)
        ]
        if own:
            level = [own_sums[k, column, z, y] for k in range(SUMS)]
        else:
            level = [pa[q] for q in LEVEL[:SUMS]]
        held_terms = [terms[k, column + 1, z, y] for k in range(TERMS if inner and own else TERMS - 3)]
        result = pull_back(
            held_terms, pa, level, sides[0, i, z, y], sides[1, i, z, y], wanted, inner and own
        )
        for q in wanted:
            earlier[q, i, z, y] = result[q]
        if inner and own:
            keep(z, *result["by"])


def far_adjoint_kernel(
    terms, own_arrived, own_sums, sides, part_resistance, part_conductivity, from_far,
    earlier, by_resistance, by_conductivity,
    arrived,
):
    def halo(k, column):
        return halo_value(from_far, ADJ_BULK, far_place(ADJ_TO_FAR, k, column), ADJ_EDGE)

    def keep(z, resistance, conductivity):
        by_resistance[0, z, :] = part_resistance[0, z, :] + resistance
        by_conductivity[0, z, :] = part_conductivity[0, z, :] + conductivity

    for column in (-1, 0):
        adjoint_step(halo, column, terms, own_arrived, own_sums, sides, arrived, earlier, -1, keep)
    by_resistance[1] = part_resistance[1]
    by_conductivity[1] = part_conductivity[1]


def near_adjoint_kernel(
    begin, terms, own_arrived, own_sums, sides, far_sides, far_earlier,
    part_resistance, part_conductivity, from_near,
    by_resistance, by_conductivity,
    arrived, earlier, last, sums,
):
    def halo(k, column):
        return halo_value(from_near, ADJ_BULK, near_place(ADJ_TO_NEAR, k, column), ADJ_EDGE)

    def keep(z, resistance, conductivity):
        sums[0, z, :] = part_resistance[1, z, :] + resistance
        sums[1, z, :] = part_conductivity[1, z, :] + conductivity

    for column in (1, 2):
        adjoint_step(halo, column, terms, own_arrived, own_sums, sides, arrived, earlier, 1, keep)
    for c in range(2):
        for q in range(MEMBERS):
            velocity = VELOCITY[q]
            column = c + velocity[0]
            source, i = (earlier, column - 1) if column >= 1 else (far_earlier, column + 1)
            if velocity[1]:
                last[q, c] = moved(split(source[q, i]), velocity, -1)[0]
            else:
                last[q, c] = turn(source[q, i, :, :LANES], -velocity[2], 0)
    narrow = pl.ds(0, LANES)
    odd = second_core()
    for c in range(2):
        i = c + odd * (1 - 2 * c)
        for z in halves():
            pa = [last[q, c, z, :] for q in range(MEMBERS)]
            mobility, rate = [(sides[k, 0, z, narrow] if c else far_sides[k, 1, z, narrow]) for k in range(2)]
            terms = [begin[k, c, z, :] for k in range(BEGIN)]
            resistance, conductivity = end_terms(terms, pa, mobility, rate)
            by_resistance[i, z, :] = resistance + (sums[0, z, :] if c else part_resistance[0, z, :])
            by_conductivity[i, z, :] = conductivity + (sums[1, z, :] if c else part_conductivity[0, z, :])


def floats(*shape):
    return jax.ShapeDtypeStruct(shape, jnp.float32)


def vmem(*shape):
    return pltpu.VMEM(shape, jnp.float32)


def swap_along_x(far, near):
    count = lax.axis_size("gx")
    across = [(i, (i + (1 if i % 2 else -1)) % count) for i in range(count)]
    within = [(i, i ^ 1) for i in range(count)]
    return lax.ppermute(far, "gx", across), lax.ppermute(near, "gx", within)


FIRST_PARAMS = pltpu.CompilerParams(vmem_limit_bytes=56 * 1024 * 1024)
PARAMS = pltpu.CompilerParams(vmem_limit_bytes=24 * 1024 * 1024)


def on_device(flow, heat, flow_weight, heat_weight, resistance, conductivity, solid):
    in_hbm = pl.BlockSpec(memory_space=pltpu.HBM)
    own, up, down = pl.pallas_call(
        first_kernel,
        in_specs=[in_hbm] * 7,
        out_specs=[in_hbm] * 3,
        out_shape=(
            floats(2 * FIELDS, ZED, LANES),
            floats(HALF_ROWS, ZED, LANES),
            floats(HALF_ROWS, ZED, LANES),
        ),
        scratch_shapes=[
            vmem(2 * FIELDS, ZED, LANES),
            vmem(STRIP_ROWS, ZED, LANES),
            vmem(19, 2, ZED, LANES),
            vmem(7, 2, ZED, LANES),
            vmem(3, 2, ZED, LANES),
            vmem(2, ZED, LANES),
            vmem(2, ZED, LANES),
            vmem(2, ZED, LANES),
            pltpu.VMEM((2, ZED, LANES), jnp.int32),
            pltpu.SemaphoreType.DMA((7,)),
            pltpu.SemaphoreType.DMA((3,)),
        ],
        compiler_params=FIRST_PARAMS,
        name="collide_own",
    )(flow, heat, flow_weight, heat_weight, resistance, conductivity, solid)

    count = lax.axis_size("gy")
    upward = [(i, (i + 1) % count) for i in range(count)]
    from_below = lax.ppermute(up, "gy", upward)
    from_above = lax.ppermute(down, "gy", [(target, source) for source, target in upward])

    own = pl.pallas_call(
        stage_kernel,
        out_shape=floats(2 * FIELDS, ZED, LANES),
        compiler_params=PARAMS,
        cost_estimate=pl.CostEstimate(flops=10**7, bytes_accessed=10**6, transcendentals=0),
        name="stage_own",
    )(own)

    far, strip = pl.pallas_call(
        far_halo_kernel,
        out_shape=(floats(SENT, ZED, LANES), floats(STRIP_ROWS, ZED, LANES)),
        compiler_params=PARAMS,
        name="far_halo",
    )(own, from_below, from_above)
    near = pl.pallas_call(
        near_halo_kernel,
        out_shape=floats(SENT, ZED, LANES),
        compiler_params=PARAMS,
        name="near_halo",
    )(own, strip)

    from_far, from_near = swap_along_x(far, near)

    columns = floats(MEMBERS, 2, ZED, WIDE)
    side_columns = floats(2, 2, ZED, WIDE)
    cells = floats(2, ZED, LANES)
    held = vmem(MEMBERS, 2, ZED, WIDE)
    busy = pl.CostEstimate(flops=10**7, bytes_accessed=10**6, transcendentals=0)

    own_state, own_seed, begin = pl.pallas_call(
        own_step_kernel,
        out_shape=(columns, columns, floats(BEGIN, 2, ZED, LANES)),
        compiler_params=PARAMS,
        cost_estimate=busy,
        name="own_step",
    )(flow, heat, own, strip)

    far_state, far_sides, near_state, near_sides, adjoint, part_resistance, part_conductivity, far = (
        pl.pallas_call(
            step_kernel,
            out_shape=(
                columns, side_columns, columns, side_columns, columns, cells, cells,
                floats(ADJ_SENT, ZED, LANES),
            ),
            scratch_shapes=[held, held, held, held],
            compiler_params=PARAMS,
            name="two_steps",
        )(own, strip, own_state, own_seed, from_far, from_near)
    )

    near = pl.pallas_call(
        near_buffer_kernel,
        out_shape=floats(ADJ_SENT, ZED, LANES),
        compiler_params=PARAMS,
        name="near_buffer",
    )(adjoint)

    from_far, from_near = swap_along_x(far, near)

    terms, own_arrived, own_sums = pl.pallas_call(
        prepare_kernel,
        out_shape=(
            floats(TERMS, 4, ZED, WIDE), floats(MEMBERS, 4, ZED, WIDE), floats(SUMS, 2, ZED, WIDE),
        ),
        compiler_params=PARAMS,
        cost_estimate=busy,
        name="prepare",
    )(own_state, far_state, far_sides, near_state, near_sides, adjoint)

    far_earlier, part_resistance, part_conductivity = pl.pallas_call(
        far_adjoint_kernel,
        out_shape=(columns, cells, cells),
        scratch_shapes=[held],
        compiler_params=PARAMS,
        cost_estimate=busy,
        name="far_adjoint",
    )(terms, own_arrived, own_sums, far_sides, part_resistance, part_conductivity, from_far)

    return pl.pallas_call(
        near_adjoint_kernel,
        out_shape=(cells, cells),
        scratch_shapes=[held, held, vmem(MEMBERS, 2, ZED, LANES), vmem(2, ZED, LANES)],
        compiler_params=PARAMS,
        name="near_adjoint",
    )(
        begin, terms, own_arrived, own_sums, near_sides, far_sides, far_earlier,
        part_resistance, part_conductivity, from_near,
    )


def solution(mesh):
    split = P("gx", None, "gy")
    stacked = P(None, "gx", None, "gy")
    return jax.shard_map(
        on_device,
        mesh=mesh,
        in_specs=(stacked, stacked, stacked, split, split, split, split),
        out_specs=(split, split),
        check_vma=False,
    )
```

```python
import jax
import jax.numpy as jnp
from jax import lax
from jax.experimental import pallas as pl
from jax.experimental.pallas import tpu as pltpu
from jax.sharding import PartitionSpec as P

ZED = 16
LANES = 128
WIDE = 2 * LANES
EDGE = 4

FLOW_VELOCITY = [
    (0, 0, 0),
    (1, 0, 0),
    (-1, 0, 0),
    (0, 1, 0),
    (0, -1, 0),
    (0, 0, 1),
    (0, 0, -1),
    (1, 1, 0),
    (-1, -1, 0),
    (1, -1, 0),
    (-1, 1, 0),
    (1, 0, 1),
    (-1, 0, -1),
    (1, 0, -1),
    (-1, 0, 1),
    (0, 1, 1),
    (0, -1, -1),
    (0, 1, -1),
    (0, -1, 1),
]
VELOCITY = FLOW_VELOCITY + FLOW_VELOCITY[:7]
STILL = (0, 0, 0)
MEMBERS = len(VELOCITY)
RIGHTWARD = [q for q in range(MEMBERS) if VELOCITY[q][0] == 1]
LEFTWARD = [q for q in range(MEMBERS) if VELOCITY[q][0] == -1]
LEVEL = [q for q in range(MEMBERS) if VELOCITY[q][0] == 0]


def mirrored(q):
    x, y, z = VELOCITY[q]
    start = 0 if q < 19 else 19
    return start + FLOW_VELOCITY.index((-x, y, z))


MOBILITY, RATE, WEIGHT = MEMBERS, MEMBERS + 1, MEMBERS + 2
FIELDS = MEMBERS + 6
SIDE_FIELDS = list(range(MEMBERS, FIELDS))

SUMS = 9
SUM_FIELDS = [FIELDS + k for k in range(SUMS)]

ADJ_EDGE = 2
SLOTS = LANES // (2 * EDGE)
STRIP_ROWS = 2 * FIELDS // SLOTS
HALF_ROWS = STRIP_ROWS // 2


def rows_of(entries):
    return {entry: row for row, entry in enumerate(entries)}


TO_NEAR = rows_of([(q, 0) for q in RIGHTWARD] + [(k, 1) for k in RIGHTWARD + SIDE_FIELDS + SUM_FIELDS])
TO_FAR = rows_of([(q, 1) for q in LEFTWARD] + [(k, 0) for k in LEFTWARD + SIDE_FIELDS + SUM_FIELDS])
ADJ_TO_NEAR = rows_of([(q, 0) for q in LEFTWARD] + [(k, 1) for k in LEFTWARD + SUM_FIELDS])
ADJ_TO_FAR = rows_of([(q, 1) for q in RIGHTWARD] + [(k, 0) for k in RIGHTWARD + SUM_FIELDS])
BULK_ROWS, ADJ_BULK = len(TO_NEAR), len(ADJ_TO_NEAR)


def with_strips(bulk, edge):
    return bulk + -(-bulk * 2 * edge // LANES)


SENT, ADJ_SENT = with_strips(BULK_ROWS, EDGE), with_strips(ADJ_BULK, ADJ_EDGE)


def level_sums(p):
    s1, s2, d1, d2 = p[3] + p[4], p[5] + p[6], p[3] - p[4], p[5] - p[6]
    s7, s8, d7, d8 = p[15] + p[16], p[17] + p[18], p[15] - p[16], p[17] - p[18]
    yz = s7 + s8
    mass = p[0] + (s1 + s2) + yz
    return [
        mass, d1 + (d7 + d8), d2 + (d7 - d8), s1 + yz, s2 + yz, s7 - s8,
        p[19] + (p[22] + p[23]) + (p[24] + p[25]), p[22] - p[23], p[24] - p[25],
    ]


def level_adjoint_sums(p):
    s1, s2, d1, d2 = p[3] + p[4], p[5] + p[6], p[3] - p[4], p[5] - p[6]
    s7, s8, d7, d8 = p[15] + p[16], p[17] + p[18], p[15] - p[16], p[17] - p[18]
    yz = s7 + s8
    t1, t2 = s1 + s1, s2 + s2
    mass = 12.0 * p[0] + (t1 + t2) + yz
    return [
        mass, (d1 + d1) + (d7 + d8), (d2 + d2) + (d7 - d8), t1 + yz, t2 + yz, s7 - s8,
        0.35 * p[19] + 0.175 * ((p[22] + p[23]) + (p[24] + p[25])),
        0.125 * (p[22] - p[23]), 0.125 * (p[24] - p[25]),
    ]


def cross_sums(p):
    pairs = [(1, 2), (7, 8), (9, 10), (11, 12), (13, 14)]
    return [p[a] + p[b] for a, b in pairs], [p[a] - p[b] for a, b in pairs]


def common(p, level, mobility):
    s, d = cross_sums(p)
    xy, xz = s[1] + s[2], s[3] + s[4]
    along = s[0] + xy + xz
    rho = level[0] + along
    j = (d[0] + (d[1] + d[2]) + (d[3] + d[4]), level[1] + (d[1] - d[2]), level[2] + (d[3] - d[4]))
    temperature = level[6] + (p[20] + p[21])
    flux = (p[20] - p[21], level[7], level[8])
    u = tuple(mobility * jk for jk in j)
    square = (u[0] * u[0], u[1] * u[1], u[2] * u[2])
    third = rho * (1.0 / 3.0)
    stress = (
        along - third - square[0],
        (level[3] + xy) - third - square[1],
        (level[4] + xz) - third - square[2],
        (s[1] - s[2]) - u[0] * u[1],
        (s[3] - s[4]) - u[0] * u[2],
        level[5] - u[1] * u[2],
    )
    decay = jnp.exp(-2.0 * (temperature - 1.0))
    omega = 1.0 / (0.5 + 0.3 * decay)
    return rho, j, u, square, stress, temperature, flux, decay, omega


def collide(p, level, mobility, rate, wanted):
    rho, _, u, square, stress, temperature, flux, _, omega = common(p, level, mobility)
    solid = mobility == 0.0
    lam = 1.2 - omega
    trace = stress[0] + stress[1] + stress[2]
    base = 1.2 * rho - 1.8 * (square[0] + square[1] + square[2]) - (1.5 * lam) * trace
    scale = 4.5 * lam
    mxx = 5.4 * square[0] + scale * stress[0]
    myy = 5.4 * square[1] + scale * stress[1]
    mzz = 5.4 * square[2] + scale * stress[2]
    mxy = 2.0 * (5.4 * (u[0] * u[1]) + scale * stress[3])
    mxz = 2.0 * (5.4 * (u[0] * u[2]) + scale * stress[4])
    myz = 2.0 * (5.4 * (u[1] * u[2]) + scale * stress[5])
    bx, by, bz = base + mxx, base + myy, base + mzz
    sxy, sxz, syz = bx + myy, bx + mzz, by + mzz
    even = [bx, by, bz, sxy + mxy, sxy - mxy, sxz + mxz, sxz - mxz, syz + myz, syz - myz]
    odd = [u[0], u[1], u[2], u[0] + u[1], u[0] - u[1], u[0] + u[2], u[0] - u[2], u[1] + u[2], u[1] - u[2]]
    result = {}
    if 0 in wanted:
        result[0] = jnp.where(solid, p[0], (1.0 / 3.0) * base - 0.2 * p[0])
    for k in range(9):
        a, b = 2 * k + 1, 2 * k + 2
        w = 1.0 / 18.0 if k < 3 else 1.0 / 36.0
        e, o = w * even[k], (3.6 * w) * odd[k]
        if a in wanted:
            result[a] = jnp.where(solid, p[b], (e + o) - 0.2 * p[a])
        if b in wanted:
            result[b] = jnp.where(solid, p[a], (e - o) - 0.2 * p[b])
    keep = 0.5 * (1.4 - rate)
    push = (0.5 * rate) * temperature
    warm = 0.175 * temperature
    if 19 in wanted:
        result[19] = 0.35 * temperature - 0.4 * p[19]
    for k in range(3):
        along = keep * flux[k] + push * u[k]
        a, b = 20 + 2 * k, 21 + 2 * k
        if a in wanted:
            result[a] = (warm + along) - 0.4 * p[a]
        if b in wanted:
            result[b] = (warm - along) - 0.4 * p[b]
    return result


def state_terms(p, level, mobility, rate, full):
    _, _, u, _, stress, temperature, flux, decay, omega = common(p, level, mobility)
    slope = jnp.where(mobility == 0.0, 0.0, (0.6 * decay) * (omega * omega))
    terms = list(u) + list(stress) + [1.2 - omega, (4.0 * rate) * temperature, slope]
    return terms + [temperature * u[k] - flux[k] for k in range(3)] if full else terms


def pull_back(terms, pa, adjoint_level, mobility, rate, wanted, sensitivity):
    u, stress, lam, push, slope, bent = terms[:3], terms[3:9], terms[9], terms[10], terms[11], terms[12:]
    solid = mobility == 0.0
    s, d = cross_sums(pa)
    w = 1.0 / 36.0
    xy, xz = s[1] + s[2], s[3] + s[4]
    along = (s[0] + s[0]) + xy + xz
    mass = w * (adjoint_level[0] + along)
    px = w * ((d[0] + d[0]) + (d[1] + d[2]) + (d[3] + d[4]))
    py = w * (adjoint_level[1] + (d[1] - d[2]))
    pz = w * (adjoint_level[2] + (d[3] - d[4]))
    rxx, ryy, rzz = w * along, w * (adjoint_level[3] + xy), w * (adjoint_level[4] + xz)
    rxy, rxz, ryz = w * (s[1] - s[2]), w * (s[3] - s[4]), w * adjoint_level[5]
    shift = 1.5 * mass
    dxx, dyy, dzz = 4.5 * rxx - shift, 4.5 * ryy - shift, 4.5 * rzz - shift
    dxy, dxz, dyz = 4.5 * rxy, 4.5 * rxz, 4.5 * ryz
    mix = 2.4 - 2.0 * lam
    b = ((pa[20] - pa[21]) * 0.125, adjoint_level[7], adjoint_level[8])
    ux = 3.6 * px + mix * (dxx * u[0] + dxy * u[1] + dxz * u[2]) + push * b[0]
    uy = 3.6 * py + mix * (dxy * u[0] + dyy * u[1] + dyz * u[2]) + push * b[1]
    uz = 3.6 * pz + mix * (dxz * u[0] + dyz * u[1] + dzz * u[2]) + push * b[2]
    result = {}
    if wanted:
        lam_bar = (
            dxx * stress[0]
            + dyy * stress[1]
            + dzz * stress[2]
            + 2.0 * (dxy * stress[3] + dxz * stress[4] + dyz * stress[5])
        )
        rho_bar = 1.2 * mass - (1.5 * lam) * ((rxx + ryy + rzz) - mass)
        jx, jy, jz = mobility * ux, mobility * uy, mobility * uz
        ex, ey, ez = lam * dxx, lam * dyy, lam * dzz
        exy, exz, eyz = (2.0 * lam) * dxy, (2.0 * lam) * dxz, (2.0 * lam) * dyz
        hx, hy, hz = rho_bar + ex, rho_bar + ey, rho_bar + ez
        gxy, gxz, gyz = hx + ey, hx + ez, hy + ez
        even = [hx, hy, hz, gxy + exy, gxy - exy, gxz + exz, gxz - exz, gyz + eyz, gyz - eyz]
        odd = [jx, jy, jz, jx + jy, jx - jy, jx + jz, jx - jz, jy + jz, jy - jz]
        if 0 in wanted:
            result[0] = jnp.where(solid, pa[0], rho_bar - 0.2 * pa[0])
        for k in range(9):
            a, m = 2 * k + 1, 2 * k + 2
            if a in wanted:
                result[a] = jnp.where(solid, pa[m], (even[k] + odd[k]) - 0.2 * pa[a])
            if m in wanted:
                result[m] = jnp.where(solid, pa[a], (even[k] - odd[k]) - 0.2 * pa[m])
        warm = (
            adjoint_level[6]
            + 0.175 * (pa[20] + pa[21])
            + (4.0 * rate) * (b[0] * u[0] + b[1] * u[1] + b[2] * u[2])
            - lam_bar * slope
        )
        keep = 5.6 - 4.0 * rate
        if 19 in wanted:
            result[19] = warm - 0.4 * pa[19]
        for k in range(3):
            along = keep * b[k]
            a, m = 20 + 2 * k, 21 + 2 * k
            if a in wanted:
                result[a] = (warm + along) - 0.4 * pa[a]
            if m in wanted:
                result[m] = (warm - along) - 0.4 * pa[m]
    if sensitivity:
        by_resistance = -mobility * (ux * u[0] + uy * u[1] + uz * u[2])
        by_conductivity = (-1.6 * (rate * rate)) * (b[0] * bent[0] + b[1] * bent[1] + b[2] * bent[2])
        result["by"] = (by_resistance, by_conductivity)
    return result


BEGIN = 8


def begin_terms(p, mobility, rate):
    _, _, u, _, _, temperature, flux, _, omega = common(p, level_sums(p), mobility)
    bent = [temperature * u[k] - flux[k] for k in range(3)]
    return list(u) + bent + [2.4 - 2.0 * (1.2 - omega), (4.0 * rate) * temperature]


def end_terms(terms, pa, mobility, rate):
    u, bent, mix, push = terms[:3], terms[3:6], terms[6], terms[7]
    level = level_adjoint_sums(pa)
    s, d = cross_sums(pa)
    w = 1.0 / 36.0
    xy, xz = s[1] + s[2], s[3] + s[4]
    along = (s[0] + s[0]) + xy + xz
    shift = (1.5 * w) * (level[0] + along)
    v = 4.5 * w
    dxx, dyy, dzz = v * along - shift, v * (level[3] + xy) - shift, v * (level[4] + xz) - shift
    dxy, dxz, dyz = v * (s[1] - s[2]), v * (s[3] - s[4]), v * level[5]
    px = (d[0] + d[0]) + (d[1] + d[2]) + (d[3] + d[4])
    py = level[1] + (d[1] - d[2])
    pz = level[2] + (d[3] - d[4])
    b = ((pa[20] - pa[21]) * 0.125, level[7], level[8])
    ux = (3.6 * w) * px + mix * (dxx * u[0] + dxy * u[1] + dxz * u[2]) + push * b[0]
    uy = (3.6 * w) * py + mix * (dxy * u[0] + dyy * u[1] + dyz * u[2]) + push * b[1]
    uz = (3.6 * w) * pz + mix * (dxz * u[0] + dyz * u[1] + dzz * u[2]) + push * b[2]
    by_resistance = -mobility * (ux * u[0] + uy * u[1] + uz * u[2])
    by_conductivity = (-1.6 * (rate * rate)) * (b[0] * bent[0] + b[1] * bent[1] + b[2] * bent[2])
    return by_resistance, by_conductivity


def turn(value, by, axis):
    count = value.shape[axis]
    by %= count
    return pltpu.roll(value, by, axis) if by else value


def side_by_side(parts, edge):
    lane = lax.broadcasted_iota(jnp.int32, (ZED, LANES), 1)
    row = None
    for slot, part in enumerate(parts):
        row = part if row is None else jnp.where(lane >= 2 * edge * slot, part, row)
    return row


def packed(value, slot, edge=EDGE):
    return turn(value, 2 * edge * slot + edge, 1)


def pack_rows(parts, edge=EDGE):
    slots = LANES // (2 * edge)
    return [
        side_by_side([part(slot) for slot, part in enumerate(parts[start : start + slots])], edge)
        for start in range(0, len(parts), slots)
    ]


def halves():
    return [pl.ds(0, 8), pl.ds(8, 8)]


def low_lanes():
    return lax.broadcasted_iota(jnp.int32, (ZED, LANES), 1) % (2 * EDGE) < EDGE


def second_core():
    return lax.rem(lax.axis_index("gx"), 2)


def framed(q, odd):
    return q + odd * (mirrored(q) - q)


def copy_rows(target, source):
    for row in range(source.shape[0]):
        target[row] = source[row]


def split(value):
    return value[:, :LANES], value[:, LANES:], 0


def beside(row, slot, edge=EDGE):
    return row, -edge - 2 * edge * slot


def moved(triple, velocity, way):
    main, extra, by = triple
    _, step_y, step_z = velocity
    step = way * step_y
    main, extra = turn(main, way * step_z, 0), turn(extra, way * step_z, 0)
    if not step:
        return main, turn(extra, by, 1)
    main, extra = turn(main, step, 1), turn(extra, by + step, 1)
    lane = lax.broadcasted_iota(jnp.int32, (ZED, LANES), 1)
    edge = lane == (0 if step == 1 else LANES - 1)
    return jnp.where(edge, extra, main), jnp.where(edge, main, extra)


def put(ref, q, i, pair):
    ref[q, i, :, :LANES], ref[q, i, :, LANES:] = pair


def tiles(lanes):
    return [(z, pl.ds(t, LANES)) for z in halves() for t in range(0, lanes, LANES)]


def own_row(k, c):
    return c * FIELDS + k


def own_value(own, strip, k, c):
    place = own_row(k, c)
    return (own[place],) + beside(strip[place // SLOTS], place % SLOTS)


def halo_value(buffer, bulk, place, edge=EDGE):
    slots = LANES // (2 * edge)
    return (buffer[place],) + beside(buffer[bulk + place // slots], place % slots, edge)


def given_state(flow, heat, odd, c, z):
    i = c + odd * (1 - 2 * c)
    return [flow[framed(q, odd), i, z, :] for q in range(19)] + [
        heat[framed(q, odd) - 19, i, z, :] for q in range(19, MEMBERS)
    ]


def first_kernel(
    flow_in, heat_in, flow_weight_in, heat_weight_in, resistance_in, conductivity_in, solid_in,
    own_out, up_out, down_out,
    own, strips, flow, heat, flow_weight, heat_weight, resistance, conductivity, solid, arrived, sent,
):
    pairs = [
        (flow_in, flow),
        (heat_in, heat),
        (resistance_in, resistance),
        (conductivity_in, conductivity),
        (solid_in, solid),
        (flow_weight_in, flow_weight),
        (heat_weight_in, heat_weight),
    ]
    copies = [pltpu.make_async_copy(a, b, arrived.at[k]) for k, (a, b) in enumerate(pairs)]
    for copy in copies:
        copy.start()
    for copy in copies:
        copy.wait()
    odd = second_core()
    sign = (1 - 2 * odd).astype(jnp.float32)
    for c in range(2):
        i = c + odd * (1 - 2 * c)
        for z in halves():
            mobility = jnp.where(solid[i, z, :] != 0, 0.0, 1.0 / (1.0 + resistance[i, z, :]))
            rate = 1.0 / (0.5 + 0.4 * conductivity[i, z, :])
            p = given_state(flow, heat, odd, c, z)
            after = collide(p, level_sums(p), mobility, rate, range(MEMBERS))
            more = [mobility, rate, sign * flow_weight[0, i, z, :]]
            more += [flow_weight[1, i, z, :], flow_weight[2, i, z, :], heat_weight[i, z, :]]
            for k, value in enumerate([after[q] for q in range(MEMBERS)] + more):
                own[own_row(k, c), z, :] = value
    copy_own = pltpu.make_async_copy(own, own_out, sent.at[0])
    copy_own.start()
    rows = pack_rows([lambda slot, k=k: packed(own[k], slot) for k in range(2 * FIELDS)])
    low = low_lanes()
    for k in range(HALF_ROWS):
        strips[k] = jnp.where(low, rows[k], turn(rows[k + HALF_ROWS], EDGE, 1))
        strips[k + HALF_ROWS] = jnp.where(low, turn(rows[k], -EDGE, 1), rows[k + HALF_ROWS])
    copies = [
        pltpu.make_async_copy(strips.at[pl.ds(0, HALF_ROWS)], up_out, sent.at[1]),
        pltpu.make_async_copy(strips.at[pl.ds(HALF_ROWS, HALF_ROWS)], down_out, sent.at[2]),
    ]
    for copy in copies:
        copy.start()
    copy_own.wait()
    for copy in copies:
        copy.wait()


def stage_kernel(own, staged):
    copy_rows(staged, own)


def halo_buffer(own, strip, side, rows, c):
    level = {q: moved(own_value(own, strip, q, c), VELOCITY[q], 1) for q in LEVEL}
    sums = [level_sums({q: level[q][t] for q in LEVEL}) for t in range(2)]
    parts = []
    for (k, column), row in rows.items():
        if k >= FIELDS:
            side[row] = sums[0][k - FIELDS]
            parts.append(lambda slot, k=k: packed(sums[1][k - FIELDS], slot))
        else:
            place = own_row(k, column)
            side[row] = own[place]
            parts.append(
                lambda slot, place=place: turn(
                    strip[place // SLOTS], 2 * EDGE * (slot - place % SLOTS), 1
                )
            )
    for k, row in enumerate(pack_rows(parts)):
        side[BULK_ROWS + k] = row


def far_halo_kernel(own, from_below, from_above, far, strip):
    low = low_lanes()
    for k in range(HALF_ROWS):
        under, over = from_below[k], from_above[k]
        strip[k] = jnp.where(low, under, turn(over, EDGE, 1))
        strip[k + HALF_ROWS] = jnp.where(low, turn(under, -EDGE, 1), over)
    halo_buffer(own, strip, far, TO_FAR, 0)


def near_halo_kernel(own, strip, near):
    halo_buffer(own, strip, near, TO_NEAR, 1)


def level_of(p, column, sums):
    return sums(p) if 0 <= column <= 1 else [p[q] for q in LEVEL[:SUMS]]


def near_place(rows, k, column):
    return rows[mirrored(k) if k < MEMBERS else k, 3 - column]


def far_place(rows, k, column):
    return rows[mirrored(k) if k < MEMBERS else k, -1 - column]


def own_fed(q, column):
    return 0 <= column <= 1 and 0 <= column - VELOCITY[q][0] <= 1


def state_of(own_state, state, first, column, z, y):
    return [
        own_state[q, column, z, y] if own_fed(q, column) else state[q, column - first, z, y]
        for q in range(MEMBERS)
    ]


def first_state(wide, column, state, sides, i):
    put(sides, 0, i, moved(wide(MOBILITY, column), STILL, 1))
    put(sides, 1, i, moved(wide(RATE, column), STILL, 1))
    for q in range(MEMBERS):
        if own_fed(q, column):
            continue
        if 0 <= column <= 1 or q not in LEVEL:
            put(state, q, i, moved(wide(q, column - VELOCITY[q][0]), VELOCITY[q], 1))
        elif q in LEVEL[:SUMS]:
            put(state, q, i, moved(wide(SUM_FIELDS[LEVEL.index(q)], column), STILL, 1))


def first_collision(column, own_state, state, sides, after, first):
    i = column - first
    wanted = [q for q in range(MEMBERS) if 0 <= column + VELOCITY[q][0] <= 1]
    for z, y in tiles(WIDE):
        p = state_of(own_state, state, first, column, z, y)
        level = level_of(p, column, level_sums)
        result = collide(p, level, sides[0, i, z, y], sides[1, i, z, y], wanted)
        for q in wanted:
            after[q, i, z, y] = result[q]


def seeds(wide, column, seed):
    weights = [wide(WEIGHT + k, column) for k in range(3)]
    weights = [(main, turn(extra, by, 1)) for main, extra, by in weights]
    if not 0 <= column <= 1:
        weights[0] = tuple(-value for value in weights[0])
    for q in range(1, MEMBERS):
        velocity = VELOCITY[q]
        c = column - velocity[0]
        if not 0 <= c <= 1:
            continue
        if q < 19:
            parts = [
                tuple(value if velocity[k] > 0 else -value for value in weights[k]) for k in range(3) if velocity[k]
            ]
            pair = parts[0] if len(parts) == 1 else tuple(a + b for a, b in zip(*parts))
            pair += (0,)
        else:
            pair = wide(WEIGHT + 3, column)
        put(seed, q, c, moved(pair, velocity, -1))


def own_step_kernel(flow, heat, own, strip, own_state, own_seed, begin):
    def wide(k, column):
        return own_value(own, strip, k, column)

    for column in (0, 1):
        for q in range(MEMBERS):
            if own_fed(q, column):
                put(own_state, q, column, moved(wide(q, column - VELOCITY[q][0]), VELOCITY[q], 1))
        seeds(wide, column, own_seed)
    odd = second_core()
    for c in range(2):
        for z in halves():
            terms = begin_terms(
                given_state(flow, heat, odd, c, z), own[own_row(MOBILITY, c), z, :], own[own_row(RATE, c), z, :]
            )
            for k, value in enumerate(terms):
                begin[k, c, z, :] = value


def step_kernel(
    own, strip, own_state, own_seed, from_far, from_near,
    far_state, far_sides, near_state, near_sides, adjoint, by_resistance, by_conductivity, far,
    after, near_after, later, halo_seed,
):
    def wide(k, column):
        if column < 0:
            return halo_value(from_far, BULK_ROWS, far_place(TO_FAR, k, column))
        if column > 1:
            return halo_value(from_near, BULK_ROWS, near_place(TO_NEAR, k, column))
        return own_value(own, strip, k, column)

    for column in (-1, 0):
        first_state(wide, column, far_state, far_sides, column + 1)
        first_collision(column, own_state, far_state, far_sides, after, -1)
    for column in (1, 2):
        first_state(wide, column, near_state, near_sides, column - 1)
        first_collision(column, own_state, near_state, near_sides, near_after, 1)
    for column in (-1, 2):
        seeds(wide, column, halo_seed)
    for c in range(2):
        for q in range(MEMBERS):
            column = c - VELOCITY[q][0]
            source = near_after[q, column - 1] if column >= 1 else after[q, column + 1]
            put(later, q, c, moved(split(source), VELOCITY[q], 1))
    for c in range(2):
        for z, y in tiles(WIDE):
            p = [later[q, c, z, y] for q in range(MEMBERS)]
            pa = [jnp.zeros((8, LANES), jnp.float32)]
            pa += [
                (own_seed if 0 <= c + VELOCITY[q][0] <= 1 else halo_seed)[q, c, z, y] for q in range(1, MEMBERS)
            ]
            inner = y.start == 0
            mobility, rate = [near_sides[k, 0, z, y] if c else far_sides[k, 1, z, y] for k in range(2)]
            terms = state_terms(p, level_sums(p), mobility, rate, inner)
            result = pull_back(terms, pa, level_adjoint_sums(pa), mobility, rate, range(MEMBERS), inner)
            if inner:
                by_resistance[c, z, :], by_conductivity[c, z, :] = result["by"]
            for q in range(MEMBERS):
                adjoint[q, c, z, y] = result[q]
    adjoint_buffer(adjoint, far, ADJ_TO_FAR, 0)


def adjoint_buffer(adjoint, side, rows, c):
    level = {q: moved(split(adjoint[q, c]), VELOCITY[q], -1) for q in LEVEL}
    sums = [level_adjoint_sums({q: level[q][t] for q in LEVEL}) for t in range(2)]
    parts = []
    for (k, column), row in rows.items():
        if k >= FIELDS:
            side[row] = sums[0][k - FIELDS]
            parts.append(lambda slot, k=k: packed(sums[1][k - FIELDS], slot, ADJ_EDGE))
        else:
            side[row] = adjoint[k, column, :, :LANES]
            parts.append(lambda slot, k=k, column=column: packed(adjoint[k, column, :, LANES:], slot, ADJ_EDGE))
    for k, row in enumerate(pack_rows(parts, ADJ_EDGE)):
        side[ADJ_BULK + k] = row


def near_buffer_kernel(adjoint, near):
    adjoint_buffer(adjoint, near, ADJ_TO_NEAR, 1)


TERMS = 15


def prepare_kernel(
    own_state, far_state, far_sides, near_state, near_sides, adjoint,
    terms, own_arrived, own_sums,
):
    for column in range(-1, 3):
        first, state, sides = (1, near_state, near_sides) if column >= 1 else (-1, far_state, far_sides)
        for z, y in tiles(WIDE):
            p = state_of(own_state, state, first, column, z, y)
            mobility, rate = sides[0, column - first, z, y], sides[1, column - first, z, y]
            full = y.start == 0 and 0 <= column <= 1
            values = state_terms(p, level_of(p, column, level_sums), mobility, rate, full)
            for k, value in enumerate(values):
                terms[k, column + 1, z, y] = value
    for column in range(-1, 3):
        level = {}
        for q in range(MEMBERS):
            if 0 <= column + VELOCITY[q][0] <= 1:
                pair = moved(split(adjoint[q, column + VELOCITY[q][0]]), VELOCITY[q], -1)
                put(own_arrived, q, column + 1, pair)
                if q in LEVEL:
                    level[q] = pair
        if 0 <= column <= 1:
            sums = [level_adjoint_sums({q: level[q][t] for q in LEVEL}) for t in range(2)]
            for k in range(SUMS):
                put(own_sums, k, column, (sums[0][k], sums[1][k]))


def adjoint_step(halo, column, terms, own_arrived, own_sums, sides, arrived, earlier, first, keep):
    own = 0 <= column <= 1
    i = column - first
    for q in range(MEMBERS):
        if 0 <= column + VELOCITY[q][0] <= 1:
            continue
        if q not in LEVEL:
            put(arrived, q, i, moved(halo(q, column + VELOCITY[q][0]), VELOCITY[q], -1))
        elif q in LEVEL[:SUMS]:
            put(arrived, q, i, moved(halo(SUM_FIELDS[LEVEL.index(q)], column), STILL, 1))
    for z, y in tiles(WIDE):
        inner = y.start == 0
        wanted = [
            q for q in range(MEMBERS) if 0 <= column - VELOCITY[q][0] <= 1 and (inner or VELOCITY[q][1])
        ]
        pa = [
            own_arrived[q, column + 1, z, y] if 0 <= column + VELOCITY[q][0] <= 1 else arrived[q, i, z, y]
            for q in range(MEMBERS)
        ]
        if own:
            level = [own_sums[k, column, z, y] for k in range(SUMS)]
        else:
            level = [pa[q] for q in LEVEL[:SUMS]]
        held_terms = [terms[k, column + 1, z, y] for k in range(TERMS if inner and own else TERMS - 3)]
        result = pull_back(
            held_terms, pa, level, sides[0, i, z, y], sides[1, i, z, y], wanted, inner and own
        )
        for q in wanted:
            earlier[q, i, z, y] = result[q]
        if inner and own:
            keep(z, *result["by"])


def far_adjoint_kernel(
    terms, own_arrived, own_sums, sides, part_resistance, part_conductivity, from_far,
    earlier, by_resistance, by_conductivity,
    arrived,
):
    def halo(k, column):
        return halo_value(from_far, ADJ_BULK, far_place(ADJ_TO_FAR, k, column), ADJ_EDGE)

    def keep(z, resistance, conductivity):
        by_resistance[0, z, :] = part_resistance[0, z, :] + resistance
        by_conductivity[0, z, :] = part_conductivity[0, z, :] + conductivity

    for column in (-1, 0):
        adjoint_step(halo, column, terms, own_arrived, own_sums, sides, arrived, earlier, -1, keep)
    by_resistance[1] = part_resistance[1]
    by_conductivity[1] = part_conductivity[1]


def near_adjoint_kernel(
    begin, terms, own_arrived, own_sums, sides, far_sides, far_earlier,
    part_resistance, part_conductivity, from_near,
    by_resistance, by_conductivity,
    arrived, earlier, last, sums,
):
    def halo(k, column):
        return halo_value(from_near, ADJ_BULK, near_place(ADJ_TO_NEAR, k, column), ADJ_EDGE)

    def keep(z, resistance, conductivity):
        sums[0, z, :] = part_resistance[1, z, :] + resistance
        sums[1, z, :] = part_conductivity[1, z, :] + conductivity

    for column in (1, 2):
        adjoint_step(halo, column, terms, own_arrived, own_sums, sides, arrived, earlier, 1, keep)
    for c in range(2):
        for q in range(MEMBERS):
            velocity = VELOCITY[q]
            column = c + velocity[0]
            source, i = (earlier, column - 1) if column >= 1 else (far_earlier, column + 1)
            if velocity[1]:
                last[q, c] = moved(split(source[q, i]), velocity, -1)[0]
            else:
                last[q, c] = turn(source[q, i, :, :LANES], -velocity[2], 0)
    narrow = pl.ds(0, LANES)
    odd = second_core()
    for c in range(2):
        i = c + odd * (1 - 2 * c)
        for z in halves():
            pa = [last[q, c, z, :] for q in range(MEMBERS)]
            mobility, rate = [(sides[k, 0, z, narrow] if c else far_sides[k, 1, z, narrow]) for k in range(2)]
            terms = [begin[k, c, z, :] for k in range(BEGIN)]
            resistance, conductivity = end_terms(terms, pa, mobility, rate)
            by_resistance[i, z, :] = resistance + (sums[0, z, :] if c else part_resistance[0, z, :])
            by_conductivity[i, z, :] = conductivity + (sums[1, z, :] if c else part_conductivity[0, z, :])


def floats(*shape):
    return jax.ShapeDtypeStruct(shape, jnp.float32)


def vmem(*shape):
    return pltpu.VMEM(shape, jnp.float32)


def swap_along_x(far, near):
    count = lax.axis_size("gx")
    across = [(i, (i + (1 if i % 2 else -1)) % count) for i in range(count)]
    within = [(i, i ^ 1) for i in range(count)]
    return lax.ppermute(far, "gx", across), lax.ppermute(near, "gx", within)


FIRST_PARAMS = pltpu.CompilerParams(vmem_limit_bytes=56 * 1024 * 1024)
PARAMS = pltpu.CompilerParams(vmem_limit_bytes=24 * 1024 * 1024)


def on_device(flow, heat, flow_weight, heat_weight, resistance, conductivity, solid):
    in_hbm = pl.BlockSpec(memory_space=pltpu.HBM)
    own, up, down = pl.pallas_call(
        first_kernel,
        in_specs=[in_hbm] * 7,
        out_specs=[in_hbm] * 3,
        out_shape=(
            floats(2 * FIELDS, ZED, LANES),
            floats(HALF_ROWS, ZED, LANES),
            floats(HALF_ROWS, ZED, LANES),
        ),
        scratch_shapes=[
            vmem(2 * FIELDS, ZED, LANES),
            vmem(STRIP_ROWS, ZED, LANES),
            vmem(19, 2, ZED, LANES),
            vmem(7, 2, ZED, LANES),
            vmem(3, 2, ZED, LANES),
            vmem(2, ZED, LANES),
            vmem(2, ZED, LANES),
            vmem(2, ZED, LANES),
            pltpu.VMEM((2, ZED, LANES), jnp.int32),
            pltpu.SemaphoreType.DMA((7,)),
            pltpu.SemaphoreType.DMA((3,)),
        ],
        compiler_params=FIRST_PARAMS,
        name="collide_own",
    )(flow, heat, flow_weight, heat_weight, resistance, conductivity, solid)

    count = lax.axis_size("gy")
    upward = [(i, (i + 1) % count) for i in range(count)]
    from_above = lax.ppermute(down, "gy", [(target, source) for source, target in upward])
    from_below = lax.ppermute(up, "gy", upward)

    own = pl.pallas_call(
        stage_kernel,
        out_shape=floats(2 * FIELDS, ZED, LANES),
        compiler_params=PARAMS,
        cost_estimate=pl.CostEstimate(flops=10**7, bytes_accessed=10**6, transcendentals=0),
        name="stage_own",
    )(own)

    far, strip = pl.pallas_call(
        far_halo_kernel,
        out_shape=(floats(SENT, ZED, LANES), floats(STRIP_ROWS, ZED, LANES)),
        compiler_params=PARAMS,
        name="far_halo",
    )(own, from_below, from_above)
    near = pl.pallas_call(
        near_halo_kernel,
        out_shape=floats(SENT, ZED, LANES),
        compiler_params=PARAMS,
        name="near_halo",
    )(own, strip)

    from_far, from_near = swap_along_x(far, near)

    columns = floats(MEMBERS, 2, ZED, WIDE)
    side_columns = floats(2, 2, ZED, WIDE)
    cells = floats(2, ZED, LANES)
    held = vmem(MEMBERS, 2, ZED, WIDE)
    busy = pl.CostEstimate(flops=10**7, bytes_accessed=10**6, transcendentals=0)

    own_state, own_seed, begin = pl.pallas_call(
        own_step_kernel,
        out_shape=(columns, columns, floats(BEGIN, 2, ZED, LANES)),
        compiler_params=PARAMS,
        cost_estimate=busy,
        name="own_step",
    )(flow, heat, own, strip)

    far_state, far_sides, near_state, near_sides, adjoint, part_resistance, part_conductivity, far = (
        pl.pallas_call(
            step_kernel,
            out_shape=(
                columns, side_columns, columns, side_columns, columns, cells, cells,
                floats(ADJ_SENT, ZED, LANES),
            ),
            scratch_shapes=[held, held, held, held],
            compiler_params=PARAMS,
            name="two_steps",
        )(own, strip, own_state, own_seed, from_far, from_near)
    )

    near = pl.pallas_call(
        near_buffer_kernel,
        out_shape=floats(ADJ_SENT, ZED, LANES),
        compiler_params=PARAMS,
        name="near_buffer",
    )(adjoint)

    from_far, from_near = swap_along_x(far, near)

    terms, own_arrived, own_sums = pl.pallas_call(
        prepare_kernel,
        out_shape=(
            floats(TERMS, 4, ZED, WIDE), floats(MEMBERS, 4, ZED, WIDE), floats(SUMS, 2, ZED, WIDE),
        ),
        compiler_params=PARAMS,
        cost_estimate=busy,
        name="prepare",
    )(own_state, far_state, far_sides, near_state, near_sides, adjoint)

    far_earlier, part_resistance, part_conductivity = pl.pallas_call(
        far_adjoint_kernel,
        out_shape=(columns, cells, cells),
        scratch_shapes=[held],
        compiler_params=PARAMS,
        cost_estimate=busy,
        name="far_adjoint",
    )(terms, own_arrived, own_sums, far_sides, part_resistance, part_conductivity, from_far)

    return pl.pallas_call(
        near_adjoint_kernel,
        out_shape=(cells, cells),
        scratch_shapes=[held, held, vmem(MEMBERS, 2, ZED, LANES), vmem(2, ZED, LANES)],
        compiler_params=PARAMS,
        name="near_adjoint",
    )(
        begin, terms, own_arrived, own_sums, near_sides, far_sides, far_earlier,
        part_resistance, part_conductivity, from_near,
    )


def solution(mesh):
    split = P("gx", None, "gy")
    stacked = P(None, "gx", None, "gy")
    return jax.shard_map(
        on_device,
        mesh=mesh,
        in_specs=(stacked, stacked, stacked, split, split, split, split),
        out_specs=(split, split),
        check_vma=False,
    )
```
